32 devices in a mesh: seq: 8 (over y, x, core), shard: 4 (over z).
Axes of the slice: x: 2, y: 2, z: 4, core: 2. Of those that a mesh axis runs over, the one named last changes fastest.
Arguments:
- tokens: bfloat16 [2, 1024, 2048], P(None, 'seq', 'shard')
- doc_starts: int32 [2, 16], replicated, may hold values from 0 to 1024, as said below
- norm_gain: float32 [2048], replicated, may hold values from 0.5 to 1.5
- query_weight: bfloat16 [2048, 2048], P('seq', 'shard'), may hold values from -0.125 to 0.125
- key_weight: bfloat16 [2048, 2048], P('seq', 'shard'), may hold values from -0.125 to 0.125
- value_weight: bfloat16 [2048, 4096], P('seq', 'shard'), may hold values from -0.125 to 0.125
- outgate_weight: bfloat16 [2048, 4096], P('seq', 'shard'), may hold values from -0.125 to 0.125
- beta_weight: bfloat16 [2048, 16], P('seq', 'shard')
- decay_weight: bfloat16 [2048, 16], P('seq', 'shard'), may hold values from -0.125 to 0.125
- query_conv: bfloat16 [2048, 4], P(('shard', 'seq')), may hold values from -3 to 3
- key_conv: bfloat16 [2048, 4], P(('shard', 'seq')), may hold values from -3 to 3
- value_conv: bfloat16 [4096, 4], P(('shard', 'seq')), may hold values from -3 to 3
- decay_log: float32 [16], replicated, may hold values from -12 to -2
- decay_bias: float32 [16], replicated, may hold values from -1 to 1
- head_gain: float32 [256], replicated, may hold values from 0.5 to 1.5
- output_weight: bfloat16 [4096, 2048], P('shard', 'seq'), may hold values from -0.1875 to 0.1875
- ffn_gain: float32 [2048], replicated, may hold values from 0.5 to 1.5
- gate_weight: bfloat16 [2048, 5632], P('seq', 'shard'), may hold values from -0.125 to 0.125
- up_weight: bfloat16 [2048, 5632], P('seq', 'shard'), may hold values from -0.125 to 0.125
- down_weight: bfloat16 [5632, 2048], P('shard', 'seq'), may hold values from -0.15625 to 0.15625
- cotangent: bfloat16 [2, 1024, 2048], P(None, 'seq', 'shard'), may hold values from -6 to 6
Outputs:
- output: float32 [2, 1024, 2048], P(None, 'seq', 'shard')
- grad_tokens: float32 [2, 1024, 2048], P(None, 'seq', 'shard')
- grad_norm_gain: float32 [2048], replicated
- grad_query_weight: float32 [2048, 2048], P('seq', 'shard')
- grad_key_weight: float32 [2048, 2048], P('seq', 'shard')
- grad_value_weight: float32 [2048, 4096], P('seq', 'shard')
- grad_outgate_weight: float32 [2048, 4096], P('seq', 'shard')
- grad_beta_weight: float32 [2048, 16], P('seq', 'shard')
- grad_decay_weight: float32 [2048, 16], P('seq', 'shard')
- grad_query_conv: float32 [2048, 4], P(('shard', 'seq'))
- grad_key_conv: float32 [2048, 4], P(('shard', 'seq'))
- grad_value_conv: float32 [4096, 4], P(('shard', 'seq'))
- grad_decay_log: float32 [16], replicated
- grad_decay_bias: float32 [16], replicated
- grad_head_gain: float32 [256], replicated
- grad_output_weight: float32 [4096, 2048], P('shard', 'seq')
- grad_ffn_gain: float32 [2048], replicated
- grad_gate_weight: float32 [2048, 5632], P('seq', 'shard')
- grad_up_weight: float32 [2048, 5632], P('seq', 'shard')
- grad_down_weight: float32 [5632, 2048], P('shard', 'seq')
The draws below stay inside these ranges and needn't reach their ends.
Inputs may be any that keep to these rules, and one draw needn't show every extreme that they name: `doc_starts`: each row lists, never falling, the positions at which the documents of that sequence begin: its first entry is 0, and entries equal to 1024 begin nothing. In every draw one sequence, drawn from the seed, is a single document.
All inputs are finite; a program needn't handle non-finite values.
Results may differ from the reference program's by a relative error of at most 0.018.
Values may be sent and summed in bfloat16 or wider, within the bound.
A program may use at most 136 MiB of HBM per device.

```python
import jax
import jax.numpy as jnp
from jax import lax

D = 2048
H = 16
DK = 128
DV = 256
FF = 5632
CONV = 4
SPAN = 64
SEQS = 2
DOCS = 16
LENGTH = 1024
HK = 2048
HV = 4096


def common_signs(key):
    picks = jax.random.randint(jax.random.fold_in(key, 5), (D,), 0, 2)
    return (2 * picks - 1).astype(jnp.float32)


def draw_tokens(key, part):
    signs = common_signs(key)
    key = jax.random.fold_in(key, 11)
    rising = jnp.exp(jnp.log(3.0) * jnp.arange(D, dtype=jnp.float32) / (D - 1))
    shared = 0.5 * signs
    values = jax.random.normal(key, (SEQS, LENGTH, D), jnp.float32) * rising + shared
    return values.astype(jnp.bfloat16)


def draw_beta_weight(key, part):
    signs = common_signs(key)
    key = jax.random.fold_in(key, 37)
    noise = jnp.clip(jax.random.normal(key, (D, H), jnp.float32), -6.0, 6.0)
    order = jax.random.permutation(jax.random.fold_in(key, 1), H)
    chosen = (order < H // 2).astype(jnp.float32)
    offset = -14.0 * signs[:, None] * chosen[None, :] / D
    return (noise * D ** (-0.5) + offset).astype(jnp.bfloat16)


def draw_doc_starts(key, part):
    key = jax.random.fold_in(key, 23)
    single = jax.random.randint(jax.random.fold_in(key, 1), (), 0, SEQS)
    raw_cuts = jax.random.randint(jax.random.fold_in(key, 2), (SEQS, DOCS - 1), 1, LENGTH)
    skewed = raw_cuts * raw_cuts // LENGTH * raw_cuts // LENGTH
    ordered = jnp.sort(skewed, axis=1)
    packed = jnp.concatenate([jnp.zeros((SEQS, 1), jnp.int32), ordered], axis=1)
    columns = jnp.arange(DOCS, dtype=jnp.int32)[None, :]
    whole_row = jnp.where(columns == 0, 0, LENGTH)
    seq_rows = jnp.arange(SEQS, dtype=jnp.int32)[:, None]
    return jnp.where(seq_rows == single, whole_row, packed).astype(jnp.int32)


def block_levels(own_key, extent, cuts, smallest, largest):
    gain = 1.0
    for position, shards_of in cuts:
        steps = jax.random.uniform(jax.random.fold_in(jax.random.fold_in(own_key, 6), position), (shards_of,), jnp.float32, smallest / len(cuts), largest / len(cuts))
        gain = gain * jnp.repeat(jnp.exp(steps), extent[position] // shards_of).reshape((-1,) + (1,) * (len(extent) - 1 - position))
    return gain


def centred(own_key, shape, deviation, most, cuts=(), kind=jnp.bfloat16):
    drawn = deviation * jax.random.normal(own_key, shape, jnp.float32)
    if cuts:
        drawn = drawn * block_levels(own_key, shape, cuts, -0.22, 0.18)
    return jnp.clip(drawn, -most, most).astype(kind)


def setup_inputs(seed: int = 0) -> dict:
    keys = jax.random.split(jax.random.key(seed), 22)
    tokens = draw_tokens(jax.random.fold_in(keys[21], 71), 0)
    doc_starts = draw_doc_starts(jax.random.fold_in(keys[21], 71), 0)
    norm_gain = jnp.clip(1.0 + 0.1 * jax.random.normal(keys[2], (D,), jnp.float32), 0.5, 1.5)
    query_weight = centred(keys[3], (D, HK), D ** -0.5, 0.125, ((0, 8), (1, 4)))
    key_weight = centred(keys[4], (D, HK), D ** -0.5, 0.125, ((0, 8), (1, 4)))
    value_weight = centred(keys[5], (D, HV), D ** -0.5, 0.125, ((0, 8), (1, 4)))
    outgate_weight = centred(keys[6], (D, HV), D ** -0.5, 0.125, ((0, 8), (1, 4)))
    beta_weight = draw_beta_weight(jax.random.fold_in(keys[21], 71), 0)
    decay_weight = centred(keys[8], (D, H), D ** -0.5, 0.125, ((0, 8), (1, 4)))
    query_conv = centred(keys[9], (HK, CONV), CONV ** -0.5, 3.0, ((0, 32),))
    key_conv = centred(keys[10], (HK, CONV), CONV ** -0.5, 3.0, ((0, 32),))
    value_conv = centred(keys[11], (HV, CONV), CONV ** -0.5, 3.0, ((0, 32),))
    decay_log = jnp.clip(jax.random.uniform(keys[12], (H,), jnp.float32, -12.0, -2.0), -12.0, -2.0)
    decay_bias = jnp.clip(jax.random.uniform(keys[13], (H,), jnp.float32, -1.0, 1.0), -1.0, 1.0)
    head_gain = jnp.clip(1.0 + 0.1 * jax.random.normal(keys[14], (DV,), jnp.float32), 0.5, 1.5)
    output_weight = centred(keys[15], (HV, D), (HV // 4) ** -0.5, 0.1875, ((0, 4), (1, 8)))
    ffn_gain = jnp.clip(1.0 + 0.1 * jax.random.normal(keys[16], (D,), jnp.float32), 0.5, 1.5)
    gate_weight = centred(keys[17], (D, FF), D ** -0.5, 0.125, ((0, 8), (1, 4)))
    up_weight = centred(keys[18], (D, FF), D ** -0.5, 0.125, ((0, 8), (1, 4)))
    down_weight = centred(keys[19], (FF, D), (FF // 4) ** -0.5, 0.15625, ((0, 4), (1, 8)))
    cotangent = centred(keys[20], (SEQS, LENGTH, D), 1.0, 6.0, ((1, 8), (2, 4)))
    return dict(tokens=tokens, doc_starts=doc_starts, norm_gain=norm_gain, query_weight=query_weight, key_weight=key_weight, value_weight=value_weight, outgate_weight=outgate_weight, beta_weight=beta_weight, decay_weight=decay_weight, query_conv=query_conv, key_conv=key_conv, value_conv=value_conv, decay_log=decay_log, decay_bias=decay_bias, head_gain=head_gain, output_weight=output_weight, ffn_gain=ffn_gain, gate_weight=gate_weight, up_weight=up_weight, down_weight=down_weight, cotangent=cotangent)


EPSILON = 1e-06
EXACT_PRECISION = lax.Precision.HIGHEST

@jax.custom_vjp
def low(v):
    return lax.optimization_barrier(v.astype(jnp.bfloat16)).astype(jnp.float32)

@jax.custom_vjp
def low_back(v):
    return v

def low_keep(v):
    return (low(v), None)

def low_pass(kept, grad):
    return (grad,)

def back_keep(v):
    return (v, None)

def back_low(kept, grad):
    return (low(grad),)
low.defvjp(low_keep, low_pass)
low_back.defvjp(back_keep, back_low)

def dense(matrix_one, matrix_two):
    return jnp.dot(matrix_one.astype(jnp.float32), matrix_two.astype(jnp.float32), precision=EXACT_PRECISION, preferred_element_type=jnp.float32)

def rms_scale(values, gain_vals):
    return values * lax.rsqrt(lax.optimization_barrier(jnp.mean(values * values, axis=-1, keepdims=True)) + EPSILON) * gain_vals

def unit_rows(values):
    return values * lax.rsqrt(lax.optimization_barrier(jnp.sum(values * values, axis=-1, keepdims=True)) + EPSILON)

def block_terms(input_keys, write_rate, log_decay, keep_flag, doc_ids):
    span_length = input_keys.shape[0]
    cumulative = jnp.cumsum(log_decay, axis=0)
    positions = jnp.arange(span_length, dtype=jnp.int32)
    same_doc = doc_ids[:, None] == doc_ids[None, :]
    causal_mask = (positions[:, None] >= positions[None, :]) & same_doc
    strict_mask = (positions[:, None] > positions[None, :]) & same_doc
    inside = causal_mask.astype(jnp.float32)[:, :, None]
    decay_ratios = jnp.exp(jnp.where(causal_mask[:, :, None], cumulative[:, None, :] - cumulative[None, :, :], 0.0)) * inside
    incoming_decay = jnp.exp(cumulative) * jnp.cumprod(keep_flag)[:, None]
    key_intersection = jnp.einsum('thk,shk->tsh', input_keys, input_keys, precision=EXACT_PRECISION)
    coupling = write_rate[:, None, :] * decay_ratios * key_intersection * strict_mask.astype(jnp.float32)[:, :, None]
    system = jnp.eye(span_length, dtype=jnp.float32)[None] + jnp.transpose(coupling, (2, 0, 1))
    return (decay_ratios, incoming_decay, system)

def block_core(carried_state, input_query, input_keys, values_in, write_rate, log_decay, keep_flag, doc_ids):
    span_length = input_keys.shape[0]
    decay_ratios, incoming_decay, system = block_terms(input_keys, write_rate, log_decay, keep_flag, doc_ids)
    state_readout = jnp.einsum('ijm,jmf->ijf', input_keys, carried_state, precision=EXACT_PRECISION)
    target = write_rate[:, :, None] * (values_in - incoming_decay[:, :, None] * state_readout)
    written_values = lax.linalg.triangular_solve(system, jnp.transpose(target, (1, 0, 2)), left_side=True, lower=True, unit_diagonal=True)
    scores = jnp.einsum('thk,shk->tsh', input_query, input_keys, precision=EXACT_PRECISION) * decay_ratios
    output_rows = incoming_decay[:, :, None] * jnp.einsum('ijm,jmf->ijf', input_query, carried_state, precision=EXACT_PRECISION)
    output_rows = output_rows + jnp.einsum('tsh,hsv->thv', scores, written_values, precision=EXACT_PRECISION)
    closing_state = incoming_decay[span_length - 1][:, None, None] * carried_state
    closing_state = closing_state + jnp.einsum('tg,tgy,gtm->gym', decay_ratios[span_length - 1], input_keys, written_values, precision=EXACT_PRECISION)
    return (closing_state, output_rows)

def block_step(carried_state, pieces):
    return block_core(carried_state, *pieces)

def causal_mix(projected, weights, doc_ids):
    tap_count = weights.shape[1]
    length = projected.shape[0]
    padded = jnp.concatenate([jnp.zeros((tap_count - 1, projected.shape[1]), jnp.float32), projected], axis=0)
    padded_ids = jnp.concatenate([jnp.full((tap_count - 1,), -1, jnp.int32), doc_ids])
    total = jnp.zeros(projected.shape, jnp.float32)
    for tap_index in range(tap_count):
        same_doc = (padded_ids[tap_index:tap_index + length] == doc_ids).astype(jnp.float32)[:, None]
        total = total + padded[tap_index:tap_index + length] * same_doc * weights[:, tap_index]
    return total

def sequence_layer(params, tokens_seq, starts_row):
    norm_gain, query_weight, key_weight, value_weight, outgate_weight, beta_weight, decay_weight, query_conv, key_conv, value_conv, decay_log, decay_bias, head_gain, output_weight, ffn_gain, gate_weight, up_weight, down_weight = params
    length = tokens_seq.shape[0]
    positions = jnp.arange(length, dtype=jnp.int32)
    doc_ids = lax.optimization_barrier(jnp.sum((starts_row[None, :] <= positions[:, None]).astype(jnp.int32), axis=1))
    keep_flag = 1.0 - lax.optimization_barrier(jnp.max((starts_row[None, :] == positions[:, None]).astype(jnp.float32), axis=1))
    normed = low(rms_scale(tokens_seq, norm_gain))
    query_proj = low_back(low(dense(normed, query_weight)))
    key_proj = low_back(low(dense(normed, key_weight)))
    value_proj = low_back(low(dense(normed, value_weight)))
    gate_proj = low_back(dense(normed, outgate_weight))
    beta_proj = low_back(dense(normed, beta_weight))
    decay_proj = low_back(dense(normed, decay_weight))
    query_act = jax.nn.silu(causal_mix(query_proj, query_conv, doc_ids)).reshape(length, H, DK)
    key_act = jax.nn.silu(causal_mix(key_proj, key_conv, doc_ids)).reshape(length, H, DK)
    value_act = jax.nn.silu(causal_mix(value_proj, value_conv, doc_ids)).reshape(length, H, DV)
    input_query = low_back(low(unit_rows(query_act) * DK ** (-0.5)))
    input_keys = low_back(low(unit_rows(key_act)))
    values_in = low_back(low(value_act))
    write_rate = jax.nn.sigmoid(beta_proj)
    log_decay = -jnp.exp(decay_log) * jax.nn.softplus(decay_proj + decay_bias)
    blocks = length // SPAN
    pieces = tuple((member.reshape((blocks, SPAN) + member.shape[1:]) for member in (input_query, input_keys, values_in, write_rate, log_decay, keep_flag, doc_ids)))
    start_state = jnp.zeros((H, DK, DV), jnp.float32)
    last_state, output_rows = lax.scan(jax.checkpoint(block_step), start_state, pieces)
    output_rows = output_rows.reshape(length, H, DV)
    gate_heads = gate_proj.reshape(length, H, DV)
    mixed_out = output_rows * lax.rsqrt(lax.optimization_barrier(jnp.mean(output_rows * output_rows, axis=-1, keepdims=True)) + EPSILON) * head_gain * jax.nn.silu(gate_heads)
    branch = low_back(low(mixed_out)).reshape(length, HV)
    residual = tokens_seq + low_back(dense(branch, output_weight))
    normed_two = low(rms_scale(residual, ffn_gain))
    gate_vals = low_back(dense(normed_two, gate_weight))
    up_vals = low_back(dense(normed_two, up_weight))
    hidden = low(jax.nn.silu(gate_vals) * up_vals)
    return residual + low_back(dense(hidden, down_weight))

def reference(tokens, doc_starts, norm_gain, query_weight, key_weight, value_weight, outgate_weight, beta_weight, decay_weight, query_conv, key_conv, value_conv, decay_log, decay_bias, head_gain, output_weight, ffn_gain, gate_weight, up_weight, down_weight, cotangent):
    weights = tuple((member.astype(jnp.float32) for member in (norm_gain, query_weight, key_weight, value_weight, outgate_weight, beta_weight, decay_weight, query_conv, key_conv, value_conv, decay_log, decay_bias, head_gain, output_weight, ffn_gain, gate_weight, up_weight, down_weight)))

    def forward(tokens_all, *params):

        def one_sequence(seq_pair):
            return sequence_layer(params, seq_pair[0], seq_pair[1])
        return lax.map(jax.checkpoint(one_sequence), (tokens_all, doc_starts))
    output, pullback = jax.vjp(forward, tokens.astype(jnp.float32), *weights)
    gradients = pullback(cotangent.astype(jnp.float32))
    return (output, gradients[0], gradients[1], gradients[2], gradients[3], gradients[4], gradients[5], gradients[6], gradients[7], gradients[8], gradients[9], gradients[10], gradients[11], gradients[12], gradients[13], gradients[14], gradients[15], gradients[16], gradients[17], gradients[18])
```

```python
import functools
import jax, jax.numpy as jnp
from jax import lax
from jax.experimental import pallas as pl
from jax.experimental.pallas import tpu as pltpu
from jax.sharding import PartitionSpec
f32=jnp.float32; bf16=jnp.bfloat16
SPAN=64
EPSILON=1e-6
HI=lax.Precision.HIGHEST

def dg(a,b,ca=1,cb=0):
    return lax.dot_general(a,b,(((ca,),(cb,)),((),())),preferred_element_type=f32)
def halves(x):
    h=x.astype(bf16)
    return h,(x-h.astype(f32)).astype(bf16)
def mm3(a,b,ca=1,cb=0):
    ah,al=halves(a); bh,bl=halves(b)
    return dg(ah,bh,ca,cb)+(dg(al,bh,ca,cb)+dg(ah,bl,ca,cb))
def mm1(a,b,ca=1,cb=0):
    return dg(a.astype(bf16),b.astype(bf16),ca,cb)
def mmx(a,b,ca=1,cb=0):
    return lax.dot_general(a,b,(((ca,),(cb,)),((),())),preferred_element_type=f32,precision=HI)

def square_masks():
    i=lax.broadcasted_iota(jnp.int32,(SPAN,SPAN),0); j=lax.broadcasted_iota(jnp.int32,(SPAN,SPAN),1)
    return i,j
def positions(base,rows,cols,axis):
    return base+lax.broadcasted_iota(jnp.int32,(rows,cols),axis)
def doc_count(starts,pos):
    n=jnp.zeros(pos.shape,jnp.int32)
    for e in range(starts.shape[0]):
        n=n+jnp.where(starts[e]<=pos,1,0)
    return n
def doc_age(starts,pos):
    s=jnp.zeros(pos.shape,jnp.int32)
    for e in range(starts.shape[0]):
        s=jnp.where(starts[e]<=pos,starts[e],s)
    return pos-s
def count_at(starts,p):
    n=jnp.int32(0)
    for e in range(starts.shape[0]):
        n=n+jnp.where(starts[e]<=p,1,0)
    return n
def sigmoid(x):
    return 1.0/(1.0+jnp.exp(-x))
def softplus(x):
    return jnp.maximum(x,0.0)+jnp.log(1.0+jnp.exp(-jnp.abs(x)))

def inverse(A):
    i,j=square_masks()
    near=(i//8)==(j//8)
    eye=jnp.where(i==j,1.0,0.0)
    X=jnp.where(near,-A,0.0); far=jnp.where(near,0.0,A)
    X2=mm3(X,X); X4=mm3(X2,X2)
    Di=eye+X; Di=Di+mm3(Di,X2); Di=Di+mm3(Di,X4)
    Y=-mm3(Di,far)
    Y2=mm3(Y,Y); Y4=mm3(Y2,Y2)
    T=Di+mm3(Y4,Di); T=T+mm3(Y2,T); T=T+mm3(Y,T)
    return T

def span_terms(n,q,k,starts,xc,xr,rate,bias):
    i,j=square_masks()
    base=n*SPAN
    docs=doc_count(starts,positions(base,SPAN,128,0))
    docr=doc_count(starts,positions(base,1,SPAN,1))
    before=count_at(starts,base-1)
    lastdoc=count_at(starts,base+SPAN-1)
    lower=jnp.where(i>=j,1.0,0.0); upper=jnp.where(i<=j,1.0,0.0)
    beta=sigmoid(xc[:,0:1])
    g=-rate*softplus(xc[:,1:2]+bias)
    gr=-rate*softplus(xr[1:2]+bias)
    G=mmx(lower,jnp.broadcast_to(g,(SPAN,128)))
    Gr=mmx(jnp.broadcast_to(gr,(8,SPAN)),upper)[0:1]
    same=docs[:,:SPAN]==docr
    incl=(i>=j)&same
    D=jnp.where(incl,jnp.exp(jnp.where(incl,G[:,:SPAN]-Gr,0.0)),0.0)
    gam=jnp.where(docs==before,jnp.exp(G),0.0)
    end=jnp.where(docs==lastdoc,jnp.exp(G[SPAN-1:SPAN]-G),0.0)
    KK=dg(k,k,1,1); QK=dg(q,k,1,1)
    return beta,g,D,gam,end,KK,QK,i,j

def conv_pre(upad,taps,age,base,rows):
    window=upad[pl.ds(base,rows+8),:]
    pre=window[8:]*taps[3:4]
    for back in range(1,4):
        ok=jnp.where(age>=back,1.0,0.0)
        pre=pre+window[8-back:8-back+rows]*ok*taps[3-back:4-back]
    return pre

def forward_kernel(u_ref,taps_ref,xc_ref,xr_ref,starts,hp,o_ref,q_ref,k_ref,v_ref,s_ref,w_ref,t_ref,qt_ref,mh_ref,ml_ref,upad,un_ref,gc_ref,on_ref):
    L=u_ref.shape[0]; NC=L//SPAN; DV=v_ref.shape[1]; DK=q_ref.shape[1]
    rate=jnp.exp(jnp.full((1,1),hp[0],f32)); bias=hp[1]
    upad[0:8]=jnp.zeros((8,upad.shape[1]),f32)
    taps=taps_ref[...]
    R=128
    def load(c,_):
        upad[pl.ds(pl.multiple_of(8+c*R,8),R),:]=u_ref[pl.ds(pl.multiple_of(c*R,R),R),:].astype(f32)
        return 0
    lax.fori_loop(0,L//R,load,0)
    def conv(c,_):
        base=pl.multiple_of(c*R,R)
        age=doc_age(starts,positions(base,R,128,0))[:,0:1]
        pre=conv_pre(upad,taps,age,base,R)
        act=pre*sigmoid(pre)
        rows=pl.ds(base,R)
        aq=act[:,:DK]; ak=act[:,DK:2*DK]
        q_ref[rows,:]=(aq*lax.rsqrt(jnp.sum(aq*aq,axis=1,keepdims=True)+EPSILON)*DK**-0.5).astype(bf16)
        k_ref[rows,:]=(ak*lax.rsqrt(jnp.sum(ak*ak,axis=1,keepdims=True)+EPSILON)).astype(bf16)
        v_ref[rows,:]=act[:,2*DK:].astype(bf16)
        return 0
    lax.fori_loop(0,L//R,conv,0)
    def local(n,_):
        rows=pl.ds(pl.multiple_of(n*SPAN,SPAN),SPAN)
        q=q_ref[rows,:]; k=k_ref[rows,:]; v=v_ref[rows,:]
        beta,g,D,gam,end,KK,QK,i,j=span_terms(n,q,k,starts,xc_ref[n],xr_ref[n],rate,bias)
        A=jnp.where(i>j,beta*D*KK,0.0)
        T=inverse(A)
        kf=k.astype(f32)
        UW=mm3(T,jnp.concatenate([beta*v.astype(f32),(beta*gam)*kf],axis=1))
        P=QK*D
        PW=mm1(P,UW)
        qt=gam*q.astype(f32)-PW[:,DV:]
        NM=mm3(end*kf,UW,0,0)
        t_ref[n]=T
        on_ref[n]=PW[:,:DV]
        w_ref[n]=UW[:,:DV]
        qt_ref[n,0:SPAN]=qt.astype(bf16)
        qt_ref[n,SPAN:]=UW[:,DV:].astype(bf16)
        un_ref[n]=NM[:,:DV]
        mh,ml=halves(NM[:,DV:])
        mh_ref[n]=mh; ml_ref[n]=ml
        gc_ref[n]=jnp.broadcast_to(gam[SPAN-1:SPAN],(8,128))
        return 0
    lax.fori_loop(0,NC,local,0,unroll=4)
    def chain(n,S):
        s_ref[n]=S
        sh,sl=halves(S); mh=mh_ref[n]; ml=ml_ref[n]
        gc=gc_ref[n][0:1]
        return jnp.concatenate([gc]*(DV//128),axis=1)*S+un_ref[n]-(dg(mh,sh)+(dg(ml,sh)+dg(mh,sl)))
    lax.fori_loop(0,NC,chain,jnp.zeros((DK,DV),f32),unroll=2)
    def emit(n,_):
        rows=pl.ds(pl.multiple_of(n*SPAN,SPAN),SPAN)
        r=dg(qt_ref[n],s_ref[n].astype(bf16))
        o_ref[rows,:]=(on_ref[n]+r[:SPAN]).astype(o_ref.dtype)
        w_ref[n]=w_ref[n]-r[SPAN:]
        return 0
    lax.fori_loop(0,NC,emit,0,unroll=4)

def backward_kernel(do_ref,u_ref,taps_ref,xc_ref,xr_ref,starts,hp,q_ref,k_ref,v_ref,s_ref,w_ref,t_ref,qt_ref,mh_ref,ml_ref,
                    du_ref,dtaps_ref,dx_ref,dh_ref,upad,dpre,ds_ref,dqkv,r_ref,gc_ref):
    L=u_ref.shape[0]; NC=L//SPAN; DV=v_ref.shape[1]; DK=q_ref.shape[1]
    rate=jnp.exp(jnp.full((1,1),hp[0],f32)); bias=hp[1]
    taps=taps_ref[...]
    R=128
    upad[0:8]=jnp.zeros((8,upad.shape[1]),f32)
    dpre[L:L+8]=jnp.zeros((8,upad.shape[1]),f32)
    def load(c,_):
        upad[pl.ds(pl.multiple_of(8+c*R,8),R),:]=u_ref[pl.ds(pl.multiple_of(c*R,R),R),:].astype(f32)
        return 0
    lax.fori_loop(0,L//R,load,0)
    def early(n,_):
        rows=pl.ds(pl.multiple_of(n*SPAN,SPAN),SPAN)
        r_ref[n]=dg(qt_ref[n][0:SPAN],do_ref[rows,:],0,0)
        base=n*SPAN
        G=jnp.sum(-rate*softplus(xc_ref[n][:,1:2]+bias),axis=0,keepdims=True)
        alive=jnp.where(count_at(starts,base+SPAN-1)==count_at(starts,base-1),1.0,0.0)
        gc_ref[n]=jnp.broadcast_to(jnp.exp(G)*alive,(8,128))
        return 0
    lax.fori_loop(0,NC,early,0,unroll=4)
    def chain(m,dS):
        n=NC-1-m
        ds_ref[n]=dS
        sh,sl=halves(dS); mh=mh_ref[n]; ml=ml_ref[n]
        gc=gc_ref[n][0:1]
        return jnp.concatenate([gc]*(DV//128),axis=1)*dS+r_ref[n]-(dg(mh,sh,0,0)+(dg(ml,sh,0,0)+dg(mh,sl,0,0)))
    lax.fori_loop(0,NC,chain,jnp.zeros((DK,DV),f32),unroll=2)
    def local(n,sums):
        rows=pl.ds(pl.multiple_of(n*SPAN,SPAN),SPAN)
        q=q_ref[rows,:]; k=k_ref[rows,:]; v=v_ref[rows,:]; dO=do_ref[rows,:]
        xc=xc_ref[n]
        beta,g,D,gam,end,KK,QK,i,j=span_terms(n,q,k,starts,xc,xr_ref[n],rate,bias)
        S0=s_ref[n]; dS1=ds_ref[n]
        S0h=S0.astype(bf16); dSh=dS1.astype(bf16)
        kf=k.astype(f32); qf=q.astype(f32); vf=v.astype(f32)
        W=w_ref[n].astype(bf16); T=t_ref[n].astype(bf16)
        P=(QK*D).astype(bf16)
        dW=dg(P,dO,0,0)+jnp.concatenate([end]*(DV//128),axis=1)*dg(k,dSh)
        Y=dg(T,dW.astype(bf16),0,0)
        dOY=jnp.concatenate([dO,Y.astype(bf16)],axis=0)
        dPA=dg(dOY,W,1,1)
        GS=dg(dOY,S0h,1,1)
        dOS=GS[:SPAN]; YS=GS[SPAN:]
        Z=dg(W,dSh,1,1)
        dPD=dPA[:SPAN]*D
        EA=jnp.where(i>j,-dPA[SPAN:]*D,0.0)
        E=beta*EA
        A1=jnp.concatenate([dPD,E],axis=0).astype(bf16)
        r1=dg(A1,k)
        r2=dg(A1,jnp.concatenate([q,k],axis=0),0,0)
        dqkv[rows,0:DK]=gam*dOS+r1[:SPAN]
        dqkv[rows,DK:2*DK]=r1[SPAN:]+r2-(beta*gam)*YS+end*Z
        dqkv[rows,2*DK:]=beta*Y
        EK=EA*KK
        kYS=jnp.sum(kf*YS,axis=1,keepdims=True)
        dbeta=jnp.sum(Y*vf,axis=1,keepdims=True)-gam*kYS+jnp.sum(EK,axis=1,keepdims=True)
        Fm=dPD*QK+beta*EK
        dgam=jnp.sum(qf*dOS,axis=1,keepdims=True)-beta*kYS
        dend=jnp.sum(kf*Z,axis=1,keepdims=True)*end
        colsum=mmx(Fm,jnp.ones((SPAN,128),f32),0,0)
        dG=jnp.sum(Fm,axis=1,keepdims=True)-colsum+dgam*gam-dend
        tail=jnp.sum(jnp.sum(S0*dS1,axis=0,keepdims=True),axis=1,keepdims=True)
        last=jnp.sum(dend,axis=0,keepdims=True)+gam[SPAN-1:SPAN]*tail
        row=lax.broadcasted_iota(jnp.int32,(SPAN,128),0)
        dG=dG+jnp.where(row==SPAN-1,last,0.0)
        upper=jnp.where(i<=j,1.0,0.0)
        dlog=mmx(upper,dG)
        dbp=(dbeta*beta*(1.0-beta))
        ddp=dlog*(-rate)*sigmoid(xc[:,1:2]+bias)
        dx_ref[n,:,0:1]=dbp[:,0:1]
        dx_ref[n,:,1:2]=ddp[:,0:1]
        sl,sb=sums
        return (sl+jnp.sum(dlog*g,axis=0,keepdims=True),sb+jnp.sum(ddp,axis=0,keepdims=True))
    zero=jnp.zeros((1,128),f32)
    sl,sb=lax.fori_loop(0,NC,local,(zero,zero),unroll=4)
    dh_ref[0:1]=sl; dh_ref[1:2]=sb
    def norms(c,dt):
        base=pl.multiple_of(c*R,R)
        age=doc_age(starts,positions(base,R,128,0))[:,0:1]
        pre=conv_pre(upad,taps,age,base,R)
        sg=sigmoid(pre); act=pre*sg
        rows=pl.ds(base,R)
        d=dqkv[rows,:]
        def unit_back(a,dd,f):
            s=lax.rsqrt(jnp.sum(a*a,axis=1,keepdims=True)+EPSILON)
            dot=jnp.sum(a*dd,axis=1,keepdims=True)
            return f*(s*dd-a*(s*s*s*dot))
        dact=jnp.concatenate([unit_back(act[:,:DK],d[:,:DK],DK**-0.5),unit_back(act[:,DK:2*DK],d[:,DK:2*DK],1.0),d[:,2*DK:]],axis=1)
        dp=dact*sg*(1.0+pre*(1.0-sg))
        dpre[rows,:]=dp
        window=upad[pl.ds(base,R+8),:]
        new=[]
        for j in range(4):
            back=3-j
            x=window[8-back:8-back+R]
            if back: x=x*jnp.where(age>=back,1.0,0.0)
            new.append(dt[j]+jnp.sum(x*dp,axis=0,keepdims=True))
        return tuple(new)
    zt=jnp.zeros((1,upad.shape[1]),f32)
    dt=lax.fori_loop(0,L//R,norms,(zt,)*4)
    for j in range(4): dtaps_ref[j:j+1]=dt[j]
    def back(c,_):
        base=pl.multiple_of(c*R,R)
        window=dpre[pl.ds(base,R+8),:]
        age=doc_age(starts,positions(base,R+8,128,0))[:,0:1]
        d=window[:R]*taps[3:4]
        for s in range(1,4):
            x=window[s:s+R]*jnp.where(age[s:s+R]>=s,1.0,0.0)
            d=d+x*taps[3-s:4-s]
        du_ref[pl.ds(base,R),:]=d.astype(bf16)
        return 0
    lax.fori_loop(0,L//R,back,0)

SM=pl.BlockSpec(memory_space=pltpu.SMEM); VM=pl.BlockSpec(memory_space=pltpu.VMEM)
def S(shape,dt=f32): return jax.ShapeDtypeStruct(shape,dt)
def forward(u,taps,xc,xr,starts,hp,DK=128,DV=256):
    L=u.shape[0]; NC=L//SPAN; CH=u.shape[1]
    return pl.pallas_call(forward_kernel,name="rec_fwd",
      out_shape=(S((L,DV),bf16),S((L,DK),bf16),S((L,DK),bf16),S((L,DV),bf16),S((NC,DK,DV)),S((NC,SPAN,DV)),S((NC,SPAN,SPAN)),S((NC,2*SPAN,DK),bf16),S((NC,DK,DK),bf16),S((NC,DK,DK),bf16)),
      in_specs=[VM,VM,VM,VM,SM,SM],out_specs=(VM,)*10,
      scratch_shapes=[pltpu.VMEM((L+8,CH),f32),pltpu.VMEM((NC,DK,DV),f32),pltpu.VMEM((NC,8,128),f32),pltpu.VMEM((NC,SPAN,DV),f32)],
      compiler_params=pltpu.CompilerParams(vmem_limit_bytes=56*2**20))(u,taps,xc,xr,starts,hp)
def backward(do,u,taps,xc,xr,starts,hp,saved):
    q,k,v,s,w,t,qt,mh,ml=saved
    L=u.shape[0]; NC=L//SPAN; CH=u.shape[1]; DK=q.shape[1]; DV=v.shape[1]
    return pl.pallas_call(backward_kernel,name="rec_bwd",
      out_shape=(S((L,CH),bf16),S((4,CH)),S((NC,SPAN,2)),S((2,128))),
      in_specs=[VM]*5+[SM]*2+[VM]*9,out_specs=(VM,)*4,
      scratch_shapes=[pltpu.VMEM((L+8,CH),f32),pltpu.VMEM((L+8,CH),f32),pltpu.VMEM((NC,DK,DV),f32),pltpu.VMEM((L,CH),f32),pltpu.VMEM((NC,DK,DV),f32),pltpu.VMEM((NC,8,128),f32)],
      compiler_params=pltpu.CompilerParams(vmem_limit_bytes=56*2**20))(do,u,taps,xc,xr,starts,hp,q,k,v,s,w,t,qt,mh,ml)


def per_device(
    tokens, doc_starts, norm_gain, query_weight, key_weight, value_weight, outgate_weight,
    beta_weight, decay_weight, query_conv, key_conv, value_conv, decay_log, decay_bias, head_gain,
    output_weight, ffn_gain, gate_weight, up_weight, down_weight, cotangent,
):
    seq_count, local_len, feature_part = tokens.shape
    row_count = seq_count * local_len
    shard_count = lax.axis_size("shard")
    shard_pos = lax.axis_index("shard")
    seq_devices = lax.axis_size("seq")
    seq_pos = lax.axis_index("seq")
    model_dim = feature_part * shard_count
    head_count = beta_weight.shape[1]
    key_dim = query_weight.shape[1] // head_count
    value_dim = value_weight.shape[1] // head_count
    tap_count = query_conv.shape[1]
    width_k = head_count * key_dim
    channels = 2 * key_dim + value_dim
    feature_start = shard_pos * feature_part
    head_start = shard_pos * head_count
    pairs = seq_count * head_count
    copies = seq_devices // pairs
    length = local_len * seq_devices
    spans = length // SPAN
    my_pair = seq_pos // copies
    my_seq = my_pair // head_count
    my_head = my_pair % head_count

    def whole_rows(part_rows):
        return lax.all_gather(part_rows, "shard", axis=2, tiled=True)

    def summed_rows(term_rows):
        return lax.psum_scatter(
            term_rows.astype(bf16), "shard", scatter_dimension=2, tiled=True
        ).astype(f32)

    def row_total(partial_rows):
        return lax.psum(partial_rows, "shard")

    def project(a, b):
        return jnp.dot(a, b, preferred_element_type=f32)

    def to_pairs(x):
        y = jnp.moveaxis(x, 2, 1).reshape((pairs,) + (local_len, x.shape[3]))
        y = jnp.repeat(y, copies, axis=0)
        y = lax.all_to_all(y, "seq", 0, 0)
        return y.reshape(length, x.shape[3])

    def from_pairs(x):
        y = x.reshape(seq_devices, local_len, x.shape[1])
        y = lax.all_to_all(y, "seq", 0, 0)[::copies]
        return jnp.moveaxis(y.reshape(seq_count, head_count, local_len, x.shape[1]), 1, 2)

    full_query, full_key, full_value, full_outgate, full_beta, full_decay = (
        lax.all_gather(w, "seq", axis=0, tiled=True)
        for w in (query_weight, key_weight, value_weight, outgate_weight, beta_weight, decay_weight)
    )
    full_qconv, full_kconv, full_vconv = (
        lax.all_gather(w, "seq", axis=0, tiled=True) for w in (query_conv, key_conv, value_conv)
    )
    full_output = lax.all_gather(output_weight, "seq", axis=1, tiled=True)
    full_gate = lax.all_gather(gate_weight, "seq", axis=0, tiled=True)
    full_up = lax.all_gather(up_weight, "seq", axis=0, tiled=True)
    full_down = lax.all_gather(down_weight, "seq", axis=1, tiled=True)

    tokens_local = tokens.astype(f32)
    whole_tokens = whole_rows(tokens).astype(f32)
    scale_one = lax.rsqrt(jnp.mean(whole_tokens * whole_tokens, axis=2, keepdims=True) + EPSILON)
    normed_one = (whole_tokens * scale_one * norm_gain).astype(bf16).reshape(row_count, model_dim)
    shape4 = (seq_count, local_len, head_count, -1)
    query_proj = project(normed_one, full_query).astype(bf16).reshape(shape4)
    key_proj = project(normed_one, full_key).astype(bf16).reshape(shape4)
    value_proj = project(normed_one, full_value).astype(bf16).reshape(shape4)
    gate_proj = project(normed_one, full_outgate).reshape(shape4)
    beta_proj = project(normed_one, full_beta).reshape(shape4)
    decay_proj = project(normed_one, full_decay).reshape(shape4)

    u = to_pairs(jnp.concatenate([query_proj, key_proj, value_proj], axis=3))
    rates = to_pairs(jnp.concatenate([beta_proj, decay_proj], axis=3)).reshape(spans, SPAN, 2)
    rates_t = jnp.swapaxes(rates, 1, 2)
    taps = jnp.concatenate(
        [
            lax.dynamic_slice_in_dim(full_qconv, my_head * key_dim, key_dim),
            lax.dynamic_slice_in_dim(full_kconv, my_head * key_dim, key_dim),
            lax.dynamic_slice_in_dim(full_vconv, my_head * value_dim, value_dim),
        ],
        axis=0,
    ).astype(f32).T
    starts = lax.dynamic_index_in_dim(doc_starts, my_seq, 0, keepdims=False)
    at_head = head_start + my_head
    decay_pair = jnp.concatenate(
        [lax.dynamic_slice_in_dim(decay_log, at_head, 1), lax.dynamic_slice_in_dim(decay_bias, at_head, 1)]
    )
    o_pair, *saved = forward(u, taps, rates, rates_t, starts, decay_pair, key_dim, value_dim)
    o = from_pairs(o_pair).astype(f32)

    rho = lax.rsqrt(jnp.mean(o * o, axis=3, keepdims=True) + EPSILON)
    gate_sig = jax.nn.sigmoid(gate_proj)
    gate_silu = gate_proj * gate_sig
    z = o * rho
    branch = (z * head_gain * gate_silu).astype(bf16).reshape(row_count, head_count * value_dim)
    attn_rows = summed_rows(project(branch, full_output).reshape(seq_count, local_len, model_dim))
    residual = tokens_local + attn_rows
    local_ffn_gain = lax.dynamic_slice_in_dim(ffn_gain, feature_start, feature_part)
    local_norm_gain = lax.dynamic_slice_in_dim(norm_gain, feature_start, feature_part)
    scale_two = lax.rsqrt(row_total(jnp.sum(residual * residual, axis=2)) / model_dim + EPSILON)[:, :, None]
    normed_two = whole_rows((residual * scale_two * local_ffn_gain).astype(bf16)).reshape(row_count, model_dim)
    gate_vals = project(normed_two, full_gate)
    up_vals = project(normed_two, full_up)
    sigmoid_gate = jax.nn.sigmoid(gate_vals)
    gate_act = gate_vals * sigmoid_gate
    hidden = (gate_act * up_vals).astype(bf16)
    output = residual + summed_rows(project(hidden, full_down).reshape(seq_count, local_len, model_dim))

    def scattered(grad, axis):
        return lax.psum_scatter(grad.astype(bf16), "seq", scatter_dimension=axis, tiled=True).astype(f32)

    cot_rows = whole_rows(cotangent).reshape(row_count, model_dim)
    grad_hidden = jnp.einsum("rd,fd->rf", cot_rows, full_down, preferred_element_type=f32)
    out_down = scattered(jnp.einsum("rf,rd->fd", hidden, cot_rows, preferred_element_type=f32), 1)
    grad_gate_vals = (grad_hidden * up_vals * sigmoid_gate * (1.0 + gate_vals * (1.0 - sigmoid_gate))).astype(bf16)
    grad_up_vals = (grad_hidden * gate_act).astype(bf16)
    out_gate = scattered(jnp.einsum("rd,rf->df", normed_two, grad_gate_vals, preferred_element_type=f32), 0)
    out_up = scattered(jnp.einsum("rd,rf->df", normed_two, grad_up_vals, preferred_element_type=f32), 0)
    grad_normed_two = jnp.einsum("rf,df->rd", grad_gate_vals, full_gate, preferred_element_type=f32) + jnp.einsum(
        "rf,df->rd", grad_up_vals, full_up, preferred_element_type=f32
    )
    grad_two = summed_rows(grad_normed_two.reshape(seq_count, local_len, model_dim))
    gained_two = local_ffn_gain * grad_two
    inner_two = row_total(jnp.sum(gained_two * residual, axis=2))[:, :, None] / model_dim
    grad_residual = cotangent.astype(f32) + scale_two * (gained_two - residual * scale_two * scale_two * inner_two)
    grad_ffn_part = jnp.sum(grad_two * residual * scale_two, axis=(0, 1))
    attn_cot = whole_rows(grad_residual.astype(bf16)).reshape(row_count, model_dim)
    out_output = scattered(jnp.einsum("rv,rd->vd", branch, attn_cot, preferred_element_type=f32), 1)
    grad_mixed = (
        jnp.einsum("rd,vd->rv", attn_cot, full_output, preferred_element_type=f32).astype(bf16).astype(f32).reshape(shape4)
    )
    grad_head_gain = jnp.sum(grad_mixed * z * gate_silu, axis=(0, 1, 2))
    dz = grad_mixed * head_gain * gate_silu
    grad_o = (rho * (dz - z * jnp.mean(dz * z, axis=3, keepdims=True))).astype(bf16)
    grad_gate_proj = (grad_mixed * z * head_gain * gate_sig * (1.0 + gate_proj * (1.0 - gate_sig))).astype(bf16)
    grad_gate_proj = grad_gate_proj.reshape(row_count, head_count * value_dim)

    du_pair, dtaps, drates, dhead = backward(
        to_pairs(grad_o), u, taps, rates, rates_t, starts, decay_pair, saved
    )
    du = from_pairs(du_pair)
    drates = from_pairs(drates.reshape(length, 2)).astype(bf16)
    grad_qproj = du[..., :key_dim].reshape(row_count, width_k)
    grad_kproj = du[..., key_dim : 2 * key_dim].reshape(row_count, width_k)
    grad_vproj = du[..., 2 * key_dim :].reshape(row_count, head_count * value_dim)
    grad_beta_proj = drates[..., 0].reshape(row_count, head_count)
    grad_decay_proj = drates[..., 1].reshape(row_count, head_count)

    def weight_grad(grad_cols):
        return scattered(jnp.einsum("rd,rc->dc", normed_one, grad_cols, preferred_element_type=f32), 0)

    def input_grad(grad_cols, weight_full):
        return jnp.einsum("rc,dc->rd", grad_cols, weight_full, preferred_element_type=f32)

    grad_normed_one = (
        input_grad(grad_qproj, full_query)
        + input_grad(grad_kproj, full_key)
        + input_grad(grad_vproj, full_value)
        + input_grad(grad_gate_proj, full_outgate)
        + input_grad(grad_beta_proj, full_beta)
        + input_grad(grad_decay_proj, full_decay)
    )
    grad_one = summed_rows(grad_normed_one.reshape(seq_count, local_len, model_dim))
    gained_one = local_norm_gain * grad_one
    inner_one = row_total(jnp.sum(gained_one * tokens_local, axis=2))[:, :, None] / model_dim
    grad_tokens = grad_residual + scale_one * (gained_one - tokens_local * scale_one * scale_one * inner_one)
    grad_norm_part = jnp.sum(grad_one * tokens_local * scale_one, axis=(0, 1))

    small = dtaps
    tap_all = lax.all_gather(small, "seq")[::copies].reshape(seq_count, head_count, tap_count, channels)
    tap_sum = jnp.sum(tap_all, axis=0)

    def own_rows(part):
        rows = jnp.swapaxes(part, 1, 2).reshape(-1, tap_count)
        count = rows.shape[0] // seq_devices
        return lax.dynamic_slice_in_dim(rows, seq_pos * count, count)

    out_qconv = own_rows(tap_sum[:, :, :key_dim])
    out_kconv = own_rows(tap_sum[:, :, key_dim : 2 * key_dim])
    out_vconv = own_rows(tap_sum[:, :, 2 * key_dim :])

    def place_into(full_length, part_vals, start_at):
        return lax.dynamic_update_slice(jnp.zeros((full_length,), f32), part_vals, (start_at,))

    total_heads = decay_log.shape[0]
    primary = jnp.where(seq_pos % copies == 0, 1.0, 0.0)
    small_sums = lax.psum(
        (
            place_into(model_dim, grad_norm_part, feature_start),
            place_into(model_dim, grad_ffn_part, feature_start),
            grad_head_gain,
            place_into(total_heads, dhead[0, :1] * primary, at_head),
            place_into(total_heads, dhead[1, :1] * primary, at_head),
        ),
        ("seq", "shard"),
    )
    return (
        output, grad_tokens, small_sums[0], weight_grad(grad_qproj), weight_grad(grad_kproj),
        weight_grad(grad_vproj), weight_grad(grad_gate_proj), weight_grad(grad_beta_proj),
        weight_grad(grad_decay_proj), out_qconv, out_kconv, out_vconv, small_sums[3], small_sums[4],
        small_sums[2], out_output, small_sums[1], out_gate, out_up, out_down,
    )


def solution(mesh):
    P = PartitionSpec
    rows, cols = P("seq", "shard"), P("shard", "seq")
    both, acts = P(("shard", "seq"), None), P(None, "seq", "shard")
    return jax.shard_map(
        per_device,
        mesh=mesh,
        in_specs=(acts, P(), P()) + (rows,) * 6 + (both,) * 3 + (P(), P(), P(), cols, P(), rows, rows, cols, acts),
        out_specs=(acts, acts, P()) + (rows,) * 6 + (both,) * 3 + (P(), P(), P(), cols, P(), rows, rows, cols),
        check_vma=False,
    )
```

```python
import functools
import jax, jax.numpy as jnp
from jax import lax
from jax.experimental import pallas as pl
from jax.experimental.pallas import tpu as pltpu
from jax.sharding import PartitionSpec
f32=jnp.float32; bf16=jnp.bfloat16
SPAN=64
EPSILON=1e-6
HI=lax.Precision.HIGHEST

def dg(a,b,ca=1,cb=0):
    return lax.dot_general(a,b,(((ca,),(cb,)),((),())),preferred_element_type=f32)
def halves(x):
    h=x.astype(bf16)
    return h,(x-h.astype(f32)).astype(bf16)
def mm3(a,b,ca=1,cb=0):
    ah,al=halves(a); bh,bl=halves(b)
    return dg(ah,bh,ca,cb)+(dg(al,bh,ca,cb)+dg(ah,bl,ca,cb))
def mm1(a,b,ca=1,cb=0):
    return dg(a.astype(bf16),b.astype(bf16),ca,cb)
def mmx(a,b,ca=1,cb=0):
    return lax.dot_general(a,b,(((ca,),(cb,)),((),())),preferred_element_type=f32,precision=HI)

def square_masks():
    i=lax.broadcasted_iota(jnp.int32,(SPAN,SPAN),0); j=lax.broadcasted_iota(jnp.int32,(SPAN,SPAN),1)
    return i,j
def positions(base,rows,cols,axis):
    return base+lax.broadcasted_iota(jnp.int32,(rows,cols),axis)
def doc_count(starts,pos):
    n=jnp.zeros(pos.shape,jnp.int32)
    for e in range(starts.shape[0]):
        n=n+jnp.where(starts[e]<=pos,1,0)
    return n
def doc_age(starts,pos):
    s=jnp.zeros(pos.shape,jnp.int32)
    for e in range(starts.shape[0]):
        s=jnp.where(starts[e]<=pos,starts[e],s)
    return pos-s
def count_at(starts,p):
    n=jnp.int32(0)
    for e in range(starts.shape[0]):
        n=n+jnp.where(starts[e]<=p,1,0)
    return n
def sigmoid(x):
    return 1.0/(1.0+jnp.exp(-x))
def softplus(x):
    return jnp.maximum(x,0.0)+jnp.log(1.0+jnp.exp(-jnp.abs(x)))

def inverse(A):
    i,j=square_masks()
    near=(i//8)==(j//8)
    eye=jnp.where(i==j,1.0,0.0)
    X=jnp.where(near,-A,0.0); far=jnp.where(near,0.0,A)
    X2=mm3(X,X); X4=mm3(X2,X2)
    Di=eye+X; Di=Di+mm3(Di,X2); Di=Di+mm3(Di,X4)
    Y=-mm3(Di,far)
    Y2=mm3(Y,Y); Y4=mm3(Y2,Y2)
    T=Di+mm3(Y4,Di); T=T+mm3(Y2,T); T=T+mm3(Y,T)
    return T

def span_terms(n,q,k,starts,xc,xr,rate,bias):
    i,j=square_masks()
    base=n*SPAN
    docs=doc_count(starts,positions(base,SPAN,128,0))
    docr=doc_count(starts,positions(base,1,SPAN,1))
    before=count_at(starts,base-1)
    lastdoc=count_at(starts,base+SPAN-1)
    lower=jnp.where(i>=j,1.0,0.0); upper=jnp.where(i<=j,1.0,0.0)
    beta=sigmoid(xc[:,0:1])
    g=-rate*softplus(xc[:,1:2]+bias)
    gr=-rate*softplus(xr[1:2]+bias)
    G=mmx(lower,jnp.broadcast_to(g,(SPAN,128)))
    Gr=mmx(jnp.broadcast_to(gr,(8,SPAN)),upper)[0:1]
    same=docs[:,:SPAN]==docr
    incl=(i>=j)&same
    D=jnp.where(incl,jnp.exp(jnp.where(incl,G[:,:SPAN]-Gr,0.0)),0.0)
    gam=jnp.where(docs==before,jnp.exp(G),0.0)
    end=jnp.where(docs==lastdoc,jnp.exp(G[SPAN-1:SPAN]-G),0.0)
    KK=dg(k,k,1,1); QK=dg(q,k,1,1)
    return beta,g,D,gam,end,KK,QK,i,j

def conv_pre(upad,taps,age,base,rows):
    window=upad[pl.ds(base,rows+8),:]
    pre=window[8:]*taps[3:4]
    for back in range(1,4):
        ok=jnp.where(age>=back,1.0,0.0)
        pre=pre+window[8-back:8-back+rows]*ok*taps[3-back:4-back]
    return pre

def forward_kernel(u_ref,taps_ref,xc_ref,xr_ref,starts,hp,o_ref,q_ref,k_ref,v_ref,s_ref,w_ref,t_ref,qt_ref,mh_ref,ml_ref,upad,un_ref,gc_ref,on_ref):
    L=u_ref.shape[0]; NC=L//SPAN; DV=v_ref.shape[1]; DK=q_ref.shape[1]
    rate=jnp.exp(jnp.full((1,1),hp[0],f32)); bias=hp[1]
    upad[0:8]=jnp.zeros((8,upad.shape[1]),f32)
    taps=taps_ref[...]
    R=128
    def load(c,_):
        upad[pl.ds(pl.multiple_of(8+c*R,8),R),:]=u_ref[pl.ds(pl.multiple_of(c*R,R),R),:].astype(f32)
        return 0
    lax.fori_loop(0,L//R,load,0)
    def conv(c,_):
        base=pl.multiple_of(c*R,R)
        age=doc_age(starts,positions(base,R,128,0))[:,0:1]
        pre=conv_pre(upad,taps,age,base,R)
        act=pre*sigmoid(pre)
        rows=pl.ds(base,R)
        aq=act[:,:DK]; ak=act[:,DK:2*DK]
        q_ref[rows,:]=(aq*lax.rsqrt(jnp.sum(aq*aq,axis=1,keepdims=True)+EPSILON)*DK**-0.5).astype(bf16)
        k_ref[rows,:]=(ak*lax.rsqrt(jnp.sum(ak*ak,axis=1,keepdims=True)+EPSILON)).astype(bf16)
        v_ref[rows,:]=act[:,2*DK:].astype(bf16)
        return 0
    lax.fori_loop(0,L//R,conv,0)
    def local(n,_):
        rows=pl.ds(pl.multiple_of(n*SPAN,SPAN),SPAN)
        q=q_ref[rows,:]; k=k_ref[rows,:]; v=v_ref[rows,:]
        beta,g,D,gam,end,KK,QK,i,j=span_terms(n,q,k,starts,xc_ref[n],xr_ref[n],rate,bias)
        A=jnp.where(i>j,beta*D*KK,0.0)
        T=inverse(A)
        kf=k.astype(f32)
        UW=mm3(T,jnp.concatenate([beta*v.astype(f32),(beta*gam)*kf],axis=1))
        P=QK*D
        PW=mm1(P,UW)
        qt=gam*q.astype(f32)-PW[:,DV:]
        NM=mm3(end*kf,UW,0,0)
        t_ref[n]=T
        on_ref[n]=PW[:,:DV]
        w_ref[n]=UW[:,:DV]
        qt_ref[n,0:SPAN]=qt.astype(bf16)
        qt_ref[n,SPAN:]=UW[:,DV:].astype(bf16)
        un_ref[n]=NM[:,:DV]
        mh,ml=halves(NM[:,DV:])
        mh_ref[n]=mh; ml_ref[n]=ml
        gc_ref[n]=jnp.broadcast_to(gam[SPAN-1:SPAN],(8,128))
        return 0
    lax.fori_loop(0,NC,local,0,unroll=4)
    def chain(n,S):
        s_ref[n]=S
        sh,sl=halves(S); mh=mh_ref[n]; ml=ml_ref[n]
        gc=gc_ref[n][0:1]
        return jnp.concatenate([gc]*(DV//128),axis=1)*S+un_ref[n]-(dg(mh,sh)+(dg(ml,sh)+dg(mh,sl)))
    lax.fori_loop(0,NC,chain,jnp.zeros((DK,DV),f32),unroll=2)
    def emit(n,_):
        rows=pl.ds(pl.multiple_of(n*SPAN,SPAN),SPAN)
        r=dg(qt_ref[n],s_ref[n].astype(bf16))
        o_ref[rows,:]=(on_ref[n]+r[:SPAN]).astype(o_ref.dtype)
        w_ref[n]=w_ref[n]-r[SPAN:]
        return 0
    lax.fori_loop(0,NC,emit,0,unroll=4)

def backward_kernel(do_ref,u_ref,taps_ref,xc_ref,xr_ref,starts,hp,q_ref,k_ref,v_ref,s_ref,w_ref,t_ref,qt_ref,mh_ref,ml_ref,
                    du_ref,dtaps_ref,dx_ref,dh_ref,upad,dpre,ds_ref,dqkv,r_ref,gc_ref):
    L=u_ref.shape[0]; NC=L//SPAN; DV=v_ref.shape[1]; DK=q_ref.shape[1]
    rate=jnp.exp(jnp.full((1,1),hp[0],f32)); bias=hp[1]
    taps=taps_ref[...]
    R=128
    upad[0:8]=jnp.zeros((8,upad.shape[1]),f32)
    dpre[L:L+8]=jnp.zeros((8,upad.shape[1]),f32)
    def load(c,_):
        upad[pl.ds(pl.multiple_of(8+c*R,8),R),:]=u_ref[pl.ds(pl.multiple_of(c*R,R),R),:].astype(f32)
        return 0
    lax.fori_loop(0,L//R,load,0)
    def early(n,_):
        rows=pl.ds(pl.multiple_of(n*SPAN,SPAN),SPAN)
        r_ref[n]=dg(qt_ref[n][0:SPAN],do_ref[rows,:],0,0)
        base=n*SPAN
        G=jnp.sum(-rate*softplus(xc_ref[n][:,1:2]+bias),axis=0,keepdims=True)
        alive=jnp.where(count_at(starts,base+SPAN-1)==count_at(starts,base-1),1.0,0.0)
        gc_ref[n]=jnp.broadcast_to(jnp.exp(G)*alive,(8,128))
        return 0
    lax.fori_loop(0,NC,early,0,unroll=4)
    def chain(m,dS):
        n=NC-1-m
        ds_ref[n]=dS
        sh,sl=halves(dS); mh=mh_ref[n]; ml=ml_ref[n]
        gc=gc_ref[n][0:1]
        return jnp.concatenate([gc]*(DV//128),axis=1)*dS+r_ref[n]-(dg(mh,sh,0,0)+(dg(ml,sh,0,0)+dg(mh,sl,0,0)))
    lax.fori_loop(0,NC,chain,jnp.zeros((DK,DV),f32),unroll=2)
    def local(n,sums):
        rows=pl.ds(pl.multiple_of(n*SPAN,SPAN),SPAN)
        q=q_ref[rows,:]; k=k_ref[rows,:]; v=v_ref[rows,:]; dO=do_ref[rows,:]
        xc=xc_ref[n]
        beta,g,D,gam,end,KK,QK,i,j=span_terms(n,q,k,starts,xc,xr_ref[n],rate,bias)
        S0=s_ref[n]; dS1=ds_ref[n]
        S0h=S0.astype(bf16); dSh=dS1.astype(bf16)
        kf=k.astype(f32); qf=q.astype(f32); vf=v.astype(f32)
        W=w_ref[n].astype(bf16); T=t_ref[n].astype(bf16)
        P=(QK*D).astype(bf16)
        dW=dg(P,dO,0,0)+jnp.concatenate([end]*(DV//128),axis=1)*dg(k,dSh)
        Y=dg(T,dW.astype(bf16),0,0)
        dOY=jnp.concatenate([dO,Y.astype(bf16)],axis=0)
        dPA=dg(dOY,W,1,1)
        GS=dg(dOY,S0h,1,1)
        dOS=GS[:SPAN]; YS=GS[SPAN:]
        Z=dg(W,dSh,1,1)
        dPD=dPA[:SPAN]*D
        EA=jnp.where(i>j,-dPA[SPAN:]*D,0.0)
        E=beta*EA
        A1=jnp.concatenate([dPD,E],axis=0).astype(bf16)
        r1=dg(A1,k)
        r2=dg(A1,jnp.concatenate([q,k],axis=0),0,0)
        dqkv[rows,0:DK]=gam*dOS+r1[:SPAN]
        dqkv[rows,DK:2*DK]=r1[SPAN:]+r2-(beta*gam)*YS+end*Z
        dqkv[rows,2*DK:]=beta*Y
        EK=EA*KK
        kYS=jnp.sum(kf*YS,axis=1,keepdims=True)
        dbeta=jnp.sum(Y*vf,axis=1,keepdims=True)-gam*kYS+jnp.sum(EK,axis=1,keepdims=True)
        Fm=dPD*QK+beta*EK
        dgam=jnp.sum(qf*dOS,axis=1,keepdims=True)-beta*kYS
        dend=jnp.sum(kf*Z,axis=1,keepdims=True)*end
        colsum=mmx(Fm,jnp.ones((SPAN,128),f32),0,0)
        dG=jnp.sum(Fm,axis=1,keepdims=True)-colsum+dgam*gam-dend
        tail=jnp.sum(jnp.sum(S0*dS1,axis=0,keepdims=True),axis=1,keepdims=True)
        last=jnp.sum(dend,axis=0,keepdims=True)+gam[SPAN-1:SPAN]*tail
        row=lax.broadcasted_iota(jnp.int32,(SPAN,128),0)
        dG=dG+jnp.where(row==SPAN-1,last,0.0)
        upper=jnp.where(i<=j,1.0,0.0)
        dlog=mmx(upper,dG)
        dbp=(dbeta*beta*(1.0-beta))
        ddp=dlog*(-rate)*sigmoid(xc[:,1:2]+bias)
        dx_ref[n,:,0:1]=dbp[:,0:1]
        dx_ref[n,:,1:2]=ddp[:,0:1]
        sl,sb=sums
        return (sl+jnp.sum(dlog*g,axis=0,keepdims=True),sb+jnp.sum(ddp,axis=0,keepdims=True))
    zero=jnp.zeros((1,128),f32)
    sl,sb=lax.fori_loop(0,NC,local,(zero,zero),unroll=4)
    dh_ref[0:1]=sl; dh_ref[1:2]=sb
    def norms(c,dt):
        base=pl.multiple_of(c*R,R)
        age=doc_age(starts,positions(base,R,128,0))[:,0:1]
        pre=conv_pre(upad,taps,age,base,R)
        sg=sigmoid(pre); act=pre*sg
        rows=pl.ds(base,R)
        d=dqkv[rows,:]
        def unit_back(a,dd,f):
            s=lax.rsqrt(jnp.sum(a*a,axis=1,keepdims=True)+EPSILON)
            dot=jnp.sum(a*dd,axis=1,keepdims=True)
            return f*(s*dd-a*(s*s*s*dot))
        dact=jnp.concatenate([unit_back(act[:,:DK],d[:,:DK],DK**-0.5),unit_back(act[:,DK:2*DK],d[:,DK:2*DK],1.0),d[:,2*DK:]],axis=1)
        dp=dact*sg*(1.0+pre*(1.0-sg))
        dpre[rows,:]=dp
        window=upad[pl.ds(base,R+8),:]
        new=[]
        for j in range(4):
            back=3-j
            x=window[8-back:8-back+R]
            if back: x=x*jnp.where(age>=back,1.0,0.0)
            new.append(dt[j]+jnp.sum(x*dp,axis=0,keepdims=True))
        return tuple(new)
    zt=jnp.zeros((1,upad.shape[1]),f32)
    dt=lax.fori_loop(0,L//R,norms,(zt,)*4)
    for j in range(4): dtaps_ref[j:j+1]=dt[j]
    def back(c,_):
        base=pl.multiple_of(c*R,R)
        window=dpre[pl.ds(base,R+8),:]
        age=doc_age(starts,positions(base,R+8,128,0))[:,0:1]
        d=window[:R]*taps[3:4]
        for s in range(1,4):
            x=window[s:s+R]*jnp.where(age[s:s+R]>=s,1.0,0.0)
            d=d+x*taps[3-s:4-s]
        du_ref[pl.ds(base,R),:]=d.astype(bf16)
        return 0
    lax.fori_loop(0,L//R,back,0)

SM=pl.BlockSpec(memory_space=pltpu.SMEM); VM=pl.BlockSpec(memory_space=pltpu.VMEM)
def S(shape,dt=f32): return jax.ShapeDtypeStruct(shape,dt)
def forward(u,taps,xc,xr,starts,hp,DK=128,DV=256):
    L=u.shape[0]; NC=L//SPAN; CH=u.shape[1]
    return pl.pallas_call(forward_kernel,name="rec_fwd",
      out_shape=(S((L,DV),bf16),S((L,DK),bf16),S((L,DK),bf16),S((L,DV),bf16),S((NC,DK,DV)),S((NC,SPAN,DV)),S((NC,SPAN,SPAN)),S((NC,2*SPAN,DK),bf16),S((NC,DK,DK),bf16),S((NC,DK,DK),bf16)),
      in_specs=[VM,VM,VM,VM,SM,SM],out_specs=(VM,)*10,
      scratch_shapes=[pltpu.VMEM((L+8,CH),f32),pltpu.VMEM((NC,DK,DV),f32),pltpu.VMEM((NC,8,128),f32),pltpu.VMEM((NC,SPAN,DV),f32)],
      compiler_params=pltpu.CompilerParams(vmem_limit_bytes=56*2**20))(u,taps,xc,xr,starts,hp)
def backward(do,u,taps,xc,xr,starts,hp,saved):
    q,k,v,s,w,t,qt,mh,ml=saved
    L=u.shape[0]; NC=L//SPAN; CH=u.shape[1]; DK=q.shape[1]; DV=v.shape[1]
    return pl.pallas_call(backward_kernel,name="rec_bwd",
      out_shape=(S((L,CH),bf16),S((4,CH)),S((NC,SPAN,2)),S((2,128))),
      in_specs=[VM]*5+[SM]*2+[VM]*9,out_specs=(VM,)*4,
      scratch_shapes=[pltpu.VMEM((L+8,CH),f32),pltpu.VMEM((L+8,CH),f32),pltpu.VMEM((NC,DK,DV),f32),pltpu.VMEM((L,CH),f32),pltpu.VMEM((NC,DK,DV),f32),pltpu.VMEM((NC,8,128),f32)],
      compiler_params=pltpu.CompilerParams(vmem_limit_bytes=56*2**20))(do,u,taps,xc,xr,starts,hp,q,k,v,s,w,t,qt,mh,ml)


MESH=pl.DeviceIdType.MESH
ANY=pl.BlockSpec(memory_space=pl.ANY)

def flip(s,bit):
    return s+bit-2*bit*lax.rem(lax.div(s,bit),2)

def flips(s,mask):
    bit=1
    while bit<=mask:
        if mask&bit: s=flip(s,bit)
        bit*=2
    return s

def greet(n,zc):
    s=lax.axis_index("seq"); z=lax.axis_index("shard")
    bar=pltpu.get_barrier_semaphore()
    for d in range(1,n):
        pl.semaphore_signal(bar,inc=1,device_id={"seq":lax.rem(s+d,n)},device_id_type=MESH)
    for d in range(1,zc):
        pl.semaphore_signal(bar,inc=1,device_id={"shard":lax.rem(z+d,zc)},device_id_type=MESH)
    pl.semaphore_wait(bar,n-1+zc-1)

def links(n):
    return 8 if n==8 else n

class SeqGather:
    def __init__(self,n,src,dst,axis,sems,r0=0,nr=None):
        self.n=n; self.src=src; self.dst=dst; self.axis=axis; self.send,self.recv,self.loc=sems
        self.R,self.C=src.shape
        self.r0=r0; self.nr=self.R if nr is None else nr
        self.s=lax.axis_index("seq")
        self.open=[]
    def slot(self,t,a,b):
        if self.axis==0:
            return self.dst.at[pl.ds(pl.multiple_of(t*self.R+self.r0+a,16),b-a),:]
        return self.dst.at[pl.ds(self.r0+a,b-a),pl.ds(pl.multiple_of(t*self.C,128),self.C)]
    def copy(self,src,t,a,b,k,to):
        c=pltpu.make_async_remote_copy(src_ref=src,dst_ref=self.slot(t,a,b),send_sem=self.send.at[k],recv_sem=self.recv.at[k],device_id={"seq":to},device_id_type=MESH)
        c.start()
        return c
    def pass_on(self,t,a,b,k,to):
        return self.copy(self.slot(t,a,b),t,a,b,k,to)
    def start(self):
        s=self.s; nr=self.nr
        mine=self.src.at[pl.ds(self.r0,nr),:]
        self.own=pltpu.make_async_copy(mine,self.slot(s,0,nr),self.loc)
        self.own.start()
        masks=(2,4) if self.n==8 else range(2,self.n,2)
        self.direct=[self.copy(mine,s,0,nr,i+1,flips(s,m)) for i,m in enumerate(masks)]
        self.open.append(self.copy(mine,s,0,nr,0,flip(s,1)))
    def middle(self):
        s=self.s; nr=self.nr; h=nr//2
        if self.n!=8: return
        x,y=flip(s,2),flip(s,4)
        self.direct[0].wait_recv()
        fa=self.pass_on(x,0,h,3,y)
        self.open.append(self.pass_on(x,0,nr,5,flip(s,1)))
        self.direct[1].wait_recv()
        fb=self.pass_on(y,h,nr,4,x)
        self.open.append(self.pass_on(y,0,nr,6,flip(s,1)))
        self.diag=(fa,fb)
    def late(self):
        s=self.s; nr=self.nr
        if self.n==8:
            for f in self.diag: f.wait_recv()
            self.open.append(self.pass_on(flips(s,6),0,nr,7,flip(s,1)))
            for f in self.diag: f.wait_send()
        else:
            for i,m in enumerate(range(2,self.n,2)):
                self.direct[i].wait_recv()
                self.open.append(self.pass_on(flips(s,m),0,nr,self.n//2+i,flip(s,1)))
        for f in self.direct: f.wait_send()
    def finish(self):
        for f in self.open: f.wait()
        self.own.wait()

class ShardGather:
    def __init__(self,zc,src,dst,send,recv):
        self.zc=zc; self.src=src; self.dst=dst; self.send=send; self.recv=recv
        self.z=lax.axis_index("shard"); self.C=src.shape[1]
    def slot(self):
        return self.dst.at[:,pl.ds(pl.multiple_of(self.z*self.C,128),self.C)]
    def start(self):
        self.own=pltpu.make_async_copy(self.src,self.slot(),self.recv.at[0]); self.own.start()
        self.cs=[]
        for d in range(1,self.zc):
            c=pltpu.make_async_remote_copy(src_ref=self.src,dst_ref=self.slot(),send_sem=self.send.at[d],recv_sem=self.recv.at[d],device_id={"shard":lax.rem(self.z+d,self.zc)},device_id_type=MESH)
            c.start(); self.cs.append(c)
    def finish(self):
        for c in self.cs: c.wait()
        self.own.wait()

class ShardSplit:
    def __init__(self,zc,src,box,send,recv):
        self.zc=zc; self.src=src; self.box=box; self.send=send; self.recv=recv
        self.z=lax.axis_index("shard"); self.C=box.shape[2]
    def start(self):
        C=self.C
        self.own=pltpu.make_async_copy(self.src.at[:,pl.ds(pl.multiple_of(self.z*C,128),C)],self.box.at[0],self.recv.at[0]); self.own.start()
        self.cs=[]
        for d in range(1,self.zc):
            to=lax.rem(self.z+d,self.zc)
            c=pltpu.make_async_remote_copy(src_ref=self.src.at[:,pl.ds(pl.multiple_of(to*C,128),C)],dst_ref=self.box.at[d],send_sem=self.send.at[d],recv_sem=self.recv.at[d],device_id={"shard":to},device_id_type=MESH)
            c.start(); self.cs.append(c)
    def finish(self):
        for c in self.cs: c.wait()
        self.own.wait()

class ShardAll:
    def __init__(self,axis,n,box,send,recv):
        self.axis=axis; self.n=n; self.box=box; self.send=send; self.recv=recv; self.me=lax.axis_index(axis)
    def start(self):
        self.cs=[]
        for d in range(1,self.n):
            c=pltpu.make_async_remote_copy(src_ref=self.box.at[self.me],dst_ref=self.box.at[self.me],send_sem=self.send.at[d],recv_sem=self.recv.at[d],device_id={self.axis:lax.rem(self.me+d,self.n)},device_id_type=MESH)
            c.start(); self.cs.append(c)
    def finish(self):
        for c in self.cs: c.wait()

class ColumnSplit:
    def __init__(self,n,src,dst,send,recv):
        self.n=n; self.src=src; self.dst=dst; self.send=send; self.recv=recv
        self.s=lax.axis_index("seq"); self.C=dst.shape[1]; self.R=src.shape[0]
    def start(self):
        n,s,C,R=self.n,self.s,self.C,self.R
        to_rows=self.dst.at[pl.ds(pl.multiple_of(s*R,16),R),:]
        block=lambda t: self.src.at[:,pl.ds(pl.multiple_of(t*C,128),C)]
        self.own=pltpu.make_async_copy(block(s),to_rows,self.recv.at[0]); self.own.start()
        self.cs=[]
        for d in range(1,n):
            t=lax.rem(s+d,n)
            c=pltpu.make_async_remote_copy(src_ref=block(t),dst_ref=to_rows,send_sem=self.send.at[d],recv_sem=self.recv.at[d],device_id={"seq":t},device_id_type=MESH)
            c.start(); self.cs.append(c)
    def finish(self):
        for c in self.cs: c.wait()
        self.own.wait()

def row_form(cols):
    return mmx(jnp.ones((8,cols.shape[1]),f32),cols,1,1)

def col_form(rows):
    r=rows.shape[1]
    i=lax.broadcasted_iota(jnp.int32,(r,r),0); j=lax.broadcasted_iota(jnp.int32,(r,r),1)
    return mmx(jnp.where(i==j,1.0,0.0),rows,1,1)

def gathers(n,pairs,sems):
    send,recv,loc=sems
    return [SeqGather(n,src,dst,axis,(send.at[i],recv.at[i],loc.at[i])) for i,(src,dst,axis) in enumerate(pairs)]
def gather_sems(n,k):
    return [pltpu.SemaphoreType.DMA((k,links(n))),pltpu.SemaphoreType.DMA((k,links(n))),pltpu.SemaphoreType.DMA((k,))]
def pair_sems(k):
    return [pltpu.SemaphoreType.DMA((k,)),pltpu.SemaphoreType.DMA((k,))]
def each(ops,name):
    for o in ops: getattr(o,name)()

def front_kernel(n,zc,tok,cot,gain,w,wo,normed,scale,cotfull,wfull,wofull,tokfull,zs,zr,cs,cr,*gs):
    greet(n,zc)
    zt=ShardGather(zc,tok,tokfull,zs,zr); zt.start()
    gw=gathers(n,[(w,wfull,0),(wo,wofull,1)],gs)
    each(gw,"start")
    zt.finish()
    zk=ShardGather(zc,cot,cotfull,cs,cr); zk.start()
    rows=tokfull.shape[0]; D=tokfull.shape[1]
    def norm(c,_):
        r=pl.ds(pl.multiple_of(c*32,32),32)
        x=tokfull[r,:].astype(f32)
        sc=lax.rsqrt(jnp.sum(x*x,axis=1,keepdims=True)/D+EPSILON)
        normed[r,:]=(x*sc*gain[...]).astype(bf16)
        scale[r,:]=jnp.broadcast_to(sc,(32,128))
        return 0
    lax.fori_loop(0,rows//32,norm,0)
    each(gw,"middle"); each(gw,"late")
    zk.finish()
    each(gw,"finish")

def attn_out_kernel(n,zc,part,tok,gain,wg,wu,wd,n1,res,scale,nfull,wgfull,wufull,wdfull,n1c,box,sums,nloc,as_,ar,bs,br,cs,cr,es,er,*gs):
    greet(n,zc)
    D=part.shape[1]
    split=ShardSplit(zc,part,box,as_,ar); split.start()
    gw=gathers(n,[(wg,wgfull,0),(wu,wufull,0),(wd,wdfull,1)],gs)
    each(gw,"start")
    cols=ColumnSplit(n,n1,n1c,es,er); cols.start()
    split.finish()
    r=tok[...].astype(f32)
    for d in range(zc): r=r+box[d].astype(f32)
    res[...]=r
    sums[lax.axis_index("shard")]=row_form(r*r)
    tot=ShardAll("shard",zc,sums,bs,br); tot.start(); tot.finish()
    t=sums[0]
    for d in range(1,zc): t=t+sums[d]
    sc=lax.rsqrt(col_form(t)[:,0:1]/D+EPSILON)
    scale[...]=jnp.broadcast_to(sc,scale.shape)
    nloc[...]=(r*sc*gain[...]).astype(bf16)
    zg=ShardGather(zc,nloc,nfull,cs,cr); zg.start()
    each(gw,"middle")
    zg.finish()
    each(gw,"late"); cols.finish(); each(gw,"finish")

def ffn_back_kernel(n,zc,part,res,scale,cot,gain,dg_,du_,hid,bra,n2,gres,afull,gffn,dgfull,dufull,hidfull,brafull,n2c,box,sums,aloc,as_,ar,bs,br,cs,cr,es,er,*gs):
    greet(n,zc)
    D=part.shape[1]
    split=ShardSplit(zc,part,box,as_,ar); split.start()
    gw=gathers(n,[(dg_,dgfull,0),(du_,dufull,0),(hid,hidfull,0),(bra,brafull,0)],gs)
    each(gw,"start")
    cols=ColumnSplit(n,n2,n2c,es,er); cols.start()
    split.finish()
    g=box[0].astype(f32)
    for d in range(1,zc): g=g+box[d].astype(f32)
    r=res[...]; sc=scale[...][:,0:1]
    gained=gain[...]*g
    sums[lax.axis_index("shard")]=row_form(gained*r)
    tot=ShardAll("shard",zc,sums,bs,br); tot.start()
    gffn[...]=jnp.broadcast_to(jnp.sum(g*r*sc,axis=0,keepdims=True),gffn.shape)
    tot.finish()
    t=sums[0]
    for d in range(1,zc): t=t+sums[d]
    inner=col_form(t)[:,0:1]/D
    gr=cot[...].astype(f32)+sc*(gained-r*(sc*sc*inner))
    gres[...]=gr
    aloc[...]=gr.astype(bf16)
    zg=ShardGather(zc,aloc,afull,cs,cr); zg.start()
    each(gw,"middle")
    zg.finish()
    each(gw,"late"); cols.finish(); each(gw,"finish")

def tail_kernel(n,zc,partdx,partout,res,gres,tok,scale,gain,small,dy,cot,att,output,gtok,dyfull,cotc,attc,smalls,totals,box,boxo,sums,as_,ar,bs,br,cs,cr,ds_,dr,es,er,fs,fr,hs,hr,*gs):
    greet(n,zc)
    D=partdx.shape[1]
    split=ShardSplit(zc,partdx,box,as_,ar); split.start()
    gw=gathers(n,[(dy,dyfull,0)],gs)
    each(gw,"start")
    cc=ColumnSplit(n,cot,cotc,ds_,dr); cc.start()
    ca=ColumnSplit(n,att,attc,es,er); ca.start()
    split.finish()
    so=ShardSplit(zc,partout,boxo,fs,fr); so.start()
    g=box[0].astype(f32)
    for d in range(1,zc): g=g+box[d].astype(f32)
    x=tok[...].astype(f32); sc=scale[...][:,0:1]
    gained=gain[...]*g
    sums[lax.axis_index("shard")]=row_form(gained*x)
    tot=ShardAll("shard",zc,sums,bs,br); tot.start()
    me=lax.axis_index("seq")
    smalls[me]=small[...]
    smalls[me,0:1,0:g.shape[1]]=jnp.sum(g*x*sc,axis=0,keepdims=True)
    sa=ShardAll("seq",n,smalls,cs,cr); sa.start()
    tot.finish()
    t=sums[0]
    for d in range(1,zc): t=t+sums[d]
    inner=col_form(t)[:,0:1]/D
    gtok[...]=gres[...]+sc*(gained-x*(sc*sc*inner))
    sa.finish()
    t=smalls[0]
    for d in range(1,n): t=t+smalls[d]
    totals[lax.axis_index("shard")]=t
    za=ShardAll("shard",zc,totals,hs,hr); za.start()
    each(gw,"middle")
    so.finish()
    o=res[...]
    for d in range(zc): o=o+boxo[d].astype(f32)
    output[...]=o
    za.finish()
    each(gw,"late"); cc.finish(); ca.finish(); each(gw,"finish")

def call(name,cid,kernel,args,specs,outs,ospecs,scratch):
    return pl.pallas_call(kernel,name=name,out_shape=tuple(outs),in_specs=specs,out_specs=tuple(ospecs),scratch_shapes=scratch,
      compiler_params=pltpu.CompilerParams(collective_id=cid,has_side_effects=True,vmem_limit_bytes=56*2**20))(*args)

def front(n,zc,tok,cot,gain,w,wo):
    R,F=tok.shape; D=F*zc
    return call("front",1,functools.partial(front_kernel,n,zc),(tok,cot,gain,w,wo),[VM,VM,VM,ANY,ANY],
      [S((R,D),bf16),S((R,128)),S((R,D),bf16),S((w.shape[0]*n,w.shape[1]),bf16),S((wo.shape[0],wo.shape[1]*n),bf16)],[VM,VM,ANY,ANY,ANY],
      [pltpu.VMEM((R,D),bf16)]+pair_sems(zc)*2+gather_sems(n,2))
def attn_out(n,zc,part,tok,gain,wg,wu,wd,n1):
    R,F=tok.shape; D=F*zc
    return call("attn_out",2,functools.partial(attn_out_kernel,n,zc),(part,tok,gain,wg,wu,wd,n1),[ANY,VM,VM]+[ANY]*4,
      [S((R,F)),S((R,128)),S((R,D),bf16),S((wg.shape[0]*n,wg.shape[1]),bf16),S((wu.shape[0]*n,wu.shape[1]),bf16),S((wd.shape[0],wd.shape[1]*n),bf16),S((R*n,D//n),bf16)],
      [VM,VM,VM,ANY,ANY,ANY,ANY],
      [pltpu.VMEM((zc,R,F),bf16),pltpu.VMEM((zc,8,R),f32),pltpu.VMEM((R,F),bf16)]+pair_sems(zc)*3+pair_sems(n)+gather_sems(n,3))
def ffn_back(n,zc,part,res,scale,cot,gain,dg_,du_,hid,bra,n2):
    R,F=cot.shape; D=F*zc
    full=lambda a: S((a.shape[0]*n,a.shape[1]),bf16)
    return call("ffn_back",3,functools.partial(ffn_back_kernel,n,zc),(part,res,scale,cot,gain,dg_,du_,hid,bra,n2),[ANY,VM,VM,VM,VM]+[ANY]*5,
      [S((R,F)),S((R,D),bf16),S((8,F)),full(dg_),full(du_),full(hid),full(bra),S((R*n,D//n),bf16)],[VM,VM,VM]+[ANY]*5,
      [pltpu.VMEM((zc,R,F),bf16),pltpu.VMEM((zc,8,R),f32),pltpu.VMEM((R,F),bf16)]+pair_sems(zc)*3+pair_sems(n)+gather_sems(n,4))
def tail(n,zc,partdx,partout,res,gres,tok,scale,gain,small,dy,cot,att):
    R,F=tok.shape; D=F*zc
    return call("tail",4,functools.partial(tail_kernel,n,zc),(partdx,partout,res,gres,tok,scale,gain,small,dy,cot,att),[ANY,ANY]+[VM]*6+[ANY]*3,
      [S((R,F)),S((R,F)),S((dy.shape[0]*n,dy.shape[1]),bf16),S((R*n,D//n),bf16),S((R*n,D//n),bf16),S((n,)+small.shape),S((zc,)+small.shape)],
      [VM,VM,ANY,ANY,ANY,VM,VM],
      [pltpu.VMEM((zc,R,F),bf16),pltpu.VMEM((zc,R,F),bf16),pltpu.VMEM((zc,8,R),f32)]+pair_sems(zc)*2+pair_sems(n)*3+pair_sems(zc)*2+gather_sems(n,1))


def per_device(
    tokens, doc_starts, norm_gain, query_weight, key_weight, value_weight, outgate_weight,
    beta_weight, decay_weight, query_conv, key_conv, value_conv, decay_log, decay_bias, head_gain,
    output_weight, ffn_gain, gate_weight, up_weight, down_weight, cotangent,
):
    seq_count, local_len, feature_part = tokens.shape
    row_count = seq_count * local_len
    shard_count = lax.axis_size("shard")
    shard_pos = lax.axis_index("shard")
    seq_devices = lax.axis_size("seq")
    seq_pos = lax.axis_index("seq")
    model_dim = feature_part * shard_count
    head_count = beta_weight.shape[1]
    key_dim = query_weight.shape[1] // head_count
    value_dim = value_weight.shape[1] // head_count
    tap_count = query_conv.shape[1]
    width_k = head_count * key_dim
    channels = 2 * key_dim + value_dim
    feature_start = shard_pos * feature_part
    head_start = shard_pos * head_count
    pairs = seq_count * head_count
    copies = seq_devices // pairs
    length = local_len * seq_devices
    spans = length // SPAN
    my_pair = seq_pos // copies
    my_seq = my_pair // head_count
    my_head = my_pair % head_count

    def project(a, b):
        return jnp.dot(a, b, preferred_element_type=f32)

    def to_pairs(x):
        y = jnp.moveaxis(x, 2, 1).reshape((pairs,) + (local_len, x.shape[3]))
        y = jnp.repeat(y, copies, axis=0)
        y = lax.all_to_all(y, "seq", 0, 0)
        return y.reshape(length, x.shape[3])

    def from_pairs(x):
        y = x.reshape(seq_devices, local_len, x.shape[1])
        y = lax.all_to_all(y, "seq", 0, 0)[::copies]
        return jnp.moveaxis(y.reshape(seq_count, head_count, local_len, x.shape[1]), 1, 2)

    taps_local = jnp.concatenate([query_conv, key_conv, value_conv], axis=0)
    tap_rows = taps_local.shape[0]
    width_v = head_count * value_dim
    widths = [width_k, width_k, width_v, width_v, head_count, head_count]
    edges = [sum(widths[:i]) for i in range(7)]
    filled = edges[6] + tap_count
    padding = -filled % 128
    taps_padded = jnp.pad(taps_local, ((0, query_weight.shape[0] - tap_rows), (0, padding)))
    weights_one = jnp.concatenate(
        [query_weight, key_weight, value_weight, outgate_weight, beta_weight, decay_weight, taps_padded], axis=1
    )
    flat = lambda x: x.reshape(row_count, x.shape[2])
    local_ffn_gain = lax.dynamic_slice_in_dim(ffn_gain, feature_start, feature_part)[None]
    local_norm_gain = lax.dynamic_slice_in_dim(norm_gain, feature_start, feature_part)[None]
    tokens_flat, cot_flat = flat(tokens), flat(cotangent)
    normed_one, scale_one, cot_rows, full_one, full_output = front(
        seq_devices, shard_count, tokens_flat, cot_flat, norm_gain[None], weights_one, output_weight
    )
    proj = project(normed_one, full_one)
    shape4 = (seq_count, local_len, head_count, -1)
    part = lambda i: proj[:, edges[i] : edges[i + 1]].reshape(shape4)
    query_proj, key_proj, value_proj = (part(i).astype(bf16) for i in range(3))
    gate_proj, beta_proj, decay_proj = (part(i) for i in range(3, 6))
    all_taps = full_one[:, edges[6] : filled].reshape(seq_devices, -1, tap_count)
    count_q, count_v = query_conv.shape[0], value_conv.shape[0]
    full_qconv = all_taps[:, :count_q].reshape(-1, tap_count)
    full_kconv = all_taps[:, count_q : 2 * count_q].reshape(-1, tap_count)
    full_vconv = all_taps[:, 2 * count_q : tap_rows].reshape(-1, tap_count)

    u = to_pairs(jnp.concatenate([query_proj, key_proj, value_proj], axis=3))
    rates = to_pairs(jnp.concatenate([beta_proj, decay_proj], axis=3)).reshape(spans, SPAN, 2)
    rates_t = jnp.swapaxes(rates, 1, 2)
    taps = jnp.concatenate(
        [
            lax.dynamic_slice_in_dim(full_qconv, my_head * key_dim, key_dim),
            lax.dynamic_slice_in_dim(full_kconv, my_head * key_dim, key_dim),
            lax.dynamic_slice_in_dim(full_vconv, my_head * value_dim, value_dim),
        ],
        axis=0,
    ).astype(f32).T
    starts = lax.dynamic_index_in_dim(doc_starts, my_seq, 0, keepdims=False)
    at_head = head_start + my_head
    decay_pair = jnp.concatenate(
        [lax.dynamic_slice_in_dim(decay_log, at_head, 1), lax.dynamic_slice_in_dim(decay_bias, at_head, 1)]
    )
    o_pair, *saved = forward(u, taps, rates, rates_t, starts, decay_pair, key_dim, value_dim)
    o = from_pairs(o_pair).astype(f32)

    rho = lax.rsqrt(jnp.mean(o * o, axis=3, keepdims=True) + EPSILON)
    gate_sig = jax.nn.sigmoid(gate_proj)
    gate_silu = gate_proj * gate_sig
    z = o * rho
    branch = (z * head_gain * gate_silu).astype(bf16).reshape(row_count, width_v)
    attn_part = project(branch, full_output).astype(bf16)
    residual, scale_two, normed_two, full_gate, full_up, full_down, normed_one_cols = attn_out(
        seq_devices, shard_count, attn_part, tokens_flat, local_ffn_gain, gate_weight, up_weight, down_weight, normed_one
    )
    gate_vals = project(normed_two, full_gate)
    up_vals = project(normed_two, full_up)
    sigmoid_gate = jax.nn.sigmoid(gate_vals)
    gate_act = gate_vals * sigmoid_gate
    hidden = (gate_act * up_vals).astype(bf16)
    out_part = project(hidden, full_down).astype(bf16)

    def back(cols, weight):
        return jnp.einsum("rc,dc->rd", cols, weight, preferred_element_type=f32)

    def grad(left, right):
        return jnp.einsum("rd,rc->dc", left, right, preferred_element_type=f32)

    grad_hidden = back(cot_rows, full_down)
    grad_gate_vals = (grad_hidden * up_vals * sigmoid_gate * (1.0 + gate_vals * (1.0 - sigmoid_gate))).astype(bf16)
    grad_up_vals = (grad_hidden * gate_act).astype(bf16)
    two_part = (back(grad_gate_vals, full_gate) + back(grad_up_vals, full_up)).astype(bf16)
    grad_residual, attn_cot, grad_ffn_part, dgate_all, dup_all, hidden_all, branch_all, normed_two_cols = ffn_back(
        seq_devices, shard_count, two_part, residual, scale_two, cot_flat, local_ffn_gain,
        grad_gate_vals, grad_up_vals, hidden, branch, normed_two,
    )
    out_gate, out_up = grad(normed_two_cols, dgate_all), grad(normed_two_cols, dup_all)
    grad_mixed = (
        back(attn_cot, full_output).astype(bf16).astype(f32).reshape(shape4)
    )
    grad_head_gain = jnp.sum(grad_mixed * z * gate_silu, axis=(0, 1, 2))
    dz = grad_mixed * head_gain * gate_silu
    grad_o = (rho * (dz - z * jnp.mean(dz * z, axis=3, keepdims=True))).astype(bf16)
    grad_gate_proj = (grad_mixed * z * head_gain * gate_sig * (1.0 + gate_proj * (1.0 - gate_sig))).astype(bf16)
    grad_gate_proj = grad_gate_proj.reshape(row_count, head_count * value_dim)

    du_pair, dtaps, drates, dhead = backward(
        to_pairs(grad_o), u, taps, rates, rates_t, starts, decay_pair, saved
    )
    du = from_pairs(du_pair)
    drates = from_pairs(drates.reshape(length, 2)).astype(bf16)
    grad_qproj = du[..., :key_dim].reshape(row_count, width_k)
    grad_kproj = du[..., key_dim : 2 * key_dim].reshape(row_count, width_k)
    grad_vproj = du[..., 2 * key_dim :].reshape(row_count, head_count * value_dim)
    grad_beta_proj = drates[..., 0].reshape(row_count, head_count)
    grad_decay_proj = drates[..., 1].reshape(row_count, head_count)

    grad_one = jnp.concatenate(
        [
            grad_qproj, grad_kproj, grad_vproj, grad_gate_proj, grad_beta_proj, grad_decay_proj,
            jnp.zeros((row_count, tap_count + padding), bf16),
        ],
        axis=1,
    )
    one_part = back(grad_one, full_one).astype(bf16)
    primary = jnp.where(seq_pos % copies == 0, 1.0, 0.0)
    total_heads = decay_log.shape[0]
    width_s = max(feature_part, channels)
    widen = lambda x: jnp.pad(x, ((0, 0), (0, width_s - x.shape[1])))
    heads_row = lax.dynamic_update_slice(
        lax.dynamic_update_slice(jnp.zeros((1, width_s), f32), dhead[0:1, :1] * primary, (0, at_head)),
        dhead[1:2, :1] * primary,
        (0, total_heads + at_head),
    )
    small = jnp.concatenate(
        [jnp.zeros((1, width_s), f32), widen(grad_ffn_part[:1]), widen(grad_head_gain[None]), heads_row, widen(dtaps)], axis=0
    )
    output, grad_tokens, one_all, cot_cols, attn_cols, smalls, totals = tail(
        seq_devices, shard_count, one_part, out_part, residual, grad_residual, tokens_flat, scale_one,
        local_norm_gain, small, grad_one, cot_rows, attn_cot,
    )
    outs_one = [grad(normed_one_cols, one_all[:, edges[i] : edges[i + 1]]) for i in range(6)]
    out_down = grad(hidden_all, cot_cols)
    out_output = grad(branch_all, attn_cols)
    tap_sum = jnp.sum(smalls[::copies, 4:].reshape(seq_count, head_count, tap_count, width_s), axis=0)

    def own_rows(taps_part):
        rows = jnp.swapaxes(taps_part, 1, 2).reshape(-1, tap_count)
        count = rows.shape[0] // seq_devices
        return lax.dynamic_slice_in_dim(rows, seq_pos * count, count)

    out_qconv = own_rows(tap_sum[:, :, :key_dim])
    out_kconv = own_rows(tap_sum[:, :, key_dim : 2 * key_dim])
    out_vconv = own_rows(tap_sum[:, :, 2 * key_dim : channels])
    out_norm = totals[:, 0, :feature_part].reshape(-1)
    out_ffn = totals[:, 1, :feature_part].reshape(-1)
    totals_all = jnp.sum(totals, axis=0)
    out_head = totals_all[2, :value_dim]
    out_log = totals_all[3, :total_heads]
    out_bias = totals_all[3, total_heads : 2 * total_heads]
    shape3 = (seq_count, local_len, feature_part)
    return (
        output.reshape(shape3), grad_tokens.reshape(shape3), out_norm, *outs_one, out_qconv, out_kconv, out_vconv,
        out_log, out_bias, out_head, out_output, out_ffn, out_gate, out_up, out_down,
    )


def solution(mesh):
    P = PartitionSpec
    rows, cols = P("seq", "shard"), P("shard", "seq")
    both, acts = P(("shard", "seq"), None), P(None, "seq", "shard")
    return jax.shard_map(
        per_device,
        mesh=mesh,
        in_specs=(acts, P(), P()) + (rows,) * 6 + (both,) * 3 + (P(), P(), P(), cols, P(), rows, rows, cols, acts),
        out_specs=(acts, acts, P()) + (rows,) * 6 + (both,) * 3 + (P(), P(), P(), cols, P(), rows, rows, cols),
        check_vma=False,
    )
```

```python
import functools
import jax, jax.numpy as jnp
from jax import lax
from jax.experimental import pallas as pl
from jax.experimental.pallas import tpu as pltpu
from jax.sharding import PartitionSpec
f32=jnp.float32; bf16=jnp.bfloat16
SPAN=64
EPSILON=1e-6
HI=lax.Precision.HIGHEST

def dg(a,b,ca=1,cb=0):
    return lax.dot_general(a,b,(((ca,),(cb,)),((),())),preferred_element_type=f32)
def halves(x):
    h=x.astype(bf16)
    return h,(x-h.astype(f32)).astype(bf16)
def mm3(a,b,ca=1,cb=0):
    ah,al=halves(a); bh,bl=halves(b)
    return dg(ah,bh,ca,cb)+(dg(al,bh,ca,cb)+dg(ah,bl,ca,cb))
def mm1(a,b,ca=1,cb=0):
    return dg(a.astype(bf16),b.astype(bf16),ca,cb)
def mmx(a,b,ca=1,cb=0):
    return lax.dot_general(a,b,(((ca,),(cb,)),((),())),preferred_element_type=f32,precision=HI)

def square_masks():
    i=lax.broadcasted_iota(jnp.int32,(SPAN,SPAN),0); j=lax.broadcasted_iota(jnp.int32,(SPAN,SPAN),1)
    return i,j
def positions(base,rows,cols,axis):
    return base+lax.broadcasted_iota(jnp.int32,(rows,cols),axis)
def doc_count(starts,pos):
    n=jnp.zeros(pos.shape,jnp.int32)
    for e in range(starts.shape[0]):
        n=n+jnp.where(starts[e]<=pos,1,0)
    return n
def doc_age(starts,pos):
    s=jnp.zeros(pos.shape,jnp.int32)
    for e in range(starts.shape[0]):
        s=jnp.where(starts[e]<=pos,starts[e],s)
    return pos-s
def count_at(starts,p):
    n=jnp.int32(0)
    for e in range(starts.shape[0]):
        n=n+jnp.where(starts[e]<=p,1,0)
    return n
def sigmoid(x):
    return 1.0/(1.0+jnp.exp(-x))
def softplus(x):
    return jnp.maximum(x,0.0)+jnp.log(1.0+jnp.exp(-jnp.abs(x)))

def inverse(A):
    i,j=square_masks()
    near=(i//8)==(j//8)
    eye=jnp.where(i==j,1.0,0.0)
    X=jnp.where(near,-A,0.0); far=jnp.where(near,0.0,A)
    X2=mm3(X,X); X4=mm3(X2,X2)
    Di=eye+X; Di=Di+mm3(Di,X2); Di=Di+mm3(Di,X4)
    Y=-mm3(Di,far)
    Y2=mm3(Y,Y); Y4=mm3(Y2,Y2)
    T=Di+mm3(Y4,Di); T=T+mm3(Y2,T); T=T+mm3(Y,T)
    return T

def span_terms(n,q,k,starts,xc,xr,rate,bias):
    i,j=square_masks()
    base=n*SPAN
    docs=doc_count(starts,positions(base,SPAN,128,0))
    docr=doc_count(starts,positions(base,1,SPAN,1))
    before=count_at(starts,base-1)
    lastdoc=count_at(starts,base+SPAN-1)
    lower=jnp.where(i>=j,1.0,0.0); upper=jnp.where(i<=j,1.0,0.0)
    beta=sigmoid(xc[:,0:1])
    g=-rate*softplus(xc[:,1:2]+bias)
    gr=-rate*softplus(xr+bias)
    G=mmx(lower,jnp.broadcast_to(g,(SPAN,128)))
    Gr=mmx(jnp.broadcast_to(gr,(8,SPAN)),upper)[0:1]
    same=docs[:,:SPAN]==docr
    incl=(i>=j)&same
    D=jnp.where(incl,jnp.exp(jnp.where(incl,G[:,:SPAN]-Gr,0.0)),0.0)
    gam=jnp.where(docs==before,jnp.exp(G),0.0)
    end=jnp.where(docs==lastdoc,jnp.exp(G[SPAN-1:SPAN]-G),0.0)
    KK=dg(k,k,1,1); QK=dg(q,k,1,1)
    return beta,g,D,gam,end,KK,QK,i,j

def conv_pre(upad,taps,age,base,rows):
    window=upad[pl.ds(base,rows+8),:]
    pre=window[8:]*taps[3:4]
    for back in range(1,4):
        ok=jnp.where(age>=back,1.0,0.0)
        pre=pre+window[8-back:8-back+rows]*ok*taps[3-back:4-back]
    return pre

def forward_kernel(n,copies,heads,proj,rows_in,taps_ref,starts,hp,wg,wo,n1,
                   oall,u_ref,xr_ref,xc_ref,q_ref,k_ref,v_ref,s_ref,w_ref,t_ref,qt_ref,mh_ref,ml_ref,wgfull,wofull,n1c,
                   upad,un_ref,gc_ref,on_ref,o_ref,is_,ir,os_,or_,es,er,*gs):
    L=u_ref.shape[0]; NC=L//SPAN; DV=v_ref.shape[1]; DK=q_ref.shape[1]; local_len=L//n; per=local_len//SPAN
    greet(n,1)
    inward=ToPairs(n,copies,heads,local_len,proj,rows_in,u_ref,xr_ref,DK,DV,is_,ir); inward.start()
    gw=gathers(n,[(wg,wgfull,0),(wo,wofull,1)],gs)
    inward.finish()
    each(gw,"start")
    cols=ColumnSplit(n,n1,n1c,es,er); cols.start()
    rate=jnp.exp(jnp.full((1,1),hp[0],f32)); bias=hp[1]
    upad[0:8]=jnp.zeros((8,upad.shape[1]),f32)
    def turn(m,_):
        xc_ref[pl.ds(pl.multiple_of(m*local_len,local_len),local_len),:]=col_form(xr_ref[pl.ds(pl.multiple_of(m*8,8),8),:])
        return 0
    lax.fori_loop(0,n,turn,0,unroll=2)
    taps=taps_ref[...]
    R=128
    def load(c,_):
        upad[pl.ds(pl.multiple_of(8+c*R,8),R),:]=u_ref[pl.ds(pl.multiple_of(c*R,R),R),:].astype(f32)
        return 0
    lax.fori_loop(0,L//R,load,0)
    def conv(c,_):
        base=pl.multiple_of(c*R,R)
        age=doc_age(starts,positions(base,R,128,0))[:,0:1]
        pre=conv_pre(upad,taps,age,base,R)
        act=pre*sigmoid(pre)
        rows=pl.ds(base,R)
        aq=act[:,:DK]; ak=act[:,DK:2*DK]
        q_ref[rows,:]=(aq*lax.rsqrt(jnp.sum(aq*aq,axis=1,keepdims=True)+EPSILON)*DK**-0.5).astype(bf16)
        k_ref[rows,:]=(ak*lax.rsqrt(jnp.sum(ak*ak,axis=1,keepdims=True)+EPSILON)).astype(bf16)
        v_ref[rows,:]=act[:,2*DK:].astype(bf16)
        return 0
    lax.fori_loop(0,L//R,conv,0)
    def one_span(n,xr):
        rows=pl.ds(pl.multiple_of(n*SPAN,SPAN),SPAN)
        q=q_ref[rows,:]; k=k_ref[rows,:]; v=v_ref[rows,:]
        beta,g,D,gam,end,KK,QK,i,j=span_terms(n,q,k,starts,xc_ref[rows,:],xr,rate,bias)
        A=jnp.where(i>j,beta*D*KK,0.0)
        T=inverse(A)
        kf=k.astype(f32)
        UW=mm3(T,jnp.concatenate([beta*v.astype(f32),(beta*gam)*kf],axis=1))
        P=QK*D
        PW=mm1(P,UW)
        qt=gam*q.astype(f32)-PW[:,DV:]
        NM=mm3(end*kf,UW,0,0)
        t_ref[n]=T
        on_ref[n]=PW[:,:DV]
        w_ref[n]=UW[:,:DV]
        qt_ref[n,0:SPAN]=qt.astype(bf16)
        qt_ref[n,SPAN:]=UW[:,DV:].astype(bf16)
        un_ref[n]=NM[:,:DV]
        mh,ml=halves(NM[:,DV:])
        mh_ref[n]=mh; ml_ref[n]=ml
        gc_ref[n]=jnp.broadcast_to(gam[SPAN-1:SPAN],(8,128))
    def local(m,_):
        xr=xr_ref[pl.ds(pl.multiple_of(m*8,8),8),:]
        for e in range(per): one_span(m*per+e,xr[1:2,e*SPAN:(e+1)*SPAN])
        return 0
    lax.fori_loop(0,n,local,0,unroll=2)
    each(gw,"middle")
    def chain(n,S):
        s_ref[n]=S
        sh,sl=halves(S); mh=mh_ref[n]; ml=ml_ref[n]
        gc=gc_ref[n][0:1]
        return jnp.concatenate([gc]*(DV//128),axis=1)*S+un_ref[n]-(dg(mh,sh)+(dg(ml,sh)+dg(mh,sl)))
    lax.fori_loop(0,NC,chain,jnp.zeros((DK,DV),f32),unroll=2)
    def emit(n,_):
        rows=pl.ds(pl.multiple_of(n*SPAN,SPAN),SPAN)
        r=dg(qt_ref[n],s_ref[n].astype(bf16))
        o_ref[rows,:]=(on_ref[n]+r[:SPAN]).astype(o_ref.dtype)
        w_ref[n]=w_ref[n]-r[SPAN:]
        return 0
    lax.fori_loop(0,NC,emit,0,unroll=4)
    outward=FromPairs(n,copies,heads,local_len,[(o_ref,lambda t: (pl.ds(pl.multiple_of(t*local_len,local_len),local_len),slice(None)),
        oall,lambda seq,head: (pl.ds(pl.multiple_of(seq*local_len,local_len),local_len),pl.ds(pl.multiple_of(head*DV,128),DV)))],os_,or_)
    outward.start()
    each(gw,"late"); outward.finish(); cols.finish(); each(gw,"finish")

def backward_kernel(n,copies,heads,dall,u_ref,taps_ref,xc_ref,xr_ref,starts,hp,q_ref,k_ref,v_ref,s_ref,w_ref,t_ref,qt_ref,mh_ref,ml_ref,hid,bra,dgp,
                    duall,rows_out,dtaps_ref,dh_ref,hidfull,brafull,dgpfull,upad,dpre,ds_ref,dqkv,r_ref,gc_ref,do_ref,du_ref,dx_ref,dxr,is_,ir,os_,or_,*gs):
    L=u_ref.shape[0]; NC=L//SPAN; DV=v_ref.shape[1]; DK=q_ref.shape[1]; local_len=L//n; per=local_len//SPAN
    greet(n,1)
    inward=ToPairs(n,copies,heads,local_len,dall,None,do_ref,None,DK,DV,is_,ir); inward.start()
    gw=gathers(n,[(hid,hidfull,0),(bra,brafull,0),(dgp,dgpfull,0)],gs)
    rate=jnp.exp(jnp.full((1,1),hp[0],f32)); bias=hp[1]
    taps=taps_ref[...]
    R=128
    upad[0:8]=jnp.zeros((8,upad.shape[1]),f32)
    dpre[L:L+8]=jnp.zeros((8,upad.shape[1]),f32)
    def load(c,_):
        upad[pl.ds(pl.multiple_of(8+c*R,8),R),:]=u_ref[pl.ds(pl.multiple_of(c*R,R),R),:].astype(f32)
        return 0
    lax.fori_loop(0,L//R,load,0)
    inward.finish()
    each(gw,"start")
    dx_ref[...]=jnp.zeros(dx_ref.shape,f32)
    def early(n,_):
        rows=pl.ds(pl.multiple_of(n*SPAN,SPAN),SPAN)
        r_ref[n]=dg(qt_ref[n][0:SPAN],do_ref[rows,:],0,0)
        base=n*SPAN
        G=jnp.sum(-rate*softplus(xc_ref[rows,1:2]+bias),axis=0,keepdims=True)
        alive=jnp.where(count_at(starts,base+SPAN-1)==count_at(starts,base-1),1.0,0.0)
        gc_ref[n]=jnp.broadcast_to(jnp.exp(G)*alive,(8,128))
        return 0
    lax.fori_loop(0,NC,early,0,unroll=4)
    def chain(m,dS):
        n=NC-1-m
        ds_ref[n]=dS
        sh,sl=halves(dS); mh=mh_ref[n]; ml=ml_ref[n]
        gc=gc_ref[n][0:1]
        return jnp.concatenate([gc]*(DV//128),axis=1)*dS+r_ref[n]-(dg(mh,sh,0,0)+(dg(ml,sh,0,0)+dg(mh,sl,0,0)))
    lax.fori_loop(0,NC,chain,jnp.zeros((DK,DV),f32),unroll=2)
    each(gw,"middle")
    def one_span(n,xr,sums):
        rows=pl.ds(pl.multiple_of(n*SPAN,SPAN),SPAN)
        q=q_ref[rows,:]; k=k_ref[rows,:]; v=v_ref[rows,:]; dO=do_ref[rows,:]
        xc=xc_ref[rows,:]
        beta,g,D,gam,end,KK,QK,i,j=span_terms(n,q,k,starts,xc,xr,rate,bias)
        S0=s_ref[n]; dS1=ds_ref[n]
        S0h=S0.astype(bf16); dSh=dS1.astype(bf16)
        kf=k.astype(f32); qf=q.astype(f32); vf=v.astype(f32)
        W=w_ref[n].astype(bf16); T=t_ref[n].astype(bf16)
        P=(QK*D).astype(bf16)
        dW=dg(P,dO,0,0)+jnp.concatenate([end]*(DV//128),axis=1)*dg(k,dSh)
        Y=dg(T,dW.astype(bf16),0,0)
        dOY=jnp.concatenate([dO,Y.astype(bf16)],axis=0)
        dPA=dg(dOY,W,1,1)
        GS=dg(dOY,S0h,1,1)
        dOS=GS[:SPAN]; YS=GS[SPAN:]
        Z=dg(W,dSh,1,1)
        dPD=dPA[:SPAN]*D
        EA=jnp.where(i>j,-dPA[SPAN:]*D,0.0)
        E=beta*EA
        A1=jnp.concatenate([dPD,E],axis=0).astype(bf16)
        r1=dg(A1,k)
        r2=dg(A1,jnp.concatenate([q,k],axis=0),0,0)
        dqkv[rows,0:DK]=gam*dOS+r1[:SPAN]
        dqkv[rows,DK:2*DK]=r1[SPAN:]+r2-(beta*gam)*YS+end*Z
        dqkv[rows,2*DK:]=beta*Y
        EK=EA*KK
        kYS=jnp.sum(kf*YS,axis=1,keepdims=True)
        dbeta=jnp.sum(Y*vf,axis=1,keepdims=True)-gam*kYS+jnp.sum(EK,axis=1,keepdims=True)
        Fm=dPD*QK+beta*EK
        dgam=jnp.sum(qf*dOS,axis=1,keepdims=True)-beta*kYS
        dend=jnp.sum(kf*Z,axis=1,keepdims=True)*end
        colsum=mmx(Fm,jnp.ones((SPAN,128),f32),0,0)
        dG=jnp.sum(Fm,axis=1,keepdims=True)-colsum+dgam*gam-dend
        tail=jnp.sum(jnp.sum(S0*dS1,axis=0,keepdims=True),axis=1,keepdims=True)
        last=jnp.sum(dend,axis=0,keepdims=True)+gam[SPAN-1:SPAN]*tail
        row=lax.broadcasted_iota(jnp.int32,(SPAN,128),0)
        dG=dG+jnp.where(row==SPAN-1,last,0.0)
        upper=jnp.where(i<=j,1.0,0.0)
        dlog=mmx(upper,dG)
        dbp=(dbeta*beta*(1.0-beta))
        ddp=dlog*(-rate)*sigmoid(xc[:,1:2]+bias)
        dx_ref[rows,0:1]=dbp[:,0:1]
        dx_ref[rows,1:2]=ddp[:,0:1]
        sl,sb=sums
        return (sl+jnp.sum(dlog*g,axis=0,keepdims=True),sb+jnp.sum(ddp,axis=0,keepdims=True))
    def local(m,sums):
        xr=xr_ref[pl.ds(pl.multiple_of(m*8,8),8),:]
        for e in range(per): sums=one_span(m*per+e,xr[1:2,e*SPAN:(e+1)*SPAN],sums)
        return sums
    zero=jnp.zeros((1,128),f32)
    sl,sb=lax.fori_loop(0,n,local,(zero,zero),unroll=2)
    def turn(m,_):
        dxr[pl.ds(pl.multiple_of(m*8,8),8),:]=flat_form(dx_ref[pl.ds(pl.multiple_of(m*local_len,local_len),local_len),:])
        return 0
    lax.fori_loop(0,n,turn,0,unroll=2)
    dh_ref[0:1]=sl; dh_ref[1:2]=sb
    def norms(c,dt):
        base=pl.multiple_of(c*R,R)
        age=doc_age(starts,positions(base,R,128,0))[:,0:1]
        pre=conv_pre(upad,taps,age,base,R)
        sg=sigmoid(pre); act=pre*sg
        rows=pl.ds(base,R)
        d=dqkv[rows,:]
        def unit_back(a,dd,f):
            s=lax.rsqrt(jnp.sum(a*a,axis=1,keepdims=True)+EPSILON)
            dot=jnp.sum(a*dd,axis=1,keepdims=True)
            return f*(s*dd-a*(s*s*s*dot))
        dact=jnp.concatenate([unit_back(act[:,:DK],d[:,:DK],DK**-0.5),unit_back(act[:,DK:2*DK],d[:,DK:2*DK],1.0),d[:,2*DK:]],axis=1)
        dp=dact*sg*(1.0+pre*(1.0-sg))
        dpre[rows,:]=dp
        window=upad[pl.ds(base,R+8),:]
        new=[]
        for j in range(4):
            back=3-j
            x=window[8-back:8-back+R]
            if back: x=x*jnp.where(age>=back,1.0,0.0)
            new.append(dt[j]+jnp.sum(x*dp,axis=0,keepdims=True))
        return tuple(new)
    zt=jnp.zeros((1,upad.shape[1]),f32)
    dt=lax.fori_loop(0,L//R,norms,(zt,)*4)
    for j in range(4): dtaps_ref[j:j+1]=dt[j]
    def back(c,_):
        base=pl.multiple_of(c*R,R)
        window=dpre[pl.ds(base,R+8),:]
        age=doc_age(starts,positions(base,R+8,128,0))[:,0:1]
        d=window[:R]*taps[3:4]
        for s in range(1,4):
            x=window[s:s+R]*jnp.where(age[s:s+R]>=s,1.0,0.0)
            d=d+x*taps[3-s:4-s]
        du_ref[pl.ds(base,R),:]=d.astype(bf16)
        return 0
    lax.fori_loop(0,L//R,back,0)
    wk=heads*DK
    at=lambda start,width: (lambda t: (pl.ds(pl.multiple_of(t*local_len,local_len),local_len),pl.ds(start,width)))
    to=lambda start,width: (lambda seq,head: (pl.ds(pl.multiple_of(seq*local_len,local_len),local_len),pl.ds(pl.multiple_of(start+head*width,128),width)))
    outward=FromPairs(n,copies,heads,local_len,[(du_ref,at(0,DK),duall,to(0,DK)),(du_ref,at(DK,DK),duall,to(wk,DK)),(du_ref,at(2*DK,DV),duall,to(2*wk,DV)),
        (dxr,lambda t: (pl.ds(pl.multiple_of(t*8,8),8),slice(None)),rows_out,lambda seq,head: (pl.ds(pl.multiple_of((seq*heads+head)*8,8),8),slice(None)))],os_,or_)
    outward.start()
    each(gw,"late"); outward.finish(); each(gw,"finish")

SM=pl.BlockSpec(memory_space=pltpu.SMEM); VM=pl.BlockSpec(memory_space=pltpu.VMEM)
def S(shape,dt=f32): return jax.ShapeDtypeStruct(shape,dt)
def forward(n,copies,heads,proj,rows_in,taps,starts,hp,wg,wo,n1,DK,DV):
    R=proj.shape[0]; CH=taps.shape[1]; local_len=rows_in.shape[1]; L=n*local_len; NC=L//SPAN; pairs=rows_in.shape[0]//8
    full=lambda a: S((a.shape[0]*n,a.shape[1]),bf16)
    return call("rec_fwd",5,functools.partial(forward_kernel,n,copies,heads),(proj,rows_in,taps,starts,hp,wg,wo,n1),[ANY,ANY,VM,SM,SM,ANY,ANY,ANY],
      [S((R,heads*DV),bf16),S((L,CH),bf16),S((n*8,local_len)),S((L,8)),S((L,DK),bf16),S((L,DK),bf16),S((L,DV),bf16),S((NC,DK,DV)),S((NC,SPAN,DV)),S((NC,SPAN,SPAN)),
       S((NC,2*SPAN,DK),bf16),S((NC,DK,DK),bf16),S((NC,DK,DK),bf16),full(wg),S((wo.shape[0],wo.shape[1]*n),bf16),S((R*n,n1.shape[1]//n),bf16)],
      [ANY]+[VM]*12+[ANY]*3,
      [pltpu.VMEM((L+8,CH),f32),pltpu.VMEM((NC,DK,DV),f32),pltpu.VMEM((NC,8,128),f32),pltpu.VMEM((NC,SPAN,DV),f32),pltpu.VMEM((L,DV),bf16),
       pltpu.SemaphoreType.DMA((4,n)),pltpu.SemaphoreType.DMA((4,n)),pltpu.SemaphoreType.DMA((1,pairs)),pltpu.SemaphoreType.DMA((1,pairs))]+pair_sems(n)+gather_sems(n,2))
def backward(n,copies,heads,dall,taps,starts,hp,saved,hid,bra,dgp):
    u,xr,xc,q,k,v,s,w,t,qt,mh,ml=saved
    L,CH=u.shape; NC=L//SPAN; DK=q.shape[1]; DV=v.shape[1]; local_len=L//n; pairs=n//copies; R=dall.shape[0]
    full=lambda a: S((a.shape[0]*n,a.shape[1]),bf16)
    return call("rec_bwd",6,functools.partial(backward_kernel,n,copies,heads),(dall,u,taps,xc,xr,starts,hp,q,k,v,s,w,t,qt,mh,ml,hid,bra,dgp),[ANY]+[VM]*4+[SM]*2+[VM]*9+[ANY]*3,
      [S((R,heads*CH),bf16),S((pairs*8,local_len)),S((4,CH)),S((2,128)),full(hid),full(bra),full(dgp)],[ANY,ANY,VM,VM,ANY,ANY,ANY],
      [pltpu.VMEM((L+8,CH),f32),pltpu.VMEM((L+8,CH),f32),pltpu.VMEM((NC,DK,DV),f32),pltpu.VMEM((L,CH),f32),pltpu.VMEM((NC,DK,DV),f32),pltpu.VMEM((NC,8,128),f32),
       pltpu.VMEM((L,DV),bf16),pltpu.VMEM((L,CH),bf16),pltpu.VMEM((L,8),f32),pltpu.VMEM((n*8,local_len),f32),
       pltpu.SemaphoreType.DMA((4,n)),pltpu.SemaphoreType.DMA((4,n)),pltpu.SemaphoreType.DMA((4,pairs)),pltpu.SemaphoreType.DMA((4,pairs))]+gather_sems(n,3))


MESH=pl.DeviceIdType.MESH
ANY=pl.BlockSpec(memory_space=pl.ANY)

def flip(s,bit):
    return s+bit-2*bit*lax.rem(lax.div(s,bit),2)

def flips(s,mask):
    bit=1
    while bit<=mask:
        if mask&bit: s=flip(s,bit)
        bit*=2
    return s

def greet(n,zc):
    s=lax.axis_index("seq"); z=lax.axis_index("shard")
    bar=pltpu.get_barrier_semaphore()
    for d in range(1,n):
        pl.semaphore_signal(bar,inc=1,device_id={"seq":lax.rem(s+d,n)},device_id_type=MESH)
    for d in range(1,zc):
        pl.semaphore_signal(bar,inc=1,device_id={"shard":lax.rem(z+d,zc)},device_id_type=MESH)
    pl.semaphore_wait(bar,n-1+zc-1)

def links(n):
    return 8 if n==8 else n

class SeqGather:
    def __init__(self,n,src,dst,axis,sems,c0=0):
        self.n=n; self.src=src; self.dst=dst; self.axis=axis; self.send,self.recv,self.loc=sems
        self.R,self.C=src.shape
        self.r0=0; self.nr=self.R; self.c0=c0
        self.s=lax.axis_index("seq")
        self.open=[]
    def slot(self,t,a,b):
        if self.axis==0:
            return self.dst.at[pl.ds(pl.multiple_of(t*self.R+self.r0+a,16),b-a),pl.ds(self.c0,self.C)]
        return self.dst.at[pl.ds(self.r0+a,b-a),pl.ds(pl.multiple_of(t*self.C,128),self.C)]
    def copy(self,src,t,a,b,k,to):
        c=pltpu.make_async_remote_copy(src_ref=src,dst_ref=self.slot(t,a,b),send_sem=self.send.at[k],recv_sem=self.recv.at[k],device_id={"seq":to},device_id_type=MESH)
        c.start()
        return c
    def pass_on(self,t,a,b,k,to):
        return self.copy(self.slot(t,a,b),t,a,b,k,to)
    def start(self):
        s=self.s; nr=self.nr
        mine=self.src.at[pl.ds(self.r0,nr),:]
        self.own=pltpu.make_async_copy(mine,self.slot(s,0,nr),self.loc)
        self.own.start()
        masks=(2,4) if self.n==8 else range(2,self.n,2)
        self.direct=[self.copy(mine,s,0,nr,i+1,flips(s,m)) for i,m in enumerate(masks)]
        self.open.append(self.copy(mine,s,0,nr,0,flip(s,1)))
    def middle(self):
        s=self.s; nr=self.nr; h=nr//2
        if self.n!=8: return
        x,y=flip(s,2),flip(s,4)
        self.direct[0].wait_recv()
        fa=self.pass_on(x,0,h,3,y)
        self.open.append(self.pass_on(x,0,nr,5,flip(s,1)))
        self.direct[1].wait_recv()
        fb=self.pass_on(y,h,nr,4,x)
        self.open.append(self.pass_on(y,0,nr,6,flip(s,1)))
        self.diag=(fa,fb)
    def late(self):
        s=self.s; nr=self.nr
        if self.n==8:
            for f in self.diag: f.wait_recv()
            self.open.append(self.pass_on(flips(s,6),0,nr,7,flip(s,1)))
            for f in self.diag: f.wait_send()
        else:
            for i,m in enumerate(range(2,self.n,2)):
                self.direct[i].wait_recv()
                self.open.append(self.pass_on(flips(s,m),0,nr,self.n//2+i,flip(s,1)))
        for f in self.direct: f.wait_send()
    def finish(self):
        for f in self.open: f.wait()
        self.own.wait()

class ShardGather:
    def __init__(self,zc,src,dst,send,recv):
        self.zc=zc; self.src=src; self.dst=dst; self.send=send; self.recv=recv
        self.z=lax.axis_index("shard"); self.C=src.shape[1]
    def slot(self):
        return self.dst.at[:,pl.ds(pl.multiple_of(self.z*self.C,128),self.C)]
    def start(self):
        self.own=pltpu.make_async_copy(self.src,self.slot(),self.recv.at[0]); self.own.start()
        self.cs=[]
        for d in range(1,self.zc):
            c=pltpu.make_async_remote_copy(src_ref=self.src,dst_ref=self.slot(),send_sem=self.send.at[d],recv_sem=self.recv.at[d],device_id={"shard":lax.rem(self.z+d,self.zc)},device_id_type=MESH)
            c.start(); self.cs.append(c)
    def finish(self):
        for c in self.cs: c.wait()
        self.own.wait()

class ShardSplit:
    def __init__(self,zc,src,box,send,recv):
        self.zc=zc; self.src=src; self.box=box; self.send=send; self.recv=recv
        self.z=lax.axis_index("shard"); self.C=box.shape[2]
    def start(self):
        C=self.C
        self.own=pltpu.make_async_copy(self.src.at[:,pl.ds(pl.multiple_of(self.z*C,128),C)],self.box.at[0],self.recv.at[0]); self.own.start()
        self.cs=[]
        for d in range(1,self.zc):
            to=lax.rem(self.z+d,self.zc)
            c=pltpu.make_async_remote_copy(src_ref=self.src.at[:,pl.ds(pl.multiple_of(to*C,128),C)],dst_ref=self.box.at[d],send_sem=self.send.at[d],recv_sem=self.recv.at[d],device_id={"shard":to},device_id_type=MESH)
            c.start(); self.cs.append(c)
    def finish(self):
        for c in self.cs: c.wait()
        self.own.wait()

class ShardAll:
    def __init__(self,axis,n,box,send,recv):
        self.axis=axis; self.n=n; self.box=box; self.send=send; self.recv=recv; self.me=lax.axis_index(axis)
    def start(self):
        self.cs=[]
        for d in range(1,self.n):
            c=pltpu.make_async_remote_copy(src_ref=self.box.at[self.me],dst_ref=self.box.at[self.me],send_sem=self.send.at[d],recv_sem=self.recv.at[d],device_id={self.axis:lax.rem(self.me+d,self.n)},device_id_type=MESH)
            c.start(); self.cs.append(c)
    def finish(self):
        for c in self.cs: c.wait()

class ColumnSplit:
    def __init__(self,n,src,dst,send,recv):
        self.n=n; self.src=src; self.dst=dst; self.send=send; self.recv=recv
        self.s=lax.axis_index("seq"); self.C=dst.shape[1]; self.R=src.shape[0]
    def start(self):
        n,s,C,R=self.n,self.s,self.C,self.R
        to_rows=self.dst.at[pl.ds(pl.multiple_of(s*R,16),R),:]
        block=lambda t: self.src.at[:,pl.ds(pl.multiple_of(t*C,128),C)]
        self.own=pltpu.make_async_copy(block(s),to_rows,self.recv.at[0]); self.own.start()
        self.cs=[]
        for d in range(1,n):
            t=lax.rem(s+d,n)
            c=pltpu.make_async_remote_copy(src_ref=block(t),dst_ref=to_rows,send_sem=self.send.at[d],recv_sem=self.recv.at[d],device_id={"seq":t},device_id_type=MESH)
            c.start(); self.cs.append(c)
    def finish(self):
        for c in self.cs: c.wait()
        self.own.wait()

class ToPairs:
    def __init__(self,n,copies,heads,local_len,src,rows_src,dst,rows_dst,DK,DV,send,recv):
        self.__dict__.update(n=n,copies=copies,heads=heads,ll=local_len,src=src,rows_src=rows_src,dst=dst,rows_dst=rows_dst,DK=DK,DV=DV,send=send,recv=recv)
    def parts(self,t):
        s=lax.axis_index("seq"); ll,DK,DV,heads=self.ll,self.DK,self.DV,self.heads
        pair=lax.div(t,self.copies); seq=lax.div(pair,heads); head=lax.rem(pair,heads)
        rows=pl.ds(pl.multiple_of(seq*ll,ll),ll); to=pl.ds(pl.multiple_of(s*ll,ll),ll)
        if self.rows_src is None:
            return [(self.src.at[rows,pl.ds(pl.multiple_of(head*DV,128),DV)],self.dst.at[to,:])]
        wk=heads*DK
        out=[]
        for start,width,at in ((0,DK,0),(wk,DK,DK),(2*wk,DV,2*DK)):
            out.append((self.src.at[rows,pl.ds(pl.multiple_of(start+head*width,128),width)],self.dst.at[to,pl.ds(at,width)]))
        out.append((self.rows_src.at[pl.ds(pl.multiple_of(pair*8,8),8),:],self.rows_dst.at[pl.ds(pl.multiple_of(s*8,8),8),:]))
        return out
    def start(self):
        s=lax.axis_index("seq"); self.cs=[]
        for d in range(self.n):
            t=lax.rem(s+d,self.n)
            for i,(a,b) in enumerate(self.parts(t)):
                if d==0: c=pltpu.make_async_copy(a,b,self.recv.at[i,0])
                else: c=pltpu.make_async_remote_copy(src_ref=a,dst_ref=b,send_sem=self.send.at[i,d],recv_sem=self.recv.at[i,d],device_id={"seq":t},device_id_type=MESH)
                c.start(); self.cs.append(c)
    def finish(self):
        for c in self.cs: c.wait()

class FromPairs:
    def __init__(self,n,copies,heads,local_len,items,send,recv):
        self.__dict__.update(n=n,copies=copies,heads=heads,items=items,send=send,recv=recv)
    def start(self):
        s=lax.axis_index("seq"); pairs=self.n//self.copies; p=lax.div(s,self.copies); r=lax.rem(s,self.copies)
        seq=lax.div(p,self.heads); head=lax.rem(p,self.heads); self.cs=[]
        for d in range(pairs):
            t=lax.rem(p+d,pairs)*self.copies+r
            for i,(src,at,dst,to) in enumerate(self.items):
                a=src.at[at(t)]; b=dst.at[to(seq,head)]
                if d==0: c=pltpu.make_async_copy(a,b,self.recv.at[i,0])
                else: c=pltpu.make_async_remote_copy(src_ref=a,dst_ref=b,send_sem=self.send.at[i,d],recv_sem=self.recv.at[i,d],device_id={"seq":t},device_id_type=MESH)
                c.start(); self.cs.append(c)
    def finish(self):
        for c in self.cs: c.wait()

def flat_form(cols):
    r=cols.shape[0]
    i=lax.broadcasted_iota(jnp.int32,(r,r),0); j=lax.broadcasted_iota(jnp.int32,(r,r),1)
    return mmx(cols,jnp.where(i==j,1.0,0.0),0,0)

def row_form(cols):
    return mmx(jnp.ones((8,cols.shape[1]),f32),cols,1,1)

def col_form(rows):
    r=rows.shape[1]
    i=lax.broadcasted_iota(jnp.int32,(r,r),0); j=lax.broadcasted_iota(jnp.int32,(r,r),1)
    return mmx(jnp.where(i==j,1.0,0.0),rows,1,1)

def gathers(n,pairs,sems):
    send,recv,loc=sems
    return [SeqGather(n,src,dst,axis,(send.at[i],recv.at[i],loc.at[i]),*c0) for i,(src,dst,axis,*c0) in enumerate(pairs)]
def gather_sems(n,k):
    return [pltpu.SemaphoreType.DMA((k,links(n))),pltpu.SemaphoreType.DMA((k,links(n))),pltpu.SemaphoreType.DMA((k,))]
def pair_sems(k):
    return [pltpu.SemaphoreType.DMA((k,)),pltpu.SemaphoreType.DMA((k,))]
def each(ops,name):
    for o in ops: getattr(o,name)()

def front_kernel(n,zc,tok,cot,gain,wq,wk,wv,ws,normed,scale,cotfull,wfull,cotc,tokfull,zs,zr,cs,cr,es,er,*gs):
    greet(n,zc)
    zt=ShardGather(zc,tok,tokfull,zs,zr); zt.start()
    parts=(wq,wk,wv,ws); at=[sum(w.shape[1] for w in parts[:i]) for i in range(4)]
    gw=gathers(n,[(w,wfull,0,a) for w,a in zip(parts,at)],gs)
    each(gw,"start")
    zt.finish()
    zk=ShardGather(zc,cot,cotfull,cs,cr); zk.start()
    rows=tokfull.shape[0]; D=tokfull.shape[1]
    def norm(c,_):
        r=pl.ds(pl.multiple_of(c*32,32),32)
        x=tokfull[r,:].astype(f32)
        sc=lax.rsqrt(jnp.sum(x*x,axis=1,keepdims=True)/D+EPSILON)
        normed[r,:]=(x*sc*gain[...]).astype(bf16)
        scale[r,:]=jnp.broadcast_to(sc,(32,128))
        return 0
    lax.fori_loop(0,rows//32,norm,0)
    each(gw,"middle"); each(gw,"late")
    zk.finish()
    cc=ColumnSplit(n,cotfull,cotc,es,er); cc.start(); cc.finish()
    each(gw,"finish")

def attn_out_kernel(n,zc,part,tok,gain,wg,wu,wd,res,scale,nfull,wgfull,wufull,wdfull,box,sums,nloc,as_,ar,bs,br,cs,cr,*gs):
    greet(n,zc)
    D=part.shape[1]
    split=ShardSplit(zc,part,box,as_,ar); split.start()
    gw=gathers(n,[(wg,wgfull,0),(wu,wufull,0),(wd,wdfull,1)],gs)
    each(gw,"start")
    split.finish()
    r=tok[...].astype(f32)
    for d in range(zc): r=r+box[d].astype(f32)
    res[...]=r
    sums[lax.axis_index("shard")]=row_form(r*r)
    tot=ShardAll("shard",zc,sums,bs,br); tot.start(); tot.finish()
    t=sums[0]
    for d in range(1,zc): t=t+sums[d]
    sc=lax.rsqrt(col_form(t)[:,0:1]/D+EPSILON)
    scale[...]=jnp.broadcast_to(sc,scale.shape)
    nloc[...]=(r*sc*gain[...]).astype(bf16)
    zg=ShardGather(zc,nloc,nfull,cs,cr); zg.start()
    each(gw,"middle")
    zg.finish()
    each(gw,"late"); each(gw,"finish")

def ffn_back_kernel(n,zc,part,res,scale,cot,gain,dg_,du_,n2,gres,afull,gffn,dgfull,dufull,n2c,box,sums,aloc,as_,ar,bs,br,cs,cr,es,er,*gs):
    greet(n,zc)
    D=part.shape[1]
    split=ShardSplit(zc,part,box,as_,ar); split.start()
    gw=gathers(n,[(dg_,dgfull,0),(du_,dufull,0)],gs)
    each(gw,"start")
    cols=ColumnSplit(n,n2,n2c,es,er); cols.start()
    split.finish()
    g=box[0].astype(f32)
    for d in range(1,zc): g=g+box[d].astype(f32)
    r=res[...]; sc=scale[...][:,0:1]
    gained=gain[...]*g
    sums[lax.axis_index("shard")]=row_form(gained*r)
    tot=ShardAll("shard",zc,sums,bs,br); tot.start()
    gffn[...]=jnp.broadcast_to(jnp.sum(g*r*sc,axis=0,keepdims=True),gffn.shape)
    tot.finish()
    t=sums[0]
    for d in range(1,zc): t=t+sums[d]
    inner=col_form(t)[:,0:1]/D
    gr=cot[...].astype(f32)+sc*(gained-r*(sc*sc*inner))
    gres[...]=gr
    aloc[...]=gr.astype(bf16)
    zg=ShardGather(zc,aloc,afull,cs,cr); zg.start()
    each(gw,"middle")
    zg.finish()
    each(gw,"late"); cols.finish(); each(gw,"finish")

def tail_kernel(n,zc,partdx,partout,res,gres,tok,scale,gain,small,dy,dsm,att,output,gtok,dyfull,dsmfull,attc,smalls,totals,box,boxo,sums,as_,ar,bs,br,cs,cr,es,er,fs,fr,hs,hr,*gs):
    greet(n,zc)
    D=partdx.shape[1]
    split=ShardSplit(zc,partdx,box,as_,ar); split.start()
    gw=gathers(n,[(dy,dyfull,0),(dsm,dsmfull,0)],gs)
    each(gw,"start")
    ca=ColumnSplit(n,att,attc,es,er); ca.start()
    split.finish()
    so=ShardSplit(zc,partout,boxo,fs,fr); so.start()
    g=box[0].astype(f32)
    for d in range(1,zc): g=g+box[d].astype(f32)
    x=tok[...].astype(f32); sc=scale[...][:,0:1]
    gained=gain[...]*g
    sums[lax.axis_index("shard")]=row_form(gained*x)
    tot=ShardAll("shard",zc,sums,bs,br); tot.start()
    me=lax.axis_index("seq")
    smalls[me]=small[...]
    smalls[me,0:1,0:g.shape[1]]=jnp.sum(g*x*sc,axis=0,keepdims=True)
    sa=ShardAll("seq",n,smalls,cs,cr); sa.start()
    tot.finish()
    t=sums[0]
    for d in range(1,zc): t=t+sums[d]
    inner=col_form(t)[:,0:1]/D
    gtok[...]=gres[...]+sc*(gained-x*(sc*sc*inner))
    sa.finish()
    t=smalls[0]
    for d in range(1,n): t=t+smalls[d]
    totals[lax.axis_index("shard")]=t
    za=ShardAll("shard",zc,totals,hs,hr); za.start()
    each(gw,"middle")
    so.finish()
    o=res[...]
    for d in range(zc): o=o+boxo[d].astype(f32)
    output[...]=o
    za.finish()
    each(gw,"late"); ca.finish(); each(gw,"finish")

def call(name,cid,kernel,args,specs,outs,ospecs,scratch):
    return pl.pallas_call(kernel,name=name,out_shape=tuple(outs),in_specs=specs,out_specs=tuple(ospecs),scratch_shapes=scratch,
      compiler_params=pltpu.CompilerParams(collective_id=cid,has_side_effects=True,vmem_limit_bytes=56*2**20))(*args)

def front(n,zc,tok,cot,gain,*ws):
    R,F=tok.shape; D=F*zc
    return call("front",1,functools.partial(front_kernel,n,zc),(tok,cot,gain)+ws,[VM,VM,VM]+[ANY]*4,
      [S((R,D),bf16),S((R,128)),S((R,D),bf16),S((ws[0].shape[0]*n,sum(w.shape[1] for w in ws)),bf16),S((R*n,D//n),bf16)],[VM,VM,ANY,ANY,ANY],
      [pltpu.VMEM((R,D),bf16)]+pair_sems(zc)*2+pair_sems(n)+gather_sems(n,4))
def attn_out(n,zc,part,tok,gain,wg,wu,wd):
    R,F=tok.shape; D=F*zc
    return call("attn_out",2,functools.partial(attn_out_kernel,n,zc),(part,tok,gain,wg,wu,wd),[ANY,VM,VM]+[ANY]*3,
      [S((R,F)),S((R,128)),S((R,D),bf16),S((wg.shape[0]*n,wg.shape[1]),bf16),S((wu.shape[0]*n,wu.shape[1]),bf16),S((wd.shape[0],wd.shape[1]*n),bf16)],
      [VM,VM,VM,ANY,ANY,ANY],
      [pltpu.VMEM((zc,R,F),bf16),pltpu.VMEM((zc,8,R),f32),pltpu.VMEM((R,F),bf16)]+pair_sems(zc)*3+gather_sems(n,3))
def ffn_back(n,zc,part,res,scale,cot,gain,dg_,du_,n2):
    R,F=cot.shape; D=F*zc
    full=lambda a: S((a.shape[0]*n,a.shape[1]),bf16)
    return call("ffn_back",3,functools.partial(ffn_back_kernel,n,zc),(part,res,scale,cot,gain,dg_,du_,n2),[ANY,VM,VM,VM,VM]+[ANY]*3,
      [S((R,F)),S((R,D),bf16),S((8,F)),full(dg_),full(du_),S((R*n,D//n),bf16)],[VM,VM,VM]+[ANY]*3,
      [pltpu.VMEM((zc,R,F),bf16),pltpu.VMEM((zc,8,R),f32),pltpu.VMEM((R,F),bf16)]+pair_sems(zc)*3+pair_sems(n)+gather_sems(n,2))
def tail(n,zc,partdx,partout,res,gres,tok,scale,gain,small,dy,dsm,att):
    R,F=tok.shape; D=F*zc
    full=lambda a: S((a.shape[0]*n,a.shape[1]),bf16)
    return call("tail",4,functools.partial(tail_kernel,n,zc),(partdx,partout,res,gres,tok,scale,gain,small,dy,dsm,att),[ANY,ANY]+[VM]*6+[ANY]*3,
      [S((R,F)),S((R,F)),full(dy),full(dsm),S((R*n,D//n),bf16),S((n,)+small.shape),S((zc,)+small.shape)],
      [VM,VM,ANY,ANY,ANY,VM,VM],
      [pltpu.VMEM((zc,R,F),bf16),pltpu.VMEM((zc,R,F),bf16),pltpu.VMEM((zc,8,R),f32)]+pair_sems(zc)*2+pair_sems(n)*2+pair_sems(zc)*2+gather_sems(n,2))


def per_device(
    tokens, doc_starts, norm_gain, query_weight, key_weight, value_weight, outgate_weight,
    beta_weight, decay_weight, query_conv, key_conv, value_conv, decay_log, decay_bias, head_gain,
    output_weight, ffn_gain, gate_weight, up_weight, down_weight, cotangent,
):
    seq_count, local_len, feature_part = tokens.shape
    row_count = seq_count * local_len
    shard_count = lax.axis_size("shard")
    shard_pos = lax.axis_index("shard")
    seq_devices = lax.axis_size("seq")
    seq_pos = lax.axis_index("seq")
    model_dim = feature_part * shard_count
    head_count = beta_weight.shape[1]
    key_dim = query_weight.shape[1] // head_count
    value_dim = value_weight.shape[1] // head_count
    tap_count = query_conv.shape[1]
    width_k = head_count * key_dim
    channels = 2 * key_dim + value_dim
    feature_start = shard_pos * feature_part
    head_start = shard_pos * head_count
    pairs = seq_count * head_count
    copies = seq_devices // pairs
    length = local_len * seq_devices
    spans = length // SPAN
    my_pair = seq_pos // copies
    my_seq = my_pair // head_count
    my_head = my_pair % head_count

    def project(a, b):
        return jnp.dot(a, b, preferred_element_type=f32)

    taps_local = jnp.concatenate([query_conv, key_conv, value_conv], axis=0)
    tap_rows = taps_local.shape[0]
    width_v = head_count * value_dim
    padding = -(2 * head_count + tap_count) % 128
    taps_padded = jnp.pad(taps_local, ((0, query_weight.shape[0] - tap_rows), (0, padding)))
    weights_small = jnp.concatenate([beta_weight, decay_weight, taps_padded], axis=1)
    edges = [0, width_k, 2 * width_k, 2 * width_k + width_v]
    flat = lambda x: x.reshape(row_count, x.shape[2])
    local_ffn_gain = lax.dynamic_slice_in_dim(ffn_gain, feature_start, feature_part)[None]
    local_norm_gain = lax.dynamic_slice_in_dim(norm_gain, feature_start, feature_part)[None]
    tokens_flat, cot_flat = flat(tokens), flat(cotangent)
    normed_one, scale_one, cot_rows, full_one, cot_cols = front(
        seq_devices, shard_count, tokens_flat, cot_flat, norm_gain[None], query_weight, key_weight, value_weight, weights_small
    )
    proj = project(normed_one, full_one)
    proj_qkv = proj[:, : edges[3]].astype(bf16)
    proj_rates = proj[:, edges[3] : edges[3] + 2 * head_count].reshape(seq_count, local_len, 2, head_count)
    rates_in = jnp.pad(jnp.transpose(proj_rates, (0, 3, 2, 1)), ((0, 0), (0, 0), (0, 6), (0, 0))).reshape(pairs * 8, local_len)
    shape4 = (seq_count, local_len, head_count, -1)
    all_taps = full_one[:, edges[3] + 2 * head_count :][:, :tap_count].reshape(seq_devices, -1, tap_count)
    count_q = query_conv.shape[0]
    full_qconv = all_taps[:, :count_q].reshape(-1, tap_count)
    full_kconv = all_taps[:, count_q : 2 * count_q].reshape(-1, tap_count)
    full_vconv = all_taps[:, 2 * count_q : tap_rows].reshape(-1, tap_count)
    taps = jnp.concatenate(
        [
            lax.dynamic_slice_in_dim(full_qconv, my_head * key_dim, key_dim),
            lax.dynamic_slice_in_dim(full_kconv, my_head * key_dim, key_dim),
            lax.dynamic_slice_in_dim(full_vconv, my_head * value_dim, value_dim),
        ],
        axis=0,
    ).astype(f32).T
    starts = lax.dynamic_index_in_dim(doc_starts, my_seq, 0, keepdims=False)
    at_head = head_start + my_head
    decay_pair = jnp.concatenate(
        [lax.dynamic_slice_in_dim(decay_log, at_head, 1), lax.dynamic_slice_in_dim(decay_bias, at_head, 1)]
    )
    o_flat, *saved = forward(
        seq_devices, copies, head_count, proj_qkv, rates_in, taps, starts, decay_pair,
        outgate_weight, output_weight, normed_one, key_dim, value_dim,
    )
    saved, (full_outgate, full_output, normed_one_cols) = saved[:12], saved[12:]
    gate_proj = project(normed_one, full_outgate).reshape(shape4)
    o = o_flat.astype(f32).reshape(shape4)

    rho = lax.rsqrt(jnp.mean(o * o, axis=3, keepdims=True) + EPSILON)
    gate_sig = jax.nn.sigmoid(gate_proj)
    gate_silu = gate_proj * gate_sig
    z = o * rho
    branch = (z * head_gain * gate_silu).astype(bf16).reshape(row_count, width_v)
    attn_part = project(branch, full_output).astype(bf16)
    residual, scale_two, normed_two, full_gate, full_up, full_down = attn_out(
        seq_devices, shard_count, attn_part, tokens_flat, local_ffn_gain, gate_weight, up_weight, down_weight
    )
    gate_vals = project(normed_two, full_gate)
    up_vals = project(normed_two, full_up)
    sigmoid_gate = jax.nn.sigmoid(gate_vals)
    gate_act = gate_vals * sigmoid_gate
    hidden = (gate_act * up_vals).astype(bf16)
    out_part = project(hidden, full_down).astype(bf16)

    def back(cols, weight):
        return jnp.einsum("rc,dc->rd", cols, weight, preferred_element_type=f32)

    def grad(left, right):
        return jnp.einsum("rd,rc->dc", left, right, preferred_element_type=f32)

    grad_hidden = back(cot_rows, full_down)
    grad_gate_vals = (grad_hidden * up_vals * sigmoid_gate * (1.0 + gate_vals * (1.0 - sigmoid_gate))).astype(bf16)
    grad_up_vals = (grad_hidden * gate_act).astype(bf16)
    two_part = (back(grad_gate_vals, full_gate) + back(grad_up_vals, full_up)).astype(bf16)
    grad_residual, attn_cot, grad_ffn_part, dgate_all, dup_all, normed_two_cols = ffn_back(
        seq_devices, shard_count, two_part, residual, scale_two, cot_flat, local_ffn_gain,
        grad_gate_vals, grad_up_vals, normed_two,
    )
    out_gate, out_up = grad(normed_two_cols, dgate_all), grad(normed_two_cols, dup_all)
    grad_mixed = (
        back(attn_cot, full_output).astype(bf16).astype(f32).reshape(shape4)
    )
    grad_head_gain = jnp.sum(grad_mixed * z * gate_silu, axis=(0, 1, 2))
    dz = grad_mixed * head_gain * gate_silu
    grad_o = (rho * (dz - z * jnp.mean(dz * z, axis=3, keepdims=True))).astype(bf16)
    grad_gate_proj = (grad_mixed * z * head_gain * gate_sig * (1.0 + gate_proj * (1.0 - gate_sig))).astype(bf16)
    grad_gate_proj = grad_gate_proj.reshape(row_count, head_count * value_dim)

    grad_qkv, drates, dtaps, dhead, hidden_all, branch_all, dgate_proj_all = backward(
        seq_devices, copies, head_count, grad_o.reshape(row_count, width_v), taps, starts, decay_pair, saved,
        hidden, branch, grad_gate_proj,
    )
    drates = jnp.transpose(drates.reshape(seq_count, head_count, 8, local_len)[:, :, :2], (0, 3, 2, 1))
    grad_small = jnp.pad(drates.reshape(row_count, 2 * head_count).astype(bf16), ((0, 0), (0, tap_count + padding)))
    one_part = (
        back(grad_qkv, full_one[:, : edges[3]]) + back(grad_small, full_one[:, edges[3] :]) + back(grad_gate_proj, full_outgate)
    ).astype(bf16)
    primary = jnp.where(seq_pos % copies == 0, 1.0, 0.0)
    total_heads = decay_log.shape[0]
    width_s = max(feature_part, channels)
    widen = lambda x: jnp.pad(x, ((0, 0), (0, width_s - x.shape[1])))
    heads_row = lax.dynamic_update_slice(
        lax.dynamic_update_slice(jnp.zeros((1, width_s), f32), dhead[0:1, :1] * primary, (0, at_head)),
        dhead[1:2, :1] * primary,
        (0, total_heads + at_head),
    )
    small = jnp.concatenate(
        [jnp.zeros((1, width_s), f32), widen(grad_ffn_part[:1]), widen(grad_head_gain[None]), heads_row, widen(dtaps)], axis=0
    )
    output, grad_tokens, qkv_all, small_all, attn_cols, smalls, totals = tail(
        seq_devices, shard_count, one_part, out_part, residual, grad_residual, tokens_flat, scale_one,
        local_norm_gain, small, grad_qkv, grad_small, attn_cot,
    )
    outs_one = [grad(normed_one_cols, qkv_all[:, edges[i] : edges[i + 1]]) for i in range(3)]
    outs_small = grad(normed_one_cols, small_all)
    outs_one += [
        grad(normed_one_cols, dgate_proj_all), outs_small[:, :head_count], outs_small[:, head_count : 2 * head_count]
    ]
    out_down = grad(hidden_all, cot_cols)
    out_output = grad(branch_all, attn_cols)
    tap_sum = jnp.sum(smalls[::copies, 4:].reshape(seq_count, head_count, tap_count, width_s), axis=0)

    def own_rows(taps_part):
        rows = jnp.swapaxes(taps_part, 1, 2).reshape(-1, tap_count)
        count = rows.shape[0] // seq_devices
        return lax.dynamic_slice_in_dim(rows, seq_pos * count, count)

    out_qconv = own_rows(tap_sum[:, :, :key_dim])
    out_kconv = own_rows(tap_sum[:, :, key_dim : 2 * key_dim])
    out_vconv = own_rows(tap_sum[:, :, 2 * key_dim : channels])
    out_norm = totals[:, 0, :feature_part].reshape(-1)
    out_ffn = totals[:, 1, :feature_part].reshape(-1)
    totals_all = jnp.sum(totals, axis=0)
    out_head = totals_all[2, :value_dim]
    out_log = totals_all[3, :total_heads]
    out_bias = totals_all[3, total_heads : 2 * total_heads]
    shape3 = (seq_count, local_len, feature_part)
    return (
        output.reshape(shape3), grad_tokens.reshape(shape3), out_norm, *outs_one, out_qconv, out_kconv, out_vconv,
        out_log, out_bias, out_head, out_output, out_ffn, out_gate, out_up, out_down,
    )


def solution(mesh):
    P = PartitionSpec
    rows, cols = P("seq", "shard"), P("shard", "seq")
    both, acts = P(("shard", "seq"), None), P(None, "seq", "shard")
    return jax.shard_map(
        per_device,
        mesh=mesh,
        in_specs=(acts, P(), P()) + (rows,) * 6 + (both,) * 3 + (P(), P(), P(), cols, P(), rows, rows, cols, acts),
        out_specs=(acts, acts, P()) + (rows,) * 6 + (both,) * 3 + (P(), P(), P(), cols, P(), rows, rows, cols),
        check_vma=False,
    )
```

```python
import functools
import jax, jax.numpy as jnp
from jax import lax
from jax.experimental import pallas as pl
from jax.experimental.pallas import tpu as pltpu
from jax.sharding import PartitionSpec
f32=jnp.float32; bf16=jnp.bfloat16
SPAN=64
EPSILON=1e-6
HI=lax.Precision.HIGHEST

def dg(a,b,ca=1,cb=0):
    return lax.dot_general(a,b,(((ca,),(cb,)),((),())),preferred_element_type=f32)
def halves(x):
    h=x.astype(bf16)
    return h,(x-h.astype(f32)).astype(bf16)
def mm3(a,b,ca=1,cb=0):
    ah,al=halves(a); bh,bl=halves(b)
    return dg(ah,bh,ca,cb)+(dg(al,bh,ca,cb)+dg(ah,bl,ca,cb))
def mm1(a,b,ca=1,cb=0):
    return dg(a.astype(bf16),b.astype(bf16),ca,cb)
def mmx(a,b,ca=1,cb=0):
    return lax.dot_general(a,b,(((ca,),(cb,)),((),())),preferred_element_type=f32,precision=HI)

def square_masks():
    i=lax.broadcasted_iota(jnp.int32,(SPAN,SPAN),0); j=lax.broadcasted_iota(jnp.int32,(SPAN,SPAN),1)
    return i,j
def positions(base,rows,cols,axis):
    return base+lax.broadcasted_iota(jnp.int32,(rows,cols),axis)
class Row:
    def __init__(self,ref,row):
        self.ref=ref; self.row=row; self.shape=ref.shape[1:]
    def __getitem__(self,e):
        return self.ref[self.row,e]

def doc_count(starts,pos):
    n=jnp.zeros(pos.shape,jnp.int32)
    for e in range(starts.shape[0]):
        n=n+jnp.where(starts[e]<=pos,1,0)
    return n
def doc_age(starts,pos):
    s=jnp.zeros(pos.shape,jnp.int32)
    for e in range(starts.shape[0]):
        s=jnp.where(starts[e]<=pos,starts[e],s)
    return pos-s
def count_at(starts,p):
    n=jnp.int32(0)
    for e in range(starts.shape[0]):
        n=n+jnp.where(starts[e]<=p,1,0)
    return n
def sigmoid(x):
    return 1.0/(1.0+jnp.exp(-x))
def softplus(x):
    return jnp.maximum(x,0.0)+jnp.log(1.0+jnp.exp(-jnp.abs(x)))

def inverse(A):
    i,j=square_masks()
    near=(i//8)==(j//8)
    eye=jnp.where(i==j,1.0,0.0)
    X=jnp.where(near,-A,0.0); far=jnp.where(near,0.0,A)
    X2=mm3(X,X); X4=mm3(X2,X2)
    Di=eye+X; Di=Di+mm3(Di,X2); Di=Di+mm3(Di,X4)
    Y=-mm3(Di,far)
    Y2=mm3(Y,Y); Y4=mm3(Y2,Y2)
    T=Di+mm3(Y4,Di); T=T+mm3(Y2,T); T=T+mm3(Y,T)
    return T

def span_terms(n,q,k,starts,xc,xr,rate,bias):
    i,j=square_masks()
    base=n*SPAN
    docs=doc_count(starts,positions(base,SPAN,128,0))
    docr=doc_count(starts,positions(base,1,SPAN,1))
    before=count_at(starts,base-1)
    lastdoc=count_at(starts,base+SPAN-1)
    lower=jnp.where(i>=j,1.0,0.0); upper=jnp.where(i<=j,1.0,0.0)
    beta=sigmoid(xc[:,0:1])
    g=-rate*softplus(xc[:,1:2]+bias)
    gr=-rate*softplus(xr+bias)
    G=mmx(lower,jnp.broadcast_to(g,(SPAN,128)))
    Gr=mmx(jnp.broadcast_to(gr,(8,SPAN)),upper)[0:1]
    same=docs[:,:SPAN]==docr
    incl=(i>=j)&same
    D=jnp.where(incl,jnp.exp(jnp.where(incl,G[:,:SPAN]-Gr,0.0)),0.0)
    gam=jnp.where(docs==before,jnp.exp(G),0.0)
    end=jnp.where(docs==lastdoc,jnp.exp(G[SPAN-1:SPAN]-G),0.0)
    KK=dg(k,k,1,1); QK=dg(q,k,1,1)
    return beta,g,D,gam,end,KK,QK,i,j

def conv_pre(upad,taps,age,base,rows):
    window=upad[pl.ds(base,rows+8),:]
    pre=window[8:]*taps[3:4]
    for back in range(1,4):
        ok=jnp.where(age>=back,1.0,0.0)
        pre=pre+window[8-back:8-back+rows]*ok*taps[3-back:4-back]
    return pre

def forward_kernel(n,zc,copies,heads,DK,DV,tok,cot,gain,hgain,starts2,dlog,dbias,wq,wk,wv,ws,wg,wo,
                   normed,scale,cotfull,wfull,wgfull,wofull,cotc,n1c,gate_ref,oall,branch,part,taps_ref,u_ref,xr_ref,xc_ref,q_ref,k_ref,v_ref,s_ref,w_ref,t_ref,qt_ref,mh_ref,ml_ref,
                   tokfull,wbuf,sbuf,pbuf,rbuf,tbuf,upad,un_ref,gc_ref,on_ref,o_ref,zs,zr,cs,cr,ks,kr,es,er,is_,ir,os_,or_,ld,*gs):
    L=u_ref.shape[0]; NC=L//SPAN; local_len=L//n; per=local_len//SPAN
    greet(n,zc)
    zt=ShardGather(zc,tok,tokfull,zs,zr); zt.start()
    ws_all=(ws,wq,wk,wv); at=(wq.shape[1]*2+wv.shape[1],0,wq.shape[1],wq.shape[1]*2)
    g1,g2=gs[:3],gs[3:]
    gw=gathers(n,[(w,wfull,0,a) for w,a in zip(ws_all,at)],g1)
    gb=gathers(n,[(wg,wgfull,0),(wo,wofull,1)],g2)
    each(gw,"start")
    zt.finish()
    zk=ShardGather(zc,cot,cotfull,cs,cr); zk.start()
    rows=tokfull.shape[0]; D=tokfull.shape[1]
    def norm(c,_):
        r=pl.ds(pl.multiple_of(c*32,32),32)
        x=tokfull[r,:].astype(f32)
        sc=lax.rsqrt(jnp.sum(x*x,axis=1,keepdims=True)/D+EPSILON)
        normed[r,:]=(x*sc*gain[...]).astype(bf16)
        scale[r,:]=jnp.broadcast_to(sc,(32,128))
        return 0
    lax.fori_loop(0,rows//32,norm,0)
    rbuf[...]=jnp.zeros(rbuf.shape,f32)
    each(gw,"middle")
    pair=lax.div(lax.axis_index("seq"),copies); my_seq=lax.div(pair,heads); my_head=lax.rem(pair,heads)
    for i,g in enumerate(gw):
        g.late(); g.finish()
        if i==0: each(gb,"start")
        width=ws_all[i].shape[1]
        buf=sbuf if i==0 else wbuf.at[:,pl.ds(0,width)]
        c=pltpu.make_async_copy(wfull.at[:,pl.ds(at[i],width)],buf,ld.at[0]); c.start(); c.wait()
        if i==0:
            small=jnp.dot(normed[...],sbuf[...],preferred_element_type=f32)
            for sq in range(rows//local_len):
                fl=flat_form(small[sq*local_len:(sq+1)*local_len,0:8*((2*heads+7)//8)])
                for h in range(heads):
                    base=(sq*heads+h)*8
                    rbuf[base:base+1]=fl[h:h+1]
                    rbuf[base+1:base+2]=fl[heads+h:heads+h+1]
            cq=heads*DK//n; cv=heads*DV//n; step=sbuf.shape[0]//n
            for kind,(width_c,count,skip) in enumerate(((cq,DK,0),(cq,DK,cq),(cv,DV,2*cq))):
                for j in range(count//width_c):
                    dev=my_head*(count//width_c)+j
                    to=(0,DK,2*DK)[kind]+j*width_c
                    tbuf[to:to+width_c]=sbuf[pl.ds(pl.multiple_of(dev*step+skip,16),width_c),:]
            ch=tbuf.shape[0]
            ident=jnp.where(lax.broadcasted_iota(jnp.int32,(ch,ch),0)==lax.broadcasted_iota(jnp.int32,(ch,ch),1),1.0,0.0).astype(bf16)
            tt=dg(tbuf[...],ident,0,0)
            taps_ref[...]=tt[2*heads:2*heads+4]
        else:
            tile=min(width,256)
            def column(j,_,i=i,tile=tile):
                cc=pl.ds(pl.multiple_of(j*tile,128),tile)
                pbuf[:,pl.ds(pl.multiple_of(at[i]+j*tile,128),tile)]=jnp.dot(normed[...],wbuf[:,cc],preferred_element_type=f32).astype(bf16)
                return 0
            lax.fori_loop(0,width//tile,column,0)
    inward=ToPairs(n,copies,heads,local_len,pbuf,rbuf,u_ref,xr_ref,DK,DV,is_,ir); inward.start()
    starts=Row(starts2,my_seq)
    at_head=lax.axis_index("shard")*heads+my_head
    rate=jnp.exp(jnp.full((1,1),dlog[at_head],f32)); bias=dbias[at_head]
    zk.finish()
    cols=ColumnSplit(n,normed,n1c,es,er); cols.start()
    ccol=ColumnSplit(n,cotfull,cotc,ks,kr); ccol.start()
    inward.finish()
    upad[0:8]=jnp.zeros((8,upad.shape[1]),f32)
    def turn(m,_):
        xc_ref[pl.ds(pl.multiple_of(m*local_len,local_len),local_len),:]=col_form(xr_ref[pl.ds(pl.multiple_of(m*8,8),8),:])
        return 0
    lax.fori_loop(0,n,turn,0,unroll=2)
    taps=taps_ref[...]
    R=128
    def load(c,_):
        upad[pl.ds(pl.multiple_of(8+c*R,8),R),:]=u_ref[pl.ds(pl.multiple_of(c*R,R),R),:].astype(f32)
        return 0
    lax.fori_loop(0,L//R,load,0)
    def conv(c,_):
        base=pl.multiple_of(c*R,R)
        age=doc_age(starts,positions(base,R,128,0))[:,0:1]
        pre=conv_pre(upad,taps,age,base,R)
        act=pre*sigmoid(pre)
        rows=pl.ds(base,R)
        aq=act[:,:DK]; ak=act[:,DK:2*DK]
        q_ref[rows,:]=(aq*lax.rsqrt(jnp.sum(aq*aq,axis=1,keepdims=True)+EPSILON)*DK**-0.5).astype(bf16)
        k_ref[rows,:]=(ak*lax.rsqrt(jnp.sum(ak*ak,axis=1,keepdims=True)+EPSILON)).astype(bf16)
        v_ref[rows,:]=act[:,2*DK:].astype(bf16)
        return 0
    lax.fori_loop(0,L//R,conv,0)
    def one_span(n,xr):
        rows=pl.ds(pl.multiple_of(n*SPAN,SPAN),SPAN)
        q=q_ref[rows,:]; k=k_ref[rows,:]; v=v_ref[rows,:]
        beta,g,D,gam,end,KK,QK,i,j=span_terms(n,q,k,starts,xc_ref[rows,:],xr,rate,bias)
        A=jnp.where(i>j,beta*D*KK,0.0)
        T=inverse(A)
        kf=k.astype(f32)
        UW=mm3(T,jnp.concatenate([beta*v.astype(f32),(beta*gam)*kf],axis=1))
        P=QK*D
        PW=mm1(P,UW)
        qt=gam*q.astype(f32)-PW[:,DV:]
        NM=mm3(end*kf,UW,0,0)
        t_ref[n]=T
        on_ref[n]=PW[:,:DV]
        w_ref[n]=UW[:,:DV]
        qt_ref[n,0:SPAN]=qt.astype(bf16)
        qt_ref[n,SPAN:]=UW[:,DV:].astype(bf16)
        un_ref[n]=NM[:,:DV]
        mh,ml=halves(NM[:,DV:])
        mh_ref[n]=mh; ml_ref[n]=ml
        gc_ref[n]=jnp.broadcast_to(gam[SPAN-1:SPAN],(8,128))
    def local(m,_):
        xr=xr_ref[pl.ds(pl.multiple_of(m*8,8),8),:]
        for e in range(per): one_span(m*per+e,xr[1:2,e*SPAN:(e+1)*SPAN])
        return 0
    lax.fori_loop(0,n,local,0,unroll=2)
    each(gb,"middle")
    def chain(n,S):
        s_ref[n]=S
        sh,sl=halves(S); mh=mh_ref[n]; ml=ml_ref[n]
        gc=gc_ref[n][0:1]
        return jnp.concatenate([gc]*(DV//128),axis=1)*S+un_ref[n]-(dg(mh,sh)+(dg(ml,sh)+dg(mh,sl)))
    lax.fori_loop(0,NC,chain,jnp.zeros((DK,DV),f32),unroll=2)
    def emit(n,_):
        rows=pl.ds(pl.multiple_of(n*SPAN,SPAN),SPAN)
        r=dg(qt_ref[n],s_ref[n].astype(bf16))
        o_ref[rows,:]=(on_ref[n]+r[:SPAN]).astype(o_ref.dtype)
        w_ref[n]=w_ref[n]-r[SPAN:]
        return 0
    lax.fori_loop(0,NC,emit,0,unroll=4)
    outward=FromPairs(n,copies,heads,local_len,[(o_ref,lambda t: (pl.ds(pl.multiple_of(t*local_len,local_len),local_len),slice(None)),
        oall,lambda seq,head: (pl.ds(pl.multiple_of(seq*local_len,local_len),local_len),pl.ds(pl.multiple_of(head*DV,128),DV)))],os_,or_)
    outward.start()
    each(gb,"late"); cols.finish(); ccol.finish(); gb[0].finish()
    width=wg.shape[1]
    c=pltpu.make_async_copy(wgfull,wbuf.at[:,pl.ds(0,width)],ld.at[0]); c.start(); c.wait()
    def column(j,_):
        cc=pl.ds(pl.multiple_of(j*256,256),256)
        gate_ref[:,cc]=jnp.dot(normed[...],wbuf[:,cc],preferred_element_type=f32)
        return 0
    lax.fori_loop(0,width//256,column,0)
    gb[1].finish()
    for j in range(D//wbuf.shape[1]):
        c=pltpu.make_async_copy(wofull.at[:,pl.ds(j*wbuf.shape[1],wbuf.shape[1])],wbuf.at[pl.ds(j*wofull.shape[0],wofull.shape[0]),:],ld.at[j]); c.start()
        c.wait()
    outward.finish()
    def mix(c,_):
        r=pl.ds(pl.multiple_of(c*32,32),32)
        for h in range(heads):
            cc=pl.ds(h*DV,DV)
            o=oall[r,cc].astype(f32); g=gate_ref[r,cc]
            rho=lax.rsqrt(jnp.sum(o*o,axis=1,keepdims=True)/DV+EPSILON)
            branch[r,cc]=(o*rho*hgain[...]*(g*sigmoid(g))).astype(bf16)
        return 0
    lax.fori_loop(0,rows//32,mix,0)
    tiles=wbuf.shape[1]//256
    def column(j,_):
        blk=lax.div(j,tiles); inner=lax.rem(j,tiles)
        w=wbuf[pl.ds(pl.multiple_of(blk*wofull.shape[0],16),wofull.shape[0]),pl.ds(pl.multiple_of(inner*256,256),256)]
        part[:,pl.ds(pl.multiple_of(j*256,256),256)]=jnp.dot(branch[...],w,preferred_element_type=f32).astype(bf16)
        return 0
    lax.fori_loop(0,D//256,column,0)

def backward_kernel(n,copies,heads,dall,u_ref,taps_ref,xc_ref,xr_ref,starts2,dlog,dbias,q_ref,k_ref,v_ref,s_ref,w_ref,t_ref,qt_ref,mh_ref,ml_ref,hid,bra,dgp,
                    duall,rows_out,dtaps_ref,dh_ref,hidfull,brafull,dgpfull,upad,dpre,ds_ref,dqkv,r_ref,gc_ref,do_ref,du_ref,dx_ref,dxr,is_,ir,os_,or_,*gs):
    L=u_ref.shape[0]; NC=L//SPAN; DV=v_ref.shape[1]; DK=q_ref.shape[1]; local_len=L//n; per=local_len//SPAN
    greet(n,1)
    inward=ToPairs(n,copies,heads,local_len,dall,None,do_ref,None,DK,DV,is_,ir); inward.start()
    gw=gathers(n,[(hid,hidfull,0),(bra,brafull,0),(dgp,dgpfull,0)],gs)
    pair=lax.div(lax.axis_index("seq"),copies)
    starts=Row(starts2,lax.div(pair,heads)); at_head=lax.axis_index("shard")*heads+lax.rem(pair,heads)
    rate=jnp.exp(jnp.full((1,1),dlog[at_head],f32)); bias=dbias[at_head]
    taps=taps_ref[...]
    R=128
    upad[0:8]=jnp.zeros((8,upad.shape[1]),f32)
    dpre[L:L+8]=jnp.zeros((8,upad.shape[1]),f32)
    def load(c,_):
        upad[pl.ds(pl.multiple_of(8+c*R,8),R),:]=u_ref[pl.ds(pl.multiple_of(c*R,R),R),:].astype(f32)
        return 0
    lax.fori_loop(0,L//R,load,0)
    inward.finish()
    each(gw,"start")
    dx_ref[...]=jnp.zeros(dx_ref.shape,f32)
    def early(n,_):
        rows=pl.ds(pl.multiple_of(n*SPAN,SPAN),SPAN)
        r_ref[n]=dg(qt_ref[n][0:SPAN],do_ref[rows,:],0,0)
        base=n*SPAN
        G=jnp.sum(-rate*softplus(xc_ref[rows,1:2]+bias),axis=0,keepdims=True)
        alive=jnp.where(count_at(starts,base+SPAN-1)==count_at(starts,base-1),1.0,0.0)
        gc_ref[n]=jnp.broadcast_to(jnp.exp(G)*alive,(8,128))
        return 0
    lax.fori_loop(0,NC,early,0,unroll=4)
    def chain(m,dS):
        n=NC-1-m
        ds_ref[n]=dS
        sh,sl=halves(dS); mh=mh_ref[n]; ml=ml_ref[n]
        gc=gc_ref[n][0:1]
        return jnp.concatenate([gc]*(DV//128),axis=1)*dS+r_ref[n]-(dg(mh,sh,0,0)+(dg(ml,sh,0,0)+dg(mh,sl,0,0)))
    lax.fori_loop(0,NC,chain,jnp.zeros((DK,DV),f32),unroll=2)
    each(gw,"middle")
    def one_span(n,xr,sums):
        rows=pl.ds(pl.multiple_of(n*SPAN,SPAN),SPAN)
        q=q_ref[rows,:]; k=k_ref[rows,:]; v=v_ref[rows,:]; dO=do_ref[rows,:]
        xc=xc_ref[rows,:]
        beta,g,D,gam,end,KK,QK,i,j=span_terms(n,q,k,starts,xc,xr,rate,bias)
        S0=s_ref[n]; dS1=ds_ref[n]
        S0h=S0.astype(bf16); dSh=dS1.astype(bf16)
        kf=k.astype(f32); qf=q.astype(f32); vf=v.astype(f32)
        W=w_ref[n].astype(bf16); T=t_ref[n].astype(bf16)
        P=(QK*D).astype(bf16)
        dW=dg(P,dO,0,0)+jnp.concatenate([end]*(DV//128),axis=1)*dg(k,dSh)
        Y=dg(T,dW.astype(bf16),0,0)
        dOY=jnp.concatenate([dO,Y.astype(bf16)],axis=0)
        dPA=dg(dOY,W,1,1)
        GS=dg(dOY,S0h,1,1)
        dOS=GS[:SPAN]; YS=GS[SPAN:]
        Z=dg(W,dSh,1,1)
        dPD=dPA[:SPAN]*D
        EA=jnp.where(i>j,-dPA[SPAN:]*D,0.0)
        E=beta*EA
        A1=jnp.concatenate([dPD,E],axis=0).astype(bf16)
        r1=dg(A1,k)
        r2=dg(A1,jnp.concatenate([q,k],axis=0),0,0)
        dqkv[rows,0:DK]=gam*dOS+r1[:SPAN]
        dqkv[rows,DK:2*DK]=r1[SPAN:]+r2-(beta*gam)*YS+end*Z
        dqkv[rows,2*DK:]=beta*Y
        EK=EA*KK
        kYS=jnp.sum(kf*YS,axis=1,keepdims=True)
        dbeta=jnp.sum(Y*vf,axis=1,keepdims=True)-gam*kYS+jnp.sum(EK,axis=1,keepdims=True)
        Fm=dPD*QK+beta*EK
        dgam=jnp.sum(qf*dOS,axis=1,keepdims=True)-beta*kYS
        dend=jnp.sum(kf*Z,axis=1,keepdims=True)*end
        colsum=mmx(Fm,jnp.ones((SPAN,128),f32),0,0)
        dG=jnp.sum(Fm,axis=1,keepdims=True)-colsum+dgam*gam-dend
        tail=jnp.sum(jnp.sum(S0*dS1,axis=0,keepdims=True),axis=1,keepdims=True)
        last=jnp.sum(dend,axis=0,keepdims=True)+gam[SPAN-1:SPAN]*tail
        row=lax.broadcasted_iota(jnp.int32,(SPAN,128),0)
        dG=dG+jnp.where(row==SPAN-1,last,0.0)
        upper=jnp.where(i<=j,1.0,0.0)
        dlog=mmx(upper,dG)
        dbp=(dbeta*beta*(1.0-beta))
        ddp=dlog*(-rate)*sigmoid(xc[:,1:2]+bias)
        dx_ref[rows,0:1]=dbp[:,0:1]
        dx_ref[rows,1:2]=ddp[:,0:1]
        sl,sb=sums
        return (sl+jnp.sum(dlog*g,axis=0,keepdims=True),sb+jnp.sum(ddp,axis=0,keepdims=True))
    def local(m,sums):
        xr=xr_ref[pl.ds(pl.multiple_of(m*8,8),8),:]
        for e in range(per): sums=one_span(m*per+e,xr[1:2,e*SPAN:(e+1)*SPAN],sums)
        return sums
    zero=jnp.zeros((1,128),f32)
    sl,sb=lax.fori_loop(0,n,local,(zero,zero),unroll=2)
    def turn(m,_):
        dxr[pl.ds(pl.multiple_of(m*8,8),8),:]=flat_form(dx_ref[pl.ds(pl.multiple_of(m*local_len,local_len),local_len),:])
        return 0
    lax.fori_loop(0,n,turn,0,unroll=2)
    dh_ref[0:1]=sl; dh_ref[1:2]=sb
    def norms(c,dt):
        base=pl.multiple_of(c*R,R)
        age=doc_age(starts,positions(base,R,128,0))[:,0:1]
        pre=conv_pre(upad,taps,age,base,R)
        sg=sigmoid(pre); act=pre*sg
        rows=pl.ds(base,R)
        d=dqkv[rows,:]
        def unit_back(a,dd,f):
            s=lax.rsqrt(jnp.sum(a*a,axis=1,keepdims=True)+EPSILON)
            dot=jnp.sum(a*dd,axis=1,keepdims=True)
            return f*(s*dd-a*(s*s*s*dot))
        dact=jnp.concatenate([unit_back(act[:,:DK],d[:,:DK],DK**-0.5),unit_back(act[:,DK:2*DK],d[:,DK:2*DK],1.0),d[:,2*DK:]],axis=1)
        dp=dact*sg*(1.0+pre*(1.0-sg))
        dpre[rows,:]=dp
        window=upad[pl.ds(base,R+8),:]
        new=[]
        for j in range(4):
            back=3-j
            x=window[8-back:8-back+R]
            if back: x=x*jnp.where(age>=back,1.0,0.0)
            new.append(dt[j]+jnp.sum(x*dp,axis=0,keepdims=True))
        return tuple(new)
    zt=jnp.zeros((1,upad.shape[1]),f32)
    dt=lax.fori_loop(0,L//R,norms,(zt,)*4)
    for j in range(4): dtaps_ref[j:j+1]=dt[j]
    def back(c,_):
        base=pl.multiple_of(c*R,R)
        window=dpre[pl.ds(base,R+8),:]
        age=doc_age(starts,positions(base,R+8,128,0))[:,0:1]
        d=window[:R]*taps[3:4]
        for s in range(1,4):
            x=window[s:s+R]*jnp.where(age[s:s+R]>=s,1.0,0.0)
            d=d+x*taps[3-s:4-s]
        du_ref[pl.ds(base,R),:]=d.astype(bf16)
        return 0
    lax.fori_loop(0,L//R,back,0)
    wk=heads*DK
    at=lambda start,width: (lambda t: (pl.ds(pl.multiple_of(t*local_len,local_len),local_len),pl.ds(start,width)))
    to=lambda start,width: (lambda seq,head: (pl.ds(pl.multiple_of(seq*local_len,local_len),local_len),pl.ds(pl.multiple_of(start+head*width,128),width)))
    outward=FromPairs(n,copies,heads,local_len,[(du_ref,at(0,DK),duall,to(0,DK)),(du_ref,at(DK,DK),duall,to(wk,DK)),(du_ref,at(2*DK,DV),duall,to(2*wk,DV)),
        (dxr,lambda t: (pl.ds(pl.multiple_of(t*8,8),8),slice(None)),rows_out,lambda seq,head: (pl.ds(pl.multiple_of((seq*heads+head)*8,8),8),slice(None)))],os_,or_)
    outward.start()
    each(gw,"late"); outward.finish(); each(gw,"finish")

SM=pl.BlockSpec(memory_space=pltpu.SMEM); VM=pl.BlockSpec(memory_space=pltpu.VMEM)
def S(shape,dt=f32): return jax.ShapeDtypeStruct(shape,dt)
def forward(n,zc,copies,heads,tok,cot,gain,hgain,starts,dlog,dbias,wq,wk,wv,ws,wg,wo,DK,DV):
    R,F=tok.shape; D=F*zc; local_len=R//starts.shape[0]; L=n*local_len; NC=L//SPAN; pairs=n//copies; CH=2*DK+DV; HV=heads*DV
    rows=lambda *w: S((w[0].shape[0]*n,sum(x.shape[1] for x in w)),bf16)
    wide=max(wv.shape[1],wg.shape[1])
    return call("mixer",5,functools.partial(forward_kernel,n,zc,copies,heads,DK,DV),(tok,cot,gain,hgain,starts,dlog,dbias,wq,wk,wv,ws,wg,wo),[VM,VM,VM,VM,SM,SM,SM]+[ANY]*6,
      [S((R,D),bf16),S((R,128)),S((R,D),bf16),rows(wq,wk,wv,ws),rows(wg),S((wo.shape[0],wo.shape[1]*n),bf16),S((R*n,D//n),bf16),S((R*n,D//n),bf16),
       S((R,HV)),S((R,HV),bf16),S((R,HV),bf16),S((R,D),bf16),S((4,CH)),
       S((L,CH),bf16),S((n*8,local_len)),S((L,8)),S((L,DK),bf16),S((L,DK),bf16),S((L,DV),bf16),S((NC,DK,DV)),S((NC,SPAN,DV)),S((NC,SPAN,SPAN)),
       S((NC,2*SPAN,DK),bf16),S((NC,DK,DK),bf16),S((NC,DK,DK),bf16)],
      [VM,VM]+[ANY]*6+[VM]*17,
      [pltpu.VMEM((R,D),bf16),pltpu.VMEM((D,wide),bf16),pltpu.VMEM((D,ws.shape[1]),bf16),pltpu.VMEM((R,heads*CH),bf16),pltpu.VMEM((pairs*8,local_len),f32),pltpu.VMEM((CH,128),bf16),
       pltpu.VMEM((L+8,CH),f32),pltpu.VMEM((NC,DK,DV),f32),pltpu.VMEM((NC,8,128),f32),pltpu.VMEM((NC,SPAN,DV),f32),pltpu.VMEM((L,DV),bf16)]
      +pair_sems(zc)*2+pair_sems(n)*2+[pltpu.SemaphoreType.DMA((4,n)),pltpu.SemaphoreType.DMA((4,n)),pltpu.SemaphoreType.DMA((1,pairs)),pltpu.SemaphoreType.DMA((1,pairs)),pltpu.SemaphoreType.DMA((D//wide,))]
      +gather_sems(n,4)+gather_sems(n,2))
def backward(n,copies,heads,dall,taps,starts,dlog,dbias,saved,hid,bra,dgp):
    u,xr,xc,q,k,v,s,w,t,qt,mh,ml=saved
    L,CH=u.shape; NC=L//SPAN; DK=q.shape[1]; DV=v.shape[1]; local_len=L//n; pairs=n//copies; R=dall.shape[0]
    full=lambda a: S((a.shape[0]*n,a.shape[1]),bf16)
    return call("rec_bwd",6,functools.partial(backward_kernel,n,copies,heads),(dall,u,taps,xc,xr,starts,dlog,dbias,q,k,v,s,w,t,qt,mh,ml,hid,bra,dgp),[ANY]+[VM]*4+[SM]*3+[VM]*9+[ANY]*3,
      [S((R,heads*CH),bf16),S((pairs*8,local_len)),S((4,CH)),S((2,128)),full(hid),full(bra),full(dgp)],[ANY,ANY,VM,VM,ANY,ANY,ANY],
      [pltpu.VMEM((L+8,CH),f32),pltpu.VMEM((L+8,CH),f32),pltpu.VMEM((NC,DK,DV),f32),pltpu.VMEM((L,CH),f32),pltpu.VMEM((NC,DK,DV),f32),pltpu.VMEM((NC,8,128),f32),
       pltpu.VMEM((L,DV),bf16),pltpu.VMEM((L,CH),bf16),pltpu.VMEM((L,8),f32),pltpu.VMEM((n*8,local_len),f32),
       pltpu.SemaphoreType.DMA((4,n)),pltpu.SemaphoreType.DMA((4,n)),pltpu.SemaphoreType.DMA((4,pairs)),pltpu.SemaphoreType.DMA((4,pairs))]+gather_sems(n,3))


MESH=pl.DeviceIdType.MESH
ANY=pl.BlockSpec(memory_space=pl.ANY)

def flip(s,bit):
    return s+bit-2*bit*lax.rem(lax.div(s,bit),2)

def flips(s,mask):
    bit=1
    while bit<=mask:
        if mask&bit: s=flip(s,bit)
        bit*=2
    return s

def greet(n,zc):
    s=lax.axis_index("seq"); z=lax.axis_index("shard")
    bar=pltpu.get_barrier_semaphore()
    for d in range(1,n):
        pl.semaphore_signal(bar,inc=1,device_id={"seq":lax.rem(s+d,n)},device_id_type=MESH)
    for d in range(1,zc):
        pl.semaphore_signal(bar,inc=1,device_id={"shard":lax.rem(z+d,zc)},device_id_type=MESH)
    pl.semaphore_wait(bar,n-1+zc-1)

def links(n):
    return 8 if n==8 else n

class SeqGather:
    def __init__(self,n,src,dst,axis,sems,c0=0):
        self.n=n; self.src=src; self.dst=dst; self.axis=axis; self.send,self.recv,self.loc=sems
        self.R,self.C=src.shape
        self.r0=0; self.nr=self.R; self.c0=c0
        self.s=lax.axis_index("seq")
        self.open=[]
    def slot(self,t,a,b):
        if self.axis==0:
            return self.dst.at[pl.ds(pl.multiple_of(t*self.R+self.r0+a,16),b-a),pl.ds(self.c0,self.C)]
        return self.dst.at[pl.ds(self.r0+a,b-a),pl.ds(pl.multiple_of(t*self.C,128),self.C)]
    def copy(self,src,t,a,b,k,to):
        c=pltpu.make_async_remote_copy(src_ref=src,dst_ref=self.slot(t,a,b),send_sem=self.send.at[k],recv_sem=self.recv.at[k],device_id={"seq":to},device_id_type=MESH)
        c.start()
        return c
    def pass_on(self,t,a,b,k,to):
        return self.copy(self.slot(t,a,b),t,a,b,k,to)
    def start(self):
        s=self.s; nr=self.nr
        mine=self.src.at[pl.ds(self.r0,nr),:]
        self.own=pltpu.make_async_copy(mine,self.slot(s,0,nr),self.loc)
        self.own.start()
        masks=(2,4) if self.n==8 else range(2,self.n,2)
        self.direct=[self.copy(mine,s,0,nr,i+1,flips(s,m)) for i,m in enumerate(masks)]
        self.open.append(self.copy(mine,s,0,nr,0,flip(s,1)))
    def middle(self):
        s=self.s; nr=self.nr; h=nr//2
        if self.n!=8: return
        x,y=flip(s,2),flip(s,4)
        self.direct[0].wait_recv()
        fa=self.pass_on(x,0,h,3,y)
        self.open.append(self.pass_on(x,0,nr,5,flip(s,1)))
        self.direct[1].wait_recv()
        fb=self.pass_on(y,h,nr,4,x)
        self.open.append(self.pass_on(y,0,nr,6,flip(s,1)))
        self.diag=(fa,fb)
    def late(self):
        s=self.s; nr=self.nr
        if self.n==8:
            for f in self.diag: f.wait_recv()
            self.open.append(self.pass_on(flips(s,6),0,nr,7,flip(s,1)))
            for f in self.diag: f.wait_send()
        else:
            for i,m in enumerate(range(2,self.n,2)):
                self.direct[i].wait_recv()
                self.open.append(self.pass_on(flips(s,m),0,nr,self.n//2+i,flip(s,1)))
        for f in self.direct: f.wait_send()
    def finish(self):
        for f in self.open: f.wait()
        self.own.wait()

class ShardGather:
    def __init__(self,zc,src,dst,send,recv):
        self.zc=zc; self.src=src; self.dst=dst; self.send=send; self.recv=recv
        self.z=lax.axis_index("shard"); self.C=src.shape[1]
    def slot(self):
        return self.dst.at[:,pl.ds(pl.multiple_of(self.z*self.C,128),self.C)]
    def start(self):
        self.own=pltpu.make_async_copy(self.src,self.slot(),self.recv.at[0]); self.own.start()
        self.cs=[]
        for d in range(1,self.zc):
            c=pltpu.make_async_remote_copy(src_ref=self.src,dst_ref=self.slot(),send_sem=self.send.at[d],recv_sem=self.recv.at[d],device_id={"shard":lax.rem(self.z+d,self.zc)},device_id_type=MESH)
            c.start(); self.cs.append(c)
    def finish(self):
        for c in self.cs: c.wait()
        self.own.wait()

class ShardSplit:
    def __init__(self,zc,src,box,send,recv):
        self.zc=zc; self.src=src; self.box=box; self.send=send; self.recv=recv
        self.z=lax.axis_index("shard"); self.C=box.shape[2]
    def start(self):
        C=self.C
        self.own=pltpu.make_async_copy(self.src.at[:,pl.ds(pl.multiple_of(self.z*C,128),C)],self.box.at[0],self.recv.at[0]); self.own.start()
        self.cs=[]
        for d in range(1,self.zc):
            to=lax.rem(self.z+d,self.zc)
            c=pltpu.make_async_remote_copy(src_ref=self.src.at[:,pl.ds(pl.multiple_of(to*C,128),C)],dst_ref=self.box.at[d],send_sem=self.send.at[d],recv_sem=self.recv.at[d],device_id={"shard":to},device_id_type=MESH)
            c.start(); self.cs.append(c)
    def finish(self):
        for c in self.cs: c.wait()
        self.own.wait()

class ShardAll:
    def __init__(self,axis,n,box,send,recv):
        self.axis=axis; self.n=n; self.box=box; self.send=send; self.recv=recv; self.me=lax.axis_index(axis)
    def start(self):
        self.cs=[]
        for d in range(1,self.n):
            c=pltpu.make_async_remote_copy(src_ref=self.box.at[self.me],dst_ref=self.box.at[self.me],send_sem=self.send.at[d],recv_sem=self.recv.at[d],device_id={self.axis:lax.rem(self.me+d,self.n)},device_id_type=MESH)
            c.start(); self.cs.append(c)
    def finish(self):
        for c in self.cs: c.wait()

class ColumnSplit:
    def __init__(self,n,src,dst,send,recv):
        self.n=n; self.src=src; self.dst=dst; self.send=send; self.recv=recv
        self.s=lax.axis_index("seq"); self.C=dst.shape[1]; self.R=src.shape[0]
    def start(self):
        n,s,C,R=self.n,self.s,self.C,self.R
        to_rows=self.dst.at[pl.ds(pl.multiple_of(s*R,16),R),:]
        block=lambda t: self.src.at[:,pl.ds(pl.multiple_of(t*C,128),C)]
        self.own=pltpu.make_async_copy(block(s),to_rows,self.recv.at[0]); self.own.start()
        self.cs=[]
        for d in range(1,n):
            t=lax.rem(s+d,n)
            c=pltpu.make_async_remote_copy(src_ref=block(t),dst_ref=to_rows,send_sem=self.send.at[d],recv_sem=self.recv.at[d],device_id={"seq":t},device_id_type=MESH)
            c.start(); self.cs.append(c)
    def finish(self):
        for c in self.cs: c.wait()
        self.own.wait()

class ToPairs:
    def __init__(self,n,copies,heads,local_len,src,rows_src,dst,rows_dst,DK,DV,send,recv):
        self.__dict__.update(n=n,copies=copies,heads=heads,ll=local_len,src=src,rows_src=rows_src,dst=dst,rows_dst=rows_dst,DK=DK,DV=DV,send=send,recv=recv)
    def parts(self,t):
        s=lax.axis_index("seq"); ll,DK,DV,heads=self.ll,self.DK,self.DV,self.heads
        pair=lax.div(t,self.copies); seq=lax.div(pair,heads); head=lax.rem(pair,heads)
        rows=pl.ds(pl.multiple_of(seq*ll,ll),ll); to=pl.ds(pl.multiple_of(s*ll,ll),ll)
        if self.rows_src is None:
            return [(self.src.at[rows,pl.ds(pl.multiple_of(head*DV,128),DV)],self.dst.at[to,:])]
        wk=heads*DK
        out=[]
        for start,width,at in ((0,DK,0),(wk,DK,DK),(2*wk,DV,2*DK)):
            out.append((self.src.at[rows,pl.ds(pl.multiple_of(start+head*width,128),width)],self.dst.at[to,pl.ds(at,width)]))
        out.append((self.rows_src.at[pl.ds(pl.multiple_of(pair*8,8),8),:],self.rows_dst.at[pl.ds(pl.multiple_of(s*8,8),8),:]))
        return out
    def start(self):
        s=lax.axis_index("seq"); self.cs=[]
        for d in range(self.n):
            t=lax.rem(s+d,self.n)
            for i,(a,b) in enumerate(self.parts(t)):
                if d==0: c=pltpu.make_async_copy(a,b,self.recv.at[i,0])
                else: c=pltpu.make_async_remote_copy(src_ref=a,dst_ref=b,send_sem=self.send.at[i,d],recv_sem=self.recv.at[i,d],device_id={"seq":t},device_id_type=MESH)
                c.start(); self.cs.append(c)
    def finish(self):
        for c in self.cs: c.wait()

class FromPairs:
    def __init__(self,n,copies,heads,local_len,items,send,recv):
        self.__dict__.update(n=n,copies=copies,heads=heads,items=items,send=send,recv=recv)
    def start(self):
        s=lax.axis_index("seq"); pairs=self.n//self.copies; p=lax.div(s,self.copies); r=lax.rem(s,self.copies)
        seq=lax.div(p,self.heads); head=lax.rem(p,self.heads); self.cs=[]
        for d in range(pairs):
            t=lax.rem(p+d,pairs)*self.copies+r
            for i,(src,at,dst,to) in enumerate(self.items):
                a=src.at[at(t)]; b=dst.at[to(seq,head)]
                if d==0: c=pltpu.make_async_copy(a,b,self.recv.at[i,0])
                else: c=pltpu.make_async_remote_copy(src_ref=a,dst_ref=b,send_sem=self.send.at[i,d],recv_sem=self.recv.at[i,d],device_id={"seq":t},device_id_type=MESH)
                c.start(); self.cs.append(c)
    def finish(self):
        for c in self.cs: c.wait()

def flat_form(cols):
    r=cols.shape[0]
    i=lax.broadcasted_iota(jnp.int32,(r,r),0); j=lax.broadcasted_iota(jnp.int32,(r,r),1)
    return mmx(cols,jnp.where(i==j,1.0,0.0),0,0)

def row_form(cols):
    return mmx(jnp.ones((8,cols.shape[1]),f32),cols,1,1)

def col_form(rows):
    r=rows.shape[1]
    i=lax.broadcasted_iota(jnp.int32,(r,r),0); j=lax.broadcasted_iota(jnp.int32,(r,r),1)
    return mmx(jnp.where(i==j,1.0,0.0),rows,1,1)

def gathers(n,pairs,sems):
    send,recv,loc=sems
    return [SeqGather(n,src,dst,axis,(send.at[i],recv.at[i],loc.at[i]),*c0) for i,(src,dst,axis,*c0) in enumerate(pairs)]
def gather_sems(n,k):
    return [pltpu.SemaphoreType.DMA((k,links(n))),pltpu.SemaphoreType.DMA((k,links(n))),pltpu.SemaphoreType.DMA((k,))]
def pair_sems(k):
    return [pltpu.SemaphoreType.DMA((k,)),pltpu.SemaphoreType.DMA((k,))]
def each(ops,name):
    for o in ops: getattr(o,name)()

def ffn_kernel(n,zc,part,tok,cot,cotfull,gain,wg,wu,wd,res,gres,afull,gffn,outpart,hidden,dgfull,dufull,n2c,
               box,sums,nloc,nfull,gw_,uw_,dw_,gv,uv,dgate,dup,two,as_,ar,bs,br,cs,cr,ds_,dr,es,er,fs,fr,hs,hr,*gs):
    greet(n,zc)
    D=part.shape[1]; R=part.shape[0]; FF=gv.shape[1]; z=lax.axis_index("shard")
    split=ShardSplit(zc,part,box,as_,ar); split.start()
    g1,g2=gs[:3],gs[3:]
    gw=gathers(n,[(wg,gw_,0),(wu,uw_,0),(wd,dw_,1)],g1)
    each(gw,"start")
    split.finish()
    r=tok[...].astype(f32)
    for d in range(zc): r=r+box[d].astype(f32)
    res[...]=r
    sums[z]=row_form(r*r)
    tot=ShardAll("shard",zc,sums,bs,br); tot.start(); tot.finish()
    t=sums[0]
    for d in range(1,zc): t=t+sums[d]
    sc=lax.rsqrt(col_form(t)[:,0:1]/D+EPSILON)
    nloc[...]=(r*sc*gain[...]).astype(bf16)
    zg=ShardGather(zc,nloc,nfull,cs,cr); zg.start()
    each(gw,"middle")
    zg.finish()
    cols=ColumnSplit(n,nfull,n2c,es,er); cols.start()
    tiles=[(a,min(a+512,FF)) for a in range(0,FF,512)]
    gw[0].late(); gw[0].finish()
    for a,b in tiles: gv[:,a:b]=jnp.dot(nfull[...],gw_[:,a:b],preferred_element_type=f32)
    gw[1].late(); gw[1].finish()
    for a,b in tiles: uv[:,a:b]=jnp.dot(nfull[...],uw_[:,a:b],preferred_element_type=f32)
    def act(c,_):
        rr=pl.ds(pl.multiple_of(c*32,32),32)
        g=gv[rr,:]
        hidden[rr,:]=(g*sigmoid(g)*uv[rr,:]).astype(bf16)
        return 0
    lax.fori_loop(0,R//32,act,0)
    gw[2].late(); gw[2].finish()
    for a,b in tiles:
        dh=dg(cotfull[...],dw_[a:b,:],1,1)
        g=gv[:,a:b]; sg=sigmoid(g)
        dgate[:,a:b]=(dh*uv[:,a:b]*sg*(1.0+g*(1.0-sg))).astype(bf16)
        dup[:,a:b]=(dh*(g*sg)).astype(bf16)
    gd=gathers(n,[(dgate,dgfull,0),(dup,dufull,0)],g2)
    each(gd,"start")
    def back(j,_):
        rr=pl.ds(pl.multiple_of(j*256,256),256)
        two[:,rr]=(dg(dgate[...],gw_[rr,:],1,1)+dg(dup[...],uw_[rr,:],1,1)).astype(bf16)
        return 0
    lax.fori_loop(0,D//256,back,0)
    split=ShardSplit(zc,two,box,fs,fr)
    split.start()
    def outp(j,_):
        cc=pl.ds(pl.multiple_of(j*256,256),256)
        outpart[:,cc]=jnp.dot(hidden[...],dw_[:,cc],preferred_element_type=f32).astype(bf16)
        return 0
    lax.fori_loop(0,D//256,outp,0)
    split.finish()
    g=box[0].astype(f32)
    for d in range(1,zc): g=g+box[d].astype(f32)
    r=res[...]
    gained=gain[...]*g
    sums[zc+z]=row_form(gained*r)
    tot=ShardAll("shard",zc,sums.at[pl.ds(zc,zc)],ds_,dr); tot.start()
    gffn[...]=jnp.broadcast_to(jnp.sum(g*r*sc,axis=0,keepdims=True),gffn.shape)
    tot.finish()
    t=sums[zc]
    for d in range(1,zc): t=t+sums[zc+d]
    inner=col_form(t)[:,0:1]/D
    gr=cot[...].astype(f32)+sc*(gained-r*(sc*sc*inner))
    gres[...]=gr
    nloc[...]=gr.astype(bf16)
    zg=ShardGather(zc,nloc,afull,hs,hr); zg.start()
    each(gd,"middle")
    zg.finish()
    each(gd,"late"); cols.finish(); each(gd,"finish")

def tail_kernel(n,zc,partdx,partout,res,gres,tok,scale,gain,small,dy,dsm,att,output,gtok,dyfull,dsmfull,attc,smalls,totals,box,boxo,sums,as_,ar,bs,br,cs,cr,es,er,fs,fr,hs,hr,*gs):
    greet(n,zc)
    D=partdx.shape[1]
    split=ShardSplit(zc,partdx,box,as_,ar); split.start()
    gw=gathers(n,[(dy,dyfull,0),(dsm,dsmfull,0)],gs)
    each(gw,"start")
    ca=ColumnSplit(n,att,attc,es,er); ca.start()
    split.finish()
    so=ShardSplit(zc,partout,boxo,fs,fr); so.start()
    g=box[0].astype(f32)
    for d in range(1,zc): g=g+box[d].astype(f32)
    x=tok[...].astype(f32); sc=scale[...][:,0:1]
    gained=gain[...]*g
    sums[lax.axis_index("shard")]=row_form(gained*x)
    tot=ShardAll("shard",zc,sums,bs,br); tot.start()
    me=lax.axis_index("seq")
    smalls[me]=small[...]
    smalls[me,0:1,0:g.shape[1]]=jnp.sum(g*x*sc,axis=0,keepdims=True)
    sa=ShardAll("seq",n,smalls,cs,cr); sa.start()
    tot.finish()
    t=sums[0]
    for d in range(1,zc): t=t+sums[d]
    inner=col_form(t)[:,0:1]/D
    gtok[...]=gres[...]+sc*(gained-x*(sc*sc*inner))
    sa.finish()
    t=smalls[0]
    for d in range(1,n): t=t+smalls[d]
    totals[lax.axis_index("shard")]=t
    za=ShardAll("shard",zc,totals,hs,hr); za.start()
    each(gw,"middle")
    so.finish()
    o=res[...]
    for d in range(zc): o=o+boxo[d].astype(f32)
    output[...]=o
    za.finish()
    each(gw,"late"); ca.finish(); each(gw,"finish")

def call(name,cid,kernel,args,specs,outs,ospecs,scratch):
    return pl.pallas_call(kernel,name=name,out_shape=tuple(outs),in_specs=specs,out_specs=tuple(ospecs),scratch_shapes=scratch,
      compiler_params=pltpu.CompilerParams(collective_id=cid,has_side_effects=True,vmem_limit_bytes=56*2**20))(*args)

def ffn(n,zc,part,tok,cot,cotfull,gain,wg,wu,wd):
    R,F=tok.shape; D=F*zc; FF=wg.shape[1]
    return call("ffn",2,functools.partial(ffn_kernel,n,zc),(part,tok,cot,cotfull,gain,wg,wu,wd),[ANY]+[VM]*4+[ANY]*3,
      [S((R,F)),S((R,F)),S((R,D),bf16),S((8,F)),S((R,D),bf16),S((R,FF),bf16),S((R*n,FF),bf16),S((R*n,FF),bf16),S((R*n,D//n),bf16)],
      [VM]*6+[ANY]*3,
      [pltpu.VMEM((zc,R,F),bf16),pltpu.VMEM((2*zc,8,R),f32),pltpu.VMEM((R,F),bf16),pltpu.VMEM((R,D),bf16),pltpu.VMEM((D,FF),bf16),pltpu.VMEM((D,FF),bf16),pltpu.VMEM((FF,D),bf16),
       pltpu.VMEM((R,FF),f32),pltpu.VMEM((R,FF),f32),pltpu.VMEM((R,FF),bf16),pltpu.VMEM((R,FF),bf16),pltpu.VMEM((R,D),bf16)]
      +pair_sems(zc)*4+pair_sems(n)+pair_sems(zc)*2+gather_sems(n,3)+gather_sems(n,2))
def tail(n,zc,partdx,partout,res,gres,tok,scale,gain,small,dy,dsm,att):
    R,F=tok.shape; D=F*zc
    full=lambda a: S((a.shape[0]*n,a.shape[1]),bf16)
    return call("tail",4,functools.partial(tail_kernel,n,zc),(partdx,partout,res,gres,tok,scale,gain,small,dy,dsm,att),[ANY,ANY]+[VM]*6+[ANY]*3,
      [S((R,F)),S((R,F)),full(dy),full(dsm),S((R*n,D//n),bf16),S((n,)+small.shape),S((zc,)+small.shape)],
      [VM,VM,ANY,ANY,ANY,VM,VM],
      [pltpu.VMEM((zc,R,F),bf16),pltpu.VMEM((zc,R,F),bf16),pltpu.VMEM((zc,8,R),f32)]+pair_sems(zc)*2+pair_sems(n)*2+pair_sems(zc)*2+gather_sems(n,2))


def per_device(
    tokens, doc_starts, norm_gain, query_weight, key_weight, value_weight, outgate_weight,
    beta_weight, decay_weight, query_conv, key_conv, value_conv, decay_log, decay_bias, head_gain,
    output_weight, ffn_gain, gate_weight, up_weight, down_weight, cotangent,
):
    seq_count, local_len, feature_part = tokens.shape
    row_count = seq_count * local_len
    shard_count = lax.axis_size("shard")
    shard_pos = lax.axis_index("shard")
    seq_devices = lax.axis_size("seq")
    seq_pos = lax.axis_index("seq")
    model_dim = feature_part * shard_count
    head_count = beta_weight.shape[1]
    key_dim = query_weight.shape[1] // head_count
    value_dim = value_weight.shape[1] // head_count
    tap_count = query_conv.shape[1]
    width_k = head_count * key_dim
    channels = 2 * key_dim + value_dim
    feature_start = shard_pos * feature_part
    head_start = shard_pos * head_count
    pairs = seq_count * head_count
    copies = seq_devices // pairs
    length = local_len * seq_devices
    spans = length // SPAN
    my_pair = seq_pos // copies
    my_seq = my_pair // head_count
    my_head = my_pair % head_count

    def project(a, b):
        return jnp.dot(a, b, preferred_element_type=f32)

    taps_local = jnp.concatenate([query_conv, key_conv, value_conv], axis=0)
    tap_rows = taps_local.shape[0]
    width_v = head_count * value_dim
    padding = -(2 * head_count + tap_count) % 128
    taps_padded = jnp.pad(taps_local, ((0, query_weight.shape[0] - tap_rows), (0, padding)))
    weights_small = jnp.concatenate([beta_weight, decay_weight, taps_padded], axis=1)
    edges = [0, width_k, 2 * width_k, 2 * width_k + width_v]
    flat = lambda x: x.reshape(row_count, x.shape[2])
    local_ffn_gain = lax.dynamic_slice_in_dim(ffn_gain, feature_start, feature_part)[None]
    local_norm_gain = lax.dynamic_slice_in_dim(norm_gain, feature_start, feature_part)[None]
    tokens_flat, cot_flat = flat(tokens), flat(cotangent)
    (
        normed_one, scale_one, cot_rows, full_one, full_outgate, full_output, cot_cols, normed_one_cols,
        gate_proj, o_flat, branch, attn_part, taps, *saved,
    ) = forward(
        seq_devices, shard_count, copies, head_count, tokens_flat, cot_flat, norm_gain[None], head_gain[None],
        doc_starts, decay_log, decay_bias, query_weight, key_weight, value_weight, weights_small, outgate_weight,
        output_weight, key_dim, value_dim,
    )
    residual, grad_residual, attn_cot, grad_ffn_part, out_part, hidden, dgate_all, dup_all, normed_two_cols = ffn(
        seq_devices, shard_count, attn_part, tokens_flat, cot_flat, cot_rows, local_ffn_gain, gate_weight, up_weight, down_weight
    )
    shape4 = (seq_count, local_len, head_count, -1)
    gate_proj = gate_proj.reshape(shape4)
    o = o_flat.astype(f32).reshape(shape4)
    rho = lax.rsqrt(jnp.mean(o * o, axis=3, keepdims=True) + EPSILON)
    gate_sig = jax.nn.sigmoid(gate_proj)
    gate_silu = gate_proj * gate_sig
    z = o * rho

    def back(cols, weight):
        return jnp.einsum("rc,dc->rd", cols, weight, preferred_element_type=f32)

    def grad(left, right):
        return jnp.einsum("rd,rc->dc", left, right, preferred_element_type=f32)

    out_gate, out_up = grad(normed_two_cols, dgate_all), grad(normed_two_cols, dup_all)
    grad_mixed = (
        back(attn_cot, full_output).astype(bf16).astype(f32).reshape(shape4)
    )
    grad_head_gain = jnp.sum(grad_mixed * z * gate_silu, axis=(0, 1, 2))
    dz = grad_mixed * head_gain * gate_silu
    grad_o = (rho * (dz - z * jnp.mean(dz * z, axis=3, keepdims=True))).astype(bf16)
    grad_gate_proj = (grad_mixed * z * head_gain * gate_sig * (1.0 + gate_proj * (1.0 - gate_sig))).astype(bf16)
    grad_gate_proj = grad_gate_proj.reshape(row_count, head_count * value_dim)

    grad_qkv, drates, dtaps, dhead, hidden_all, branch_all, dgate_proj_all = backward(
        seq_devices, copies, head_count, grad_o.reshape(row_count, width_v), taps, doc_starts, decay_log, decay_bias, saved,
        hidden, branch, grad_gate_proj,
    )
    drates = jnp.transpose(drates.reshape(seq_count, head_count, 8, local_len)[:, :, :2], (0, 3, 2, 1))
    grad_small = jnp.pad(drates.reshape(row_count, 2 * head_count).astype(bf16), ((0, 0), (0, tap_count + padding)))
    one_part = (
        back(grad_qkv, full_one[:, : edges[3]]) + back(grad_small, full_one[:, edges[3] :]) + back(grad_gate_proj, full_outgate)
    ).astype(bf16)
    at_head = head_start + my_pair % head_count
    primary = jnp.where(seq_pos % copies == 0, 1.0, 0.0)
    total_heads = decay_log.shape[0]
    width_s = max(feature_part, channels)
    widen = lambda x: jnp.pad(x, ((0, 0), (0, width_s - x.shape[1])))
    heads_row = lax.dynamic_update_slice(
        lax.dynamic_update_slice(jnp.zeros((1, width_s), f32), dhead[0:1, :1] * primary, (0, at_head)),
        dhead[1:2, :1] * primary,
        (0, total_heads + at_head),
    )
    small = jnp.concatenate(
        [jnp.zeros((1, width_s), f32), widen(grad_ffn_part[:1]), widen(grad_head_gain[None]), heads_row, widen(dtaps)], axis=0
    )
    output, grad_tokens, qkv_all, small_all, attn_cols, smalls, totals = tail(
        seq_devices, shard_count, one_part, out_part, residual, grad_residual, tokens_flat, scale_one,
        local_norm_gain, small, grad_qkv, grad_small, attn_cot,
    )
    outs_one = [grad(normed_one_cols, qkv_all[:, edges[i] : edges[i + 1]]) for i in range(3)]
    outs_small = grad(normed_one_cols, small_all)
    outs_one += [
        grad(normed_one_cols, dgate_proj_all), outs_small[:, :head_count], outs_small[:, head_count : 2 * head_count]
    ]
    out_down = grad(hidden_all, cot_cols)
    out_output = grad(branch_all, attn_cols)
    tap_sum = jnp.sum(smalls[::copies, 4:].reshape(seq_count, head_count, tap_count, width_s), axis=0)

    def own_rows(taps_part):
        rows = jnp.swapaxes(taps_part, 1, 2).reshape(-1, tap_count)
        count = rows.shape[0] // seq_devices
        return lax.dynamic_slice_in_dim(rows, seq_pos * count, count)

    out_qconv = own_rows(tap_sum[:, :, :key_dim])
    out_kconv = own_rows(tap_sum[:, :, key_dim : 2 * key_dim])
    out_vconv = own_rows(tap_sum[:, :, 2 * key_dim : channels])
    out_norm = totals[:, 0, :feature_part].reshape(-1)
    out_ffn = totals[:, 1, :feature_part].reshape(-1)
    totals_all = jnp.sum(totals, axis=0)
    out_head = totals_all[2, :value_dim]
    out_log = totals_all[3, :total_heads]
    out_bias = totals_all[3, total_heads : 2 * total_heads]
    shape3 = (seq_count, local_len, feature_part)
    return (
        output.reshape(shape3), grad_tokens.reshape(shape3), out_norm, *outs_one, out_qconv, out_kconv, out_vconv,
        out_log, out_bias, out_head, out_output, out_ffn, out_gate, out_up, out_down,
    )


def solution(mesh):
    P = PartitionSpec
    rows, cols = P("seq", "shard"), P("shard", "seq")
    both, acts = P(("shard", "seq"), None), P(None, "seq", "shard")
    return jax.shard_map(
        per_device,
        mesh=mesh,
        in_specs=(acts, P(), P()) + (rows,) * 6 + (both,) * 3 + (P(), P(), P(), cols, P(), rows, rows, cols, acts),
        out_specs=(acts, acts, P()) + (rows,) * 6 + (both,) * 3 + (P(), P(), P(), cols, P(), rows, rows, cols),
        check_vma=False,
    )
```

```python
import functools
import jax, jax.numpy as jnp
from jax import lax
from jax.experimental import pallas as pl
from jax.experimental.pallas import tpu as pltpu
from jax.sharding import PartitionSpec
f32=jnp.float32; bf16=jnp.bfloat16
SPAN=64
EPSILON=1e-6
HI=lax.Precision.HIGHEST

def dg(a,b,ca=1,cb=0):
    return lax.dot_general(a,b,(((ca,),(cb,)),((),())),preferred_element_type=f32)
def halves(x):
    h=x.astype(bf16)
    return h,(x-h.astype(f32)).astype(bf16)
def mm3(a,b,ca=1,cb=0):
    ah,al=halves(a); bh,bl=halves(b)
    return dg(ah,bh,ca,cb)+(dg(al,bh,ca,cb)+dg(ah,bl,ca,cb))
def mm1(a,b,ca=1,cb=0):
    return dg(a.astype(bf16),b.astype(bf16),ca,cb)
def mmx(a,b,ca=1,cb=0):
    return lax.dot_general(a,b,(((ca,),(cb,)),((),())),preferred_element_type=f32,precision=HI)

def square_masks():
    i=lax.broadcasted_iota(jnp.int32,(SPAN,SPAN),0); j=lax.broadcasted_iota(jnp.int32,(SPAN,SPAN),1)
    return i,j
def positions(base,rows,cols,axis):
    return base+lax.broadcasted_iota(jnp.int32,(rows,cols),axis)
class Row:
    def __init__(self,ref,row):
        self.ref=ref; self.row=row; self.shape=ref.shape[1:]
    def __getitem__(self,e):
        return self.ref[self.row,e]

def doc_count(starts,pos):
    n=jnp.zeros(pos.shape,jnp.int32)
    for e in range(starts.shape[0]):
        n=n+jnp.where(starts[e]<=pos,1,0)
    return n
def doc_age(starts,pos):
    s=jnp.zeros(pos.shape,jnp.int32)
    for e in range(starts.shape[0]):
        s=jnp.where(starts[e]<=pos,starts[e],s)
    return pos-s
def count_at(starts,p):
    n=jnp.int32(0)
    for e in range(starts.shape[0]):
        n=n+jnp.where(starts[e]<=p,1,0)
    return n
def sigmoid(x):
    return 1.0/(1.0+jnp.exp(-x))
def softplus(x):
    return jnp.maximum(x,0.0)+jnp.log(1.0+jnp.exp(-jnp.abs(x)))

def inverse(A):
    i,j=square_masks()
    near=(i//8)==(j//8)
    eye=jnp.where(i==j,1.0,0.0)
    X=jnp.where(near,-A,0.0); far=jnp.where(near,0.0,A)
    X2=mm3(X,X); X4=mm3(X2,X2)
    Di=eye+X; Di=Di+mm3(Di,X2); Di=Di+mm3(Di,X4)
    Y=-mm3(Di,far)
    Y2=mm3(Y,Y); Y4=mm3(Y2,Y2)
    T=Di+mm3(Y4,Di); T=T+mm3(Y2,T); T=T+mm3(Y,T)
    return T

def span_terms(n,q,k,starts,xc,xr,rate,bias):
    i,j=square_masks()
    base=n*SPAN
    docs=doc_count(starts,positions(base,SPAN,128,0))
    docr=doc_count(starts,positions(base,1,SPAN,1))
    before=count_at(starts,base-1)
    lastdoc=count_at(starts,base+SPAN-1)
    lower=jnp.where(i>=j,1.0,0.0); upper=jnp.where(i<=j,1.0,0.0)
    beta=sigmoid(xc[:,0:1])
    g=-rate*softplus(xc[:,1:2]+bias)
    gr=-rate*softplus(xr+bias)
    G=mmx(lower,jnp.broadcast_to(g,(SPAN,128)))
    Gr=mmx(jnp.broadcast_to(gr,(8,SPAN)),upper)[0:1]
    same=docs[:,:SPAN]==docr
    incl=(i>=j)&same
    D=jnp.where(incl,jnp.exp(jnp.where(incl,G[:,:SPAN]-Gr,0.0)),0.0)
    gam=jnp.where(docs==before,jnp.exp(G),0.0)
    end=jnp.where(docs==lastdoc,jnp.exp(G[SPAN-1:SPAN]-G),0.0)
    KK=dg(k,k,1,1); QK=dg(q,k,1,1)
    return beta,g,D,gam,end,KK,QK,i,j

def conv_pre(upad,taps,age,base,rows):
    window=upad[pl.ds(base,rows+8),:]
    pre=window[8:]*taps[3:4]
    for back in range(1,4):
        ok=jnp.where(age>=back,1.0,0.0)
        pre=pre+window[8-back:8-back+rows]*ok*taps[3-back:4-back]
    return pre

def forward_kernel(n,zc,copies,heads,DK,DV,tok,cot,gain,hgain,starts2,dlog,dbias,wb,wd,qc,kc,vc,wq,wk,wv,wg,wo,wgate,
                   scale,cotfull,wfull,wgfull,wofull,wgatefull,cotc,n1c,gate_ref,oall,branch,part,taps_ref,u_ref,xr_ref,xc_ref,q_ref,k_ref,v_ref,s_ref,w_ref,t_ref,qt_ref,mh_ref,ml_ref,
                   tokfull,normed,ws,wbuf,sbuf,pbuf,rbuf,tbuf,upad,un_ref,gc_ref,on_ref,o_ref,zs,zr,cs,cr,ks,kr,es,er,fs,fr,hs,hr,is_,ir,os_,or_,ld,*gs):
    L=u_ref.shape[0]; NC=L//SPAN; local_len=L//n; per=local_len//SPAN
    put=lambda x,first: dg(x[...],jnp.where(lax.broadcasted_iota(jnp.int32,(x.shape[1],128),0)+first==lax.broadcasted_iota(jnp.int32,(x.shape[1],128),1),1.0,0.0).astype(bf16))
    ws[...]=(put(wb,0)+put(wd,heads)).astype(bf16)
    at_row=0
    for x in (qc,kc,vc):
        ws[at_row:at_row+x.shape[0]]=(ws[at_row:at_row+x.shape[0]].astype(f32)+put(x,2*heads)).astype(bf16)
        at_row+=x.shape[0]
    greet(n,zc)
    zt=ShardGather(zc,tok,tokfull,zs,zr); zt.start()
    ws_all=(ws,wq,wk,wv); at=(wq.shape[1]*2+wv.shape[1],0,wq.shape[1],wq.shape[1]*2)
    g1,g2=gs[:3],gs[3:]
    gw=gathers(n,[(w,wfull,0,a) for w,a in zip(ws_all,at)],g1)
    gb=gathers(n,[(wg,wgfull,0),(wo,wofull,1),(wgate,wgatefull,0)],g2)
    each(gw,"start")
    zt.finish()
    zk=ShardGather(zc,cot,cotfull,cs,cr); zk.start()
    rows=tokfull.shape[0]; D=tokfull.shape[1]
    def norm(c,_):
        r=pl.ds(pl.multiple_of(c*32,32),32)
        x=tokfull[r,:].astype(f32)
        sc=lax.rsqrt(jnp.sum(x*x,axis=1,keepdims=True)/D+EPSILON)
        normed[r,:]=(x*sc*gain[...]).astype(bf16)
        scale[r,:]=jnp.broadcast_to(sc,(32,128))
        return 0
    lax.fori_loop(0,rows//32,norm,0)
    rbuf[...]=jnp.zeros(rbuf.shape,f32)
    each(gw,"middle")
    pair=lax.div(lax.axis_index("seq"),copies); my_seq=lax.div(pair,heads); my_head=lax.rem(pair,heads)
    for i,g in enumerate(gw):
        g.late(); g.finish()
        width=ws_all[i].shape[1]
        buf=sbuf if i==0 else wbuf.at[:,pl.ds(0,width)]
        c=pltpu.make_async_copy(wfull.at[:,pl.ds(at[i],width)],buf,ld.at[0]); c.start(); c.wait()
        if i==0:
            small=jnp.dot(normed[...],sbuf[...],preferred_element_type=f32)
            for sq in range(rows//local_len):
                fl=flat_form(small[sq*local_len:(sq+1)*local_len,0:8*((2*heads+7)//8)])
                for h in range(heads):
                    base=(sq*heads+h)*8
                    rbuf[base:base+1]=fl[h:h+1]
                    rbuf[base+1:base+2]=fl[heads+h:heads+h+1]
            cq=heads*DK//n; cv=heads*DV//n; step=sbuf.shape[0]//n
            for kind,(width_c,count,skip) in enumerate(((cq,DK,0),(cq,DK,cq),(cv,DV,2*cq))):
                for j in range(count//width_c):
                    dev=my_head*(count//width_c)+j
                    to=(0,DK,2*DK)[kind]+j*width_c
                    tbuf[to:to+width_c]=sbuf[pl.ds(pl.multiple_of(dev*step+skip,16),width_c),:]
            ch=tbuf.shape[0]
            ident=jnp.where(lax.broadcasted_iota(jnp.int32,(ch,ch),0)==lax.broadcasted_iota(jnp.int32,(ch,ch),1),1.0,0.0).astype(bf16)
            tt=dg(tbuf[...],ident,0,0)
            taps_ref[...]=tt[2*heads:2*heads+4]
        else:
            tile=min(width,256)
            def column(j,_,i=i,tile=tile):
                cc=pl.ds(pl.multiple_of(j*tile,128),tile)
                pbuf[:,pl.ds(pl.multiple_of(at[i]+j*tile,128),tile)]=jnp.dot(normed[...],wbuf[:,cc],preferred_element_type=f32).astype(bf16)
                return 0
            lax.fori_loop(0,width//tile,column,0)
    inward=ToPairs(n,copies,heads,local_len,pbuf,rbuf,u_ref,xr_ref,DK,DV,is_,ir); inward.start()
    starts=Row(starts2,my_seq)
    at_head=lax.axis_index("shard")*heads+my_head
    rate=jnp.exp(jnp.full((1,1),dlog[at_head],f32)); bias=dbias[at_head]
    zk.finish()
    inward.finish()
    each(gb,"start")
    cols=SharedColumns(n,zc,normed,n1c,(es,er,fs,fr)); cols.start()
    ccol=SharedColumns(n,zc,cotfull,cotc,(ks,kr,hs,hr)); ccol.start()
    upad[0:8]=jnp.zeros((8,upad.shape[1]),f32)
    def turn(m,_):
        xc_ref[pl.ds(pl.multiple_of(m*local_len,local_len),local_len),:]=col_form(xr_ref[pl.ds(pl.multiple_of(m*8,8),8),:])
        return 0
    lax.fori_loop(0,n,turn,0,unroll=2)
    taps=taps_ref[...]
    R=128
    def load(c,_):
        upad[pl.ds(pl.multiple_of(8+c*R,8),R),:]=u_ref[pl.ds(pl.multiple_of(c*R,R),R),:].astype(f32)
        return 0
    lax.fori_loop(0,L//R,load,0)
    def conv(c,_):
        base=pl.multiple_of(c*R,R)
        age=doc_age(starts,positions(base,R,128,0))[:,0:1]
        pre=conv_pre(upad,taps,age,base,R)
        act=pre*sigmoid(pre)
        rows=pl.ds(base,R)
        aq=act[:,:DK]; ak=act[:,DK:2*DK]
        q_ref[rows,:]=(aq*lax.rsqrt(jnp.sum(aq*aq,axis=1,keepdims=True)+EPSILON)*DK**-0.5).astype(bf16)
        k_ref[rows,:]=(ak*lax.rsqrt(jnp.sum(ak*ak,axis=1,keepdims=True)+EPSILON)).astype(bf16)
        v_ref[rows,:]=act[:,2*DK:].astype(bf16)
        return 0
    lax.fori_loop(0,L//R,conv,0)
    def one_span(n,xr):
        rows=pl.ds(pl.multiple_of(n*SPAN,SPAN),SPAN)
        q=q_ref[rows,:]; k=k_ref[rows,:]; v=v_ref[rows,:]
        beta,g,D,gam,end,KK,QK,i,j=span_terms(n,q,k,starts,xc_ref[rows,:],xr,rate,bias)
        A=jnp.where(i>j,beta*D*KK,0.0)
        T=inverse(A)
        kf=k.astype(f32)
        UW=mm3(T,jnp.concatenate([beta*v.astype(f32),(beta*gam)*kf],axis=1))
        P=QK*D
        PW=mm1(P,UW)
        qt=gam*q.astype(f32)-PW[:,DV:]
        NM=mm3(end*kf,UW,0,0)
        t_ref[n]=T
        on_ref[n]=PW[:,:DV]
        w_ref[n]=UW[:,:DV]
        qt_ref[n,0:SPAN]=qt.astype(bf16)
        qt_ref[n,SPAN:]=UW[:,DV:].astype(bf16)
        un_ref[n]=NM[:,:DV]
        mh,ml=halves(NM[:,DV:])
        mh_ref[n]=mh; ml_ref[n]=ml
        gc_ref[n]=jnp.broadcast_to(gam[SPAN-1:SPAN],(8,128))
    def local(m,_):
        xr=xr_ref[pl.ds(pl.multiple_of(m*8,8),8),:]
        for e in range(per): one_span(m*per+e,xr[1:2,e*SPAN:(e+1)*SPAN])
        return 0
    lax.fori_loop(0,n,local,0,unroll=2)
    each(gb,"middle"); cols.middle(); ccol.middle()
    def chain(n,S):
        s_ref[n]=S
        sh,sl=halves(S); mh=mh_ref[n]; ml=ml_ref[n]
        gc=gc_ref[n][0:1]
        return jnp.concatenate([gc]*(DV//128),axis=1)*S+un_ref[n]-(dg(mh,sh)+(dg(ml,sh)+dg(mh,sl)))
    lax.fori_loop(0,NC,chain,jnp.zeros((DK,DV),f32),unroll=2)
    def emit(n,_):
        rows=pl.ds(pl.multiple_of(n*SPAN,SPAN),SPAN)
        r=dg(qt_ref[n],s_ref[n].astype(bf16))
        o_ref[rows,:]=(on_ref[n]+r[:SPAN]).astype(o_ref.dtype)
        w_ref[n]=w_ref[n]-r[SPAN:]
        return 0
    lax.fori_loop(0,NC,emit,0,unroll=4)
    outward=FromPairs(n,copies,heads,local_len,[(o_ref,lambda t: (pl.ds(pl.multiple_of(t*local_len,local_len),local_len),slice(None)),
        oall,lambda seq,head: (pl.ds(pl.multiple_of(seq*local_len,local_len),local_len),pl.ds(pl.multiple_of(head*DV,128),DV)))],os_,or_)
    outward.start()
    gb[0].late(); gb[1].late(); gb[0].finish()
    width=wg.shape[1]
    c=pltpu.make_async_copy(wgfull,wbuf.at[:,pl.ds(0,width)],ld.at[0]); c.start(); c.wait()
    def column(j,_):
        cc=pl.ds(pl.multiple_of(j*256,256),256)
        gate_ref[:,cc]=jnp.dot(normed[...],wbuf[:,cc],preferred_element_type=f32)
        return 0
    lax.fori_loop(0,width//256,column,0)
    gb[1].finish()
    for j in range(D//wbuf.shape[1]):
        c=pltpu.make_async_copy(wofull.at[:,pl.ds(j*wbuf.shape[1],wbuf.shape[1])],wbuf.at[pl.ds(j*wofull.shape[0],wofull.shape[0]),:],ld.at[j]); c.start()
        c.wait()
    outward.finish()
    def mix(c,_):
        r=pl.ds(pl.multiple_of(c*32,32),32)
        for h in range(heads):
            cc=pl.ds(h*DV,DV)
            o=oall[r,cc].astype(f32); g=gate_ref[r,cc]
            rho=lax.rsqrt(jnp.sum(o*o,axis=1,keepdims=True)/DV+EPSILON)
            branch[r,cc]=(o*rho*hgain[...]*(g*sigmoid(g))).astype(bf16)
        return 0
    lax.fori_loop(0,rows//32,mix,0)
    tiles=wbuf.shape[1]//256
    def column(j,_):
        blk=lax.div(j,tiles); inner=lax.rem(j,tiles)
        w=wbuf[pl.ds(pl.multiple_of(blk*wofull.shape[0],16),wofull.shape[0]),pl.ds(pl.multiple_of(inner*256,256),256)]
        part[:,pl.ds(pl.multiple_of(j*256,256),256)]=jnp.dot(branch[...],w,preferred_element_type=f32).astype(bf16)
        return 0
    lax.fori_loop(0,D//256,column,0)
    gb[2].late(); cols.finish(); ccol.finish(); gb[2].finish()

def back_kernel(n,zc,copies,heads,total_heads,afull,gate_ref,oall,hgain,tok,scale,gain,res,gres,gffn,taps_ref,u_ref,xc_ref,xr_ref,starts2,dlog,dbias,
                q_ref,k_ref,v_ref,s_ref,w_ref,t_ref,qt_ref,mh_ref,ml_ref,wofull,wfull,wgfull,outpart,branch,hidfull,dgfull,dufull,n2c,n1c,cotc,
                output,gtok,smalls,totals,ogate,oup,odown,oout,oog,dyqfull,dsmfull,brafull,dgpfull,attc,
                upad,dpre,ds_ref,gc_ref,do_ref,du_ref,dx_ref,dxr,bufa,bufb,cola,colb,colc,dob,dgp,dyq,rbuf,dsm,part,upart,box,boxo,sums,
                is_,ir,os_,or_,as_,ar,bs,br,cs,cr,es,er,fs,fr,hs,hr,zs,zr,ld,*gs):
    L=u_ref.shape[0]; NC=L//SPAN; DV=v_ref.shape[1]; DK=q_ref.shape[1]; local_len=L//n; per=local_len//SPAN
    rows_n=tok.shape[0]; F=tok.shape[1]; D=F*zc; VW=wofull.shape[0]; FF=dgfull.shape[1]; wk=heads*DK; wv=heads*DV
    bufs=(bufa,bufb)
    loads={}
    def load_job(key,i,pieces):
        loads[key]=[]
        for j,(src,at) in enumerate(pieces):
            c=pltpu.make_async_copy(src,bufs[i].at[at],ld.at[i,j]); c.start(); loads[key].append(c)
    def ready(key):
        for c in loads[key]: c.wait()
    whole=lambda w: (pl.ds(0,D),pl.ds(0,w))
    every=lambda w: (pl.ds(0,n*rows_n),pl.ds(0,w))
    N=n*rows_n
    load_job("wo",0,[(wofull.at[:,pl.ds(j*VW,VW)],(pl.ds(j*VW,VW),pl.ds(0,VW))) for j in range(D//VW)])
    load_job("og",1,[(wgfull,whole(wv))])
    greet(n,zc)
    so=ShardSplit(zc,outpart,boxo,fs,fr); so.start()
    ready("wo")
    dsm[...]=jnp.zeros(dsm.shape,bf16)
    def heads_back(c,gh):
        r=pl.ds(pl.multiple_of(c*64,64),64)
        for h in range(heads):
            cc=pl.ds(h*DV,DV)
            dm=dg(afull[r,0:VW],bufa[h*DV:(h+1)*DV,0:VW],1,1)
            for j in range(1,D//VW):
                dm=dm+dg(afull[r,j*VW:(j+1)*VW],bufa[j*VW+h*DV:j*VW+(h+1)*DV,0:VW],1,1)
            dm=dm.astype(bf16).astype(f32)
            o=oall[r,cc].astype(f32); g=gate_ref[r,cc]
            rho=lax.rsqrt(jnp.sum(o*o,axis=1,keepdims=True)/DV+EPSILON)
            z=o*rho; sg=sigmoid(g); sil=g*sg
            gh=gh+jnp.sum(dm*z*sil,axis=0,keepdims=True)
            dmg=dm*hgain[...]
            dz=dmg*sil
            dob[r,cc]=(rho*(dz-z*(jnp.sum(dz*z,axis=1,keepdims=True)/DV))).astype(bf16)
            dgp[r,cc]=(dmg*z*sg*(1.0+g*(1.0-sg))).astype(bf16)
        return gh
    gh=lax.fori_loop(0,rows_n//64,heads_back,jnp.zeros((1,DV),f32))
    inward=ToPairs(n,copies,heads,local_len,dob,None,do_ref,None,DK,DV,is_,ir); inward.start()
    load_job("dgate",0,[(dgfull,every(FF))])
    c2=pltpu.make_async_copy(n2c,cola,ld.at[0,4]); c2.start()
    g1,g2=gs[:3],gs[3:]
    gw=gathers(n,[(dgp,dgpfull,0),(branch,brafull,0)],g1)
    pair=lax.div(lax.axis_index("seq"),copies); my_head=lax.rem(pair,heads)
    starts=Row(starts2,lax.div(pair,heads)); at_head=lax.axis_index("shard")*heads+my_head
    rate=jnp.exp(jnp.full((1,1),dlog[at_head],f32)); bias=dbias[at_head]
    taps=taps_ref[...]
    R=128
    upad[0:8]=jnp.zeros((8,upad.shape[1]),f32)
    dpre[L:L+8]=jnp.zeros((8,upad.shape[1]),f32)
    def load(c,_):
        upad[pl.ds(pl.multiple_of(8+c*R,8),R),:]=u_ref[pl.ds(pl.multiple_of(c*R,R),R),:].astype(f32)
        return 0
    lax.fori_loop(0,L//R,load,0)
    inward.finish()
    each(gw,"start")
    ca=SharedColumns(n,zc,afull,attc,(es,er,zs,zr)); ca.start()
    dx_ref[...]=jnp.zeros(dx_ref.shape,f32)
    def early(n,_):
        rows=pl.ds(pl.multiple_of(n*SPAN,SPAN),SPAN)
        ds_ref[n]=dg(qt_ref[n][0:SPAN],do_ref[rows,:],0,0)
        base=n*SPAN
        G=jnp.sum(-rate*softplus(xc_ref[rows,1:2]+bias),axis=0,keepdims=True)
        alive=jnp.where(count_at(starts,base+SPAN-1)==count_at(starts,base-1),1.0,0.0)
        gc_ref[n]=jnp.broadcast_to(jnp.exp(G)*alive,(8,128))
        return 0
    lax.fori_loop(0,NC,early,0,unroll=4)
    def chain(m,dS):
        n=NC-1-m
        r=ds_ref[n]
        ds_ref[n]=dS
        sh,sl=halves(dS); mh=mh_ref[n]; ml=ml_ref[n]
        gc=gc_ref[n][0:1]
        return jnp.concatenate([gc]*(DV//128),axis=1)*dS+r-(dg(mh,sh,0,0)+(dg(ml,sh,0,0)+dg(mh,sl,0,0)))
    lax.fori_loop(0,NC,chain,jnp.zeros((DK,DV),f32),unroll=2)
    each(gw,"middle"); ca.middle()
    def one_span(n,xr,sums):
        rows=pl.ds(pl.multiple_of(n*SPAN,SPAN),SPAN)
        q=q_ref[rows,:]; k=k_ref[rows,:]; v=v_ref[rows,:]; dO=do_ref[rows,:]
        xc=xc_ref[rows,:]
        beta,g,D,gam,end,KK,QK,i,j=span_terms(n,q,k,starts,xc,xr,rate,bias)
        S0=s_ref[n]; dS1=ds_ref[n]
        S0h=S0.astype(bf16); dSh=dS1.astype(bf16)
        kf=k.astype(f32); qf=q.astype(f32); vf=v.astype(f32)
        W=w_ref[n].astype(bf16); T=t_ref[n].astype(bf16)
        P=(QK*D).astype(bf16)
        dW=dg(P,dO,0,0)+jnp.concatenate([end]*(DV//128),axis=1)*dg(k,dSh)
        Y=dg(T,dW.astype(bf16),0,0)
        dOY=jnp.concatenate([dO,Y.astype(bf16)],axis=0)
        dPA=dg(dOY,W,1,1)
        GS=dg(dOY,S0h,1,1)
        dOS=GS[:SPAN]; YS=GS[SPAN:]
        Z=dg(W,dSh,1,1)
        dPD=dPA[:SPAN]*D
        EA=jnp.where(i>j,-dPA[SPAN:]*D,0.0)
        E=beta*EA
        A1=jnp.concatenate([dPD,E],axis=0).astype(bf16)
        r1=dg(A1,k)
        r2=dg(A1,jnp.concatenate([q,k],axis=0),0,0)
        dpre[rows,0:DK]=gam*dOS+r1[:SPAN]
        dpre[rows,DK:2*DK]=r1[SPAN:]+r2-(beta*gam)*YS+end*Z
        dpre[rows,2*DK:]=beta*Y
        EK=EA*KK
        kYS=jnp.sum(kf*YS,axis=1,keepdims=True)
        dbeta=jnp.sum(Y*vf,axis=1,keepdims=True)-gam*kYS+jnp.sum(EK,axis=1,keepdims=True)
        Fm=dPD*QK+beta*EK
        dgam=jnp.sum(qf*dOS,axis=1,keepdims=True)-beta*kYS
        dend=jnp.sum(kf*Z,axis=1,keepdims=True)*end
        colsum=mmx(Fm,jnp.ones((SPAN,128),f32),0,0)
        dG=jnp.sum(Fm,axis=1,keepdims=True)-colsum+dgam*gam-dend
        tail=jnp.sum(jnp.sum(S0*dS1,axis=0,keepdims=True),axis=1,keepdims=True)
        last=jnp.sum(dend,axis=0,keepdims=True)+gam[SPAN-1:SPAN]*tail
        row=lax.broadcasted_iota(jnp.int32,(SPAN,128),0)
        dG=dG+jnp.where(row==SPAN-1,last,0.0)
        upper=jnp.where(i<=j,1.0,0.0)
        dlog=mmx(upper,dG)
        dbp=(dbeta*beta*(1.0-beta))
        ddp=dlog*(-rate)*sigmoid(xc[:,1:2]+bias)
        dx_ref[rows,0:1]=dbp[:,0:1]
        dx_ref[rows,1:2]=ddp[:,0:1]
        sl,sb=sums
        return (sl+jnp.sum(dlog*g,axis=0,keepdims=True),sb+jnp.sum(ddp,axis=0,keepdims=True))
    def local(m,sums):
        xr=xr_ref[pl.ds(pl.multiple_of(m*8,8),8),:]
        for e in range(per): sums=one_span(m*per+e,xr[1:2,e*SPAN:(e+1)*SPAN],sums)
        return sums
    zero=jnp.zeros((1,128),f32)
    sl,sb=lax.fori_loop(0,n,local,(zero,zero),unroll=2)
    def turn(m,_):
        dxr[pl.ds(pl.multiple_of(m*8,8),8),:]=flat_form(dx_ref[pl.ds(pl.multiple_of(m*local_len,local_len),local_len),:])
        return 0
    lax.fori_loop(0,n,turn,0,unroll=2)
    def norms(c,dt):
        base=pl.multiple_of(c*R,R)
        age=doc_age(starts,positions(base,R,128,0))[:,0:1]
        pre=conv_pre(upad,taps,age,base,R)
        sg=sigmoid(pre); act=pre*sg
        rows=pl.ds(base,R)
        d=dpre[rows,:]
        def unit_back(a,dd,f):
            s=lax.rsqrt(jnp.sum(a*a,axis=1,keepdims=True)+EPSILON)
            dot=jnp.sum(a*dd,axis=1,keepdims=True)
            return f*(s*dd-a*(s*s*s*dot))
        dact=jnp.concatenate([unit_back(act[:,:DK],d[:,:DK],DK**-0.5),unit_back(act[:,DK:2*DK],d[:,DK:2*DK],1.0),d[:,2*DK:]],axis=1)
        dp=dact*sg*(1.0+pre*(1.0-sg))
        dpre[rows,:]=dp
        window=upad[pl.ds(base,R+8),:]
        new=[]
        for j in range(4):
            back=3-j
            x=window[8-back:8-back+R]
            if back: x=x*jnp.where(age>=back,1.0,0.0)
            new.append(dt[j]+jnp.sum(x*dp,axis=0,keepdims=True))
        return tuple(new)
    zt=jnp.zeros((1,upad.shape[1]),f32)
    dt=lax.fori_loop(0,L//R,norms,(zt,)*4)
    each(gw,"late")
    so.finish()
    y=res[...]
    for d in range(zc): y=y+boxo[d].astype(f32)
    output[...]=y
    def back(c,_):
        base=pl.multiple_of(c*R,R)
        window=dpre[pl.ds(base,R+8),:]
        age=doc_age(starts,positions(base,R+8,128,0))[:,0:1]
        d=window[:R]*taps[3:4]
        for s in range(1,4):
            x=window[s:s+R]*jnp.where(age[s:s+R]>=s,1.0,0.0)
            d=d+x*taps[3-s:4-s]
        du_ref[pl.ds(base,R),:]=d.astype(bf16)
        return 0
    lax.fori_loop(0,L//R,back,0)
    cut=lambda start,width: (lambda t: (pl.ds(pl.multiple_of(t*local_len,local_len),local_len),pl.ds(start,width)))
    to=lambda start,width: (lambda seq,head: (pl.ds(pl.multiple_of(seq*local_len,local_len),local_len),pl.ds(pl.multiple_of(start+head*width,128),width)))
    outward=FromPairs(n,copies,heads,local_len,[(du_ref,cut(0,DK),dyq,to(0,DK)),(du_ref,cut(DK,DK),dyq,to(wk,DK)),(du_ref,cut(2*DK,DV),dyq,to(2*wk,DV)),
        (dxr,lambda t: (pl.ds(pl.multiple_of(t*8,8),8),slice(None)),rbuf,lambda seq,head: (pl.ds(pl.multiple_of((seq*heads+head)*8,8),8),slice(None)))],os_,or_)
    outward.start()
    def tiles(width,step): return [(a,min(a+step,width)) for a in range(0,width,step)]
    def spread(first,buf,terms):
        def one(j,_):
            rr=pl.ds(pl.multiple_of(j*256,256),256)
            t=0.0
            for x,a,b in terms: t=t+dg(x[...],buf[rr,a:b],1,1)
            part[:,rr]=t if first else part[:,rr]+t
            return 0
        lax.fori_loop(0,D//256,one,0)
    ready("og"); spread(True,bufb,[(dgp,0,wv)])
    load_job("dup",1,[(dufull,every(FF))])
    ready("dgate"); c2.wait()
    for a,b in tiles(FF,512): ogate[:,a:b]=dg(cola[...],bufa[0:N,a:b],0,0)
    load_job("wv",0,[(wfull.at[:,pl.ds(2*wk,wv+128)],whole(wv+128))])
    outward.finish()
    for sq in range(rows_n//local_len):
        fl=[]
        for e in range(2):
            for h in range(heads): fl.append(rbuf[(sq*heads+h)*8+e:(sq*heads+h)*8+e+1])
        fl=jnp.concatenate(fl+[jnp.zeros((-2*heads%8,local_len),f32)]*(1 if 2*heads%8 else 0),axis=0)
        dsm[sq*local_len:(sq+1)*local_len,0:fl.shape[0]]=col_form(fl).astype(bf16)
    gd=gathers(n,[(dsm,dsmfull,0),(dyq,dyqfull,0)],g2)
    each(gd,"start")
    ready("wv"); spread(False,bufa,[(dyq.at[:,pl.ds(2*wk,wv)],0,wv),(dsm,wv,wv+128)])
    ready("dup")
    for a,b in tiles(FF,512): oup[:,a:b]=dg(cola[...],bufb[0:N,a:b],0,0)
    load_job("wqk",1,[(wfull.at[:,pl.ds(0,2*wk)],whole(2*wk))])
    load_job("hid",0,[(hidfull,every(FF))])
    cc_=pltpu.make_async_copy(cotc,colb,ld.at[1,5]); cc_.start()
    ready("wqk")
    def last(j,_):
        rr=pl.ds(pl.multiple_of(j*256,256),256)
        upart[:,rr]=(part[:,rr]+dg(dyq[:,0:2*wk],bufb[rr,0:2*wk],1,1)).astype(bf16)
        return 0
    lax.fori_loop(0,D//256,last,0)
    split=ShardSplit(zc,upart,box,as_,ar); split.start()
    each(gd,"middle")
    for g in gw: g.finish()
    ca.finish()
    load_job("bra",1,[(brafull,every(VW))])
    ready("hid"); cc_.wait()
    cots=colb[...].reshape(n*rows_n,colb.shape[2])
    for a,b in tiles(FF,256): odown[a:b,:]=dg(bufa[0:N,a:b],cots,0,0)
    load_job("dgp",0,[(dgpfull,every(wv))])
    cc_=pltpu.make_async_copy(attc,colb,ld.at[1,5]); cc_.start()
    c2=pltpu.make_async_copy(n1c,colc,ld.at[0,4]); c2.start()
    ready("bra"); cc_.wait()
    atts=colb[...].reshape(n*rows_n,colb.shape[2])
    for a,b in tiles(VW,256): oout[a:b,:]=dg(bufb[0:N,a:b],atts,0,0)
    split.finish()
    g=box[0].astype(f32)
    for d in range(1,zc): g=g+box[d].astype(f32)
    x=tok[...].astype(f32); sc=scale[...][:,0:1]
    z=lax.axis_index("shard")
    gained=gain[:,pl.ds(pl.multiple_of(z*F,128),F)]*g
    sums[z]=row_form(gained*x)
    tot=ShardAll("shard",zc,sums,bs,br); tot.start()
    me=lax.axis_index("seq")
    W=smalls.shape[2]
    smalls[me]=jnp.zeros(smalls.shape[1:],f32)
    smalls[me,0:1,0:F]=jnp.sum(g*x*sc,axis=0,keepdims=True)
    smalls[me,1:2,0:F]=gffn[0:1]
    smalls[me,2:3,0:DV]=gh
    lane=lax.broadcasted_iota(jnp.int32,(1,128),1)
    first=jnp.where(lax.rem(me,copies)==0,1.0,0.0)
    smalls[me,3:4,0:128]=first*(jnp.where(lane==at_head,sl,0.0)+jnp.where(lane==total_heads+at_head,sb,0.0))
    for j in range(4): smalls[me,4+j:5+j,0:2*DK+DV]=dt[j]
    sa=ShardAll("seq",n,smalls,cs,cr); sa.start()
    tot.finish()
    t=sums[0]
    for d in range(1,zc): t=t+sums[d]
    inner=col_form(t)[:,0:1]/D
    gtok[...]=gres[...]+sc*(gained-x*(sc*sc*inner))
    ready("dgp"); c2.wait()
    n1=colc[...].reshape(n*rows_n,colc.shape[2])
    for a,b in tiles(wv,512): oog[:,a:b]=dg(n1,bufa[0:N,a:b],0,0)
    sa.finish()
    t=smalls[0]
    for d in range(1,n): t=t+smalls[d]
    totals[z]=t
    za=ShardAll("shard",zc,totals,hs,hr); za.start()
    each(gd,"late"); za.finish(); each(gd,"finish")

SM=pl.BlockSpec(memory_space=pltpu.SMEM); VM=pl.BlockSpec(memory_space=pltpu.VMEM)
def S(shape,dt=f32): return jax.ShapeDtypeStruct(shape,dt)
def forward(n,zc,copies,heads,tok,cot,gain,hgain,starts,dlog,dbias,wb,wd,qc,kc,vc,wq,wk,wv,wg,wo,wgate,DK,DV):
    R,F=tok.shape; D=F*zc; local_len=R//starts.shape[0]; L=n*local_len; NC=L//SPAN; pairs=n//copies; CH=2*DK+DV; HV=heads*DV
    rows=lambda *w: S((w[0].shape[0]*n,sum(x.shape[1] for x in w)),bf16)
    wide=max(wv.shape[1],wg.shape[1])
    small=S((D//n,128),bf16)
    return call("mixer",5,functools.partial(forward_kernel,n,zc,copies,heads,DK,DV),(tok,cot,gain,hgain,starts,dlog,dbias,wb,wd,qc,kc,vc,wq,wk,wv,wg,wo,wgate),[VM,VM,VM,VM,SM,SM,SM]+[VM]*5+[ANY]*6,
      [S((R,128)),S((R,D),bf16),rows(wq,wk,wv,small),rows(wg),S((wo.shape[0],wo.shape[1]*n),bf16),rows(wgate),S((n,R,D//n),bf16),S((n,R,D//n),bf16),
       S((R,HV)),S((R,HV),bf16),S((R,HV),bf16),S((R,D),bf16),S((4,CH)),
       S((L,CH),bf16),S((n*8,local_len)),S((L,8)),S((L,DK),bf16),S((L,DK),bf16),S((L,DV),bf16),S((NC,DK,DV)),S((NC,SPAN,DV)),S((NC,SPAN,SPAN)),
       S((NC,2*SPAN,DK),bf16),S((NC,DK,DK),bf16),S((NC,DK,DK),bf16)],
      [VM]+[ANY]*7+[VM]*17,
      [pltpu.VMEM((R,D),bf16),pltpu.VMEM((R,D),bf16),pltpu.VMEM((D//n,128),bf16),pltpu.VMEM((D,wide),bf16),pltpu.VMEM((D,128),bf16),pltpu.VMEM((R,heads*CH),bf16),pltpu.VMEM((pairs*8,local_len),f32),pltpu.VMEM((CH,128),bf16),
       pltpu.VMEM((L+8,CH),f32),pltpu.VMEM((NC,DK,DV),f32),pltpu.VMEM((NC,8,128),f32),pltpu.VMEM((NC,SPAN,DV),f32),pltpu.VMEM((L,DV),bf16)]
      +pair_sems(zc)*2+pair_sems(n)*2+pair_sems(zc)*2+[pltpu.SemaphoreType.DMA((4,n)),pltpu.SemaphoreType.DMA((4,n)),pltpu.SemaphoreType.DMA((1,pairs)),pltpu.SemaphoreType.DMA((1,pairs)),pltpu.SemaphoreType.DMA((D//wide,))]
      +gather_sems(n,4)+gather_sems(n,3))
def back(n,zc,copies,heads,total_heads,afull,gate,oall,hgain,tok,scale,gain,res,gres,gffn,taps,saved,starts,dlog,dbias,wofull,wfull,wgfull,outpart,branch,hidfull,dgfull,dufull,n2c,n1c,cotc):
    u,xr,xc,q,k,v,s,w,t,qt,mh,ml=saved
    L,CH=u.shape; NC=L//SPAN; DK=q.shape[1]; DV=v.shape[1]; local_len=L//n; pairs=n//copies; R,F=tok.shape; D=F*zc; FF=dgfull.shape[1]; HV=heads*DV; VW=wofull.shape[0]
    Dc=D//n; W=max(F,CH)
    bw=max(FF,HV+128,VW,2*heads*DK)
    ins=(afull,gate,oall,hgain,tok,scale,gain,res,gres,gffn,taps,u,xc,xr,starts,dlog,dbias,q,k,v,s,w,t,qt,mh,ml,wofull,wfull,wgfull,outpart,branch,hidfull,dgfull,dufull,n2c,n1c,cotc)
    sem=pltpu.SemaphoreType.DMA
    return call("back",6,functools.partial(back_kernel,n,zc,copies,heads,total_heads),ins,[VM]*14+[SM]*3+[VM]*9+[ANY]*11,
      [S((R,F)),S((R,F)),S((n,8,W)),S((zc,8,W)),S((Dc,FF)),S((Dc,FF)),S((FF,Dc)),S((VW,Dc)),S((Dc,HV)),S((R*n,heads*CH),bf16),S((R*n,128),bf16),S((R*n,HV),bf16),S((R*n,HV),bf16),S((n,R,Dc),bf16)],
      [VM]*9+[ANY]*5,
      [pltpu.VMEM((L+8,CH),f32),pltpu.VMEM((L+8,CH),f32),pltpu.VMEM((NC,DK,DV),f32),pltpu.VMEM((NC,8,128),f32),
       pltpu.VMEM((L,DV),bf16),pltpu.VMEM((L,CH),bf16),pltpu.VMEM((L,8),f32),pltpu.VMEM((n*8,local_len),f32),
       pltpu.VMEM((max(D,R*n),bw),bf16),pltpu.VMEM((max(D,R*n),bw),bf16),pltpu.VMEM((R*n,Dc),bf16),pltpu.VMEM((n,R,Dc),bf16),pltpu.VMEM((n,R,Dc),bf16),
       pltpu.VMEM((R,HV),bf16),pltpu.VMEM((R,HV),bf16),pltpu.VMEM((R,heads*CH),bf16),pltpu.VMEM((pairs*8,local_len),f32),pltpu.VMEM((R,128),bf16),pltpu.VMEM((R,D),f32),pltpu.VMEM((R,D),bf16),
       pltpu.VMEM((zc,R,F),bf16),pltpu.VMEM((zc,R,F),bf16),pltpu.VMEM((zc,8,R),f32)]
      +[sem((1,n)),sem((1,n)),sem((4,pairs)),sem((4,pairs))]+pair_sems(zc)*2+pair_sems(n)*2+pair_sems(zc)*3+[sem((2,6))]+gather_sems(n,2)+gather_sems(n,2))

def last_kernel(n,copies,heads,DK,DV,F,H,n1c,dyq,dsm,smalls,totals,oq,ok,ov,ob,od,qc,kc,vc,onorm,offn,ohead,olog,obias):
    n1=n1c[...].reshape(n1c.shape[0]*n1c.shape[1],n1c.shape[2])
    wk=heads*DK
    for ref,start in ((oq,0),(ok,wk),(ov,2*wk)):
        width=ref.shape[1]
        for a in range(0,width,512):
            b=min(a+512,width)
            ref[:,a:b]=dg(n1,dyq[:,start+a:start+b],0,0)
    sm=dg(n1,dsm[...],0,0)
    ob[...]=sm[:,0:heads]; od[...]=sm[:,heads:2*heads]
    zc=totals.shape[0]
    for z in range(zc):
        onorm[0:1,z*F:(z+1)*F]=totals[z,0:1,0:F]
        offn[0:1,z*F:(z+1)*F]=totals[z,1:2,0:F]
    t=totals[0]
    for z in range(1,zc): t=t+totals[z]
    ohead[...]=t[2:3,0:DV]
    olog[...]=t[3:4,0:H]; obias[...]=t[3:4,H:2*H]
    s=lax.axis_index("seq")
    head=lax.div(s*heads,n)
    taps=0.0
    for sq in range(n//copies//heads): taps=taps+smalls[(sq*heads+head)*copies]
    cols=col_form(taps)
    cq,cv=qc.shape[0],vc.shape[0]
    for part in range(n//heads):
        @pl.when(lax.rem(s,n//heads)==part)
        def _():
            qc[...]=cols[part*cq:(part+1)*cq,4:8]
            kc[...]=cols[DK+part*cq:DK+(part+1)*cq,4:8]
            vc[...]=cols[2*DK+part*cv:2*DK+(part+1)*cv,4:8]
def last(n,copies,heads,DK,DV,F,H,n1c,dyq,dsm,smalls,totals,cq,cv):
    D=F*totals.shape[0]; Dc=n1c.shape[2]
    return pl.pallas_call(functools.partial(last_kernel,n,copies,heads,DK,DV,F,H),name="last",
      out_shape=(S((Dc,heads*DK)),S((Dc,heads*DK)),S((Dc,heads*DV)),S((Dc,heads)),S((Dc,heads)),S((cq,4)),S((cq,4)),S((cv,4)),S((1,D)),S((1,D)),S((1,DV)),S((1,H)),S((1,H))),
      in_specs=[VM]*5,out_specs=(VM,)*13,compiler_params=pltpu.CompilerParams(vmem_limit_bytes=56*2**20))(n1c,dyq,dsm,smalls,totals)


MESH=pl.DeviceIdType.MESH
ANY=pl.BlockSpec(memory_space=pl.ANY)

def flip(s,bit):
    return s+bit-2*bit*lax.rem(lax.div(s,bit),2)

def flips(s,mask):
    bit=1
    while bit<=mask:
        if mask&bit: s=flip(s,bit)
        bit*=2
    return s

def greet(n,zc):
    s=lax.axis_index("seq"); z=lax.axis_index("shard")
    bar=pltpu.get_barrier_semaphore()
    for d in range(1,n):
        pl.semaphore_signal(bar,inc=1,device_id={"seq":lax.rem(s+d,n)},device_id_type=MESH)
    for d in range(1,zc):
        pl.semaphore_signal(bar,inc=1,device_id={"shard":lax.rem(z+d,zc)},device_id_type=MESH)
    pl.semaphore_wait(bar,n-1+zc-1)

def links(n):
    return 8 if n==8 else n

class SeqGather:
    def __init__(self,n,src,dst,axis,sems,c0=0):
        self.n=n; self.src=src; self.dst=dst; self.axis=axis; self.send,self.recv,self.loc=sems
        self.R,self.C=src.shape
        self.r0=0; self.nr=self.R; self.c0=c0
        self.s=lax.axis_index("seq")
        self.open=[]
    def slot(self,t,a,b):
        if self.axis==0:
            return self.dst.at[pl.ds(pl.multiple_of(t*self.R+self.r0+a,16),b-a),pl.ds(self.c0,self.C)]
        return self.dst.at[pl.ds(self.r0+a,b-a),pl.ds(pl.multiple_of(t*self.C,128),self.C)]
    def copy(self,src,t,a,b,k,to):
        c=pltpu.make_async_remote_copy(src_ref=src,dst_ref=self.slot(t,a,b),send_sem=self.send.at[k],recv_sem=self.recv.at[k],device_id={"seq":to},device_id_type=MESH)
        c.start()
        return c
    def pass_on(self,t,a,b,k,to):
        return self.copy(self.slot(t,a,b),t,a,b,k,to)
    def start(self):
        s=self.s; nr=self.nr
        mine=self.src.at[pl.ds(self.r0,nr),:]
        self.own=pltpu.make_async_copy(mine,self.slot(s,0,nr),self.loc)
        self.own.start()
        masks=(2,4) if self.n==8 else range(2,self.n,2)
        self.direct=[self.copy(mine,s,0,nr,i+1,flips(s,m)) for i,m in enumerate(masks)]
        self.open.append(self.copy(mine,s,0,nr,0,flip(s,1)))
    def middle(self):
        s=self.s; nr=self.nr; h=nr//2
        if self.n!=8: return
        x,y=flip(s,2),flip(s,4)
        self.direct[0].wait_recv()
        fa=self.pass_on(x,0,h,3,y)
        self.open.append(self.pass_on(x,0,nr,5,flip(s,1)))
        self.direct[1].wait_recv()
        fb=self.pass_on(y,h,nr,4,x)
        self.open.append(self.pass_on(y,0,nr,6,flip(s,1)))
        self.diag=(fa,fb)
    def late(self):
        s=self.s; nr=self.nr
        if self.n==8:
            for f in self.diag: f.wait_recv()
            self.open.append(self.pass_on(flips(s,6),0,nr,7,flip(s,1)))
            for f in self.diag: f.wait_send()
        else:
            for i,m in enumerate(range(2,self.n,2)):
                self.direct[i].wait_recv()
                self.open.append(self.pass_on(flips(s,m),0,nr,self.n//2+i,flip(s,1)))
        for f in self.direct: f.wait_send()
    def finish(self):
        for f in self.open: f.wait()
        self.own.wait()

class ShardGather:
    def __init__(self,zc,src,dst,send,recv):
        self.zc=zc; self.src=src; self.dst=dst; self.send=send; self.recv=recv
        self.z=lax.axis_index("shard"); self.C=src.shape[1]
    def slot(self):
        return self.dst.at[:,pl.ds(pl.multiple_of(self.z*self.C,128),self.C)]
    def start(self):
        self.own=pltpu.make_async_copy(self.src,self.slot(),self.recv.at[0]); self.own.start()
        self.cs=[]
        for d in range(1,self.zc):
            c=pltpu.make_async_remote_copy(src_ref=self.src,dst_ref=self.slot(),send_sem=self.send.at[d],recv_sem=self.recv.at[d],device_id={"shard":lax.rem(self.z+d,self.zc)},device_id_type=MESH)
            c.start(); self.cs.append(c)
    def finish(self):
        for c in self.cs: c.wait()
        self.own.wait()

class ShardSplit:
    def __init__(self,zc,src,box,send,recv):
        self.zc=zc; self.src=src; self.box=box; self.send=send; self.recv=recv
        self.z=lax.axis_index("shard"); self.C=box.shape[2]
    def start(self):
        C=self.C
        self.own=pltpu.make_async_copy(self.src.at[:,pl.ds(pl.multiple_of(self.z*C,128),C)],self.box.at[0],self.recv.at[0]); self.own.start()
        self.cs=[]
        for d in range(1,self.zc):
            to=lax.rem(self.z+d,self.zc)
            c=pltpu.make_async_remote_copy(src_ref=self.src.at[:,pl.ds(pl.multiple_of(to*C,128),C)],dst_ref=self.box.at[d],send_sem=self.send.at[d],recv_sem=self.recv.at[d],device_id={"shard":to},device_id_type=MESH)
            c.start(); self.cs.append(c)
    def finish(self):
        for c in self.cs: c.wait()
        self.own.wait()

class ShardAll:
    def __init__(self,axis,n,box,send,recv):
        self.axis=axis; self.n=n; self.box=box; self.send=send; self.recv=recv; self.me=lax.axis_index(axis)
    def start(self):
        self.cs=[]
        for d in range(1,self.n):
            c=pltpu.make_async_remote_copy(src_ref=self.box.at[self.me],dst_ref=self.box.at[self.me],send_sem=self.send.at[d],recv_sem=self.recv.at[d],device_id={self.axis:lax.rem(self.me+d,self.n)},device_id_type=MESH)
            c.start(); self.cs.append(c)
    def finish(self):
        for c in self.cs: c.wait()

class ColumnSplit:
    def __init__(self,n,src,dst,send,recv):
        self.n=n; self.src=src; self.dst=dst; self.send=send; self.recv=recv
        self.s=lax.axis_index("seq"); self.C=dst.shape[1]; self.R=src.shape[0]
    def start(self):
        n,s,C,R=self.n,self.s,self.C,self.R
        to_rows=self.dst.at[pl.ds(pl.multiple_of(s*R,16),R),:]
        block=lambda t: self.src.at[:,pl.ds(pl.multiple_of(t*C,128),C)]
        self.own=pltpu.make_async_copy(block(s),to_rows,self.recv.at[0]); self.own.start()
        self.cs=[]
        for d in range(1,n):
            t=lax.rem(s+d,n)
            c=pltpu.make_async_remote_copy(src_ref=block(t),dst_ref=to_rows,send_sem=self.send.at[d],recv_sem=self.recv.at[d],device_id={"seq":t},device_id_type=MESH)
            c.start(); self.cs.append(c)
    def finish(self):
        for c in self.cs: c.wait()
        self.own.wait()

class ToPairs:
    def __init__(self,n,copies,heads,local_len,src,rows_src,dst,rows_dst,DK,DV,send,recv):
        self.__dict__.update(n=n,copies=copies,heads=heads,ll=local_len,src=src,rows_src=rows_src,dst=dst,rows_dst=rows_dst,DK=DK,DV=DV,send=send,recv=recv)
    def parts(self,t):
        s=lax.axis_index("seq"); ll,DK,DV,heads=self.ll,self.DK,self.DV,self.heads
        pair=lax.div(t,self.copies); seq=lax.div(pair,heads); head=lax.rem(pair,heads)
        rows=pl.ds(pl.multiple_of(seq*ll,ll),ll); to=pl.ds(pl.multiple_of(s*ll,ll),ll)
        if self.rows_src is None:
            return [(self.src.at[rows,pl.ds(pl.multiple_of(head*DV,128),DV)],self.dst.at[to,:])]
        wk=heads*DK
        out=[]
        for start,width,at in ((0,DK,0),(wk,DK,DK),(2*wk,DV,2*DK)):
            out.append((self.src.at[rows,pl.ds(pl.multiple_of(start+head*width,128),width)],self.dst.at[to,pl.ds(at,width)]))
        out.append((self.rows_src.at[pl.ds(pl.multiple_of(pair*8,8),8),:],self.rows_dst.at[pl.ds(pl.multiple_of(s*8,8),8),:]))
        return out
    def start(self):
        s=lax.axis_index("seq"); self.cs=[]
        for d in range(self.n):
            t=lax.rem(s+d,self.n)
            for i,(a,b) in enumerate(self.parts(t)):
                if d==0: c=pltpu.make_async_copy(a,b,self.recv.at[i,0])
                else: c=pltpu.make_async_remote_copy(src_ref=a,dst_ref=b,send_sem=self.send.at[i,d],recv_sem=self.recv.at[i,d],device_id={"seq":t},device_id_type=MESH)
                c.start(); self.cs.append(c)
    def finish(self):
        for c in self.cs: c.wait()

class FromPairs:
    def __init__(self,n,copies,heads,local_len,items,send,recv):
        self.__dict__.update(n=n,copies=copies,heads=heads,items=items,send=send,recv=recv)
    def start(self):
        s=lax.axis_index("seq"); pairs=self.n//self.copies; p=lax.div(s,self.copies); r=lax.rem(s,self.copies)
        seq=lax.div(p,self.heads); head=lax.rem(p,self.heads); self.cs=[]
        for d in range(pairs):
            t=lax.rem(p+d,pairs)*self.copies+r
            for i,(src,at,dst,to) in enumerate(self.items):
                a=src.at[at(t)]; b=dst.at[to(seq,head)]
                if d==0: c=pltpu.make_async_copy(a,b,self.recv.at[i,0])
                else: c=pltpu.make_async_remote_copy(src_ref=a,dst_ref=b,send_sem=self.send.at[i,d],recv_sem=self.recv.at[i,d],device_id={"seq":t},device_id_type=MESH)
                c.start(); self.cs.append(c)
    def finish(self):
        for c in self.cs: c.wait()

def flat_form(cols):
    r=cols.shape[0]
    i=lax.broadcasted_iota(jnp.int32,(r,r),0); j=lax.broadcasted_iota(jnp.int32,(r,r),1)
    return mmx(cols,jnp.where(i==j,1.0,0.0),0,0)

class SharedColumns:
    def __init__(self,n,zc,src,dst,sems):
        self.n=n; self.zc=zc; self.src=src; self.dst=dst; self.send,self.recv,self.zsend,self.zrecv=sems
        self.s=lax.axis_index("seq"); self.z=lax.axis_index("shard"); self.C=dst.shape[2]; self.q=src.shape[0]//zc
    def start(self):
        rows=pl.ds(pl.multiple_of(self.z*self.q,16),self.q)
        block=lambda t: self.src.at[rows,pl.ds(pl.multiple_of(t*self.C,128),self.C)]
        self.cs=[]
        for d in range(self.n):
            t=lax.rem(self.s+d,self.n)
            if d==0: c=pltpu.make_async_copy(block(t),self.dst.at[self.s,rows,:],self.recv.at[0])
            else: c=pltpu.make_async_remote_copy(src_ref=block(t),dst_ref=self.dst.at[self.s,rows,:],send_sem=self.send.at[d],recv_sem=self.recv.at[d],device_id={"seq":t},device_id_type=MESH)
            c.start(); self.cs.append(c)
    def middle(self):
        for c in self.cs: c.wait()
        strip=self.dst.at[:,pl.ds(pl.multiple_of(self.z*self.q,16),self.q),:]
        self.cs=[]
        for d in range(1,self.zc):
            c=pltpu.make_async_remote_copy(src_ref=strip,dst_ref=strip,send_sem=self.zsend.at[d],recv_sem=self.zrecv.at[d],device_id={"shard":lax.rem(self.z+d,self.zc)},device_id_type=MESH)
            c.start(); self.cs.append(c)
    def finish(self):
        for c in self.cs: c.wait()

def row_form(cols):
    return mmx(jnp.ones((8,cols.shape[1]),f32),cols,1,1)

def col_form(rows):
    r=rows.shape[1]
    i=lax.broadcasted_iota(jnp.int32,(r,r),0); j=lax.broadcasted_iota(jnp.int32,(r,r),1)
    return mmx(jnp.where(i==j,1.0,0.0),rows,1,1)

def gathers(n,pairs,sems):
    send,recv,loc=sems
    return [SeqGather(n,src,dst,axis,(send.at[i],recv.at[i],loc.at[i]),*c0) for i,(src,dst,axis,*c0) in enumerate(pairs)]
def gather_sems(n,k):
    return [pltpu.SemaphoreType.DMA((k,links(n))),pltpu.SemaphoreType.DMA((k,links(n))),pltpu.SemaphoreType.DMA((k,))]
def pair_sems(k):
    return [pltpu.SemaphoreType.DMA((k,)),pltpu.SemaphoreType.DMA((k,))]
def each(ops,name):
    for o in ops: getattr(o,name)()

def ffn_kernel(n,zc,part,tok,cot,cotfull,gain_all,wgfull,wu,wd,res,gres,afull,gffn,outpart,hidfull,dgfull,dufull,n2c,
               box,sums,nloc,nfull,gw_,uw_,dw_,gv,uv,hidden,dgate,dup,two,ld,as_,ar,bs,br,cs,cr,ds_,dr,es,er,fs,fr,hs,hr,*gs):
    greet(n,zc)
    D=part.shape[1]; R=part.shape[0]; FF=gv.shape[1]; z=lax.axis_index("shard")
    split=ShardSplit(zc,part,box,as_,ar); split.start()
    g1,g2=gs[:3],gs[3:]
    gw=gathers(n,[(wu,uw_,0),(wd,dw_,1)],g1)
    each(gw,"start")
    lg=pltpu.make_async_copy(wgfull,gw_,ld.at[0]); lg.start()
    gain=gain_all[:,pl.ds(pl.multiple_of(z*tok.shape[1],128),tok.shape[1])]
    split.finish()
    r=tok[...].astype(f32)
    for d in range(zc): r=r+box[d].astype(f32)
    res[...]=r
    sums[z]=row_form(r*r)
    tot=ShardAll("shard",zc,sums,bs,br); tot.start(); tot.finish()
    t=sums[0]
    for d in range(1,zc): t=t+sums[d]
    sc=lax.rsqrt(col_form(t)[:,0:1]/D+EPSILON)
    nloc[...]=(r*sc*gain).astype(bf16)
    zg=ShardGather(zc,nloc,nfull,cs,cr); zg.start()
    each(gw,"middle")
    zg.finish()
    cols=ColumnSplit(n,nfull,n2c,es,er); cols.start()
    tiles=[(a,min(a+512,FF)) for a in range(0,FF,512)]
    lg.wait()
    for a,b in tiles: gv[:,a:b]=jnp.dot(nfull[...],gw_[:,a:b],preferred_element_type=f32)
    gw[0].late(); gw[0].finish()
    for a,b in tiles: uv[:,a:b]=jnp.dot(nfull[...],uw_[:,a:b],preferred_element_type=f32)
    def act(c,_):
        rr=pl.ds(pl.multiple_of(c*32,32),32)
        g=gv[rr,:]
        hidden[rr,:]=(g*sigmoid(g)*uv[rr,:]).astype(bf16)
        return 0
    lax.fori_loop(0,R//32,act,0)
    gh=gathers(n,[(hidden,hidfull,0),(dgate,dgfull,0),(dup,dufull,0)],g2)
    gh[0].start()
    gw[1].late(); gw[1].finish()
    for a,b in tiles:
        dh=dg(cotfull[...],dw_[a:b,:],1,1)
        g=gv[:,a:b]; sg=sigmoid(g)
        dgate[:,a:b]=(dh*uv[:,a:b]*sg*(1.0+g*(1.0-sg))).astype(bf16)
        dup[:,a:b]=(dh*(g*sg)).astype(bf16)
    gd=gh
    each(gd[1:],"start")
    def back(j,_):
        rr=pl.ds(pl.multiple_of(j*256,256),256)
        two[:,rr]=(dg(dgate[...],gw_[rr,:],1,1)+dg(dup[...],uw_[rr,:],1,1)).astype(bf16)
        return 0
    lax.fori_loop(0,D//256,back,0)
    split=ShardSplit(zc,two,box,fs,fr)
    split.start()
    def outp(j,_):
        cc=pl.ds(pl.multiple_of(j*256,256),256)
        outpart[:,cc]=jnp.dot(hidden[...],dw_[:,cc],preferred_element_type=f32).astype(bf16)
        return 0
    lax.fori_loop(0,D//256,outp,0)
    split.finish()
    g=box[0].astype(f32)
    for d in range(1,zc): g=g+box[d].astype(f32)
    r=res[...]
    gained=gain*g
    sums[zc+z]=row_form(gained*r)
    tot=ShardAll("shard",zc,sums.at[pl.ds(zc,zc)],ds_,dr); tot.start()
    gffn[...]=jnp.broadcast_to(jnp.sum(g*r*sc,axis=0,keepdims=True),gffn.shape)
    tot.finish()
    t=sums[zc]
    for d in range(1,zc): t=t+sums[zc+d]
    inner=col_form(t)[:,0:1]/D
    gr=cot[...].astype(f32)+sc*(gained-r*(sc*sc*inner))
    gres[...]=gr
    nloc[...]=gr.astype(bf16)
    zg=ShardGather(zc,nloc,afull,hs,hr); zg.start()
    each(gd,"middle")
    zg.finish()
    each(gd,"late"); cols.finish(); each(gd,"finish")

def call(name,cid,kernel,args,specs,outs,ospecs,scratch):
    return pl.pallas_call(kernel,name=name,out_shape=tuple(outs),in_specs=specs,out_specs=tuple(ospecs),scratch_shapes=scratch,
      compiler_params=pltpu.CompilerParams(collective_id=cid,has_side_effects=True,vmem_limit_bytes=61*2**20))(*args)

def ffn(n,zc,part,tok,cot,cotfull,gain,wgfull,wu,wd):
    R,F=tok.shape; D=F*zc; FF=wu.shape[1]
    return call("ffn",2,functools.partial(ffn_kernel,n,zc),(part,tok,cot,cotfull,gain,wgfull,wu,wd),[ANY]+[VM]*4+[ANY]*3,
      [S((R,F)),S((R,F)),S((R,D),bf16),S((8,F)),S((R,D),bf16),S((R*n,FF),bf16),S((R*n,FF),bf16),S((R*n,FF),bf16),S((R*n,D//n),bf16)],
      [VM]*5+[ANY]*4,
      [pltpu.VMEM((zc,R,F),bf16),pltpu.VMEM((2*zc,8,R),f32),pltpu.VMEM((R,F),bf16),pltpu.VMEM((R,D),bf16),pltpu.VMEM((D,FF),bf16),pltpu.VMEM((D,FF),bf16),pltpu.VMEM((FF,D),bf16),
       pltpu.VMEM((R,FF),f32),pltpu.VMEM((R,FF),f32),pltpu.VMEM((R,FF),bf16),pltpu.VMEM((R,FF),bf16),pltpu.VMEM((R,FF),bf16),pltpu.VMEM((R,D),bf16),pltpu.SemaphoreType.DMA((1,))]
      +pair_sems(zc)*4+pair_sems(n)+pair_sems(zc)*2+gather_sems(n,2)+gather_sems(n,3))


def per_device(
    tokens, doc_starts, norm_gain, query_weight, key_weight, value_weight, outgate_weight,
    beta_weight, decay_weight, query_conv, key_conv, value_conv, decay_log, decay_bias, head_gain,
    output_weight, ffn_gain, gate_weight, up_weight, down_weight, cotangent,
):
    seq_count, local_len, feature_part = tokens.shape
    row_count = seq_count * local_len
    shard_count = lax.axis_size("shard")
    seq_devices = lax.axis_size("seq")
    head_count = beta_weight.shape[1]
    key_dim = query_weight.shape[1] // head_count
    value_dim = value_weight.shape[1] // head_count
    pairs = seq_count * head_count
    copies = seq_devices // pairs
    flat = lambda x: x.reshape(row_count, x.shape[2])
    tokens_flat, cot_flat = flat(tokens), flat(cotangent)
    head_row, norm_row, ffn_row = head_gain[None], norm_gain[None], ffn_gain[None]
    (
        scale_one, cot_rows, full_one, full_outgate, full_output, full_gate, cot_cols, normed_one_cols,
        gate_proj, o_flat, branch, attn_part, taps, *saved,
    ) = forward(
        seq_devices, shard_count, copies, head_count, tokens_flat, cot_flat, norm_row, head_row, doc_starts, decay_log,
        decay_bias, beta_weight, decay_weight, query_conv, key_conv, value_conv, query_weight, key_weight, value_weight,
        outgate_weight, output_weight, gate_weight, key_dim, value_dim,
    )
    residual, grad_residual, attn_cot, grad_ffn_part, out_part, hidden_all, dgate_all, dup_all, normed_two_cols = ffn(
        seq_devices, shard_count, attn_part, tokens_flat, cot_flat, cot_rows, ffn_row, full_gate, up_weight, down_weight
    )
    (
        output, grad_tokens, smalls, totals, out_gate, out_up, out_down, out_output, out_outgate, qkv_all, small_all,
        unused_branch, unused_gate, unused_cols,
    ) = back(
        seq_devices, shard_count, copies, head_count, decay_log.shape[0], attn_cot, gate_proj, o_flat, head_row, tokens_flat,
        scale_one, norm_row, residual, grad_residual, grad_ffn_part, taps, saved, doc_starts, decay_log, decay_bias,
        full_output, full_one, full_outgate, out_part, branch, hidden_all, dgate_all, dup_all, normed_two_cols,
        normed_one_cols, cot_cols,
    )
    out_query, out_key, out_value, out_beta, out_decay, out_qconv, out_kconv, out_vconv, out_norm, out_ffn, out_head, out_log, out_bias = last(
        seq_devices, copies, head_count, key_dim, value_dim, feature_part, decay_log.shape[0], normed_one_cols, qkv_all,
        small_all, smalls, totals, query_conv.shape[0], value_conv.shape[0],
    )
    shape3 = (seq_count, local_len, feature_part)
    return (
        output.reshape(shape3), grad_tokens.reshape(shape3), out_norm[0], out_query, out_key, out_value, out_outgate,
        out_beta, out_decay, out_qconv, out_kconv, out_vconv, out_log[0], out_bias[0], out_head[0], out_output,
        out_ffn[0], out_gate, out_up, out_down,
    )


def solution(mesh):
    P = PartitionSpec
    rows, cols = P("seq", "shard"), P("shard", "seq")
    both, acts = P(("shard", "seq"), None), P(None, "seq", "shard")
    return jax.shard_map(
        per_device,
        mesh=mesh,
        in_specs=(acts, P(), P()) + (rows,) * 6 + (both,) * 3 + (P(), P(), P(), cols, P(), rows, rows, cols, acts),
        out_specs=(acts, acts, P()) + (rows,) * 6 + (both,) * 3 + (P(), P(), P(), cols, P(), rows, rows, cols),
        check_vma=False,
    )
```

```python
import functools
import jax, jax.numpy as jnp
from jax import lax
from jax.experimental import pallas as pl
from jax.experimental.pallas import tpu as pltpu
from jax.sharding import PartitionSpec
f32=jnp.float32; bf16=jnp.bfloat16
SPAN=64
EPSILON=1e-6
HI=lax.Precision.HIGHEST

def dg(a,b,ca=1,cb=0):
    return lax.dot_general(a,b,(((ca,),(cb,)),((),())),preferred_element_type=f32)
def halves(x):
    h=x.astype(bf16)
    return h,(x-h.astype(f32)).astype(bf16)
def mm3(a,b,ca=1,cb=0):
    ah,al=halves(a); bh,bl=halves(b)
    return dg(ah,bh,ca,cb)+(dg(al,bh,ca,cb)+dg(ah,bl,ca,cb))
def mm1(a,b,ca=1,cb=0):
    return dg(a.astype(bf16),b.astype(bf16),ca,cb)
def mmx(a,b,ca=1,cb=0):
    return lax.dot_general(a,b,(((ca,),(cb,)),((),())),preferred_element_type=f32,precision=HI)

def square_masks():
    i=lax.broadcasted_iota(jnp.int32,(SPAN,SPAN),0); j=lax.broadcasted_iota(jnp.int32,(SPAN,SPAN),1)
    return i,j
def positions(base,rows,cols,axis):
    return base+lax.broadcasted_iota(jnp.int32,(rows,cols),axis)
class Row:
    def __init__(self,ref,row):
        self.ref=ref; self.row=row; self.shape=ref.shape[1:]
    def __getitem__(self,e):
        return self.ref[self.row,e]

def doc_count(starts,pos):
    n=jnp.zeros(pos.shape,jnp.int32)
    for e in range(starts.shape[0]):
        n=n+jnp.where(starts[e]<=pos,1,0)
    return n
def doc_age(starts,pos):
    s=jnp.zeros(pos.shape,jnp.int32)
    for e in range(starts.shape[0]):
        s=jnp.where(starts[e]<=pos,starts[e],s)
    return pos-s
def count_at(starts,p):
    n=jnp.int32(0)
    for e in range(starts.shape[0]):
        n=n+jnp.where(starts[e]<=p,1,0)
    return n
def sigmoid(x):
    return 1.0/(1.0+jnp.exp(-x))
def softplus(x):
    return jnp.maximum(x,0.0)+jnp.log(1.0+jnp.exp(-jnp.abs(x)))

def inverse(A):
    i,j=square_masks()
    eye=jnp.where(i==j,1.0,0.0)
    T=eye-jnp.where((i//2)==(j//2),A,0.0)
    size=2
    while size<SPAN:
        C=jnp.where(((i//(2*size))==(j//(2*size)))&((i//size)!=(j//size)),A,0.0).astype(bf16)
        Tb=T.astype(bf16)
        T=T-dg(Tb,dg(C,Tb).astype(bf16))
        size*=2
    Tb=T.astype(bf16); Ah,Al=halves(A)
    rest=eye-Tb.astype(f32)-(dg(Ah,Tb)+dg(Al,Tb))
    return Tb.astype(f32)+dg(Tb,rest.astype(bf16))

def position_rows(raw,starts,base,rate,bias):
    r=raw.shape[1]
    row=lax.broadcasted_iota(jnp.int32,(8,r),0)
    g=-rate*softplus(raw[1:2]+bias)
    i=lax.broadcasted_iota(jnp.int32,(r,r),0); j=lax.broadcasted_iota(jnp.int32,(r,r),1)
    G=mmx(jnp.broadcast_to(g,(8,r)),jnp.where((i<=j)&((i//SPAN)==(j//SPAN)),1.0,0.0))
    docs=doc_count(starts,positions(base,8,r,1)).astype(f32)
    out=jnp.where(row==0,sigmoid(raw[0:1]),0.0)
    for k,x in ((1,g),(2,G),(3,raw[1:2]),(4,docs)): out=jnp.where(row==k,x,out)
    return out

def span_terms(n,q,k,starts,xc,xr):
    i,j=square_masks()
    before=count_at(starts,n*SPAN-1).astype(f32)
    wide=lambda c: jnp.broadcast_to(c,(SPAN,128))
    beta=wide(xc[:,0:1]); G=wide(xc[:,2:3]); docs=wide(xc[:,4:5])
    incl=(i>=j)&(docs[:,:SPAN]==xr[4:5])
    D=jnp.where(incl,jnp.exp(jnp.where(incl,G[:,:SPAN]-xr[2:3],0.0)),0.0)
    gam=jnp.where(docs==before,jnp.exp(G),0.0)
    end=jnp.where(docs==docs[SPAN-1:SPAN],jnp.exp(G[SPAN-1:SPAN]-G),0.0)
    KK=dg(k,k,1,1); QK=dg(q,k,1,1)
    return beta,D,gam,end,KK,QK,i,j

def conv_pre(upad,taps,age,base,rows):
    window=upad[pl.ds(base,rows+8),:]
    pre=window[8:]*taps[3:4]
    for back in range(1,4):
        ok=jnp.where(age>=back,1.0,0.0)
        pre=pre+window[8-back:8-back+rows]*ok*taps[3-back:4-back]
    return pre

def forward_kernel(n,zc,copies,heads,DK,DV,tok,cot,gain,hgain,starts2,dlog,dbias,wb,wd,qc,kc,vc,wq,wk,wv,wg,wo,wgate,
                   scale,cotfull,wfull,wgfull,wofull,wgatefull,cotc,n1c,gate_ref,oall,branch,part,taps_ref,u_ref,xr_ref,xc_ref,q_ref,k_ref,v_ref,s_ref,w_ref,t_ref,qt_ref,mh_ref,
                   tokfull,normed,ws,wbuf,sbuf,pbuf,rbuf,tbuf,upad,un_ref,gc_ref,on_ref,o_ref,zs,zr,cs,cr,ks,kr,es,er,fs,fr,hs,hr,is_,ir,os_,or_,ld,*gs):
    L=u_ref.shape[0]; NC=L//SPAN; local_len=L//n; per=local_len//SPAN
    put=lambda x,first: dg(x[...],jnp.where(lax.broadcasted_iota(jnp.int32,(x.shape[0],128),0)+first==lax.broadcasted_iota(jnp.int32,(x.shape[0],128),1),1.0,0.0).astype(bf16),0,0)
    ws[...]=(put(wb,0)+put(wd,heads)).astype(bf16)
    at_row=0
    for x in (qc,kc,vc):
        ws[at_row:at_row+x.shape[1]]=(ws[at_row:at_row+x.shape[1]].astype(f32)+put(x,2*heads)).astype(bf16)
        at_row+=x.shape[1]
    greet(n,zc)
    zt=ShardGather(zc,tok,tokfull,zs,zr); zt.start()
    ws_all=(ws,wq,wk,wv); at=(wq.shape[1]*2+wv.shape[1],0,wq.shape[1],wq.shape[1]*2)
    g1,g2=gs[:3],gs[3:]
    gw=gathers(n,[(w,wfull,0,a) for w,a in zip(ws_all,at)],g1)
    gb=gathers(n,[(wg,wgfull,0),(wo,wofull,1),(wgate,wgatefull,0)],g2)
    each(gw,"start")
    each(gw,"middle")
    zt.finish()
    zk=ShardGather(zc,cot,cotfull,cs,cr); zk.start()
    rows=tokfull.shape[0]; D=tokfull.shape[1]
    def norm(c,_):
        r=pl.ds(pl.multiple_of(c*32,32),32)
        x=tokfull[r,:].astype(f32)
        sc=lax.rsqrt(jnp.sum(x*x,axis=1,keepdims=True)/D+EPSILON)
        normed[r,:]=(x*sc*gain[...]).astype(bf16)
        scale[r,:]=jnp.broadcast_to(sc,(32,128))
        return 0
    lax.fori_loop(0,rows//32,norm,0)
    rbuf[...]=jnp.zeros(rbuf.shape,f32)
    inward=ToPairs(n,copies,heads,local_len,pbuf,rbuf,u_ref,xr_ref,DK,DV,is_,ir)
    pair=lax.div(lax.axis_index("seq"),copies); my_seq=lax.div(pair,heads); my_head=lax.rem(pair,heads)
    for i,g in enumerate(gw):
        g.late(); g.finish()
        width=ws_all[i].shape[1]
        buf=sbuf if i==0 else wbuf.at[:,pl.ds(0,width)]
        c=pltpu.make_async_copy(wfull.at[:,pl.ds(at[i],width)],buf,ld.at[0]); c.start(); c.wait()
        if i==0:
            small=jnp.dot(normed[...],sbuf[...],preferred_element_type=f32)
            for sq in range(rows//local_len):
                fl=flat_form(small[sq*local_len:(sq+1)*local_len,0:8*((2*heads+7)//8)])
                for h in range(heads):
                    base=(sq*heads+h)*8
                    rbuf[base:base+1]=fl[h:h+1]
                    rbuf[base+1:base+2]=fl[heads+h:heads+h+1]
            cq=heads*DK//n; cv=heads*DV//n; step=sbuf.shape[0]//n
            for kind,(width_c,count,skip) in enumerate(((cq,DK,0),(cq,DK,cq),(cv,DV,2*cq))):
                for j in range(count//width_c):
                    dev=my_head*(count//width_c)+j
                    to=(0,DK,2*DK)[kind]+j*width_c
                    tbuf[to:to+width_c]=sbuf[pl.ds(pl.multiple_of(dev*step+skip,16),width_c),:]
            ch=tbuf.shape[0]
            ident=jnp.where(lax.broadcasted_iota(jnp.int32,(ch,ch),0)==lax.broadcasted_iota(jnp.int32,(ch,ch),1),1.0,0.0).astype(bf16)
            tt=dg(tbuf[...],ident,0,0)
            taps_ref[...]=tt[2*heads:2*heads+4]
        else:
            tile=min(width,256)
            def column(j,_,i=i,tile=tile):
                cc=pl.ds(pl.multiple_of(j*tile,128),tile)
                pbuf[:,pl.ds(pl.multiple_of(at[i]+j*tile,128),tile)]=jnp.dot(normed[...],wbuf[:,cc],preferred_element_type=f32).astype(bf16)
                return 0
            lax.fori_loop(0,width//tile,column,0)
        inward.start((3,0,1,2)[i])
    starts=Row(starts2,my_seq)
    at_head=lax.axis_index("shard")*heads+my_head
    rate=jnp.exp(jnp.full((1,1),dlog[at_head],f32)); bias=dbias[at_head]
    zk.finish()
    inward.finish()
    cols=SharedColumns(n,zc,normed,n1c,(es,er,fs,fr)); cols.start()
    ccol=SharedColumns(n,zc,cotfull,cotc,(ks,kr,hs,hr)); ccol.start()
    each(gb,"start")
    upad[0:8]=jnp.zeros((8,upad.shape[1]),f32)
    def turn(m,_):
        r=pl.ds(pl.multiple_of(m*8,8),8)
        x=position_rows(xr_ref[r,:],starts,m*local_len,rate,bias)
        xr_ref[r,:]=x
        xc_ref[pl.ds(pl.multiple_of(m*local_len,local_len),local_len),:]=col_form(x)
        return 0
    lax.fori_loop(0,n,turn,0,unroll=4)
    taps=taps_ref[...]
    R=128
    def load(c,_):
        upad[pl.ds(pl.multiple_of(8+c*R,8),R),:]=u_ref[pl.ds(pl.multiple_of(c*R,R),R),:].astype(f32)
        return 0
    lax.fori_loop(0,L//R,load,0)
    def conv(c,_):
        base=pl.multiple_of(c*R,R)
        age=doc_age(starts,positions(base,R,128,0))[:,0:1]
        pre=conv_pre(upad,taps,age,base,R)
        act=pre*sigmoid(pre)
        rows=pl.ds(base,R)
        aq=act[:,:DK]; ak=act[:,DK:2*DK]
        q_ref[rows,:]=(aq*lax.rsqrt(jnp.sum(aq*aq,axis=1,keepdims=True)+EPSILON)*DK**-0.5).astype(bf16)
        k_ref[rows,:]=(ak*lax.rsqrt(jnp.sum(ak*ak,axis=1,keepdims=True)+EPSILON)).astype(bf16)
        v_ref[rows,:]=act[:,2*DK:].astype(bf16)
        return 0
    lax.fori_loop(0,L//R,conv,0)
    cols.middle(); ccol.middle()
    def one_span(n,xr):
        rows=pl.ds(pl.multiple_of(n*SPAN,SPAN),SPAN)
        q=q_ref[rows,:]; k=k_ref[rows,:]; v=v_ref[rows,:]
        beta,D,gam,end,KK,QK,i,j=span_terms(n,q,k,starts,xc_ref[rows,:],xr)
        A=jnp.where(i>j,beta[:,:SPAN]*D*KK,0.0)
        T=inverse(A)
        kf=k.astype(f32)
        UW=mm1(T,jnp.concatenate([jnp.concatenate([beta]*(DV//128),axis=1)*v.astype(f32),(beta*gam)*kf],axis=1))
        UWb=UW.astype(bf16)
        PW=dg((QK*D).astype(bf16),UWb)
        NM=dg((end*kf).astype(bf16),UWb,0,0)
        t_ref[n]=T
        on_ref[n]=PW[:,:DV]
        w_ref[n]=UW[:,:DV]
        qt_ref[n,0:SPAN]=(gam*q.astype(f32)-PW[:,DV:]).astype(bf16)
        qt_ref[n,SPAN:]=UWb[:,DV:]
        un_ref[n]=NM[:,:DV]
        mh_ref[n]=NM[:,DV:].astype(bf16)
        gc_ref[n]=jnp.broadcast_to(gam[SPAN-1:SPAN],(8,128))
    def local(m,_):
        xr=xr_ref[pl.ds(pl.multiple_of(m*8,8),8),:]
        for e in range(per): one_span(m*per+e,xr[:,e*SPAN:(e+1)*SPAN])
        return 0
    lax.fori_loop(0,n,local,0,unroll=2)
    each(gb,"middle")
    def chain(n,S):
        s_ref[n]=S
        sh,sl=halves(S); mh=mh_ref[n]
        gc=gc_ref[n][0:1]
        return jnp.concatenate([gc]*(DV//128),axis=1)*S+un_ref[n]-(dg(mh,sh)+dg(mh,sl))
    lax.fori_loop(0,NC,chain,jnp.zeros((DK,DV),f32),unroll=2)
    def emit(n,_):
        rows=pl.ds(pl.multiple_of(n*SPAN,SPAN),SPAN)
        r=dg(qt_ref[n],s_ref[n].astype(bf16))
        o_ref[rows,:]=(on_ref[n]+r[:SPAN]).astype(o_ref.dtype)
        w_ref[n]=w_ref[n]-r[SPAN:]
        return 0
    lax.fori_loop(0,NC,emit,0,unroll=4)
    outward=FromPairs(n,copies,heads,local_len,[(o_ref,lambda t: (pl.ds(pl.multiple_of(t*local_len,local_len),local_len),slice(None)),
        oall,lambda seq,head: (pl.ds(pl.multiple_of(seq*local_len,local_len),local_len),pl.ds(pl.multiple_of(head*DV,128),DV)))],os_,or_)
    outward.start()
    gb[0].late(); gb[1].late(); gb[0].finish()
    width=wg.shape[1]
    c=pltpu.make_async_copy(wgfull,wbuf.at[:,pl.ds(0,width)],ld.at[0]); c.start(); c.wait()
    def column(j,_):
        cc=pl.ds(pl.multiple_of(j*256,256),256)
        gate_ref[:,cc]=jnp.dot(normed[...],wbuf[:,cc],preferred_element_type=f32)
        return 0
    lax.fori_loop(0,width//256,column,0)
    gb[1].finish()
    for j in range(D//wbuf.shape[1]):
        c=pltpu.make_async_copy(wofull.at[:,pl.ds(j*wbuf.shape[1],wbuf.shape[1])],wbuf.at[pl.ds(j*wofull.shape[0],wofull.shape[0]),:],ld.at[j]); c.start()
        c.wait()
    outward.finish()
    def mix(c,_):
        r=pl.ds(pl.multiple_of(c*32,32),32)
        for h in range(heads):
            cc=pl.ds(h*DV,DV)
            o=oall[r,cc].astype(f32); g=gate_ref[r,cc]
            rho=lax.rsqrt(jnp.sum(o*o,axis=1,keepdims=True)/DV+EPSILON)
            branch[r,cc]=(o*rho*hgain[...]*(g*sigmoid(g))).astype(bf16)
        return 0
    lax.fori_loop(0,rows//32,mix,0)
    tiles=wbuf.shape[1]//256
    def column(j,_):
        blk=lax.div(j,tiles); inner=lax.rem(j,tiles)
        w=wbuf[pl.ds(pl.multiple_of(blk*wofull.shape[0],16),wofull.shape[0]),pl.ds(pl.multiple_of(inner*256,256),256)]
        part[:,pl.ds(pl.multiple_of(j*256,256),256)]=jnp.dot(branch[...],w,preferred_element_type=f32).astype(bf16)
        return 0
    lax.fori_loop(0,D//256,column,0)
    gb[2].late(); cols.finish(); ccol.finish(); gb[2].finish()

def back_kernel(n,zc,copies,heads,total_heads,afull,gate_ref,oall,hgain,tok,scale,gain,res,gres,gffn,taps_ref,u_ref,xc_ref,xr_ref,starts2,dlog,dbias,
                q_ref,k_ref,v_ref,s_ref,w_ref,t_ref,qt_ref,mh_ref,wofull,wfull,wgfull,outpart,branch,hidfull,dgfull,dufull,n2c,n1c,cotc,
                output,gtok,smalls,totals,ogate,oup,odown,oout,oog,dyqfull,dsmfull,brafull,dgpfull,attc,
                upad,dpre,ds_ref,gc_ref,do_ref,du_ref,dx_ref,dxr,bufa,bufb,cola,colb,colc,dob,dgp,dyq,rbuf,dsm,part,upart,box,boxo,sums,
                is_,ir,os_,or_,as_,ar,bs,br,cs,cr,es,er,fs,fr,hs,hr,zs,zr,ld,*gs):
    L=u_ref.shape[0]; NC=L//SPAN; DV=v_ref.shape[1]; DK=q_ref.shape[1]; local_len=L//n; per=local_len//SPAN
    rows_n=tok.shape[0]; F=tok.shape[1]; D=F*zc; VW=wofull.shape[0]; FF=dgfull.shape[1]; wk=heads*DK; wv=heads*DV
    bufs=(bufa,bufb)
    loads={}
    def load_job(key,i,pieces):
        loads[key]=[]
        for j,(src,at) in enumerate(pieces):
            c=pltpu.make_async_copy(src,bufs[i].at[at],ld.at[i,j]); c.start(); loads[key].append(c)
    def ready(key):
        for c in loads[key]: c.wait()
    whole=lambda w: (pl.ds(0,D),pl.ds(0,w))
    every=lambda w: (pl.ds(0,n*rows_n),pl.ds(0,w))
    N=n*rows_n
    load_job("wo",0,[(wofull.at[:,pl.ds(j*VW,VW)],(pl.ds(j*VW,VW),pl.ds(0,VW))) for j in range(D//VW)])
    load_job("og",1,[(wgfull,whole(wv))])
    greet(n,zc)
    so=ShardSplit(zc,outpart,boxo,fs,fr); so.start()
    ready("wo")
    dsm[...]=jnp.zeros(dsm.shape,bf16)
    def heads_back(c,gh):
        r=pl.ds(pl.multiple_of(c*64,64),64)
        for h in range(heads):
            cc=pl.ds(h*DV,DV)
            dm=dg(afull[r,0:VW],bufa[h*DV:(h+1)*DV,0:VW],1,1)
            for j in range(1,D//VW):
                dm=dm+dg(afull[r,j*VW:(j+1)*VW],bufa[j*VW+h*DV:j*VW+(h+1)*DV,0:VW],1,1)
            dm=dm.astype(bf16).astype(f32)
            o=oall[r,cc].astype(f32); g=gate_ref[r,cc]
            rho=lax.rsqrt(jnp.sum(o*o,axis=1,keepdims=True)/DV+EPSILON)
            z=o*rho; sg=sigmoid(g); sil=g*sg
            gh=gh+jnp.sum(dm*z*sil,axis=0,keepdims=True)
            dmg=dm*hgain[...]
            dz=dmg*sil
            dob[r,cc]=(rho*(dz-z*(jnp.sum(dz*z,axis=1,keepdims=True)/DV))).astype(bf16)
            dgp[r,cc]=(dmg*z*sg*(1.0+g*(1.0-sg))).astype(bf16)
        return gh
    gh=lax.fori_loop(0,rows_n//64,heads_back,jnp.zeros((1,DV),f32))
    inward=ToPairs(n,copies,heads,local_len,dob,None,do_ref,None,DK,DV,is_,ir); inward.start(0)
    load_job("dgate",0,[(dgfull,every(FF))])
    c2=pltpu.make_async_copy(n2c,cola,ld.at[0,4]); c2.start()
    g1,g2=gs[:3],gs[3:]
    gw=gathers(n,[(dgp,dgpfull,0),(branch,brafull,0)],g1)
    pair=lax.div(lax.axis_index("seq"),copies); my_head=lax.rem(pair,heads)
    starts=Row(starts2,lax.div(pair,heads)); at_head=lax.axis_index("shard")*heads+my_head
    rate=jnp.exp(jnp.full((1,1),dlog[at_head],f32)); bias=dbias[at_head]
    taps=taps_ref[...]
    R=128
    upad[0:8]=jnp.zeros((8,upad.shape[1]),f32)
    dpre[L:L+8]=jnp.zeros((8,upad.shape[1]),f32)
    def load(c,_):
        upad[pl.ds(pl.multiple_of(8+c*R,8),R),:]=u_ref[pl.ds(pl.multiple_of(c*R,R),R),:].astype(f32)
        return 0
    lax.fori_loop(0,L//R,load,0)
    inward.finish()
    each(gw,"start")
    ca=SharedColumns(n,zc,afull,attc,(es,er,zs,zr)); ca.start()
    dx_ref[...]=jnp.zeros(dx_ref.shape,f32)
    def early(n,_):
        rows=pl.ds(pl.multiple_of(n*SPAN,SPAN),SPAN)
        ds_ref[n]=dg(qt_ref[n][0:SPAN],do_ref[rows,:],0,0)
        tail_row=xc_ref[rows,:][SPAN-1:SPAN]
        gam=jnp.where(tail_row[:,4:5]==count_at(starts,n*SPAN-1).astype(f32),jnp.exp(tail_row[:,2:3]),0.0)
        gc_ref[n]=jnp.broadcast_to(gam,(8,128))
        return 0
    lax.fori_loop(0,NC,early,0,unroll=4)
    def chain(m,dS):
        n=NC-1-m
        r=ds_ref[n]
        ds_ref[n]=dS
        sh,sl=halves(dS); mh=mh_ref[n]
        gc=gc_ref[n][0:1]
        return jnp.concatenate([gc]*(DV//128),axis=1)*dS+r-(dg(mh,sh,0,0)+dg(mh,sl,0,0))
    lax.fori_loop(0,NC,chain,jnp.zeros((DK,DV),f32),unroll=2)
    each(gw,"middle"); ca.middle()
    def one_span(n,xr):
        rows=pl.ds(pl.multiple_of(n*SPAN,SPAN),SPAN)
        q=q_ref[rows,:]; k=k_ref[rows,:]; v=v_ref[rows,:]; dO=do_ref[rows,:]
        beta,D,gam,end,KK,QK,i,j=span_terms(n,q,k,starts,xc_ref[rows,:],xr)
        beta2=jnp.concatenate([beta]*(DV//128),axis=1)
        S0=s_ref[n]; dS1=ds_ref[n]
        S0h=S0.astype(bf16); dSh=dS1.astype(bf16)
        kf=k.astype(f32); qf=q.astype(f32); vf=v.astype(f32)
        W=w_ref[n].astype(bf16); T=t_ref[n].astype(bf16)
        P=(QK*D).astype(bf16)
        dW=dg(P,dO,0,0)+jnp.concatenate([end]*(DV//128),axis=1)*dg(k,dSh)
        Y=dg(T,dW.astype(bf16),0,0)
        dOY=jnp.concatenate([dO,Y.astype(bf16)],axis=0)
        dPA=dg(dOY,W,1,1)
        GS=dg(dOY,S0h,1,1)
        dOS=GS[:SPAN]; YS=GS[SPAN:]
        Z=dg(W,dSh,1,1)
        dPD=dPA[:SPAN]*D
        EA=jnp.where(i>j,-dPA[SPAN:]*D,0.0)
        E=beta[:,:SPAN]*EA
        A1=jnp.concatenate([dPD,E],axis=0).astype(bf16)
        r1=dg(A1,k)
        r2=dg(A1,jnp.concatenate([q,k],axis=0),0,0)
        dpre[rows,0:DK]=gam*dOS+r1[:SPAN]
        dpre[rows,DK:2*DK]=r1[SPAN:]+r2-(beta*gam)*YS+end*Z
        dpre[rows,2*DK:]=beta2*Y
        EK=EA*KK
        kYS=jnp.sum(kf*YS,axis=1,keepdims=True)
        dbeta=jnp.sum(Y*vf,axis=1,keepdims=True)-gam*kYS+jnp.sum(EK,axis=1,keepdims=True)
        Fm=dPD*QK+beta[:,:SPAN]*EK
        dgam=jnp.sum(qf*dOS,axis=1,keepdims=True)-beta*kYS
        dend=jnp.sum(kf*Z,axis=1,keepdims=True)*end
        dG=jnp.sum(Fm,axis=1,keepdims=True)+dgam*gam-dend
        tail=jnp.sum(jnp.sum(S0*dS1,axis=0,keepdims=True),axis=1,keepdims=True)
        last=jnp.sum(dend,axis=0,keepdims=True)+gam[SPAN-1:SPAN]*tail
        row=lax.broadcasted_iota(jnp.int32,(SPAN,128),0)
        dG=dG+jnp.where(row==SPAN-1,last,0.0)
        dx_ref[rows,0:1]=(dbeta*beta*(1.0-beta))[:,0:1]
        dx_ref[rows,1:2]=dG[:,0:1]
        return jnp.sum(Fm,axis=0,keepdims=True)
    def local(m,_):
        xr=xr_ref[pl.ds(pl.multiple_of(m*8,8),8),:]
        dxr[pl.ds(pl.multiple_of(m*8,8),8),:]=jnp.broadcast_to(jnp.concatenate([one_span(m*per+e,xr[:,e*SPAN:(e+1)*SPAN]) for e in range(per)],axis=1),(8,local_len))
        return 0
    lax.fori_loop(0,n,local,0,unroll=2)
    i128=lax.broadcasted_iota(jnp.int32,(local_len,local_len),0); j128=lax.broadcasted_iota(jnp.int32,(local_len,local_len),1)
    later=jnp.where((i128>=j128)&((i128//SPAN)==(j128//SPAN)),1.0,0.0)
    def turn(m,sums):
        r=pl.ds(pl.multiple_of(m*8,8),8)
        f=flat_form(dx_ref[pl.ds(pl.multiple_of(m*local_len,local_len),local_len),:])
        dlog=mmx(jnp.broadcast_to(f[1:2]-dxr[r,:][0:1],(8,local_len)),later)
        x=xr_ref[r,:]
        ddp=dlog*(-rate)*sigmoid(x[3:4]+bias)
        row=lax.broadcasted_iota(jnp.int32,(8,local_len),0)
        dxr[r,:]=jnp.where(row==0,f[0:1],jnp.where(row==1,ddp,0.0))
        return (sums[0]+jnp.sum(dlog[0:1]*x[1:2],axis=1,keepdims=True),sums[1]+jnp.sum(ddp[0:1],axis=1,keepdims=True))
    zero=jnp.zeros((1,1),f32)
    sl,sb=lax.fori_loop(0,n,turn,(zero,zero),unroll=4)
    def norms(c,dt):
        base=pl.multiple_of(c*R,R)
        age=doc_age(starts,positions(base,R,128,0))[:,0:1]
        pre=conv_pre(upad,taps,age,base,R)
        sg=sigmoid(pre); act=pre*sg
        rows=pl.ds(base,R)
        d=dpre[rows,:]
        def unit_back(a,dd,f):
            s=lax.rsqrt(jnp.sum(a*a,axis=1,keepdims=True)+EPSILON)
            dot=jnp.sum(a*dd,axis=1,keepdims=True)
            return f*(s*dd-a*(s*s*s*dot))
        dact=jnp.concatenate([unit_back(act[:,:DK],d[:,:DK],DK**-0.5),unit_back(act[:,DK:2*DK],d[:,DK:2*DK],1.0),d[:,2*DK:]],axis=1)
        dp=dact*sg*(1.0+pre*(1.0-sg))
        dpre[rows,:]=dp
        window=upad[pl.ds(base,R+8),:]
        new=[]
        for j in range(4):
            back=3-j
            x=window[8-back:8-back+R]
            if back: x=x*jnp.where(age>=back,1.0,0.0)
            new.append(dt[j]+jnp.sum(x*dp,axis=0,keepdims=True))
        return tuple(new)
    zt=jnp.zeros((1,upad.shape[1]),f32)
    dt=lax.fori_loop(0,L//R,norms,(zt,)*4)
    so.finish()
    y=res[...]
    for d in range(zc): y=y+boxo[d].astype(f32)
    output[...]=y
    def back(c,_):
        base=pl.multiple_of(c*R,R)
        window=dpre[pl.ds(base,R+8),:]
        age=doc_age(starts,positions(base,R+8,128,0))[:,0:1]
        d=window[:R]*taps[3:4]
        for s in range(1,4):
            x=window[s:s+R]*jnp.where(age[s:s+R]>=s,1.0,0.0)
            d=d+x*taps[3-s:4-s]
        du_ref[pl.ds(base,R),:]=d.astype(bf16)
        return 0
    lax.fori_loop(0,L//R,back,0)
    cut=lambda start,width: (lambda t: (pl.ds(pl.multiple_of(t*local_len,local_len),local_len),pl.ds(start,width)))
    to=lambda start,width: (lambda seq,head: (pl.ds(pl.multiple_of(seq*local_len,local_len),local_len),pl.ds(pl.multiple_of(start+head*width,128),width)))
    outward=FromPairs(n,copies,heads,local_len,[(du_ref,cut(0,DK),dyq,to(0,DK)),(du_ref,cut(DK,DK),dyq,to(wk,DK)),(du_ref,cut(2*DK,DV),dyq,to(2*wk,DV)),
        (dxr,lambda t: (pl.ds(pl.multiple_of(t*8,8),8),slice(None)),rbuf,lambda seq,head: (pl.ds(pl.multiple_of((seq*heads+head)*8,8),8),slice(None)))],os_,or_)
    outward.start()
    def tiles(width,step): return [(a,min(a+step,width)) for a in range(0,width,step)]
    def spread(first,buf,terms):
        def one(j,_):
            rr=pl.ds(pl.multiple_of(j*256,256),256)
            t=0.0
            for x,a,b in terms: t=t+dg(x[...],buf[rr,a:b],1,1)
            part[:,rr]=t if first else part[:,rr]+t
            return 0
        lax.fori_loop(0,D//256,one,0)
    ready("og"); spread(True,bufb,[(dgp,0,wv)])
    load_job("dup",1,[(dufull,every(FF))])
    ready("dgate"); c2.wait()
    for a,b in tiles(FF,512): ogate[:,a:b]=dg(cola[...],bufa[0:N,a:b],0,0)
    load_job("wv",0,[(wfull.at[:,pl.ds(2*wk,wv+128)],whole(wv+128))])
    outward.finish()
    for sq in range(rows_n//local_len):
        fl=[]
        for e in range(2):
            for h in range(heads): fl.append(rbuf[(sq*heads+h)*8+e:(sq*heads+h)*8+e+1])
        fl=jnp.concatenate(fl+[jnp.zeros((-2*heads%8,local_len),f32)]*(1 if 2*heads%8 else 0),axis=0)
        dsm[sq*local_len:(sq+1)*local_len,0:fl.shape[0]]=col_form(fl).astype(bf16)
    gd=gathers(n,[(dsm,dsmfull,0),(dyq,dyqfull,0)],g2)
    each(gd,"start")
    ready("wv"); spread(False,bufa,[(dyq.at[:,pl.ds(2*wk,wv)],0,wv),(dsm,wv,wv+128)])
    ready("dup")
    for a,b in tiles(FF,512): oup[:,a:b]=dg(cola[...],bufb[0:N,a:b],0,0)
    load_job("wqk",1,[(wfull.at[:,pl.ds(0,2*wk)],whole(2*wk))])
    load_job("hid",0,[(hidfull,every(FF))])
    cc_=pltpu.make_async_copy(cotc,colb,ld.at[1,5]); cc_.start()
    ready("wqk")
    def last(j,_):
        rr=pl.ds(pl.multiple_of(j*256,256),256)
        upart[:,rr]=(part[:,rr]+dg(dyq[:,0:2*wk],bufb[rr,0:2*wk],1,1)).astype(bf16)
        return 0
    lax.fori_loop(0,D//256,last,0)
    split=ShardSplit(zc,upart,box,as_,ar); split.start()
    each(gw,"late")
    each(gd,"middle")
    for g in gw: g.finish()
    ca.finish()
    load_job("bra",1,[(brafull,every(VW))])
    ready("hid"); cc_.wait()
    cots=colb[...].reshape(n*rows_n,colb.shape[2])
    for a,b in tiles(FF,256): odown[a:b,:]=dg(bufa[0:N,a:b],cots,0,0)
    load_job("dgp",0,[(dgpfull,every(wv))])
    cc_=pltpu.make_async_copy(attc,colb,ld.at[1,5]); cc_.start()
    c2=pltpu.make_async_copy(n1c,colc,ld.at[0,4]); c2.start()
    ready("bra"); cc_.wait()
    atts=colb[...].reshape(n*rows_n,colb.shape[2])
    for a,b in tiles(VW,256): oout[a:b,:]=dg(bufb[0:N,a:b],atts,0,0)
    split.finish()
    g=box[0].astype(f32)
    for d in range(1,zc): g=g+box[d].astype(f32)
    x=tok[...].astype(f32); sc=scale[...][:,0:1]
    z=lax.axis_index("shard")
    gained=gain[:,pl.ds(pl.multiple_of(z*F,128),F)]*g
    sums[z]=row_form(gained*x)
    tot=ShardAll("shard",zc,sums,bs,br); tot.start()
    me=lax.axis_index("seq")
    W=smalls.shape[2]
    smalls[me]=jnp.zeros(smalls.shape[1:],f32)
    smalls[me,0:1,0:F]=jnp.sum(g*x*sc,axis=0,keepdims=True)
    smalls[me,1:2,0:F]=gffn[0:1]
    smalls[me,2:3,0:DV]=gh
    lane=lax.broadcasted_iota(jnp.int32,(1,128),1)
    first=jnp.where(lax.rem(me,copies)==0,1.0,0.0)
    smalls[me,3:4,0:128]=first*(jnp.where(lane==at_head,sl,0.0)+jnp.where(lane==total_heads+at_head,sb,0.0))
    for j in range(4): smalls[me,4+j:5+j,0:2*DK+DV]=dt[j]
    sa=ShardAll("seq",n,smalls,cs,cr); sa.start()
    tot.finish()
    t=sums[0]
    for d in range(1,zc): t=t+sums[d]
    inner=col_form(t)[:,0:1]/D
    gtok[...]=gres[...]+sc*(gained-x*(sc*sc*inner))
    ready("dgp"); c2.wait()
    n1=colc[...].reshape(n*rows_n,colc.shape[2])
    for a,b in tiles(wv,512): oog[:,a:b]=dg(n1,bufa[0:N,a:b],0,0)
    sa.finish()
    t=smalls[0]
    for d in range(1,n): t=t+smalls[d]
    totals[z]=t
    za=ShardAll("shard",zc,totals,hs,hr); za.start()
    each(gd,"late"); za.finish(); each(gd,"finish")

SM=pl.BlockSpec(memory_space=pltpu.SMEM); VM=pl.BlockSpec(memory_space=pltpu.VMEM)
def S(shape,dt=f32): return jax.ShapeDtypeStruct(shape,dt)
def forward(n,zc,copies,heads,tok,cot,gain,hgain,starts,dlog,dbias,wb,wd,qc,kc,vc,wq,wk,wv,wg,wo,wgate,DK,DV):
    R,F=tok.shape; D=F*zc; local_len=R//starts.shape[0]; L=n*local_len; NC=L//SPAN; pairs=n//copies; CH=2*DK+DV; HV=heads*DV
    rows=lambda *w: S((w[0].shape[0]*n,sum(x.shape[1] for x in w)),bf16)
    wide=max(wv.shape[1],wg.shape[1])
    small=S((D//n,128),bf16)
    return call("mixer",5,functools.partial(forward_kernel,n,zc,copies,heads,DK,DV),(tok,cot,gain,hgain,starts,dlog,dbias,wb,wd,qc,kc,vc,wq,wk,wv,wg,wo,wgate),[VM,VM,VM,VM,SM,SM,SM]+[VM]*5+[ANY]*6,
      [S((R,128)),S((R,D),bf16),rows(wq,wk,wv,small),rows(wg),S((wo.shape[0],wo.shape[1]*n),bf16),rows(wgate),S((n,R,D//n),bf16),S((n,R,D//n),bf16),
       S((R,HV)),S((R,HV),bf16),S((R,HV),bf16),S((R,D),bf16),S((4,CH)),
       S((L,CH),bf16),S((n*8,local_len)),S((L,8)),S((L,DK),bf16),S((L,DK),bf16),S((L,DV),bf16),S((NC,DK,DV)),S((NC,SPAN,DV)),S((NC,SPAN,SPAN)),
       S((NC,2*SPAN,DK),bf16),S((NC,DK,DK),bf16)],
      [VM]+[ANY]*7+[VM]*16,
      [pltpu.VMEM((R,D),bf16),pltpu.VMEM((R,D),bf16),pltpu.VMEM((D//n,128),bf16),pltpu.VMEM((D,wide),bf16),pltpu.VMEM((D,128),bf16),pltpu.VMEM((R,heads*CH),bf16),pltpu.VMEM((pairs*8,local_len),f32),pltpu.VMEM((CH,128),bf16),
       pltpu.VMEM((L+8,CH),f32),pltpu.VMEM((NC,DK,DV),f32),pltpu.VMEM((NC,8,128),f32),pltpu.VMEM((NC,SPAN,DV),f32),pltpu.VMEM((L,DV),bf16)]
      +pair_sems(zc)*2+pair_sems(n)*2+pair_sems(zc)*2+[pltpu.SemaphoreType.DMA((4,n)),pltpu.SemaphoreType.DMA((4,n)),pltpu.SemaphoreType.DMA((1,pairs)),pltpu.SemaphoreType.DMA((1,pairs)),pltpu.SemaphoreType.DMA((D//wide,))]
      +gather_sems(n,4)+gather_sems(n,3))
def back(n,zc,copies,heads,total_heads,afull,gate,oall,hgain,tok,scale,gain,res,gres,gffn,taps,saved,starts,dlog,dbias,wofull,wfull,wgfull,outpart,branch,hidfull,dgfull,dufull,n2c,n1c,cotc):
    u,xr,xc,q,k,v,s,w,t,qt,mh=saved
    L,CH=u.shape; NC=L//SPAN; DK=q.shape[1]; DV=v.shape[1]; local_len=L//n; pairs=n//copies; R,F=tok.shape; D=F*zc; FF=dgfull.shape[1]; HV=heads*DV; VW=wofull.shape[0]
    Dc=D//n; W=max(F,CH)
    bw=max(FF,HV+128,VW,2*heads*DK)
    ins=(afull,gate,oall,hgain,tok,scale,gain,res,gres,gffn,taps,u,xc,xr,starts,dlog,dbias,q,k,v,s,w,t,qt,mh,wofull,wfull,wgfull,outpart,branch,hidfull,dgfull,dufull,n2c,n1c,cotc)
    sem=pltpu.SemaphoreType.DMA
    return call("back",6,functools.partial(back_kernel,n,zc,copies,heads,total_heads),ins,[VM]*14+[SM]*3+[VM]*8+[ANY]*11,
      [S((R,F)),S((R,F)),S((n,8,W)),S((zc,8,W)),S((Dc,FF)),S((Dc,FF)),S((FF,Dc)),S((VW,Dc)),S((Dc,HV)),S((R*n,heads*CH),bf16),S((R*n,128),bf16),S((R*n,HV),bf16),S((R*n,HV),bf16),S((n,R,Dc),bf16)],
      [VM]*9+[ANY]*5,
      [pltpu.VMEM((L+8,CH),f32),pltpu.VMEM((L+8,CH),f32),pltpu.VMEM((NC,DK,DV),f32),pltpu.VMEM((NC,8,128),f32),
       pltpu.VMEM((L,DV),bf16),pltpu.VMEM((L,CH),bf16),pltpu.VMEM((L,8),f32),pltpu.VMEM((n*8,local_len),f32),
       pltpu.VMEM((max(D,R*n),bw),bf16),pltpu.VMEM((max(D,R*n),bw),bf16),pltpu.VMEM((R*n,Dc),bf16),pltpu.VMEM((n,R,Dc),bf16),pltpu.VMEM((n,R,Dc),bf16),
       pltpu.VMEM((R,HV),bf16),pltpu.VMEM((R,HV),bf16),pltpu.VMEM((R,heads*CH),bf16),pltpu.VMEM((pairs*8,local_len),f32),pltpu.VMEM((R,128),bf16),pltpu.VMEM((R,D),f32),pltpu.VMEM((R,D),bf16),
       pltpu.VMEM((zc,R,F),bf16),pltpu.VMEM((zc,R,F),bf16),pltpu.VMEM((zc,8,R),f32)]
      +[sem((1,n)),sem((1,n)),sem((4,pairs)),sem((4,pairs))]+pair_sems(zc)*2+pair_sems(n)*2+pair_sems(zc)*3+[sem((2,6))]+gather_sems(n,2)+gather_sems(n,2))

def last_kernel(n,copies,heads,DK,DV,F,H,n1c,dyq,dsm,smalls,totals,*refs):
    moved=refs[:7]; oq,ok,ov,ob,od,qc,kc,vc,onorm,offn,ohead,olog,obias=refs[7:20]; moved_out=refs[20:27]; buf,sem,msem=refs[27:30]; held=refs[30:]
    step=buf.shape[1]//4
    jobs=[pltpu.make_async_copy(dyq.at[:,pl.ds(j*step,step)],buf.at[:,pl.ds(j*step,step)],sem.at[j]) for j in range(4)]
    for c in jobs: c.start()
    fetch=[pltpu.make_async_copy(a,b,msem.at[j]) for j,(a,b) in enumerate(zip(moved,held))]
    for c in fetch: c.start()
    n1=n1c[...].reshape(n1c.shape[0]*n1c.shape[1],n1c.shape[2])
    sm=dg(dsm[...],n1,0,0)
    ob[...]=sm[0:heads]; od[...]=sm[heads:2*heads]
    wk=heads*DK
    got=0
    for ref,start in ((oq,0),(ok,wk),(ov,2*wk)):
        for a in range(0,ref.shape[1],256):
            b=min(a+256,ref.shape[1])
            while got*step<start+b: jobs[got].wait(); got+=1
            ref[:,a:b]=dg(n1,buf[:,start+a:start+b],0,0)
    moves=[pltpu.make_async_copy(a,b,msem.at[j]) for j,(a,b) in enumerate(zip(held,moved_out))]
    for f,c in zip(fetch,moves): f.wait(); c.start()
    zc=totals.shape[0]
    for z in range(zc):
        onorm[0:1,z*F:(z+1)*F]=totals[z,0:1,0:F]
        offn[0:1,z*F:(z+1)*F]=totals[z,1:2,0:F]
    t=totals[0]
    for z in range(1,zc): t=t+totals[z]
    ohead[...]=t[2:3,0:DV]
    olog[...]=t[3:4,0:H]; obias[...]=t[3:4,H:2*H]
    s=lax.axis_index("seq")
    head=lax.div(s*heads,n)
    taps=0.0
    for sq in range(n//copies//heads): taps=taps+smalls[(sq*heads+head)*copies]
    cq,cv=qc.shape[1],vc.shape[1]
    for part in range(n//heads):
        @pl.when(lax.rem(s,n//heads)==part)
        def _():
            qc[...]=taps[4:8,part*cq:(part+1)*cq]
            kc[...]=taps[4:8,DK+part*cq:DK+(part+1)*cq]
            vc[...]=taps[4:8,2*DK+part*cv:2*DK+(part+1)*cv]
    for c in moves: c.wait()
def last(n,copies,heads,DK,DV,F,H,n1c,dyq,dsm,smalls,totals,cq,cv,moved):
    D=F*totals.shape[0]; Dc=n1c.shape[2]
    r=pl.pallas_call(functools.partial(last_kernel,n,copies,heads,DK,DV,F,H),name="last",
      out_shape=(S((Dc,heads*DK)),S((Dc,heads*DK)),S((Dc,heads*DV)),S((heads,Dc)),S((heads,Dc)),S((4,cq)),S((4,cq)),S((4,cv)),S((1,D)),S((1,D)),S((1,DV)),S((1,H)),S((1,H)))+tuple(S(x.shape) for x in moved),
      in_specs=[VM,ANY,VM,VM,VM]+[ANY]*7,out_specs=(VM,)*13+(ANY,)*7,scratch_shapes=[pltpu.VMEM(dyq.shape,bf16),pltpu.SemaphoreType.DMA((4,)),pltpu.SemaphoreType.DMA((7,))]+[pltpu.VMEM(x.shape,f32) for x in moved],
      compiler_params=pltpu.CompilerParams(vmem_limit_bytes=56*2**20))(n1c,dyq,dsm,smalls,totals,*moved)
    return r


MESH=pl.DeviceIdType.MESH
ANY=pl.BlockSpec(memory_space=pl.ANY)

def flip(s,bit):
    return s+bit-2*bit*lax.rem(lax.div(s,bit),2)

def flips(s,mask):
    bit=1
    while bit<=mask:
        if mask&bit: s=flip(s,bit)
        bit*=2
    return s

def greet(n,zc):
    s=lax.axis_index("seq"); z=lax.axis_index("shard")
    bar=pltpu.get_barrier_semaphore()
    for d in range(1,n):
        pl.semaphore_signal(bar,inc=1,device_id={"seq":lax.rem(s+d,n)},device_id_type=MESH)
    for d in range(1,zc):
        pl.semaphore_signal(bar,inc=1,device_id={"shard":lax.rem(z+d,zc)},device_id_type=MESH)
    pl.semaphore_wait(bar,n-1+zc-1)

def links(n):
    return 8 if n==8 else n

class SeqGather:
    def __init__(self,n,src,dst,axis,sems,c0=0):
        self.n=n; self.src=src; self.dst=dst; self.axis=axis; self.send,self.recv,self.loc=sems
        self.R,self.C=src.shape
        self.r0=0; self.nr=self.R; self.c0=c0
        self.s=lax.axis_index("seq")
        self.open=[]
    def slot(self,t,a,b):
        if self.axis==0:
            return self.dst.at[pl.ds(pl.multiple_of(t*self.R+self.r0+a,16),b-a),pl.ds(self.c0,self.C)]
        return self.dst.at[pl.ds(self.r0+a,b-a),pl.ds(pl.multiple_of(t*self.C,128),self.C)]
    def copy(self,src,t,a,b,k,to):
        c=pltpu.make_async_remote_copy(src_ref=src,dst_ref=self.slot(t,a,b),send_sem=self.send.at[k],recv_sem=self.recv.at[k],device_id={"seq":to},device_id_type=MESH)
        c.start()
        return c
    def pass_on(self,t,a,b,k,to):
        return self.copy(self.slot(t,a,b),t,a,b,k,to)
    def start(self):
        s=self.s; nr=self.nr
        mine=self.src.at[pl.ds(self.r0,nr),:]
        self.own=pltpu.make_async_copy(mine,self.slot(s,0,nr),self.loc)
        self.own.start()
        masks=(2,4) if self.n==8 else range(2,self.n,2)
        self.direct=[self.copy(mine,s,0,nr,i+1,flips(s,m)) for i,m in enumerate(masks)]
        self.open.append(self.copy(mine,s,0,nr,0,flip(s,1)))
    def middle(self):
        s=self.s; nr=self.nr; h=nr//2
        if self.n!=8: return
        x,y=flip(s,2),flip(s,4)
        self.direct[0].wait_recv()
        fa=self.pass_on(x,0,h,3,y)
        self.open.append(self.pass_on(x,0,nr,5,flip(s,1)))
        self.direct[1].wait_recv()
        fb=self.pass_on(y,h,nr,4,x)
        self.open.append(self.pass_on(y,0,nr,6,flip(s,1)))
        self.diag=(fa,fb)
    def late(self):
        s=self.s; nr=self.nr
        if self.n==8:
            for f in self.diag: f.wait_recv()
            self.open.append(self.pass_on(flips(s,6),0,nr,7,flip(s,1)))
            for f in self.diag: f.wait_send()
        else:
            for i,m in enumerate(range(2,self.n,2)):
                self.direct[i].wait_recv()
                self.open.append(self.pass_on(flips(s,m),0,nr,self.n//2+i,flip(s,1)))
        for f in self.direct: f.wait_send()
    def finish(self):
        for f in self.open: f.wait()
        self.own.wait()

class ShardGather:
    def __init__(self,zc,src,dst,send,recv):
        self.zc=zc; self.src=src; self.dst=dst; self.send=send; self.recv=recv
        self.z=lax.axis_index("shard"); self.C=src.shape[1]
    def slot(self):
        return self.dst.at[:,pl.ds(pl.multiple_of(self.z*self.C,128),self.C)]
    def start(self):
        self.own=pltpu.make_async_copy(self.src,self.slot(),self.recv.at[0]); self.own.start()
        self.cs=[]
        for d in range(1,self.zc):
            c=pltpu.make_async_remote_copy(src_ref=self.src,dst_ref=self.slot(),send_sem=self.send.at[d],recv_sem=self.recv.at[d],device_id={"shard":lax.rem(self.z+d,self.zc)},device_id_type=MESH)
            c.start(); self.cs.append(c)
    def finish(self):
        for c in self.cs: c.wait()
        self.own.wait()

class ShardSplit:
    def __init__(self,zc,src,box,send,recv):
        self.zc=zc; self.src=src; self.box=box; self.send=send; self.recv=recv
        self.z=lax.axis_index("shard"); self.C=box.shape[2]
    def start(self):
        C=self.C
        self.own=pltpu.make_async_copy(self.src.at[:,pl.ds(pl.multiple_of(self.z*C,128),C)],self.box.at[0],self.recv.at[0]); self.own.start()
        self.cs=[]
        for d in range(1,self.zc):
            to=lax.rem(self.z+d,self.zc)
            c=pltpu.make_async_remote_copy(src_ref=self.src.at[:,pl.ds(pl.multiple_of(to*C,128),C)],dst_ref=self.box.at[d],send_sem=self.send.at[d],recv_sem=self.recv.at[d],device_id={"shard":to},device_id_type=MESH)
            c.start(); self.cs.append(c)
    def finish(self):
        for c in self.cs: c.wait()
        self.own.wait()

class ShardAll:
    def __init__(self,axis,n,box,send,recv):
        self.axis=axis; self.n=n; self.box=box; self.send=send; self.recv=recv; self.me=lax.axis_index(axis)
    def start(self):
        self.cs=[]
        for d in range(1,self.n):
            c=pltpu.make_async_remote_copy(src_ref=self.box.at[self.me],dst_ref=self.box.at[self.me],send_sem=self.send.at[d],recv_sem=self.recv.at[d],device_id={self.axis:lax.rem(self.me+d,self.n)},device_id_type=MESH)
            c.start(); self.cs.append(c)
    def finish(self):
        for c in self.cs: c.wait()

class ColumnSplit:
    def __init__(self,n,src,dst,send,recv):
        self.n=n; self.src=src; self.dst=dst; self.send=send; self.recv=recv
        self.s=lax.axis_index("seq"); self.C=dst.shape[1]; self.R=src.shape[0]
    def start(self):
        n,s,C,R=self.n,self.s,self.C,self.R
        to_rows=self.dst.at[pl.ds(pl.multiple_of(s*R,16),R),:]
        block=lambda t: self.src.at[:,pl.ds(pl.multiple_of(t*C,128),C)]
        self.own=pltpu.make_async_copy(block(s),to_rows,self.recv.at[0]); self.own.start()
        self.cs=[]
        for d in range(1,n):
            t=lax.rem(s+d,n)
            c=pltpu.make_async_remote_copy(src_ref=block(t),dst_ref=to_rows,send_sem=self.send.at[d],recv_sem=self.recv.at[d],device_id={"seq":t},device_id_type=MESH)
            c.start(); self.cs.append(c)
    def finish(self):
        for c in self.cs: c.wait()
        self.own.wait()

class ToPairs:
    def __init__(self,n,copies,heads,local_len,src,rows_src,dst,rows_dst,DK,DV,send,recv):
        self.cs=[]
        self.__dict__.update(n=n,copies=copies,heads=heads,ll=local_len,src=src,rows_src=rows_src,dst=dst,rows_dst=rows_dst,DK=DK,DV=DV,send=send,recv=recv)
    def parts(self,t):
        s=lax.axis_index("seq"); ll,DK,DV,heads=self.ll,self.DK,self.DV,self.heads
        pair=lax.div(t,self.copies); seq=lax.div(pair,heads); head=lax.rem(pair,heads)
        rows=pl.ds(pl.multiple_of(seq*ll,ll),ll); to=pl.ds(pl.multiple_of(s*ll,ll),ll)
        if self.rows_src is None:
            return [(self.src.at[rows,pl.ds(pl.multiple_of(head*DV,128),DV)],self.dst.at[to,:])]
        wk=heads*DK
        out=[]
        for start,width,at in ((0,DK,0),(wk,DK,DK),(2*wk,DV,2*DK)):
            out.append((self.src.at[rows,pl.ds(pl.multiple_of(start+head*width,128),width)],self.dst.at[to,pl.ds(at,width)]))
        out.append((self.rows_src.at[pl.ds(pl.multiple_of(pair*8,8),8),:],self.rows_dst.at[pl.ds(pl.multiple_of(s*8,8),8),:]))
        return out
    def start(self,i):
        s=lax.axis_index("seq")
        for d in range(self.n):
            t=lax.rem(s+d,self.n)
            a,b=self.parts(t)[i]
            if d==0: c=pltpu.make_async_copy(a,b,self.recv.at[i,0])
            else: c=pltpu.make_async_remote_copy(src_ref=a,dst_ref=b,send_sem=self.send.at[i,d],recv_sem=self.recv.at[i,d],device_id={"seq":t},device_id_type=MESH)
            c.start(); self.cs.append(c)
    def finish(self):
        for c in self.cs: c.wait()

class FromPairs:
    def __init__(self,n,copies,heads,local_len,items,send,recv):
        self.__dict__.update(n=n,copies=copies,heads=heads,items=items,send=send,recv=recv)
    def start(self):
        s=lax.axis_index("seq"); pairs=self.n//self.copies; p=lax.div(s,self.copies); r=lax.rem(s,self.copies)
        seq=lax.div(p,self.heads); head=lax.rem(p,self.heads); self.cs=[]
        for d in range(pairs):
            t=lax.rem(p+d,pairs)*self.copies+r
            for i,(src,at,dst,to) in enumerate(self.items):
                a=src.at[at(t)]; b=dst.at[to(seq,head)]
                if d==0: c=pltpu.make_async_copy(a,b,self.recv.at[i,0])
                else: c=pltpu.make_async_remote_copy(src_ref=a,dst_ref=b,send_sem=self.send.at[i,d],recv_sem=self.recv.at[i,d],device_id={"seq":t},device_id_type=MESH)
                c.start(); self.cs.append(c)
    def finish(self):
        for c in self.cs: c.wait()

def flat_form(cols):
    r=cols.shape[0]
    i=lax.broadcasted_iota(jnp.int32,(r,r),0); j=lax.broadcasted_iota(jnp.int32,(r,r),1)
    return mmx(cols,jnp.where(i==j,1.0,0.0),0,0)

class SharedColumns:
    def __init__(self,n,zc,src,dst,sems):
        self.n=n; self.zc=zc; self.src=src; self.dst=dst; self.send,self.recv,self.zsend,self.zrecv=sems
        self.s=lax.axis_index("seq"); self.z=lax.axis_index("shard"); self.C=dst.shape[2]; self.q=src.shape[0]//zc
    def start(self):
        rows=pl.ds(pl.multiple_of(self.z*self.q,16),self.q)
        block=lambda t: self.src.at[rows,pl.ds(pl.multiple_of(t*self.C,128),self.C)]
        self.cs=[]
        for d in range(self.n):
            t=lax.rem(self.s+d,self.n)
            if d==0: c=pltpu.make_async_copy(block(t),self.dst.at[self.s,rows,:],self.recv.at[0])
            else: c=pltpu.make_async_remote_copy(src_ref=block(t),dst_ref=self.dst.at[self.s,rows,:],send_sem=self.send.at[d],recv_sem=self.recv.at[d],device_id={"seq":t},device_id_type=MESH)
            c.start(); self.cs.append(c)
    def middle(self):
        for c in self.cs: c.wait()
        strip=self.dst.at[:,pl.ds(pl.multiple_of(self.z*self.q,16),self.q),:]
        self.cs=[]
        for d in range(1,self.zc):
            c=pltpu.make_async_remote_copy(src_ref=strip,dst_ref=strip,send_sem=self.zsend.at[d],recv_sem=self.zrecv.at[d],device_id={"shard":lax.rem(self.z+d,self.zc)},device_id_type=MESH)
            c.start(); self.cs.append(c)
    def finish(self):
        for c in self.cs: c.wait()

def row_form(cols):
    return mmx(jnp.ones((8,cols.shape[1]),f32),cols,1,1)

def col_form(rows):
    r=rows.shape[1]
    i=lax.broadcasted_iota(jnp.int32,(r,r),0); j=lax.broadcasted_iota(jnp.int32,(r,r),1)
    return mmx(jnp.where(i==j,1.0,0.0),rows,1,1)

def gathers(n,pairs,sems):
    send,recv,loc=sems
    return [SeqGather(n,src,dst,axis,(send.at[i],recv.at[i],loc.at[i]),*c0) for i,(src,dst,axis,*c0) in enumerate(pairs)]
def gather_sems(n,k):
    return [pltpu.SemaphoreType.DMA((k,links(n))),pltpu.SemaphoreType.DMA((k,links(n))),pltpu.SemaphoreType.DMA((k,))]
def pair_sems(k):
    return [pltpu.SemaphoreType.DMA((k,)),pltpu.SemaphoreType.DMA((k,))]
def each(ops,name):
    for o in ops: getattr(o,name)()

def ffn_kernel(n,zc,part,tok,cot,cotfull,gain_all,wgfull,wu,wd,res,gres,afull,gffn,outpart,hidfull,dgfull,dufull,n2c,
               box,sums,nloc,nfull,gw_,uw_,dw_,gv,uv,hidden,dgate,dup,two,ld,as_,ar,bs,br,cs,cr,ds_,dr,es,er,fs,fr,hs,hr,*gs):
    greet(n,zc)
    D=part.shape[1]; R=part.shape[0]; FF=gv.shape[1]; z=lax.axis_index("shard")
    split=ShardSplit(zc,part,box,as_,ar); split.start()
    g1,g2=gs[:3],gs[3:]
    gw=gathers(n,[(wu,uw_,0),(wd,dw_,1)],g1)
    each(gw,"start")
    lg=pltpu.make_async_copy(wgfull,gw_,ld.at[0]); lg.start()
    gain=gain_all[:,pl.ds(pl.multiple_of(z*tok.shape[1],128),tok.shape[1])]
    split.finish()
    r=tok[...].astype(f32)
    for d in range(zc): r=r+box[d].astype(f32)
    res[...]=r
    sums[z]=row_form(r*r)
    tot=ShardAll("shard",zc,sums,bs,br); tot.start(); tot.finish()
    t=sums[0]
    for d in range(1,zc): t=t+sums[d]
    sc=lax.rsqrt(col_form(t)[:,0:1]/D+EPSILON)
    nloc[...]=(r*sc*gain).astype(bf16)
    zg=ShardGather(zc,nloc,nfull,cs,cr); zg.start()
    each(gw,"middle")
    zg.finish()
    cols=ColumnSplit(n,nfull,n2c,es,er); cols.start()
    tiles=[(a,min(a+512,FF)) for a in range(0,FF,512)]
    lg.wait()
    for a,b in tiles: gv[:,a:b]=jnp.dot(nfull[...],gw_[:,a:b],preferred_element_type=f32)
    gw[0].late(); gw[0].finish()
    for a,b in tiles: uv[:,a:b]=jnp.dot(nfull[...],uw_[:,a:b],preferred_element_type=f32)
    def act(c,_):
        rr=pl.ds(pl.multiple_of(c*32,32),32)
        g=gv[rr,:]
        hidden[rr,:]=(g*sigmoid(g)*uv[rr,:]).astype(bf16)
        return 0
    lax.fori_loop(0,R//32,act,0)
    gh=gathers(n,[(hidden,hidfull,0),(dgate,dgfull,0),(dup,dufull,0)],g2)
    gh[0].start()
    gw[1].late(); gw[1].finish()
    for a,b in tiles:
        dh=dg(cotfull[...],dw_[a:b,:],1,1)
        g=gv[:,a:b]; sg=sigmoid(g)
        dgate[:,a:b]=(dh*uv[:,a:b]*sg*(1.0+g*(1.0-sg))).astype(bf16)
        dup[:,a:b]=(dh*(g*sg)).astype(bf16)
    gd=gh
    each(gd[1:],"start")
    def back(j,_):
        rr=pl.ds(pl.multiple_of(j*256,256),256)
        two[:,rr]=(dg(dgate[...],gw_[rr,:],1,1)+dg(dup[...],uw_[rr,:],1,1)).astype(bf16)
        return 0
    lax.fori_loop(0,D//256,back,0)
    split=ShardSplit(zc,two,box,fs,fr)
    split.start()
    def outp(j,_):
        cc=pl.ds(pl.multiple_of(j*256,256),256)
        outpart[:,cc]=jnp.dot(hidden[...],dw_[:,cc],preferred_element_type=f32).astype(bf16)
        return 0
    lax.fori_loop(0,D//256,outp,0)
    split.finish()
    g=box[0].astype(f32)
    for d in range(1,zc): g=g+box[d].astype(f32)
    r=res[...]
    gained=gain*g
    sums[zc+z]=row_form(gained*r)
    tot=ShardAll("shard",zc,sums.at[pl.ds(zc,zc)],ds_,dr); tot.start()
    gffn[...]=jnp.broadcast_to(jnp.sum(g*r*sc,axis=0,keepdims=True),gffn.shape)
    tot.finish()
    t=sums[zc]
    for d in range(1,zc): t=t+sums[zc+d]
    inner=col_form(t)[:,0:1]/D
    gr=cot[...].astype(f32)+sc*(gained-r*(sc*sc*inner))
    gres[...]=gr
    nloc[...]=gr.astype(bf16)
    zg=ShardGather(zc,nloc,afull,hs,hr); zg.start()
    each(gd,"middle")
    zg.finish()
    each(gd,"late"); cols.finish(); each(gd,"finish")

def call(name,cid,kernel,args,specs,outs,ospecs,scratch):
    return pl.pallas_call(kernel,name=name,out_shape=tuple(outs),in_specs=specs,out_specs=tuple(ospecs),scratch_shapes=scratch,
      compiler_params=pltpu.CompilerParams(collective_id=cid,has_side_effects=True,vmem_limit_bytes=61*2**20))(*args)

def ffn(n,zc,part,tok,cot,cotfull,gain,wgfull,wu,wd):
    R,F=tok.shape; D=F*zc; FF=wu.shape[1]
    return call("ffn",2,functools.partial(ffn_kernel,n,zc),(part,tok,cot,cotfull,gain,wgfull,wu,wd),[ANY]+[VM]*4+[ANY]*3,
      [S((R,F)),S((R,F)),S((R,D),bf16),S((8,F)),S((R,D),bf16),S((R*n,FF),bf16),S((R*n,FF),bf16),S((R*n,FF),bf16),S((R*n,D//n),bf16)],
      [VM]*5+[ANY]*4,
      [pltpu.VMEM((zc,R,F),bf16),pltpu.VMEM((2*zc,8,R),f32),pltpu.VMEM((R,F),bf16),pltpu.VMEM((R,D),bf16),pltpu.VMEM((D,FF),bf16),pltpu.VMEM((D,FF),bf16),pltpu.VMEM((FF,D),bf16),
       pltpu.VMEM((R,FF),f32),pltpu.VMEM((R,FF),f32),pltpu.VMEM((R,FF),bf16),pltpu.VMEM((R,FF),bf16),pltpu.VMEM((R,FF),bf16),pltpu.VMEM((R,D),bf16),pltpu.SemaphoreType.DMA((1,))]
      +pair_sems(zc)*4+pair_sems(n)+pair_sems(zc)*2+gather_sems(n,2)+gather_sems(n,3))


def per_device(
    tokens, doc_starts, norm_gain, query_weight, key_weight, value_weight, outgate_weight,
    beta_weight, decay_weight, query_conv, key_conv, value_conv, decay_log, decay_bias, head_gain,
    output_weight, ffn_gain, gate_weight, up_weight, down_weight, cotangent,
):
    seq_count, local_len, feature_part = tokens.shape
    row_count = seq_count * local_len
    shard_count = lax.axis_size("shard")
    seq_devices = lax.axis_size("seq")
    head_count = beta_weight.shape[1]
    key_dim = query_weight.shape[1] // head_count
    value_dim = value_weight.shape[1] // head_count
    pairs = seq_count * head_count
    copies = seq_devices // pairs
    flat = lambda x: x.reshape(row_count, x.shape[2])
    tokens_flat, cot_flat = flat(tokens), flat(cotangent)
    head_row, norm_row, ffn_row = head_gain[None], norm_gain[None], ffn_gain[None]
    (
        scale_one, cot_rows, full_one, full_outgate, full_output, full_gate, cot_cols, normed_one_cols,
        gate_proj, o_flat, branch, attn_part, taps, *saved,
    ) = forward(
        seq_devices, shard_count, copies, head_count, tokens_flat, cot_flat, norm_row, head_row, doc_starts, decay_log,
        decay_bias, beta_weight.T, decay_weight.T, query_conv.T, key_conv.T, value_conv.T, query_weight, key_weight, value_weight,
        outgate_weight, output_weight, gate_weight, key_dim, value_dim,
    )
    residual, grad_residual, attn_cot, grad_ffn_part, out_part, hidden_all, dgate_all, dup_all, normed_two_cols = ffn(
        seq_devices, shard_count, attn_part, tokens_flat, cot_flat, cot_rows, ffn_row, full_gate, up_weight, down_weight
    )
    (
        output, grad_tokens, smalls, totals, out_gate, out_up, out_down, out_output, out_outgate, qkv_all, small_all,
        unused_branch, unused_gate, unused_cols,
    ) = back(
        seq_devices, shard_count, copies, head_count, decay_log.shape[0], attn_cot, gate_proj, o_flat, head_row, tokens_flat,
        scale_one, norm_row, residual, grad_residual, grad_ffn_part, taps, saved, doc_starts, decay_log, decay_bias,
        full_output, full_one, full_outgate, out_part, branch, hidden_all, dgate_all, dup_all, normed_two_cols,
        normed_one_cols, cot_cols,
    )
    (
        out_query, out_key, out_value, out_beta, out_decay, out_qconv, out_kconv, out_vconv, out_norm, out_ffn, out_head,
        out_log, out_bias, output, grad_tokens, out_gate, out_up, out_down, out_output, out_outgate,
    ) = last(
        seq_devices, copies, head_count, key_dim, value_dim, feature_part, decay_log.shape[0], normed_one_cols, qkv_all,
        small_all, smalls, totals, query_conv.shape[0], value_conv.shape[0],
        (output, grad_tokens, out_gate, out_up, out_down, out_output, out_outgate),
    )
    shape3 = (seq_count, local_len, feature_part)
    return (
        output.reshape(shape3), grad_tokens.reshape(shape3), out_norm[0], out_query, out_key, out_value, out_outgate,
        out_beta.T, out_decay.T, out_qconv.T, out_kconv.T, out_vconv.T, out_log[0], out_bias[0], out_head[0], out_output,
        out_ffn[0], out_gate, out_up, out_down,
    )


def solution(mesh):
    P = PartitionSpec
    rows, cols = P("seq", "shard"), P("shard", "seq")
    both, acts = P(("shard", "seq"), None), P(None, "seq", "shard")
    return jax.shard_map(
        per_device,
        mesh=mesh,
        in_specs=(acts, P(), P()) + (rows,) * 6 + (both,) * 3 + (P(), P(), P(), cols, P(), rows, rows, cols, acts),
        out_specs=(acts, acts, P()) + (rows,) * 6 + (both,) * 3 + (P(), P(), P(), cols, P(), rows, rows, cols),
        check_vma=False,
    )
```

```python
import functools
from types import SimpleNamespace
import jax, jax.numpy as jnp
from jax import lax
from jax.experimental import pallas as pl
from jax.experimental.pallas import tpu as pltpu
from jax.sharding import PartitionSpec
f32=jnp.float32; bf16=jnp.bfloat16
SPAN=128
EPSILON=1e-6
HI=lax.Precision.HIGHEST

def dg(a,b,ca=1,cb=0):
    return lax.dot_general(a,b,(((ca,),(cb,)),((),())),preferred_element_type=f32)
def halves(x):
    h=x.astype(bf16)
    return h,(x-h.astype(f32)).astype(bf16)
def mm3(a,b,ca=1,cb=0):
    ah,al=halves(a); bh,bl=halves(b)
    return dg(ah,bh,ca,cb)+(dg(al,bh,ca,cb)+dg(ah,bl,ca,cb))
def mm1(a,b,ca=1,cb=0):
    return dg(a.astype(bf16),b.astype(bf16),ca,cb)
def mmx(a,b,ca=1,cb=0):
    return lax.dot_general(a,b,(((ca,),(cb,)),((),())),preferred_element_type=f32,precision=HI)

def square_masks():
    i=lax.broadcasted_iota(jnp.int32,(SPAN,SPAN),0); j=lax.broadcasted_iota(jnp.int32,(SPAN,SPAN),1)
    return i,j
def positions(base,rows,cols,axis):
    return base+lax.broadcasted_iota(jnp.int32,(rows,cols),axis)
class Row:
    def __init__(self,ref,row):
        self.ref=ref; self.row=row; self.shape=ref.shape[1:]
    def __getitem__(self,e):
        return self.ref[self.row,e]

def doc_count(starts,pos):
    n=jnp.zeros(pos.shape,jnp.int32)
    for e in range(starts.shape[0]):
        n=n+jnp.where(starts[e]<=pos,1,0)
    return n
def doc_age(starts,pos):
    s=jnp.zeros(pos.shape,jnp.int32)
    for e in range(starts.shape[0]):
        s=jnp.where(starts[e]<=pos,starts[e],s)
    return pos-s
def count_at(starts,p):
    n=jnp.int32(0)
    for e in range(starts.shape[0]):
        n=n+jnp.where(starts[e]<=p,1,0)
    return n
def sigmoid(x):
    return 1.0/(1.0+jnp.exp(-x))
def softplus(x):
    return jnp.maximum(x,0.0)+jnp.log(1.0+jnp.exp(-jnp.abs(x)))

def inverses(blocks_a,t_ref):
    i,j=square_masks()
    eye=jnp.where(i==j,1.0,0.0)
    blocks=range(t_ref.shape[0])
    for n in blocks: t_ref[n]=eye-jnp.where((i//2)==(j//2),blocks_a(n),0.0)
    size=2
    while size<SPAN:
        part=((i//(2*size))==(j//(2*size)))&((i//size)!=(j//size))
        x=[dg(jnp.where(part,blocks_a(n),0.0).astype(bf16),t_ref[n].astype(bf16)).astype(bf16) for n in blocks]
        for n in blocks: t_ref[n]=t_ref[n]-dg(t_ref[n].astype(bf16),x[n])
        size*=2
    for n in blocks:
        Tb=t_ref[n].astype(bf16); Ah,Al=halves(blocks_a(n))
        rest=eye-Tb.astype(f32)-(dg(Ah,Tb)+dg(Al,Tb))
        t_ref[n]=Tb.astype(f32)+dg(Tb,rest.astype(bf16))

def position_rows(raw,starts,base,rate,bias):
    r=raw.shape[1]
    row=lax.broadcasted_iota(jnp.int32,(8,r),0)
    g=-rate*softplus(raw[1:2]+bias)
    i=lax.broadcasted_iota(jnp.int32,(r,r),0); j=lax.broadcasted_iota(jnp.int32,(r,r),1)
    G=mmx(jnp.broadcast_to(g,(8,r)),jnp.where((i<=j)&((i//SPAN)==(j//SPAN)),1.0,0.0))
    docs=doc_count(starts,positions(base,8,r,1)).astype(f32)
    out=jnp.where(row==0,sigmoid(raw[0:1]),0.0)
    for k,x in ((1,g),(2,G),(3,raw[1:2]),(4,docs)): out=jnp.where(row==k,x,out)
    return out

def span_terms(n,q,k,starts,xc,xr):
    i,j=square_masks()
    before=count_at(starts,n*SPAN-1).astype(f32)
    wide=lambda c: jnp.broadcast_to(c,(SPAN,128))
    beta=wide(xc[:,0:1]); G=wide(xc[:,2:3]); docs=wide(xc[:,4:5])
    incl=(i>=j)&(docs[:,:SPAN]==xr[4:5])
    D=jnp.where(incl,jnp.exp(jnp.where(incl,G[:,:SPAN]-xr[2:3],0.0)),0.0)
    gam=jnp.where(docs==before,jnp.exp(G),0.0)
    end=jnp.where(docs==docs[SPAN-1:SPAN],jnp.exp(G[SPAN-1:SPAN]-G),0.0)
    KK=dg(k,k,1,1); QK=dg(q,k,1,1)
    return beta,D,gam,end,KK,QK,i,j


SM=pl.BlockSpec(memory_space=pltpu.SMEM); VM=pl.BlockSpec(memory_space=pltpu.VMEM)
def S(shape,dt=f32): return jax.ShapeDtypeStruct(shape,dt)


MESH=pl.DeviceIdType.MESH
ANY=pl.BlockSpec(memory_space=pl.ANY)

def flip(s,bit):
    return s+bit-2*bit*lax.rem(lax.div(s,bit),2)

def flips(s,mask):
    bit=1
    while bit<=mask:
        if mask&bit: s=flip(s,bit)
        bit*=2
    return s

def greet(n,zc):
    s=lax.axis_index("seq"); z=lax.axis_index("shard")
    bar=pltpu.get_barrier_semaphore()
    for d in range(1,n):
        pl.semaphore_signal(bar,inc=1,device_id={"seq":lax.rem(s+d,n)},device_id_type=MESH)
    for d in range(1,zc):
        pl.semaphore_signal(bar,inc=1,device_id={"shard":lax.rem(z+d,zc)},device_id_type=MESH)
    pl.semaphore_wait(bar,n-1+zc-1)

def links(n):
    return 8 if n==8 else n

class SeqGather:
    def __init__(self,n,src,dst,axis,sems,c0=0):
        self.n=n; self.src=src; self.dst=dst; self.axis=axis; self.send,self.recv,self.loc=sems
        self.R,self.C=src.shape
        self.r0=0; self.nr=self.R; self.c0=c0
        self.s=lax.axis_index("seq")
        self.open=[]
    def slot(self,t,a,b):
        if self.axis==0:
            return self.dst.at[pl.ds(pl.multiple_of(t*self.R+self.r0+a,16),b-a),pl.ds(self.c0,self.C)]
        return self.dst.at[pl.ds(self.r0+a,b-a),pl.ds(pl.multiple_of(t*self.C,128),self.C)]
    def copy(self,src,t,a,b,k,to):
        c=pltpu.make_async_remote_copy(src_ref=src,dst_ref=self.slot(t,a,b),send_sem=self.send.at[k],recv_sem=self.recv.at[k],device_id={"seq":to},device_id_type=MESH)
        c.start()
        return c
    def pass_on(self,t,a,b,k,to):
        return self.copy(self.slot(t,a,b),t,a,b,k,to)
    def start(self):
        s=self.s; nr=self.nr
        mine=self.src.at[pl.ds(self.r0,nr),:]
        self.own=pltpu.make_async_copy(mine,self.slot(s,0,nr),self.loc)
        self.own.start()
        masks=(2,4) if self.n==8 else range(2,self.n,2)
        self.direct=[self.copy(mine,s,0,nr,i+1,flips(s,m)) for i,m in enumerate(masks)]
        self.open.append(self.copy(mine,s,0,nr,0,flip(s,1)))
    def middle(self):
        s=self.s; nr=self.nr; h=nr//2
        if self.n!=8: return
        x,y=flip(s,2),flip(s,4)
        self.direct[0].wait_recv()
        fa=self.pass_on(x,0,h,3,y)
        self.open.append(self.pass_on(x,0,nr,5,flip(s,1)))
        self.direct[1].wait_recv()
        fb=self.pass_on(y,h,nr,4,x)
        self.open.append(self.pass_on(y,0,nr,6,flip(s,1)))
        self.diag=(fa,fb)
    def late(self):
        s=self.s; nr=self.nr
        if self.n==8:
            for f in self.diag: f.wait_recv()
            self.open.append(self.pass_on(flips(s,6),0,nr,7,flip(s,1)))
            for f in self.diag: f.wait_send()
        else:
            for i,m in enumerate(range(2,self.n,2)):
                self.direct[i].wait_recv()
                self.open.append(self.pass_on(flips(s,m),0,nr,self.n//2+i,flip(s,1)))
        for f in self.direct: f.wait_send()
    def finish(self):
        for f in self.open: f.wait()
        self.own.wait()

class ShardGather:
    def __init__(self,zc,src,dst,send,recv):
        self.zc=zc; self.src=src; self.dst=dst; self.send=send; self.recv=recv
        self.z=lax.axis_index("shard"); self.C=src.shape[1]
    def slot(self):
        return self.dst.at[:,pl.ds(pl.multiple_of(self.z*self.C,128),self.C)]
    def start(self):
        self.own=pltpu.make_async_copy(self.src,self.slot(),self.recv.at[0]); self.own.start()
        self.cs=[]
        for d in range(1,self.zc):
            c=pltpu.make_async_remote_copy(src_ref=self.src,dst_ref=self.slot(),send_sem=self.send.at[d],recv_sem=self.recv.at[d],device_id={"shard":lax.rem(self.z+d,self.zc)},device_id_type=MESH)
            c.start(); self.cs.append(c)
    def finish(self):
        for c in self.cs: c.wait()
        self.own.wait()

class ShardSplit:
    def __init__(self,zc,src,box,send,recv):
        self.zc=zc; self.src=src; self.box=box; self.send=send; self.recv=recv
        self.z=lax.axis_index("shard"); self.C=box.shape[2]
    def start(self):
        C=self.C
        self.own=pltpu.make_async_copy(self.src.at[:,pl.ds(pl.multiple_of(self.z*C,128),C)],self.box.at[0],self.recv.at[0]); self.own.start()
        self.cs=[]
        for d in range(1,self.zc):
            to=lax.rem(self.z+d,self.zc)
            c=pltpu.make_async_remote_copy(src_ref=self.src.at[:,pl.ds(pl.multiple_of(to*C,128),C)],dst_ref=self.box.at[d],send_sem=self.send.at[d],recv_sem=self.recv.at[d],device_id={"shard":to},device_id_type=MESH)
            c.start(); self.cs.append(c)
    def finish(self):
        for c in self.cs: c.wait()
        self.own.wait()

class ShardAll:
    def __init__(self,axis,n,box,send,recv):
        self.axis=axis; self.n=n; self.box=box; self.send=send; self.recv=recv; self.me=lax.axis_index(axis)
    def start(self):
        self.cs=[]
        for d in range(1,self.n):
            c=pltpu.make_async_remote_copy(src_ref=self.box.at[self.me],dst_ref=self.box.at[self.me],send_sem=self.send.at[d],recv_sem=self.recv.at[d],device_id={self.axis:lax.rem(self.me+d,self.n)},device_id_type=MESH)
            c.start(); self.cs.append(c)
    def finish(self):
        for c in self.cs: c.wait()

class ColumnSplit:
    def __init__(self,n,src,dst,send,recv):
        self.n=n; self.src=src; self.dst=dst; self.send=send; self.recv=recv
        self.s=lax.axis_index("seq"); self.C=dst.shape[1]; self.R=src.shape[0]
    def start(self):
        n,s,C,R=self.n,self.s,self.C,self.R
        to_rows=self.dst.at[pl.ds(pl.multiple_of(s*R,16),R),:]
        block=lambda t: self.src.at[:,pl.ds(pl.multiple_of(t*C,128),C)]
        self.own=pltpu.make_async_copy(block(s),to_rows,self.recv.at[0]); self.own.start()
        self.cs=[]
        for d in range(1,n):
            t=lax.rem(s+d,n)
            c=pltpu.make_async_remote_copy(src_ref=block(t),dst_ref=to_rows,send_sem=self.send.at[d],recv_sem=self.recv.at[d],device_id={"seq":t},device_id_type=MESH)
            c.start(); self.cs.append(c)
    def finish(self):
        for c in self.cs: c.wait()
        self.own.wait()

class ToPairs:
    def __init__(self,n,copies,heads,local_len,src,rows_src,dst,rows_dst,DK,DV,send,recv,off=0):
        self.cs=[]
        self.__dict__.update(n=n,copies=copies,heads=heads,ll=local_len,src=src,rows_src=rows_src,dst=dst,rows_dst=rows_dst,DK=DK,DV=DV,send=send,recv=recv,off=off)
    def parts(self,t):
        s=lax.axis_index("seq"); ll,DK,DV,heads=self.ll,self.DK,self.DV,self.heads
        pair=lax.div(t,self.copies); seq=lax.div(pair,heads); head=lax.rem(pair,heads)
        rows=pl.ds(pl.multiple_of(seq*ll,ll),ll); to=pl.ds(pl.multiple_of(s*ll+self.off,16),ll)
        if self.rows_src is None:
            return [(self.src.at[rows,pl.ds(pl.multiple_of(head*DV,128),DV)],self.dst.at[to,:])]
        wk=heads*DK
        out=[]
        for start,width,at in ((0,DK,0),(wk,DK,DK),(2*wk,DV,2*DK)):
            out.append((self.src.at[rows,pl.ds(pl.multiple_of(start+head*width,128),width)],self.dst.at[to,pl.ds(at,width)]))
        out.append((self.rows_src.at[pl.ds(pl.multiple_of(pair*8,8),8),:],self.rows_dst.at[pl.ds(pl.multiple_of(s*8,8),8),:]))
        return out
    def start(self,i):
        s=lax.axis_index("seq")
        for d in range(self.n):
            t=lax.rem(s+d,self.n)
            a,b=self.parts(t)[i]
            if d==0: c=pltpu.make_async_copy(a,b,self.recv.at[i,0])
            else: c=pltpu.make_async_remote_copy(src_ref=a,dst_ref=b,send_sem=self.send.at[i,d],recv_sem=self.recv.at[i,d],device_id={"seq":t},device_id_type=MESH)
            c.start(); self.cs.append(c)
    def finish(self):
        for c in self.cs: c.wait()

class FromPairs:
    def __init__(self,n,copies,heads,local_len,items,send,recv):
        self.__dict__.update(n=n,copies=copies,heads=heads,items=items,send=send,recv=recv)
    def start(self):
        s=lax.axis_index("seq"); pairs=self.n//self.copies; p=lax.div(s,self.copies); r=lax.rem(s,self.copies)
        seq=lax.div(p,self.heads); head=lax.rem(p,self.heads); self.cs=[]
        for d in range(pairs):
            t=lax.rem(p+d,pairs)*self.copies+r
            for i,(src,at,dst,to) in enumerate(self.items):
                a=src.at[at(t)]; b=dst.at[to(seq,head)]
                if d==0: c=pltpu.make_async_copy(a,b,self.recv.at[i,0])
                else: c=pltpu.make_async_remote_copy(src_ref=a,dst_ref=b,send_sem=self.send.at[i,d],recv_sem=self.recv.at[i,d],device_id={"seq":t},device_id_type=MESH)
                c.start(); self.cs.append(c)
    def finish(self):
        for c in self.cs: c.wait()

def flat_form(cols):
    r=cols.shape[0]
    i=lax.broadcasted_iota(jnp.int32,(r,r),0); j=lax.broadcasted_iota(jnp.int32,(r,r),1)
    return mmx(cols,jnp.where(i==j,1.0,0.0),0,0)

class SharedColumns:
    def __init__(self,n,zc,src,dst,sems):
        self.n=n; self.zc=zc; self.src=src; self.dst=dst; self.send,self.recv,self.zsend,self.zrecv=sems
        self.s=lax.axis_index("seq"); self.z=lax.axis_index("shard"); self.C=dst.shape[2]; self.q=src.shape[0]//zc
    def start(self):
        rows=pl.ds(pl.multiple_of(self.z*self.q,16),self.q)
        block=lambda t: self.src.at[rows,pl.ds(pl.multiple_of(t*self.C,128),self.C)]
        self.cs=[]
        for d in range(self.n):
            t=lax.rem(self.s+d,self.n)
            if d==0: c=pltpu.make_async_copy(block(t),self.dst.at[self.s,rows,:],self.recv.at[0])
            else: c=pltpu.make_async_remote_copy(src_ref=block(t),dst_ref=self.dst.at[self.s,rows,:],send_sem=self.send.at[d],recv_sem=self.recv.at[d],device_id={"seq":t},device_id_type=MESH)
            c.start(); self.cs.append(c)
    def middle(self):
        for c in self.cs: c.wait()
        strip=self.dst.at[:,pl.ds(pl.multiple_of(self.z*self.q,16),self.q),:]
        self.cs=[]
        for d in range(1,self.zc):
            c=pltpu.make_async_remote_copy(src_ref=strip,dst_ref=strip,send_sem=self.zsend.at[d],recv_sem=self.zrecv.at[d],device_id={"shard":lax.rem(self.z+d,self.zc)},device_id_type=MESH)
            c.start(); self.cs.append(c)
    def finish(self):
        for c in self.cs: c.wait()

def row_form(cols):
    return mmx(jnp.ones((8,cols.shape[1]),f32),cols,1,1)

def col_form(rows):
    r=rows.shape[1]
    i=lax.broadcasted_iota(jnp.int32,(r,r),0); j=lax.broadcasted_iota(jnp.int32,(r,r),1)
    return mmx(jnp.where(i==j,1.0,0.0),rows,1,1)

def gathers(n,pairs,sems):
    send,recv,loc=sems
    return [SeqGather(n,src,dst,axis,(send.at[i],recv.at[i],loc.at[i]),*c0) for i,(src,dst,axis,*c0) in enumerate(pairs)]
def gather_sems(n,k):
    return [pltpu.SemaphoreType.DMA((k,links(n))),pltpu.SemaphoreType.DMA((k,links(n))),pltpu.SemaphoreType.DMA((k,))]
def pair_sems(k):
    return [pltpu.SemaphoreType.DMA((k,)),pltpu.SemaphoreType.DMA((k,))]
def each(ops,name):
    for o in ops: getattr(o,name)()


def conv_pre(u,taps,age,base,rows):
    window=u[pl.ds(base,rows+16),:].astype(f32)
    pre=window[16:]*taps[3:4]
    for back in range(1,4):
        ok=jnp.where(age>=back,1.0,0.0)
        pre=pre+window[16-back:16-back+rows]*ok*taps[3-back:4-back]
    return pre,window

def tiles(width,step): return [(a,min(a+step,width)) for a in range(0,width,step)]

def layer_kernel(cfg,names,*refs):
    n,zc,copies,heads,DK,DV,H=cfg
    r_=SimpleNamespace(**dict(zip(names,refs)))
    tok,cot=r_.tok,r_.cot
    RN,F=tok.shape; D=F*zc; seqs=r_.starts.shape[0]; ll=RN//seqs; L=n*ll; NC=L//SPAN; per=ll//SPAN
    wk=heads*DK; wv=heads*DV; CH=2*DK+DV; FF=r_.wup.shape[1]; N=n*RN; VW=wv
    s=lax.axis_index("seq"); z=lax.axis_index("shard")
    pair=lax.div(s,copies); my_head=lax.rem(pair,heads); at_head=z*heads+my_head
    starts=Row(r_.starts,lax.div(pair,heads))
    count=[0,0,0]
    def zsems():
        count[0]+=1; return r_.zsend.at[count[0]-1],r_.zrecv.at[count[0]-1]
    def qsems():
        count[1]+=1; return r_.qsend.at[count[1]-1],r_.qrecv.at[count[1]-1]
    def gather(src,dst,axis,c0=0):
        count[2]+=1; i=count[2]-1
        return SeqGather(n,src,dst,axis,(r_.gsend.at[i],r_.grecv.at[i],r_.gloc.at[i]),c0)
    def span(m): return pl.ds(pl.multiple_of(m*SPAN,SPAN),SPAN)
    def loop(count_,body,unroll=1): lax.fori_loop(0,count_,lambda i,c: (body(i),c)[1],0,unroll=unroll)
    normed,scale=r_.normed,r_.scale
    pbuf=r_.tokfull.at[:,pl.ds(0,heads*CH)]
    gw_=r_.bufa.at[pl.ds(0,D),pl.ds(0,FF)]; uw_=r_.bufb.at[pl.ds(0,D),pl.ds(0,FF)]; dw_=r_.dw
    wbuf=r_.bufb
    gv=r_.gv; uv=r_.uv
    cotfull,oall,branch,pbf,u_ref,taps_ref=r_.cotfull,r_.oall,r_.branch,r_.pbf,r_.u,r_.taps
    xr_ref,xc_ref,q_ref,k_ref,v_ref,s_ref,w_ref,t_ref,qt_ref,mh_ref,gc_ref=r_.xr,r_.xc,r_.q,r_.k,r_.v,r_.s,r_.w,r_.t,r_.qt,r_.mh,r_.gc
    gate_ref,rbuf,dpre,du_ref,dx_ref,do_ref,dxr,ds_ref=r_.gate,r_.rbuf,r_.dpre,r_.du,r_.dx,r_.do,r_.dxr,r_.ds
    heads_v=pl.ds(0,DV); rest_v=pl.ds(DV,DV)

    put=lambda x,first: dg(x[...],jnp.where(lax.broadcasted_iota(jnp.int32,(x.shape[0],128),0)+first==lax.broadcasted_iota(jnp.int32,(x.shape[0],128),1),1.0,0.0).astype(bf16),0,0)
    ws=r_.ws
    ws[...]=(put(r_.wb,0)+put(r_.wd,heads)).astype(bf16)
    at_row=0
    for x in (r_.qc,r_.kc,r_.vc):
        ws[at_row:at_row+x.shape[1]]=(ws[at_row:at_row+x.shape[1]].astype(f32)+put(x,2*heads)).astype(bf16)
        at_row+=x.shape[1]
    greet(n,zc)
    zt=ShardGather(zc,tok,r_.tokfull,*zsems()); zt.start()
    ws_all=(ws,r_.wq,r_.wk,r_.wv); at=(wk*2+wv,0,wk,wk*2)
    gw=[gather(w,r_.wfull,0,a) for w,a in zip(ws_all,at)]
    each(gw,"start")
    u_ref[0:16]=jnp.zeros((16,CH),bf16)
    rbuf[...]=jnp.zeros(rbuf.shape,f32)
    dx_ref[...]=jnp.zeros(dx_ref.shape,f32)
    rate=jnp.exp(jnp.full((1,1),r_.dlog[at_head],f32)); bias=r_.dbias[at_head]
    each(gw,"middle")
    zt.finish()
    zk=ShardGather(zc,cot,cotfull,*zsems()); zk.start()
    def norm(c):
        r=pl.ds(pl.multiple_of(c*32,32),32)
        x=r_.tokfull[r,:].astype(f32)
        sc=lax.rsqrt(jnp.sum(x*x,axis=1,keepdims=True)/D+EPSILON)
        normed[r,:]=(x*sc*r_.gain[...]).astype(bf16)
        scale[r,:]=jnp.broadcast_to(sc,(32,128))
    loop(RN//32,norm)
    inward=ToPairs(n,copies,heads,ll,pbuf,rbuf,u_ref,xr_ref,DK,DV,r_.isend,r_.irecv,16)
    for i,g in enumerate(gw):
        g.late(); g.finish()
        width=ws_all[i].shape[1]
        buf=r_.sbuf if i==0 else wbuf.at[pl.ds(0,D),pl.ds(0,width)]
        c=pltpu.make_async_copy(r_.wfull.at[:,pl.ds(at[i],width)],buf,r_.ld.at[0,0]); c.start(); c.wait()
        if i==0:
            small=jnp.dot(normed[...],r_.sbuf[...],preferred_element_type=f32)
            for sq in range(seqs):
                fl=flat_form(small[sq*ll:(sq+1)*ll,0:8*((2*heads+7)//8)])
                for h in range(heads):
                    base=(sq*heads+h)*8
                    rbuf[base:base+1]=fl[h:h+1]
                    rbuf[base+1:base+2]=fl[heads+h:heads+h+1]
            cq=wk//n; cv=wv//n; step=D//n
            for kind,(width_c,total,skip) in enumerate(((cq,DK,0),(cq,DK,cq),(cv,DV,2*cq))):
                for j in range(total//width_c):
                    dev=my_head*(total//width_c)+j
                    to=(0,DK,2*DK)[kind]+j*width_c
                    r_.tbuf[to:to+width_c]=r_.sbuf[pl.ds(pl.multiple_of(dev*step+skip,16),width_c),:]
            ident=jnp.where(lax.broadcasted_iota(jnp.int32,(CH,CH),0)==lax.broadcasted_iota(jnp.int32,(CH,CH),1),1.0,0.0).astype(bf16)
            tt=dg(r_.tbuf[...],ident,0,0)
            taps_ref[...]=tt[2*heads:2*heads+4]
        else:
            def column(j,i=i):
                pbuf[:,pl.ds(pl.multiple_of(at[i]+j*256,128),256)]=jnp.dot(normed[...],wbuf[0:D,pl.ds(pl.multiple_of(j*256,256),256)],preferred_element_type=f32).astype(bf16)
            loop(width//256,column)
        inward.start((3,0,1,2)[i])
    n1=SharedColumns(n,zc,normed,r_.n1c,(*qsems(),*zsems())); n1.start()
    zk.finish()
    cc=SharedColumns(n,zc,cotfull,r_.cotc,(*qsems(),*zsems())); cc.start()
    inward.finish()
    gb=[gather(r_.wg,r_.wgfull,0),gather(r_.wo,r_.wofull,1),gather(r_.wgate,gw_,0)]
    each(gb,"start")

    def turn(m):
        r=pl.ds(pl.multiple_of(m*8,8),8)
        x=position_rows(xr_ref[r,:],starts,m*ll,rate,bias)
        xr_ref[r,:]=x
        xc_ref[pl.ds(pl.multiple_of(m*ll,ll),ll),:]=col_form(x)
    loop(n,turn,4)
    taps=taps_ref[...]
    R=128
    def conv(c):
        base=pl.multiple_of(c*R,R)
        age=doc_age(starts,positions(base,R,128,0))[:,0:1]
        pre,unused=conv_pre(u_ref,taps,age,base,R)
        act=pre*sigmoid(pre)
        rows=pl.ds(base,R)
        aq=act[:,:DK]; ak=act[:,DK:2*DK]
        q_ref[rows,:]=(aq*lax.rsqrt(jnp.sum(aq*aq,axis=1,keepdims=True)+EPSILON)*DK**-0.5).astype(bf16)
        k_ref[rows,:]=(ak*lax.rsqrt(jnp.sum(ak*ak,axis=1,keepdims=True)+EPSILON)).astype(bf16)
        v_ref[rows,:]=act[:,2*DK:].astype(bf16)
    loop(L//R,conv)
    n1.middle(); cc.middle()
    kcol,pcol,ecol=pl.ds(0,DK),pl.ds(DK,SPAN),pl.ds(DK+SPAN,DK)
    def local(m):
        xr=xr_ref[pl.ds(pl.multiple_of(m*8,8),8),:]
        for e in range(per):
            b=m*per+e; rows=span(b)
            q=q_ref[rows,:]; k=k_ref[rows,:]; v=v_ref[rows,:]
            beta,Dm,gam,end,KK,QK,i,j=span_terms(b,q,k,starts,xc_ref[rows,:],xr[:,e*SPAN:(e+1)*SPAN])
            dx_ref[rows,0:SPAN]=jnp.where(i>j,beta[:,:SPAN]*Dm*KK,0.0)
            kf=k.astype(f32)
            dpre[rows,rest_v]=jnp.concatenate([beta]*(DV//128),axis=1)*v.astype(f32)
            du_ref[rows,kcol]=((beta*gam)*kf).astype(bf16)
            du_ref[rows,pcol]=(QK*Dm).astype(bf16)
            qt_ref[b,0:SPAN]=(gam*q.astype(f32)).astype(bf16)
            du_ref[rows,ecol]=(end*kf).astype(bf16)
            gc_ref[b]=jnp.broadcast_to(gam[SPAN-1:SPAN],(8,128))
    loop(n,local,4)
    inverses(lambda b: dx_ref[b*SPAN:(b+1)*SPAN,0:SPAN],t_ref)
    def solve(b):
        rows=span(b)
        T=t_ref[b].astype(bf16)
        U=dg(T,dpre[rows,rest_v].astype(bf16)); Wk=dg(T,du_ref[rows,kcol])
        Ub=U.astype(bf16); Wb=Wk.astype(bf16); Pm=du_ref[rows,pcol]; ek=du_ref[rows,ecol]
        dpre[rows,heads_v]=dg(Pm,Ub)
        w_ref[b]=U
        qt_ref[b,0:SPAN]=(qt_ref[b,0:SPAN].astype(f32)-dg(Pm,Wb)).astype(bf16)
        qt_ref[b,SPAN:]=Wb
        ds_ref[b]=dg(ek,Ub,0,0)
        mh_ref[b]=dg(ek,Wb,0,0).astype(bf16)
    loop(NC,solve,4)
    def chain(b,St):
        s_ref[b]=St
        sh,sl=halves(St); mh=mh_ref[b]
        return jnp.concatenate([gc_ref[b][0:1]]*(DV//128),axis=1)*St+ds_ref[b]-(dg(mh,sh)+dg(mh,sl))
    lax.fori_loop(0,NC,chain,jnp.zeros((DK,DV),f32),unroll=2)
    def emit(b):
        rows=span(b)
        x=dg(qt_ref[b],s_ref[b].astype(bf16))
        do_ref[rows,:]=(dpre[rows,heads_v]+x[:SPAN]).astype(bf16)
        w_ref[b]=w_ref[b]-x[SPAN:]
    loop(NC,emit,4)
    seq_rows=lambda t: pl.ds(pl.multiple_of(t*ll,ll),ll)
    outward=FromPairs(n,copies,heads,ll,[(do_ref,lambda t: (seq_rows(t),slice(None)),oall,lambda seq,head: (seq_rows(seq),pl.ds(pl.multiple_of(head*DV,128),DV)))],r_.osend,r_.orecv)
    outward.start()

    gb[0].middle(); gb[0].late(); gb[0].finish()
    c=pltpu.make_async_copy(r_.wgfull,wbuf.at[pl.ds(0,D),pl.ds(0,wv)],r_.ld.at[0,0]); c.start(); c.wait()
    def column(j):
        k_=pl.ds(pl.multiple_of(j*256,256),256)
        gate_ref[:,k_]=jnp.dot(normed[...],wbuf[0:D,k_],preferred_element_type=f32)
    loop(wv//256,column)
    gb[1].middle(); gb[1].late(); gb[1].finish()
    blocks=D//VW
    def load_wo(buf,sems):
        cs=[pltpu.make_async_copy(r_.wofull.at[:,pl.ds(j*VW,VW)],buf.at[pl.ds(j*VW,VW),pl.ds(0,VW)],sems.at[j]) for j in range(blocks)]
        for c in cs: c.start()
        return cs
    for c in load_wo(wbuf,r_.ld.at[0]): c.wait()
    outward.finish()
    def mix(c):
        r=pl.ds(pl.multiple_of(c*32,32),32)
        for h in range(heads):
            hc=pl.ds(h*DV,DV)
            o=oall[r,hc].astype(f32); g=gate_ref[r,hc]
            rho=lax.rsqrt(jnp.sum(o*o,axis=1,keepdims=True)/DV+EPSILON)
            branch[r,hc]=(o*rho*r_.hgain[...]*(g*sigmoid(g))).astype(bf16)
    loop(RN//32,mix)
    inner_tiles=VW//256
    def column(j):
        blk=lax.div(j,inner_tiles); at_=lax.rem(j,inner_tiles)
        w=wbuf[pl.ds(pl.multiple_of(blk*VW,16),VW),pl.ds(pl.multiple_of(at_*256,256),256)]
        pbf[:,pl.ds(pl.multiple_of(j*256,256),256)]=jnp.dot(branch[...],w,preferred_element_type=f32).astype(bf16)
    loop(D//256,column)
    split=ShardSplit(zc,pbf,r_.box,*zsems()); split.start()
    for d in range(1,n): pl.semaphore_signal(r_.free,inc=1,device_id={"seq":lax.rem(s+d,n)},device_id_type=MESH)
    pl.semaphore_wait(r_.free,n-1)
    gu=[gather(r_.wup,uw_,0),gather(r_.wdown,dw_,1)]
    each(gu,"start")
    gb[2].middle()

    F_at=pl.ds(pl.multiple_of(z*F,128),F)
    fgain=r_.fgain[:,F_at]
    sums=r_.sums
    def shard_sum(k,rows8,meanwhile=None):
        sums[k*zc+z]=rows8
        tot=ShardAll("shard",zc,sums.at[pl.ds(k*zc,zc)],*zsems()); tot.start()
        if meanwhile: meanwhile()
        tot.finish()
        t=sums[k*zc]
        for d in range(1,zc): t=t+sums[k*zc+d]
        return col_form(t)[:,0:1]/D
    def boxed(box):
        g=box[0].astype(f32)
        for d in range(1,zc): g=g+box[d].astype(f32)
        return g
    res,gres,nloc,nfull,afull=r_.res,r_.gres,r_.nloc,r_.nfull,r_.normed
    split.finish()
    x=tok[...].astype(f32)+boxed(r_.box)
    res[...]=x
    sc=lax.rsqrt(shard_sum(0,row_form(x*x))+EPSILON)
    nloc[...]=(res[...]*sc*fgain).astype(bf16)
    zg=ShardGather(zc,nloc,nfull,*zsems()); zg.start()
    gb[2].late(); each(gu,"middle"); gb[2].finish()
    zg.finish()
    n2=ColumnSplit(n,nfull,r_.n2c,*qsems()); n2.start()
    for a,b in tiles(FF,512): gv[:,a:b]=jnp.dot(nfull[...],gw_[:,a:b],preferred_element_type=f32)
    gu[0].late(); gu[0].finish()
    for a,b in tiles(FF,512): uv[:,a:b]=jnp.dot(nfull[...],uw_[:,a:b],preferred_element_type=f32)
    hidden,dgate,dup=r_.hidden,r_.dgate,r_.dup
    def act(c):
        rr=pl.ds(pl.multiple_of(c*32,32),32)
        g=gv[rr,:]
        hidden[rr,:]=(g*sigmoid(g)*uv[rr,:]).astype(bf16)
    loop(RN//32,act)
    gh=[gather(hidden,r_.hidfull,0),gather(dgate,r_.dgfull,0),gather(dup,r_.dufull,0)]
    gu[1].late(); gu[1].finish()
    for a,b in tiles(FF,512):
        dh=dg(cotfull[...],dw_[a:b,:],1,1)
        g=gv[:,a:b]; sg=sigmoid(g)
        dgate[:,a:b]=(dh*uv[:,a:b]*sg*(1.0+g*(1.0-sg))).astype(bf16)
        dup[:,a:b]=(dh*(g*sg)).astype(bf16)
    each(gh[1:]+gh[:1],"start")
    def back_two(j):
        rr=pl.ds(pl.multiple_of(j*256,256),256)
        pbf[:,rr]=(dg(dgate[...],gw_[rr,:],1,1)+dg(dup[...],uw_[rr,:],1,1)).astype(bf16)
    loop(D//256,back_two)
    split=ShardSplit(zc,pbf,r_.box,*zsems()); split.start()
    ld=r_.ld
    bufs=(r_.bufa,r_.bufb)
    loads={}
    def load_job(key,i,pieces):
        loads[key]=[]
        for j,(src,to) in enumerate(pieces):
            c=pltpu.make_async_copy(src,bufs[i].at[to],ld.at[i,j]); c.start(); loads[key].append(c)
    def ready(key):
        for c in loads[key]: c.wait()
    whole=lambda w: (pl.ds(0,D),pl.ds(0,w))
    every=lambda w: (pl.ds(0,N),pl.ds(0,w))
    loads["wo"]=load_wo(r_.bufa,ld.at[0])
    load_job("og",1,[(r_.wgfull,whole(wv))])
    def outp(j):
        c_=pl.ds(pl.multiple_of(j*256,256),256)
        r_.outpart[:,c_]=jnp.dot(hidden[...],dw_[:,c_],preferred_element_type=f32).astype(bf16)
    loop(D//256,outp)
    split.finish()
    g=boxed(r_.box)
    gained=fgain*g
    gffn=[None]
    def meanwhile(): gffn[0]=jnp.sum(g*res[...]*sc,axis=0,keepdims=True)
    inner=shard_sum(1,row_form(gained*res[...]),meanwhile)
    gr=cot[...].astype(f32)+sc*(gained-res[...]*(sc*sc*inner))
    gres[...]=gr
    nloc[...]=gr.astype(bf16)
    zg=ShardGather(zc,nloc,afull,*zsems()); zg.start()
    each(gh[1:]+gh[:1],"middle")
    zg.finish()
    so=ShardSplit(zc,r_.outpart,r_.boxo,*zsems()); so.start()

    ready("wo")
    r_.dsm[...]=jnp.zeros(r_.dsm.shape,bf16)
    dob,dgp,bufa,bufb=r_.dob,r_.dgp,r_.bufa,r_.bufb
    def heads_back(c,gh_):
        r=pl.ds(pl.multiple_of(c*64,64),64)
        for h in range(heads):
            hc=pl.ds(h*DV,DV)
            dm=dg(afull[r,0:VW],bufa[h*DV:(h+1)*DV,0:VW],1,1)
            for j in range(1,blocks):
                dm=dm+dg(afull[r,j*VW:(j+1)*VW],bufa[j*VW+h*DV:j*VW+(h+1)*DV,0:VW],1,1)
            dm=dm.astype(bf16).astype(f32)
            o=oall[r,hc].astype(f32); g=gate_ref[r,hc]
            rho=lax.rsqrt(jnp.sum(o*o,axis=1,keepdims=True)/DV+EPSILON)
            zz=o*rho; sg=sigmoid(g); sil=g*sg
            gh_=gh_+jnp.sum(dm*zz*sil,axis=0,keepdims=True)
            dmg=dm*r_.hgain[...]
            dz=dmg*sil
            dob[r,hc]=(rho*(dz-zz*(jnp.sum(dz*zz,axis=1,keepdims=True)/DV))).astype(bf16)
            dgp[r,hc]=(dmg*zz*sg*(1.0+g*(1.0-sg))).astype(bf16)
        return gh_
    grad_head=lax.fori_loop(0,RN//64,heads_back,jnp.zeros((1,DV),f32))
    inward=ToPairs(n,copies,heads,ll,dob,None,do_ref,None,DK,DV,r_.i2send,r_.i2recv); inward.start(0)
    each(gh[1:]+gh[:1],"late")
    n2.finish()
    gk=[gather(dgp,r_.dgpfull,0),gather(branch,r_.brafull,0)]
    inward.finish()
    ca=SharedColumns(n,zc,afull,r_.attc,(*qsems(),*zsems())); ca.start()
    each(gk,"start")

    dpre[L:L+8]=jnp.zeros((8,CH),f32)
    def early(b):
        ds_ref[b]=dg(qt_ref[b][0:SPAN],do_ref[span(b),:],0,0)
    loop(NC,early,4)
    def chain_back(m,dS):
        b=NC-1-m
        x=ds_ref[b]
        ds_ref[b]=dS
        sh,sl=halves(dS); mh=mh_ref[b]
        return jnp.concatenate([gc_ref[b][0:1]]*(DV//128),axis=1)*dS+x-(dg(mh,sh,0,0)+dg(mh,sl,0,0))
    lax.fori_loop(0,NC,chain_back,jnp.zeros((DK,DV),f32),unroll=2)
    def one_span(b,xr):
        rows=span(b)
        q=q_ref[rows,:]; k=k_ref[rows,:]; v=v_ref[rows,:]; dO=do_ref[rows,:]
        beta,Dm,gam,end,KK,QK,i,j=span_terms(b,q,k,starts,xc_ref[rows,:],xr)
        beta2=jnp.concatenate([beta]*(DV//128),axis=1)
        S0=s_ref[b]; dS1=ds_ref[b]
        S0h=S0.astype(bf16); dSh=dS1.astype(bf16)
        kf=k.astype(f32); qf=q.astype(f32); vf=v.astype(f32)
        W=w_ref[b].astype(bf16); T=t_ref[b].astype(bf16)
        Pm=(QK*Dm).astype(bf16)
        dW=dg(Pm,dO,0,0)+jnp.concatenate([end]*(DV//128),axis=1)*dg(k,dSh)
        Y=dg(T,dW.astype(bf16),0,0)
        dOY=jnp.concatenate([dO,Y.astype(bf16)],axis=0)
        dPA=dg(dOY,W,1,1)
        GS=dg(dOY,S0h,1,1)
        dOS=GS[:SPAN]; YS=GS[SPAN:]
        Z=dg(W,dSh,1,1)
        dPD=dPA[:SPAN]*Dm
        EA=jnp.where(i>j,-dPA[SPAN:]*Dm,0.0)
        A1=jnp.concatenate([dPD,beta[:,:SPAN]*EA],axis=0).astype(bf16)
        r1=dg(A1,k)
        r2=dg(A1,jnp.concatenate([q,k],axis=0),0,0)
        dpre[rows,0:DK]=gam*dOS+r1[:SPAN]
        dpre[rows,DK:2*DK]=r1[SPAN:]+r2-(beta*gam)*YS+end*Z
        dpre[rows,2*DK:]=beta2*Y
        EK=EA*KK
        kYS=jnp.sum(kf*YS,axis=1,keepdims=True)
        dbeta=jnp.sum(Y*vf,axis=1,keepdims=True)-gam*kYS+jnp.sum(EK,axis=1,keepdims=True)
        Fm=dPD*QK+beta[:,:SPAN]*EK
        dgam=jnp.sum(qf*dOS,axis=1,keepdims=True)-beta*kYS
        dend=jnp.sum(kf*Z,axis=1,keepdims=True)*end
        dG=jnp.sum(Fm,axis=1,keepdims=True)+dgam*gam-dend
        tail=jnp.sum(jnp.sum(S0*dS1,axis=0,keepdims=True),axis=1,keepdims=True)
        last=jnp.sum(dend,axis=0,keepdims=True)+gam[SPAN-1:SPAN]*tail
        row=lax.broadcasted_iota(jnp.int32,(SPAN,128),0)
        dG=dG+jnp.where(row==SPAN-1,last,0.0)
        dx_ref[rows,0:1]=(dbeta*beta*(1.0-beta))[:,0:1]
        dx_ref[rows,1:2]=dG[:,0:1]
        return jnp.sum(Fm,axis=0,keepdims=True)
    def local_back(m):
        r=pl.ds(pl.multiple_of(m*8,8),8)
        xr=xr_ref[r,:]
        dxr[r,:]=jnp.broadcast_to(jnp.concatenate([one_span(m*per+e,xr[:,e*SPAN:(e+1)*SPAN]) for e in range(per)],axis=1),(8,ll))
    loop(n,local_back,2)
    ca.middle()
    il=lax.broadcasted_iota(jnp.int32,(ll,ll),0); jl=lax.broadcasted_iota(jnp.int32,(ll,ll),1)
    later=jnp.where((il>=jl)&((il//SPAN)==(jl//SPAN)),1.0,0.0)
    def turn_back(m,carry):
        r=pl.ds(pl.multiple_of(m*8,8),8)
        f=flat_form(dx_ref[pl.ds(pl.multiple_of(m*ll,ll),ll),0:8])
        dlog=mmx(jnp.broadcast_to(f[1:2]-dxr[r,:][0:1],(8,ll)),later)
        x=xr_ref[r,:]
        ddp=dlog*(-rate)*sigmoid(x[3:4]+bias)
        row=lax.broadcasted_iota(jnp.int32,(8,ll),0)
        dxr[r,:]=jnp.where(row==0,f[0:1],jnp.where(row==1,ddp,0.0))
        return (carry[0]+jnp.sum(dlog[0:1]*x[1:2],axis=1,keepdims=True),carry[1]+jnp.sum(ddp[0:1],axis=1,keepdims=True))
    zero=jnp.zeros((1,1),f32)
    sl,sb=lax.fori_loop(0,n,turn_back,(zero,zero),unroll=4)
    def norms(c,dt):
        base=pl.multiple_of(c*R,R)
        age=doc_age(starts,positions(base,R,128,0))[:,0:1]
        pre,window=conv_pre(u_ref,taps,age,base,R)
        sg=sigmoid(pre); a_=pre*sg
        rows=pl.ds(base,R)
        d=dpre[rows,:]
        def unit_back(a,dd,f):
            sc_=lax.rsqrt(jnp.sum(a*a,axis=1,keepdims=True)+EPSILON)
            dot=jnp.sum(a*dd,axis=1,keepdims=True)
            return f*(sc_*dd-a*(sc_*sc_*sc_*dot))
        dact=jnp.concatenate([unit_back(a_[:,:DK],d[:,:DK],DK**-0.5),unit_back(a_[:,DK:2*DK],d[:,DK:2*DK],1.0),d[:,2*DK:]],axis=1)
        dp=dact*sg*(1.0+pre*(1.0-sg))
        dpre[rows,:]=dp
        new=[]
        for j in range(4):
            back=3-j
            x=window[16-back:16-back+R]
            if back: x=x*jnp.where(age>=back,1.0,0.0)
            new.append(dt[j]+jnp.sum(x*dp,axis=0,keepdims=True))
        return tuple(new)
    dt=lax.fori_loop(0,L//R,norms,(jnp.zeros((1,CH),f32),)*4)
    def back(c):
        base=pl.multiple_of(c*R,R)
        window=dpre[pl.ds(base,R+8),:]
        age=doc_age(starts,positions(base,R+8,128,0))[:,0:1]
        d=window[:R]*taps[3:4]
        for sh in range(1,4):
            d=d+window[sh:sh+R]*jnp.where(age[sh:sh+R]>=sh,1.0,0.0)*taps[3-sh:4-sh]
        du_ref[pl.ds(base,R),:]=d.astype(bf16)
    loop(L//R,back)
    dyq,dsm=pbuf,r_.dsm
    cut=lambda start,width: (lambda t: (seq_rows(t),pl.ds(start,width)))
    to=lambda start,width: (lambda seq,head: (seq_rows(seq),pl.ds(pl.multiple_of(start+head*width,128),width)))
    outward=FromPairs(n,copies,heads,ll,[(du_ref,cut(0,DK),dyq,to(0,DK)),(du_ref,cut(DK,DK),dyq,to(wk,DK)),(du_ref,cut(2*DK,DV),dyq,to(2*wk,DV)),
        (dxr,lambda t: (pl.ds(pl.multiple_of(t*8,8),8),slice(None)),rbuf,lambda seq,head: (pl.ds(pl.multiple_of((seq*heads+head)*8,8),8),slice(None)))],r_.o2send,r_.o2recv)
    outward.start()

    part=r_.acc
    def spread(first,buf,terms):
        def one(j):
            rr=pl.ds(pl.multiple_of(j*256,256),256)
            t=0.0
            for x,a,b in terms: t=t+dg(x[...],buf[rr,a:b],1,1)
            part[:,rr]=t if first else part[:,rr]+t
        loop(D//256,one)
    staged={}
    def stage(k,ref,shape):
        if k in staged: staged[k].wait()
        return r_.sta.at[pl.ds(0,shape[0]),pl.ds(0,shape[1])] if k==0 else r_.stb.at[pl.ds(0,shape[0]),pl.ds(0,shape[1])]
    def send(k,view,ref):
        staged[k]=pltpu.make_async_copy(view,ref,r_.stsem.at[k]); staged[k].start()
    ready("og"); spread(True,bufb,[(dgp,0,wv)])
    each(gh,"finish")
    load_job("dgate",0,[(r_.dgfull,every(FF))])
    c2=pltpu.make_async_copy(r_.n2c,r_.cola,ld.at[0,4]); c2.start()
    load_job("wqk",1,[(r_.wfull.at[:,pl.ds(0,2*wk)],whole(2*wk))])
    so.finish()
    r_.output[...]=res[...]+boxed(r_.boxo)
    ready("dgate"); c2.wait()
    v_=stage(0,r_.ogate,(D//n,FF))
    for a,b in tiles(FF,512): v_[:,a:b]=dg(r_.cola[...],bufa[0:N,a:b],0,0)
    send(0,v_,r_.ogate)
    load_job("wv",0,[(r_.wfull.at[:,pl.ds(2*wk,wv+128)],whole(wv+128))])
    outward.finish()
    for sq in range(seqs):
        fl=[]
        for e in range(2):
            for h in range(heads): fl.append(rbuf[(sq*heads+h)*8+e:(sq*heads+h)*8+e+1])
        fl=jnp.concatenate(fl+[jnp.zeros((-2*heads%8,ll),f32)]*(1 if 2*heads%8 else 0),axis=0)
        dsm[sq*ll:(sq+1)*ll,0:fl.shape[0]]=col_form(fl).astype(bf16)
    gd=[gather(dsm,r_.dsmfull,0),gather(dyq,r_.dyqfull,0)]
    each(gd,"start")
    ready("wqk"); spread(False,bufb,[(dyq.at[:,pl.ds(0,2*wk)],0,2*wk)])
    load_job("dup",1,[(r_.dufull,every(FF))])
    ready("wv")
    def final(j):
        rr=pl.ds(pl.multiple_of(j*256,256),256)
        pbf[:,rr]=(part[:,rr]+dg(dyq[:,2*wk:],bufa[rr,0:wv],1,1)+dg(dsm[...],bufa[rr,wv:wv+128],1,1)).astype(bf16)
    loop(D//256,final)
    split=ShardSplit(zc,pbf,r_.box,*zsems()); split.start()
    load_job("hid",0,[(r_.hidfull,every(FF))])
    each(gk,"middle"); each(gk,"late")
    ready("dup")
    v_=stage(0,r_.oup,(D//n,FF))
    for a,b in tiles(FF,512): v_[:,a:b]=dg(r_.cola[...],bufb[0:N,a:b],0,0)
    send(0,v_,r_.oup)
    n1.finish(); cc.finish(); ca.finish()
    for g in gk: g.finish()
    cb=pltpu.make_async_copy(r_.cotc,r_.colb,ld.at[1,5]); cb.start()
    load_job("bra",1,[(r_.brafull,every(VW))])
    ready("hid"); cb.wait()
    cots=r_.colb[...].reshape(N,D//n)
    v_=stage(1,r_.odown,(FF,D//n))
    for a,b in tiles(FF,256): v_[a:b,:]=dg(bufa[0:N,a:b],cots,0,0)
    send(1,v_,r_.odown)
    load_job("dgp",0,[(r_.dgpfull,every(wv))])
    split.finish()
    g=boxed(r_.box)
    sc=scale[...][:,0:1]
    gained=r_.gain[:,F_at]*g
    smalls,totals=r_.smalls,r_.totals
    smalls[s]=jnp.zeros(smalls.shape[1:],f32)
    smalls[s,0:1,0:F]=jnp.sum(g*tok[...].astype(f32)*sc,axis=0,keepdims=True)
    smalls[s,1:2,0:F]=gffn[0]
    smalls[s,2:3,0:DV]=grad_head
    lane=lax.broadcasted_iota(jnp.int32,(1,128),1)
    first=jnp.where(lax.rem(s,copies)==0,1.0,0.0)
    smalls[s,3:4,0:128]=first*(jnp.where(lane==at_head,sl,0.0)+jnp.where(lane==H+at_head,sb,0.0))
    for j in range(4): smalls[s,4+j:5+j,0:CH]=dt[j]
    sa=ShardAll("seq",n,smalls,*qsems()); sa.start()
    inner=shard_sum(2,row_form(gained*tok[...].astype(f32)))
    r_.gtok[...]=gres[...]+sc*(gained-tok[...].astype(f32)*(sc*sc*inner))
    each(gd,"middle")
    sa.finish()
    t=smalls[0]
    for d in range(1,n): t=t+smalls[d]
    totals[z]=t
    za=ShardAll("shard",zc,totals,*zsems()); za.start()
    cb=pltpu.make_async_copy(r_.attc,r_.colb,ld.at[1,5]); cb.start()
    ready("bra"); cb.wait()
    atts=r_.colb[...].reshape(N,D//n)
    v_=stage(1,r_.oout,(VW,D//n))
    for a,b in tiles(VW,256): v_[a:b,:]=dg(bufb[0:N,a:b],atts,0,0)
    send(1,v_,r_.oout)
    cb=pltpu.make_async_copy(r_.n1c,r_.colb,ld.at[1,5]); cb.start()
    ready("dgp"); cb.wait()
    n1s=r_.colb[...].reshape(N,D//n)
    v_=stage(0,r_.oog,(D//n,wv))
    for a,b in tiles(wv,512): v_[:,a:b]=dg(n1s,bufa[0:N,a:b],0,0)
    send(0,v_,r_.oog)
    each(gd,"late"); za.finish(); each(gd,"finish")
    staged[0].wait(); staged[1].wait()

def layer(n,zc,copies,heads,DK,DV,H,ins):
    names=("tok","cot","gain","hgain","fgain","starts","dlog","dbias","wb","wd","qc","kc","vc","wq","wk","wv","wg","wo","wgate","wup","wdown")
    RN,F=ins[0].shape; D=F*zc; seqs=ins[5].shape[0]; ll=RN//seqs; L=n*ll; NC=L//SPAN; pairs=n//copies
    wk=heads*DK; wv=heads*DV; CH=2*DK+DV; FF=ins[19].shape[1]; N=n*RN; Dc=D//n; W=max(F,CH)
    bw=max(FF,wv+128,2*wk); big=max(D,N)
    specs=[VM]*5+[SM]*3+[VM]*10+[ANY]*3
    outs=[("output",S((RN,F)),VM),("gtok",S((RN,F)),VM),("smalls",S((n,8,W)),VM),("totals",S((zc,8,W)),VM)]
    for name,shape in (("ogate",(Dc,FF)),("oup",(Dc,FF)),("odown",(FF,Dc)),("oout",(wv,Dc)),("oog",(Dc,wv))): outs.append((name,S(shape),ANY))
    for name,shape in (("dyqfull",(N,heads*CH)),("dsmfull",(N,128)),("n1c",(n,RN,Dc)),("cotc",(n,RN,Dc)),("attc",(n,RN,Dc)),("n2c",(N,Dc)),("wfull",(D,heads*CH+128)),("wgfull",(D,wv)),("wofull",(wv,D)),
        ("hidfull",(N,FF)),("dgfull",(N,FF)),("dufull",(N,FF)),("dgpfull",(N,wv)),("brafull",(N,wv))): outs.append((name,S(shape,bf16),ANY))
    V=pltpu.VMEM; sem=pltpu.SemaphoreType.DMA
    scratch=[("scale",V((RN,128),f32)),("ws",V((Dc,128),bf16)),("sbuf",V((D,128),bf16)),("tbuf",V((CH,128),bf16)),("tokfull",V((RN,D),bf16)),("normed",V((RN,D),bf16)),("cotfull",V((RN,D),bf16)),
        ("nfull",V((RN,D),bf16)),("pbf",V((RN,D),bf16)),("outpart",V((RN,D),bf16)),("acc",V((RN,D),f32)),("uv",V((RN,FF),f32)),("gv",V((RN,FF),f32)),("rbuf",V((pairs*8,ll),f32)),("taps",V((4,CH),f32)),
        ("bufa",V((big,bw),bf16)),("bufb",V((big,bw),bf16)),("dw",V((FF,D),bf16)),("u",V((L+16,CH),bf16)),("xr",V((n*8,ll),f32)),("xc",V((L,8),f32)),("q",V((L,DK),bf16)),("k",V((L,DK),bf16)),("v",V((L,DV),bf16)),
        ("s",V((NC,DK,DV),f32)),("w",V((NC,SPAN,DV),f32)),("t",V((NC,SPAN,SPAN),f32)),("qt",V((NC,2*SPAN,DK),bf16)),("mh",V((NC,DK,DK),bf16)),("gc",V((NC,8,128),f32)),("ds",V((NC,DK,DV),f32)),
        ("dpre",V((L+8,CH),f32)),("du",V((L,CH),bf16)),("dx",V((L,SPAN),f32)),("do",V((L,DV),bf16)),("dxr",V((n*8,ll),f32)),("gate",V((RN,wv),f32)),("oall",V((RN,wv),bf16)),("branch",V((RN,wv),bf16)),
        ("dob",V((RN,wv),bf16)),("dgp",V((RN,wv),bf16)),("dsm",V((RN,128),bf16)),("res",V((RN,F),f32)),("gres",V((RN,F),f32)),("nloc",V((RN,F),bf16)),("box",V((zc,RN,F),bf16)),("boxo",V((zc,RN,F),bf16)),
        ("hidden",V((RN,FF),bf16)),("dgate",V((RN,FF),bf16)),("dup",V((RN,FF),bf16)),("sums",V((3*zc,8,RN),f32)),("cola",V((N,Dc),bf16)),("colb",V((n,RN,Dc),bf16)),("sta",V((Dc,max(FF,wv)),f32)),("stb",V((max(FF,wv),Dc),f32)),
        ("zsend",sem((16,zc))),("zrecv",sem((16,zc))),("qsend",sem((6,n))),("qrecv",sem((6,n))),("gsend",sem((16,links(n)))),("grecv",sem((16,links(n)))),("gloc",sem((16,))),("isend",sem((4,n))),("irecv",sem((4,n))),("i2send",sem((1,n))),("i2recv",sem((1,n))),
        ("osend",sem((1,pairs))),("orecv",sem((1,pairs))),("o2send",sem((4,pairs))),("o2recv",sem((4,pairs))),("ld",sem((2,6))),("stsem",sem((2,))),("free",pltpu.SemaphoreType.REGULAR)]
    all_names=names+tuple(o[0] for o in outs)+tuple(x[0] for x in scratch)
    r=pl.pallas_call(functools.partial(layer_kernel,(n,zc,copies,heads,DK,DV,H),all_names),name="layer",out_shape=tuple(o[1] for o in outs),in_specs=specs,out_specs=tuple(o[2] for o in outs),
        scratch_shapes=[x[1] for x in scratch],compiler_params=pltpu.CompilerParams(collective_id=1,has_side_effects=True,vmem_limit_bytes=63*2**20))(*ins)
    return SimpleNamespace(**{o[0]:x for o,x in zip(outs,r)})


def last_kernel(n,copies,heads,DK,DV,F,H,n1c,dyq,dsm,smalls,totals,*refs):
    moved=refs[:7]; oq,ok,ov,ob,od,qc,kc,vc,onorm,offn,ohead,olog,obias=refs[7:20]; moved_out=refs[20:27]; buf,sem,msem=refs[27:30]; held=refs[30:]
    step=buf.shape[1]//4
    jobs=[pltpu.make_async_copy(dyq.at[:,pl.ds(j*step,step)],buf.at[:,pl.ds(j*step,step)],sem.at[j]) for j in range(4)]
    for c in jobs: c.start()
    fetch=[pltpu.make_async_copy(a,b,msem.at[j]) for j,(a,b) in enumerate(zip(moved,held))]
    for c in fetch: c.start()
    n1=n1c[...].reshape(n1c.shape[0]*n1c.shape[1],n1c.shape[2])
    sm=dg(dsm[...],n1,0,0)
    ob[...]=sm[0:heads]; od[...]=sm[heads:2*heads]
    wk=heads*DK
    got=0
    for ref,start in ((oq,0),(ok,wk),(ov,2*wk)):
        for a in range(0,ref.shape[1],256):
            b=min(a+256,ref.shape[1])
            while got*step<start+b: jobs[got].wait(); got+=1
            ref[:,a:b]=dg(n1,buf[:,start+a:start+b],0,0)
    moves=[pltpu.make_async_copy(a,b,msem.at[j]) for j,(a,b) in enumerate(zip(held,moved_out))]
    for f,c in zip(fetch,moves): f.wait(); c.start()
    zc=totals.shape[0]
    for z in range(zc):
        onorm[0:1,z*F:(z+1)*F]=totals[z,0:1,0:F]
        offn[0:1,z*F:(z+1)*F]=totals[z,1:2,0:F]
    t=totals[0]
    for z in range(1,zc): t=t+totals[z]
    ohead[...]=t[2:3,0:DV]
    olog[...]=t[3:4,0:H]; obias[...]=t[3:4,H:2*H]
    s=lax.axis_index("seq")
    head=lax.div(s*heads,n)
    taps=0.0
    for sq in range(n//copies//heads): taps=taps+smalls[(sq*heads+head)*copies]
    cq,cv=qc.shape[1],vc.shape[1]
    for part in range(n//heads):
        @pl.when(lax.rem(s,n//heads)==part)
        def _():
            qc[...]=taps[4:8,part*cq:(part+1)*cq]
            kc[...]=taps[4:8,DK+part*cq:DK+(part+1)*cq]
            vc[...]=taps[4:8,2*DK+part*cv:2*DK+(part+1)*cv]
    for c in moves: c.wait()
def last(n,copies,heads,DK,DV,F,H,n1c,dyq,dsm,smalls,totals,cq,cv,moved):
    D=F*totals.shape[0]; Dc=n1c.shape[2]
    r=pl.pallas_call(functools.partial(last_kernel,n,copies,heads,DK,DV,F,H),name="last",
      out_shape=(S((Dc,heads*DK)),S((Dc,heads*DK)),S((Dc,heads*DV)),S((heads,Dc)),S((heads,Dc)),S((4,cq)),S((4,cq)),S((4,cv)),S((1,D)),S((1,D)),S((1,DV)),S((1,H)),S((1,H)))+tuple(S(x.shape) for x in moved),
      in_specs=[VM,ANY,VM,VM,VM]+[ANY]*7,out_specs=(VM,)*13+(ANY,)*7,scratch_shapes=[pltpu.VMEM(dyq.shape,bf16),pltpu.SemaphoreType.DMA((4,)),pltpu.SemaphoreType.DMA((7,))]+[pltpu.VMEM(x.shape,f32) for x in moved],
      compiler_params=pltpu.CompilerParams(vmem_limit_bytes=56*2**20))(n1c,dyq,dsm,smalls,totals,*moved)
    return r


def per_device(
    tokens, doc_starts, norm_gain, query_weight, key_weight, value_weight, outgate_weight,
    beta_weight, decay_weight, query_conv, key_conv, value_conv, decay_log, decay_bias, head_gain,
    output_weight, ffn_gain, gate_weight, up_weight, down_weight, cotangent,
):
    seq_count, local_len, feature_part = tokens.shape
    row_count = seq_count * local_len
    shard_count = lax.axis_size("shard")
    seq_devices = lax.axis_size("seq")
    head_count = beta_weight.shape[1]
    key_dim = query_weight.shape[1] // head_count
    value_dim = value_weight.shape[1] // head_count
    pairs = seq_count * head_count
    copies = seq_devices // pairs
    flat = lambda x: x.reshape(row_count, x.shape[2])
    tokens_flat, cot_flat = flat(tokens), flat(cotangent)
    head_row, norm_row, ffn_row = head_gain[None], norm_gain[None], ffn_gain[None]
    ran = layer(
        seq_devices, shard_count, copies, head_count, key_dim, value_dim, decay_log.shape[0],
        (
            tokens_flat, cot_flat, norm_row, head_row, ffn_row, doc_starts, decay_log, decay_bias, beta_weight.T,
            decay_weight.T, query_conv.T, key_conv.T, value_conv.T, query_weight, key_weight, value_weight, outgate_weight,
            output_weight, gate_weight, up_weight, down_weight,
        ),
    )
    (
        out_query, out_key, out_value, out_beta, out_decay, out_qconv, out_kconv, out_vconv, out_norm, out_ffn, out_head,
        out_log, out_bias, output, grad_tokens, out_gate, out_up, out_down, out_output, out_outgate,
    ) = last(
        seq_devices, copies, head_count, key_dim, value_dim, feature_part, decay_log.shape[0], ran.n1c, ran.dyqfull,
        ran.dsmfull, ran.smalls, ran.totals, query_conv.shape[0], value_conv.shape[0],
        (ran.output, ran.gtok, ran.ogate, ran.oup, ran.odown, ran.oout, ran.oog),
    )
    shape3 = (seq_count, local_len, feature_part)
    return (
        output.reshape(shape3), grad_tokens.reshape(shape3), out_norm[0], out_query, out_key, out_value, out_outgate,
        out_beta.T, out_decay.T, out_qconv.T, out_kconv.T, out_vconv.T, out_log[0], out_bias[0], out_head[0], out_output,
        out_ffn[0], out_gate, out_up, out_down,
    )


def solution(mesh):
    P = PartitionSpec
    rows, cols = P("seq", "shard"), P("shard", "seq")
    both, acts = P(("shard", "seq"), None), P(None, "seq", "shard")
    return jax.shard_map(
        per_device,
        mesh=mesh,
        in_specs=(acts, P(), P()) + (rows,) * 6 + (both,) * 3 + (P(), P(), P(), cols, P(), rows, rows, cols, acts),
        out_specs=(acts, acts, P()) + (rows,) * 6 + (both,) * 3 + (P(), P(), P(), cols, P(), rows, rows, cols),
        check_vma=False,
    )
```

```python
import functools
from types import SimpleNamespace
import jax, jax.numpy as jnp
from jax import lax
from jax.experimental import pallas as pl
from jax.experimental.pallas import tpu as pltpu
from jax.sharding import PartitionSpec
f32=jnp.float32; bf16=jnp.bfloat16
SPAN=128
EPSILON=1e-6
HI=lax.Precision.HIGHEST

def dg(a,b,ca=1,cb=0):
    return lax.dot_general(a,b,(((ca,),(cb,)),((),())),preferred_element_type=f32)
def halves(x):
    h=x.astype(bf16)
    return h,(x-h.astype(f32)).astype(bf16)
def mm3(a,b,ca=1,cb=0):
    ah,al=halves(a); bh,bl=halves(b)
    return dg(ah,bh,ca,cb)+(dg(al,bh,ca,cb)+dg(ah,bl,ca,cb))
def mm1(a,b,ca=1,cb=0):
    return dg(a.astype(bf16),b.astype(bf16),ca,cb)
def mmx(a,b,ca=1,cb=0):
    return lax.dot_general(a,b,(((ca,),(cb,)),((),())),preferred_element_type=f32,precision=HI)

def square_masks():
    i=lax.broadcasted_iota(jnp.int32,(SPAN,SPAN),0); j=lax.broadcasted_iota(jnp.int32,(SPAN,SPAN),1)
    return i,j
def positions(base,rows,cols,axis):
    return base+lax.broadcasted_iota(jnp.int32,(rows,cols),axis)
class Row:
    def __init__(self,ref,row):
        self.ref=ref; self.row=row; self.shape=ref.shape[1:]
    def __getitem__(self,e):
        return self.ref[self.row,e]

def doc_count(starts,pos):
    n=jnp.zeros(pos.shape,jnp.int32)
    for e in range(starts.shape[0]):
        n=n+jnp.where(starts[e]<=pos,1,0)
    return n
def doc_age(starts,pos):
    s=jnp.zeros(pos.shape,jnp.int32)
    for e in range(starts.shape[0]):
        s=jnp.where(starts[e]<=pos,starts[e],s)
    return pos-s
def count_at(starts,p):
    n=jnp.int32(0)
    for e in range(starts.shape[0]):
        n=n+jnp.where(starts[e]<=p,1,0)
    return n
def sigmoid(x):
    return 1.0/(1.0+jnp.exp(-x))
def softplus(x):
    return jnp.maximum(x,0.0)+jnp.log(1.0+jnp.exp(-jnp.abs(x)))

def inverses(blocks_a,t_ref):
    i,j=square_masks()
    eye=jnp.where(i==j,1.0,0.0)
    blocks=range(t_ref.shape[0])
    for n in blocks: t_ref[n]=eye-jnp.where((i//2)==(j//2),blocks_a(n),0.0)
    size=2
    while size<SPAN:
        part=((i//(2*size))==(j//(2*size)))&((i//size)!=(j//size))
        x=[dg(jnp.where(part,blocks_a(n),0.0).astype(bf16),t_ref[n].astype(bf16)).astype(bf16) for n in blocks]
        for n in blocks: t_ref[n]=t_ref[n]-dg(t_ref[n].astype(bf16),x[n])
        size*=2
    for n in blocks:
        Tb=t_ref[n].astype(bf16); Ah,Al=halves(blocks_a(n))
        rest=eye-Tb.astype(f32)-(dg(Ah,Tb)+dg(Al,Tb))
        t_ref[n]=Tb.astype(f32)+dg(Tb,rest.astype(bf16))

def position_rows(raw,starts,base,rate,bias):
    r=raw.shape[1]
    row=lax.broadcasted_iota(jnp.int32,(8,r),0)
    g=-rate*softplus(raw[1:2]+bias)
    i=lax.broadcasted_iota(jnp.int32,(r,r),0); j=lax.broadcasted_iota(jnp.int32,(r,r),1)
    G=mmx(jnp.broadcast_to(g,(8,r)),jnp.where((i<=j)&((i//SPAN)==(j//SPAN)),1.0,0.0))
    docs=doc_count(starts,positions(base,8,r,1)).astype(f32)
    out=jnp.where(row==0,sigmoid(raw[0:1]),0.0)
    for k,x in ((1,g),(2,G),(3,raw[1:2]),(4,docs)): out=jnp.where(row==k,x,out)
    return out

def span_terms(n,q,k,starts,xc,xr):
    i,j=square_masks()
    before=count_at(starts,n*SPAN-1).astype(f32)
    wide=lambda c: jnp.broadcast_to(c,(SPAN,128))
    beta=wide(xc[:,0:1]); G=wide(xc[:,2:3]); docs=wide(xc[:,4:5])
    incl=(i>=j)&(docs[:,:SPAN]==xr[4:5])
    D=jnp.where(incl,jnp.exp(jnp.where(incl,G[:,:SPAN]-xr[2:3],0.0)),0.0)
    gam=jnp.where(docs==before,jnp.exp(G),0.0)
    end=jnp.where(docs==docs[SPAN-1:SPAN],jnp.exp(G[SPAN-1:SPAN]-G),0.0)
    KK=dg(k,k,1,1); QK=dg(q,k,1,1)
    return beta,D,gam,end,KK,QK,i,j


SM=pl.BlockSpec(memory_space=pltpu.SMEM); VM=pl.BlockSpec(memory_space=pltpu.VMEM)
def S(shape,dt=f32): return jax.ShapeDtypeStruct(shape,dt)


MESH=pl.DeviceIdType.MESH
ANY=pl.BlockSpec(memory_space=pl.ANY)

def flip(s,bit):
    return s+bit-2*bit*lax.rem(lax.div(s,bit),2)

def flips(s,mask):
    bit=1
    while bit<=mask:
        if mask&bit: s=flip(s,bit)
        bit*=2
    return s

def greet(n,zc):
    s=lax.axis_index("seq"); z=lax.axis_index("shard")
    bar=pltpu.get_barrier_semaphore()
    for d in range(1,n):
        pl.semaphore_signal(bar,inc=1,device_id={"seq":lax.rem(s+d,n)},device_id_type=MESH)
    for d in range(1,zc):
        pl.semaphore_signal(bar,inc=1,device_id={"shard":lax.rem(z+d,zc)},device_id_type=MESH)
    pl.semaphore_wait(bar,n-1+zc-1)

def links(n):
    return 8 if n==8 else n

class SeqGather:
    def __init__(self,n,src,dst,axis,sems,c0=0):
        self.n=n; self.src=src; self.dst=dst; self.axis=axis; self.send,self.recv,self.loc=sems
        self.R,self.C=src.shape
        self.r0=0; self.nr=self.R; self.c0=c0
        self.s=lax.axis_index("seq")
        self.open=[]
    def slot(self,t,a,b):
        if self.axis==0:
            return self.dst.at[pl.ds(pl.multiple_of(t*self.R+self.r0+a,16),b-a),pl.ds(self.c0,self.C)]
        return self.dst.at[pl.ds(self.r0+a,b-a),pl.ds(pl.multiple_of(t*self.C,128),self.C)]
    def copy(self,src,t,a,b,k,to):
        c=pltpu.make_async_remote_copy(src_ref=src,dst_ref=self.slot(t,a,b),send_sem=self.send.at[k],recv_sem=self.recv.at[k],device_id={"seq":to},device_id_type=MESH)
        c.start()
        return c
    def pass_on(self,t,a,b,k,to):
        return self.copy(self.slot(t,a,b),t,a,b,k,to)
    def start(self):
        s=self.s; nr=self.nr
        mine=self.src.at[pl.ds(self.r0,nr),:]
        self.own=pltpu.make_async_copy(mine,self.slot(s,0,nr),self.loc)
        self.own.start()
        masks=(2,4) if self.n==8 else range(2,self.n,2)
        self.direct=[self.copy(mine,s,0,nr,i+1,flips(s,m)) for i,m in enumerate(masks)]
        self.open.append(self.copy(mine,s,0,nr,0,flip(s,1)))
    def middle(self):
        s=self.s; nr=self.nr; h=nr//2
        if self.n!=8: return
        x,y=flip(s,2),flip(s,4)
        self.direct[0].wait_recv()
        fa=self.pass_on(x,0,h,3,y)
        self.open.append(self.pass_on(x,0,nr,5,flip(s,1)))
        self.direct[1].wait_recv()
        fb=self.pass_on(y,h,nr,4,x)
        self.open.append(self.pass_on(y,0,nr,6,flip(s,1)))
        self.diag=(fa,fb)
    def late(self):
        s=self.s; nr=self.nr
        if self.n==8:
            for f in self.diag: f.wait_recv()
            self.open.append(self.pass_on(flips(s,6),0,nr,7,flip(s,1)))
            for f in self.diag: f.wait_send()
        else:
            for i,m in enumerate(range(2,self.n,2)):
                self.direct[i].wait_recv()
                self.open.append(self.pass_on(flips(s,m),0,nr,self.n//2+i,flip(s,1)))
        for f in self.direct: f.wait_send()
    def finish(self):
        for f in self.open: f.wait()
        self.own.wait()

class ShardGather:
    def __init__(self,zc,src,dst,send,recv):
        self.zc=zc; self.src=src; self.dst=dst; self.send=send; self.recv=recv
        self.z=lax.axis_index("shard"); self.C=src.shape[1]
    def slot(self):
        return self.dst.at[:,pl.ds(pl.multiple_of(self.z*self.C,128),self.C)]
    def start(self):
        self.own=pltpu.make_async_copy(self.src,self.slot(),self.recv.at[0]); self.own.start()
        self.cs=[]
        for d in range(1,self.zc):
            c=pltpu.make_async_remote_copy(src_ref=self.src,dst_ref=self.slot(),send_sem=self.send.at[d],recv_sem=self.recv.at[d],device_id={"shard":lax.rem(self.z+d,self.zc)},device_id_type=MESH)
            c.start(); self.cs.append(c)
    def finish(self):
        for c in self.cs: c.wait()
        self.own.wait()

class ShardSplit:
    def __init__(self,zc,src,box,send,recv):
        self.zc=zc; self.src=src; self.box=box; self.send=send; self.recv=recv
        self.z=lax.axis_index("shard"); self.C=box.shape[2]
    def start(self):
        C=self.C
        self.own=pltpu.make_async_copy(self.src.at[:,pl.ds(pl.multiple_of(self.z*C,128),C)],self.box.at[0],self.recv.at[0]); self.own.start()
        self.cs=[]
        for d in range(1,self.zc):
            to=lax.rem(self.z+d,self.zc)
            c=pltpu.make_async_remote_copy(src_ref=self.src.at[:,pl.ds(pl.multiple_of(to*C,128),C)],dst_ref=self.box.at[d],send_sem=self.send.at[d],recv_sem=self.recv.at[d],device_id={"shard":to},device_id_type=MESH)
            c.start(); self.cs.append(c)
    def finish(self):
        for c in self.cs: c.wait()
        self.own.wait()

class ShardAll:
    def __init__(self,axis,n,box,send,recv):
        self.axis=axis; self.n=n; self.box=box; self.send=send; self.recv=recv; self.me=lax.axis_index(axis)
    def start(self):
        self.cs=[]
        for d in range(1,self.n):
            c=pltpu.make_async_remote_copy(src_ref=self.box.at[self.me],dst_ref=self.box.at[self.me],send_sem=self.send.at[d],recv_sem=self.recv.at[d],device_id={self.axis:lax.rem(self.me+d,self.n)},device_id_type=MESH)
            c.start(); self.cs.append(c)
    def finish(self):
        for c in self.cs: c.wait()

class ColumnSplit:
    def __init__(self,n,src,dst,send,recv):
        self.n=n; self.src=src; self.dst=dst; self.send=send; self.recv=recv
        self.s=lax.axis_index("seq"); self.C=dst.shape[1]; self.R=src.shape[0]
    def start(self):
        n,s,C,R=self.n,self.s,self.C,self.R
        to_rows=self.dst.at[pl.ds(pl.multiple_of(s*R,16),R),:]
        block=lambda t: self.src.at[:,pl.ds(pl.multiple_of(t*C,128),C)]
        self.own=pltpu.make_async_copy(block(s),to_rows,self.recv.at[0]); self.own.start()
        self.cs=[]
        for d in range(1,n):
            t=lax.rem(s+d,n)
            c=pltpu.make_async_remote_copy(src_ref=block(t),dst_ref=to_rows,send_sem=self.send.at[d],recv_sem=self.recv.at[d],device_id={"seq":t},device_id_type=MESH)
            c.start(); self.cs.append(c)
    def finish(self):
        for c in self.cs: c.wait()
        self.own.wait()

class ToPairs:
    def __init__(self,n,copies,heads,local_len,src,rows_src,dst,rows_dst,DK,DV,send,recv,off=0):
        self.cs=[]
        self.__dict__.update(n=n,copies=copies,heads=heads,ll=local_len,src=src,rows_src=rows_src,dst=dst,rows_dst=rows_dst,DK=DK,DV=DV,send=send,recv=recv,off=off)
    def parts(self,t):
        s=lax.axis_index("seq"); ll,DK,DV,heads=self.ll,self.DK,self.DV,self.heads
        pair=lax.div(t,self.copies); seq=lax.div(pair,heads); head=lax.rem(pair,heads)
        rows=pl.ds(pl.multiple_of(seq*ll,ll),ll); to=pl.ds(pl.multiple_of(s*ll+self.off,16),ll)
        if self.rows_src is None:
            return [(self.src.at[rows,pl.ds(pl.multiple_of(head*DV,128),DV)],self.dst.at[to,:])]
        wk=heads*DK
        out=[]
        for start,width,at in ((0,DK,0),(wk,DK,DK),(2*wk,DV,2*DK)):
            out.append((self.src.at[rows,pl.ds(pl.multiple_of(start+head*width,128),width)],self.dst.at[to,pl.ds(at,width)]))
        out.append((self.rows_src.at[pl.ds(pl.multiple_of(pair*8,8),8),:],self.rows_dst.at[pl.ds(pl.multiple_of(s*8,8),8),:]))
        return out
    def start(self,i):
        s=lax.axis_index("seq")
        for d in range(self.n):
            t=lax.rem(s+d,self.n)
            a,b=self.parts(t)[i]
            if d==0: c=pltpu.make_async_copy(a,b,self.recv.at[i,0])
            else: c=pltpu.make_async_remote_copy(src_ref=a,dst_ref=b,send_sem=self.send.at[i,d],recv_sem=self.recv.at[i,d],device_id={"seq":t},device_id_type=MESH)
            c.start(); self.cs.append(c)
    def finish(self):
        for c in self.cs: c.wait()

class FromPairs:
    def __init__(self,n,copies,heads,local_len,items,send,recv):
        self.__dict__.update(n=n,copies=copies,heads=heads,items=items,send=send,recv=recv)
    def start(self):
        s=lax.axis_index("seq"); pairs=self.n//self.copies; p=lax.div(s,self.copies); r=lax.rem(s,self.copies)
        seq=lax.div(p,self.heads); head=lax.rem(p,self.heads); self.cs=[]
        for d in range(pairs):
            t=lax.rem(p+d,pairs)*self.copies+r
            for i,(src,at,dst,to) in enumerate(self.items):
                a=src.at[at(t)]; b=dst.at[to(seq,head)]
                if d==0: c=pltpu.make_async_copy(a,b,self.recv.at[i,0])
                else: c=pltpu.make_async_remote_copy(src_ref=a,dst_ref=b,send_sem=self.send.at[i,d],recv_sem=self.recv.at[i,d],device_id={"seq":t},device_id_type=MESH)
                c.start(); self.cs.append(c)
    def finish(self):
        for c in self.cs: c.wait()

def flat_form(cols):
    r=cols.shape[0]
    i=lax.broadcasted_iota(jnp.int32,(r,r),0); j=lax.broadcasted_iota(jnp.int32,(r,r),1)
    return mmx(cols,jnp.where(i==j,1.0,0.0),0,0)

class SharedColumns:
    def __init__(self,n,zc,src,dst,sems):
        self.n=n; self.zc=zc; self.src=src; self.dst=dst; self.send,self.recv,self.zsend,self.zrecv=sems
        self.s=lax.axis_index("seq"); self.z=lax.axis_index("shard"); self.C=dst.shape[2]; self.q=src.shape[0]//zc
    def start(self):
        rows=pl.ds(pl.multiple_of(self.z*self.q,16),self.q)
        block=lambda t: self.src.at[rows,pl.ds(pl.multiple_of(t*self.C,128),self.C)]
        self.cs=[]
        for d in range(self.n):
            t=lax.rem(self.s+d,self.n)
            if d==0: c=pltpu.make_async_copy(block(t),self.dst.at[self.s,rows,:],self.recv.at[0])
            else: c=pltpu.make_async_remote_copy(src_ref=block(t),dst_ref=self.dst.at[self.s,rows,:],send_sem=self.send.at[d],recv_sem=self.recv.at[d],device_id={"seq":t},device_id_type=MESH)
            c.start(); self.cs.append(c)
    def middle(self):
        for c in self.cs: c.wait()
        strip=self.dst.at[:,pl.ds(pl.multiple_of(self.z*self.q,16),self.q),:]
        self.cs=[]
        for d in range(1,self.zc):
            c=pltpu.make_async_remote_copy(src_ref=strip,dst_ref=strip,send_sem=self.zsend.at[d],recv_sem=self.zrecv.at[d],device_id={"shard":lax.rem(self.z+d,self.zc)},device_id_type=MESH)
            c.start(); self.cs.append(c)
    def finish(self):
        for c in self.cs: c.wait()

def row_form(cols):
    return mmx(jnp.ones((8,cols.shape[1]),f32),cols,1,1)

def col_form(rows):
    r=rows.shape[1]
    i=lax.broadcasted_iota(jnp.int32,(r,r),0); j=lax.broadcasted_iota(jnp.int32,(r,r),1)
    return mmx(jnp.where(i==j,1.0,0.0),rows,1,1)

def gathers(n,pairs,sems):
    send,recv,loc=sems
    return [SeqGather(n,src,dst,axis,(send.at[i],recv.at[i],loc.at[i]),*c0) for i,(src,dst,axis,*c0) in enumerate(pairs)]
def gather_sems(n,k):
    return [pltpu.SemaphoreType.DMA((k,links(n))),pltpu.SemaphoreType.DMA((k,links(n))),pltpu.SemaphoreType.DMA((k,))]
def pair_sems(k):
    return [pltpu.SemaphoreType.DMA((k,)),pltpu.SemaphoreType.DMA((k,))]
def each(ops,name):
    for o in ops: getattr(o,name)()


def conv_pre(u,taps,age,base,rows):
    window=u[pl.ds(base,rows+16),:].astype(f32)
    pre=window[16:]*taps[3:4]
    for back in range(1,4):
        ok=jnp.where(age>=back,1.0,0.0)
        pre=pre+window[16-back:16-back+rows]*ok*taps[3-back:4-back]
    return pre,window

def tiles(width,step): return [(a,min(a+step,width)) for a in range(0,width,step)]

def layer_kernel(cfg,names,*refs):
    n,zc,copies,heads,DK,DV,H=cfg
    r_=SimpleNamespace(**dict(zip(names,refs)))
    tok,cot=r_.tok,r_.cot
    RN,F=tok.shape; D=F*zc; seqs=r_.starts.shape[0]; ll=RN//seqs; L=n*ll; NC=L//SPAN; per=ll//SPAN
    wk=heads*DK; wv=heads*DV; CH=2*DK+DV; FF=r_.wup.shape[1]; N=n*RN; VW=wv
    s=lax.axis_index("seq"); z=lax.axis_index("shard")
    pair=lax.div(s,copies); my_head=lax.rem(pair,heads); at_head=z*heads+my_head
    starts=Row(r_.starts,lax.div(pair,heads))
    count=[0,0,0]
    def zsems():
        count[0]+=1; return r_.zsend.at[count[0]-1],r_.zrecv.at[count[0]-1]
    def qsems():
        count[1]+=1; return r_.qsend.at[count[1]-1],r_.qrecv.at[count[1]-1]
    def gather(src,dst,axis,c0=0):
        count[2]+=1; i=count[2]-1
        return SeqGather(n,src,dst,axis,(r_.gsend.at[i],r_.grecv.at[i],r_.gloc.at[i]),c0)
    def span(m): return pl.ds(pl.multiple_of(m*SPAN,SPAN),SPAN)
    def loop(count_,body,unroll=1): lax.fori_loop(0,count_,lambda i,c: (body(i),c)[1],0,unroll=unroll)
    normed,scale=r_.normed,r_.scale
    pbuf=r_.tokfull.at[:,pl.ds(0,heads*CH)]
    gw_=r_.bufa.at[pl.ds(0,D),pl.ds(0,FF)]; uw_=r_.bufb.at[pl.ds(0,D),pl.ds(0,FF)]; dw_=r_.dw
    wbuf=r_.bufb
    gv=r_.gv; uv=r_.uv
    cotfull,oall,branch,pbf,u_ref,taps_ref=r_.cotfull,r_.oall,r_.branch,r_.pbf,r_.u,r_.taps
    xr_ref,xc_ref,q_ref,k_ref,v_ref,s_ref,w_ref,t_ref,qt_ref,mh_ref,gc_ref=r_.xr,r_.xc,r_.q,r_.k,r_.v,r_.s,r_.w,r_.t,r_.qt,r_.mh,r_.gc
    gate_ref,rbuf,dpre,du_ref,dx_ref,do_ref,dxr,ds_ref=r_.gate,r_.rbuf,r_.dpre,r_.du,r_.dx,r_.do,r_.dxr,r_.ds
    heads_v=pl.ds(0,DV); rest_v=pl.ds(DV,DV)

    greet(n,zc)
    zt=ShardGather(zc,tok,r_.tokfull,*zsems()); zt.start()
    put=lambda x,first: dg(x[...],jnp.where(lax.broadcasted_iota(jnp.int32,(x.shape[0],128),0)+first==lax.broadcasted_iota(jnp.int32,(x.shape[0],128),1),1.0,0.0).astype(bf16),0,0)
    ws=r_.ws
    ws[...]=(put(r_.wb,0)+put(r_.wd,heads)).astype(bf16)
    at_row=0
    for x in (r_.qc,r_.kc,r_.vc):
        ws[at_row:at_row+x.shape[1]]=(ws[at_row:at_row+x.shape[1]].astype(f32)+put(x,2*heads)).astype(bf16)
        at_row+=x.shape[1]
    ws_all=(ws,r_.wq,r_.wk,r_.wv); at=(wk*2+wv,0,wk,wk*2)
    gw=[gather(w,r_.wfull,0,a) for w,a in zip(ws_all,at)]
    each(gw,"start")
    u_ref[0:16]=jnp.zeros((16,CH),bf16)
    rbuf[...]=jnp.zeros(rbuf.shape,f32)
    dx_ref[...]=jnp.zeros(dx_ref.shape,f32)
    rate=jnp.exp(jnp.full((1,1),r_.dlog[at_head],f32)); bias=r_.dbias[at_head]
    each(gw,"middle")
    gb=[gather(r_.wg,r_.wgfull,0),gather(r_.wo,r_.wofull,1),gather(r_.wgate,gw_,0)]
    gu=[gather(r_.wup,uw_,0),gather(r_.wdown,dw_,1)]
    gb[0].start()
    zt.finish()
    zk=ShardGather(zc,cot,cotfull,*zsems()); zk.start()
    def norm(c):
        r=pl.ds(pl.multiple_of(c*32,32),32)
        x=r_.tokfull[r,:].astype(f32)
        sc=lax.rsqrt(jnp.sum(x*x,axis=1,keepdims=True)/D+EPSILON)
        normed[r,:]=(x*sc*r_.gain[...]).astype(bf16)
        scale[r,:]=jnp.broadcast_to(sc,(32,128))
    loop(RN//32,norm)
    n1=SharedColumns(n,zc,normed,r_.n1c,(*qsems(),*zsems())); n1.start()
    inward=ToPairs(n,copies,heads,ll,pbuf,rbuf,u_ref,xr_ref,DK,DV,r_.isend,r_.irecv,16)
    for i,g in enumerate(gw):
        g.late(); g.finish()
        width=ws_all[i].shape[1]
        buf=r_.sbuf if i==0 else wbuf.at[pl.ds(0,D),pl.ds(0,width)]
        c=pltpu.make_async_copy(r_.wfull.at[:,pl.ds(at[i],width)],buf,r_.ld.at[0,0]); c.start(); c.wait()
        if i==0:
            small=jnp.dot(normed[...],r_.sbuf[...],preferred_element_type=f32)
            for sq in range(seqs):
                fl=flat_form(small[sq*ll:(sq+1)*ll,0:8*((2*heads+7)//8)])
                for h in range(heads):
                    base=(sq*heads+h)*8
                    rbuf[base:base+1]=fl[h:h+1]
                    rbuf[base+1:base+2]=fl[heads+h:heads+h+1]
            cq=wk//n; cv=wv//n; step=D//n
            for kind,(width_c,total,skip) in enumerate(((cq,DK,0),(cq,DK,cq),(cv,DV,2*cq))):
                for j in range(total//width_c):
                    dev=my_head*(total//width_c)+j
                    to=(0,DK,2*DK)[kind]+j*width_c
                    r_.tbuf[to:to+width_c]=r_.sbuf[pl.ds(pl.multiple_of(dev*step+skip,16),width_c),:]
            ident=jnp.where(lax.broadcasted_iota(jnp.int32,(CH,CH),0)==lax.broadcasted_iota(jnp.int32,(CH,CH),1),1.0,0.0).astype(bf16)
            tt=dg(r_.tbuf[...],ident,0,0)
            taps_ref[...]=tt[2*heads:2*heads+4]
        else:
            def column(j,i=i):
                pbuf[:,pl.ds(pl.multiple_of(at[i]+j*256,128),256)]=jnp.dot(normed[...],wbuf[0:D,pl.ds(pl.multiple_of(j*256,256),256)],preferred_element_type=f32).astype(bf16)
            loop(width//256,column)
        inward.start((3,0,1,2)[i])
    gb[1].start()
    zk.finish()
    cc=SharedColumns(n,zc,cotfull,r_.cotc,(*qsems(),*zsems())); cc.start()
    n1.middle()
    gb[0].middle()
    inward.finish()
    gb[2].start()
    cc.middle()

    def turn(m):
        r=pl.ds(pl.multiple_of(m*8,8),8)
        x=position_rows(xr_ref[r,:],starts,m*ll,rate,bias)
        xr_ref[r,:]=x
        xc_ref[pl.ds(pl.multiple_of(m*ll,ll),ll),:]=col_form(x)
    loop(n,turn,4)
    taps=taps_ref[...]
    R=128
    def conv(c):
        base=pl.multiple_of(c*R,R)
        age=doc_age(starts,positions(base,R,128,0))[:,0:1]
        pre,unused=conv_pre(u_ref,taps,age,base,R)
        act=pre*sigmoid(pre)
        rows=pl.ds(base,R)
        aq=act[:,:DK]; ak=act[:,DK:2*DK]
        q_ref[rows,:]=(aq*lax.rsqrt(jnp.sum(aq*aq,axis=1,keepdims=True)+EPSILON)*DK**-0.5).astype(bf16)
        k_ref[rows,:]=(ak*lax.rsqrt(jnp.sum(ak*ak,axis=1,keepdims=True)+EPSILON)).astype(bf16)
        v_ref[rows,:]=act[:,2*DK:].astype(bf16)
    loop(L//R,conv)
    gb[1].middle()
    gu[1].start()
    kcol,pcol,ecol=pl.ds(0,DK),pl.ds(DK,SPAN),pl.ds(DK+SPAN,DK)
    def local(m):
        xr=xr_ref[pl.ds(pl.multiple_of(m*8,8),8),:]
        for e in range(per):
            b=m*per+e; rows=span(b)
            q=q_ref[rows,:]; k=k_ref[rows,:]; v=v_ref[rows,:]
            beta,Dm,gam,end,KK,QK,i,j=span_terms(b,q,k,starts,xc_ref[rows,:],xr[:,e*SPAN:(e+1)*SPAN])
            dx_ref[rows,0:SPAN]=jnp.where(i>j,beta[:,:SPAN]*Dm*KK,0.0)
            kf=k.astype(f32)
            dpre[rows,rest_v]=jnp.concatenate([beta]*(DV//128),axis=1)*v.astype(f32)
            du_ref[rows,kcol]=((beta*gam)*kf).astype(bf16)
            du_ref[rows,pcol]=(QK*Dm).astype(bf16)
            qt_ref[b,0:SPAN]=(gam*q.astype(f32)).astype(bf16)
            du_ref[rows,ecol]=(end*kf).astype(bf16)
            gc_ref[b]=jnp.broadcast_to(gam[SPAN-1:SPAN],(8,128))
    loop(n,local,4)
    inverses(lambda b: dx_ref[b*SPAN:(b+1)*SPAN,0:SPAN],t_ref)
    def solve(b):
        rows=span(b)
        Th,Tl=halves(t_ref[b]); Vh,Vl=halves(dpre[rows,rest_v]); bk=du_ref[rows,kcol]
        U=dg(Th,Vh)+(dg(Tl,Vh)+dg(Th,Vl)); Wk=dg(Th,bk)+dg(Tl,bk)
        Ub,Ul=halves(U); Wb,Wl=halves(Wk); Pm=du_ref[rows,pcol]; ek=du_ref[rows,ecol]
        dpre[rows,heads_v]=dg(Pm,Ub)
        w_ref[b]=U
        qt_ref[b,0:SPAN]=(qt_ref[b,0:SPAN].astype(f32)-dg(Pm,Wb)).astype(bf16)
        qt_ref[b,SPAN:]=Wb
        ds_ref[b]=dg(ek,Ub,0,0)+dg(ek,Ul,0,0)
        mh_ref[b,0],mh_ref[b,1]=halves(dg(ek,Wb,0,0)+dg(ek,Wl,0,0))
    loop(NC,solve,4)
    def chain(b,St):
        s_ref[b]=St
        sh,sl=halves(St); mh=mh_ref[b,0]
        return jnp.concatenate([gc_ref[b][0:1]]*(DV//128),axis=1)*St+ds_ref[b]-(dg(mh,sh)+(dg(mh,sl)+dg(mh_ref[b,1],sh)))
    lax.fori_loop(0,NC,chain,jnp.zeros((DK,DV),f32),unroll=2)
    def emit(b):
        rows=span(b)
        x=dg(qt_ref[b],s_ref[b].astype(bf16))
        do_ref[rows,:]=(dpre[rows,heads_v]+x[:SPAN]).astype(bf16)
        w_ref[b]=w_ref[b]-x[SPAN:]
    loop(NC,emit,4)
    seq_rows=lambda t: pl.ds(pl.multiple_of(t*ll,ll),ll)
    outward=FromPairs(n,copies,heads,ll,[(do_ref,lambda t: (seq_rows(t),slice(None)),oall,lambda seq,head: (seq_rows(seq),pl.ds(pl.multiple_of(head*DV,128),DV)))],r_.osend,r_.orecv)
    outward.start()

    gb[0].late(); gb[0].finish()
    c=pltpu.make_async_copy(r_.wgfull,wbuf.at[pl.ds(0,D),pl.ds(0,wv)],r_.ld.at[0,0]); c.start(); c.wait()
    def column(j):
        k_=pl.ds(pl.multiple_of(j*256,256),256)
        gate_ref[:,k_]=jnp.dot(normed[...],wbuf[0:D,k_],preferred_element_type=f32)
    loop(wv//256,column)
    gb[1].late(); gb[1].finish(); gb[2].middle()
    blocks=D//VW
    def load_wo(buf,sems):
        cs=[pltpu.make_async_copy(r_.wofull.at[:,pl.ds(j*VW,VW)],buf.at[pl.ds(j*VW,VW),pl.ds(0,VW)],sems.at[j]) for j in range(blocks)]
        for c in cs: c.start()
        return cs
    for c in load_wo(wbuf,r_.ld.at[0]): c.wait()
    outward.finish()
    def mix(c):
        r=pl.ds(pl.multiple_of(c*32,32),32)
        for h in range(heads):
            hc=pl.ds(h*DV,DV)
            o=oall[r,hc].astype(f32); g=gate_ref[r,hc]
            rho=lax.rsqrt(jnp.sum(o*o,axis=1,keepdims=True)/DV+EPSILON)
            branch[r,hc]=(o*rho*r_.hgain[...]*(g*sigmoid(g))).astype(bf16)
    loop(RN//32,mix)
    inner_tiles=VW//256
    def column(j):
        blk=lax.div(j,inner_tiles); at_=lax.rem(j,inner_tiles)
        w=wbuf[pl.ds(pl.multiple_of(blk*VW,16),VW),pl.ds(pl.multiple_of(at_*256,256),256)]
        pbf[:,pl.ds(pl.multiple_of(j*256,256),256)]=jnp.dot(branch[...],w,preferred_element_type=f32).astype(bf16)
    loop(D//256,column)
    split=ShardSplit(zc,pbf,r_.box,*zsems()); split.start()
    for d in range(1,n): pl.semaphore_signal(r_.free,inc=1,device_id={"seq":lax.rem(s+d,n)},device_id_type=MESH)
    pl.semaphore_wait(r_.free,n-1)
    gu[0].start()
    gu[1].middle()

    F_at=pl.ds(pl.multiple_of(z*F,128),F)
    fgain=r_.fgain[:,F_at]
    sums=r_.sums
    def shard_sum(k,rows8,meanwhile=None):
        sums[k*zc+z]=rows8
        tot=ShardAll("shard",zc,sums.at[pl.ds(k*zc,zc)],*zsems()); tot.start()
        if meanwhile: meanwhile()
        tot.finish()
        t=sums[k*zc]
        for d in range(1,zc): t=t+sums[k*zc+d]
        return col_form(t)[:,0:1]/D
    def boxed(box):
        g=box[0].astype(f32)
        for d in range(1,zc): g=g+box[d].astype(f32)
        return g
    res,gres,nloc,nfull,afull=r_.res,r_.gres,r_.nloc,r_.nfull,r_.normed
    split.finish()
    x=tok[...].astype(f32)+boxed(r_.box)
    res[...]=x
    sc=lax.rsqrt(shard_sum(0,row_form(x*x))+EPSILON)
    nloc[...]=(res[...]*sc*fgain).astype(bf16)
    zg=ShardGather(zc,nloc,nfull,*zsems()); zg.start()
    gb[2].late(); gb[2].finish(); gu[0].middle(); gu[1].late()
    gk=[gather(r_.dgp,r_.dgpfull,0),gather(branch,r_.brafull,0)]
    gk[1].start()
    zg.finish()
    for a,b in tiles(FF,512): gv[:,a:b]=jnp.dot(nfull[...],gw_[:,a:b],preferred_element_type=f32)
    gu[0].late(); gu[0].finish()
    for a,b in tiles(FF,512): uv[:,a:b]=jnp.dot(nfull[...],uw_[:,a:b],preferred_element_type=f32)
    hidden,dgate,dup=r_.hidden,r_.dgate,r_.dup
    def act(c):
        rr=pl.ds(pl.multiple_of(c*32,32),32)
        g=gv[rr,:]
        hidden[rr,:]=(g*sigmoid(g)*uv[rr,:]).astype(bf16)
    loop(RN//32,act)
    gh=[gather(hidden,r_.hidfull,0),gather(dgate,r_.dgfull,0),gather(dup,r_.dufull,0)]
    gu[1].finish()
    for a,b in tiles(FF,512):
        dh=dg(cotfull[...],dw_[a:b,:],1,1)
        g=gv[:,a:b]; sg=sigmoid(g)
        dgate[:,a:b]=(dh*uv[:,a:b]*sg*(1.0+g*(1.0-sg))).astype(bf16)
        dup[:,a:b]=(dh*(g*sg)).astype(bf16)
    each(gh[1:],"start")
    def back_two(j):
        rr=pl.ds(pl.multiple_of(j*256,256),256)
        pbf[:,rr]=(dg(dgate[...],gw_[rr,:],1,1)+dg(dup[...],uw_[rr,:],1,1)).astype(bf16)
    loop(D//256,back_two)
    split=ShardSplit(zc,pbf,r_.box,*zsems()); split.start()
    ld=r_.ld
    bufs=(r_.bufa,r_.bufb)
    loads={}
    def load_job(key,i,pieces):
        loads[key]=[]
        for j,(src,to) in enumerate(pieces):
            c=pltpu.make_async_copy(src,bufs[i].at[to],ld.at[i,j]); c.start(); loads[key].append(c)
    def ready(key):
        for c in loads[key]: c.wait()
    whole=lambda w: (pl.ds(0,D),pl.ds(0,w))
    every=lambda w: (pl.ds(0,N),pl.ds(0,w))
    loads["wo"]=load_wo(r_.bufa,ld.at[0])
    load_job("og",1,[(r_.wgfull,whole(wv))])
    def outp(j):
        c_=pl.ds(pl.multiple_of(j*256,256),256)
        r_.outpart[:,c_]=jnp.dot(hidden[...],dw_[:,c_],preferred_element_type=f32).astype(bf16)
    loop(D//256,outp)
    split.finish()
    gk[1].middle(); gh[1].middle()
    gh[0].start()
    g=boxed(r_.box)
    gained=fgain*g
    gffn=[None]
    def meanwhile(): gffn[0]=jnp.sum(g*res[...]*sc,axis=0,keepdims=True)
    inner=shard_sum(1,row_form(gained*res[...]),meanwhile)
    gr=cot[...].astype(f32)+sc*(gained-res[...]*(sc*sc*inner))
    gres[...]=gr
    nloc[...]=gr.astype(bf16)
    zg=ShardGather(zc,nloc,afull,*zsems()); zg.start()
    gh[2].middle()
    zg.finish()
    n2=SharedColumns(n,zc,nfull,r_.n2c,(*qsems(),*zsems())); n2.start()
    so=ShardSplit(zc,r_.outpart,r_.boxo,*zsems()); so.start()

    ready("wo")
    r_.dsm[...]=jnp.zeros(r_.dsm.shape,bf16)
    dob,dgp,bufa,bufb=r_.dob,r_.dgp,r_.bufa,r_.bufb
    def heads_back(c,gh_):
        r=pl.ds(pl.multiple_of(c*64,64),64)
        for h in range(heads):
            hc=pl.ds(h*DV,DV)
            dm=dg(afull[r,0:VW],bufa[h*DV:(h+1)*DV,0:VW],1,1)
            for j in range(1,blocks):
                dm=dm+dg(afull[r,j*VW:(j+1)*VW],bufa[j*VW+h*DV:j*VW+(h+1)*DV,0:VW],1,1)
            dm=dm.astype(bf16).astype(f32)
            o=oall[r,hc].astype(f32); g=gate_ref[r,hc]
            rho=lax.rsqrt(jnp.sum(o*o,axis=1,keepdims=True)/DV+EPSILON)
            zz=o*rho; sg=sigmoid(g); sil=g*sg
            gh_=gh_+jnp.sum(dm*zz*sil,axis=0,keepdims=True)
            dmg=dm*r_.hgain[...]
            dz=dmg*sil
            dob[r,hc]=(rho*(dz-zz*(jnp.sum(dz*zz,axis=1,keepdims=True)/DV))).astype(bf16)
            dgp[r,hc]=(dmg*zz*sg*(1.0+g*(1.0-sg))).astype(bf16)
        return gh_
    grad_head=lax.fori_loop(0,RN//64,heads_back,jnp.zeros((1,DV),f32))
    inward=ToPairs(n,copies,heads,ll,dob,None,do_ref,None,DK,DV,r_.i2send,r_.i2recv); inward.start(0)
    each(gh[1:],"late"); gh[0].middle()
    gk[1].late()
    inward.finish()
    ca=SharedColumns(n,zc,afull,r_.attc,(*qsems(),*zsems())); ca.start()
    gk[0].start()

    dpre[L:L+8]=jnp.zeros((8,CH),f32)
    def early(b):
        ds_ref[b]=dg(qt_ref[b][0:SPAN],do_ref[span(b),:],0,0)
    loop(NC,early,4)
    def chain_back(m,dS):
        b=NC-1-m
        x=ds_ref[b]
        ds_ref[b]=dS
        sh,sl=halves(dS); mh=mh_ref[b,0]
        return jnp.concatenate([gc_ref[b][0:1]]*(DV//128),axis=1)*dS+x-(dg(mh,sh,0,0)+(dg(mh,sl,0,0)+dg(mh_ref[b,1],sh,0,0)))
    lax.fori_loop(0,NC,chain_back,jnp.zeros((DK,DV),f32),unroll=2)
    def one_span(b,xr):
        rows=span(b)
        q=q_ref[rows,:]; k=k_ref[rows,:]; v=v_ref[rows,:]; dO=do_ref[rows,:]
        beta,Dm,gam,end,KK,QK,i,j=span_terms(b,q,k,starts,xc_ref[rows,:],xr)
        beta2=jnp.concatenate([beta]*(DV//128),axis=1)
        S0=s_ref[b]; dS1=ds_ref[b]
        S0h,S0l=halves(S0); dSh,dSl=halves(dS1)
        kf=k.astype(f32); qf=q.astype(f32); vf=v.astype(f32)
        W,Wl=halves(w_ref[b])
        Ph,Pl=halves(QK*Dm)
        dW=dg(Ph,dO,0,0)+dg(Pl,dO,0,0)+jnp.concatenate([end]*(DV//128),axis=1)*(dg(k,dSh)+dg(k,dSl))
        Y=mm3(t_ref[b],dW,0,0)
        dOY=jnp.concatenate([dO,Y.astype(bf16)],axis=0)
        dPA=dg(dOY,W,1,1)+dg(dOY,Wl,1,1)
        GS=dg(dOY,S0h,1,1)+dg(dOY,S0l,1,1)
        dOS=GS[:SPAN]; YS=GS[SPAN:]
        Z=dg(W,dSh,1,1)
        dPD=dPA[:SPAN]*Dm
        EA=jnp.where(i>j,-dPA[SPAN:]*Dm,0.0)
        A1=jnp.concatenate([dPD,beta[:,:SPAN]*EA],axis=0).astype(bf16)
        r1=dg(A1,k)
        r2=dg(A1,jnp.concatenate([q,k],axis=0),0,0)
        dpre[rows,0:DK]=gam*dOS+r1[:SPAN]
        dpre[rows,DK:2*DK]=r1[SPAN:]+r2-(beta*gam)*YS+end*Z
        dpre[rows,2*DK:]=beta2*Y
        EK=EA*KK
        kYS=jnp.sum(kf*YS,axis=1,keepdims=True)
        dbeta=jnp.sum(Y*vf,axis=1,keepdims=True)-gam*kYS+jnp.sum(EK,axis=1,keepdims=True)
        Fm=dPD*QK+beta[:,:SPAN]*EK
        dgam=jnp.sum(qf*dOS,axis=1,keepdims=True)-beta*kYS
        dend=jnp.sum(kf*Z,axis=1,keepdims=True)*end
        dG=jnp.sum(Fm,axis=1,keepdims=True)+dgam*gam-dend
        tail=jnp.sum(jnp.sum(S0*dS1,axis=0,keepdims=True),axis=1,keepdims=True)
        last=jnp.sum(dend,axis=0,keepdims=True)+gam[SPAN-1:SPAN]*tail
        row=lax.broadcasted_iota(jnp.int32,(SPAN,128),0)
        dG=dG+jnp.where(row==SPAN-1,last,0.0)
        dx_ref[rows,0:1]=(dbeta*beta*(1.0-beta))[:,0:1]
        dx_ref[rows,1:2]=dG[:,0:1]
        return jnp.sum(Fm,axis=0,keepdims=True)
    def local_back(m):
        r=pl.ds(pl.multiple_of(m*8,8),8)
        xr=xr_ref[r,:]
        dxr[r,:]=jnp.broadcast_to(jnp.concatenate([one_span(m*per+e,xr[:,e*SPAN:(e+1)*SPAN]) for e in range(per)],axis=1),(8,ll))
    loop(n,local_back,2)
    n2.middle(); ca.middle()
    il=lax.broadcasted_iota(jnp.int32,(ll,ll),0); jl=lax.broadcasted_iota(jnp.int32,(ll,ll),1)
    later=jnp.where((il>=jl)&((il//SPAN)==(jl//SPAN)),1.0,0.0)
    def turn_back(m,carry):
        r=pl.ds(pl.multiple_of(m*8,8),8)
        f=flat_form(dx_ref[pl.ds(pl.multiple_of(m*ll,ll),ll),0:8])
        dlog=mmx(jnp.broadcast_to(f[1:2]-dxr[r,:][0:1],(8,ll)),later)
        x=xr_ref[r,:]
        ddp=dlog*(-rate)*sigmoid(x[3:4]+bias)
        row=lax.broadcasted_iota(jnp.int32,(8,ll),0)
        dxr[r,:]=jnp.where(row==0,f[0:1],jnp.where(row==1,ddp,0.0))
        return (carry[0]+jnp.sum(dlog[0:1]*x[1:2],axis=1,keepdims=True),carry[1]+jnp.sum(ddp[0:1],axis=1,keepdims=True))
    zero=jnp.zeros((1,1),f32)
    sl,sb=lax.fori_loop(0,n,turn_back,(zero,zero),unroll=4)
    def norms(c,dt):
        base=pl.multiple_of(c*R,R)
        age=doc_age(starts,positions(base,R,128,0))[:,0:1]
        pre,window=conv_pre(u_ref,taps,age,base,R)
        sg=sigmoid(pre); a_=pre*sg
        rows=pl.ds(base,R)
        d=dpre[rows,:]
        def unit_back(a,dd,f):
            sc_=lax.rsqrt(jnp.sum(a*a,axis=1,keepdims=True)+EPSILON)
            dot=jnp.sum(a*dd,axis=1,keepdims=True)
            return f*(sc_*dd-a*(sc_*sc_*sc_*dot))
        dact=jnp.concatenate([unit_back(a_[:,:DK],d[:,:DK],DK**-0.5),unit_back(a_[:,DK:2*DK],d[:,DK:2*DK],1.0),d[:,2*DK:]],axis=1)
        dp=dact*sg*(1.0+pre*(1.0-sg))
        dpre[rows,:]=dp
        new=[]
        for j in range(4):
            back=3-j
            x=window[16-back:16-back+R]
            if back: x=x*jnp.where(age>=back,1.0,0.0)
            new.append(dt[j]+jnp.sum(x*dp,axis=0,keepdims=True))
        return tuple(new)
    dt=lax.fori_loop(0,L//R,norms,(jnp.zeros((1,CH),f32),)*4)
    def back(c):
        base=pl.multiple_of(c*R,R)
        window=dpre[pl.ds(base,R+8),:]
        age=doc_age(starts,positions(base,R+8,128,0))[:,0:1]
        d=window[:R]*taps[3:4]
        for sh in range(1,4):
            d=d+window[sh:sh+R]*jnp.where(age[sh:sh+R]>=sh,1.0,0.0)*taps[3-sh:4-sh]
        du_ref[pl.ds(base,R),:]=d.astype(bf16)
    loop(L//R,back)
    gk[0].middle()
    dyq,dsm=pbuf,r_.dsm
    cut=lambda start,width: (lambda t: (seq_rows(t),pl.ds(start,width)))
    to=lambda start,width: (lambda seq,head: (seq_rows(seq),pl.ds(pl.multiple_of(start+head*width,128),width)))
    outward=FromPairs(n,copies,heads,ll,[(du_ref,cut(0,DK),dyq,to(0,DK)),(du_ref,cut(DK,DK),dyq,to(wk,DK)),(du_ref,cut(2*DK,DV),dyq,to(2*wk,DV)),
        (dxr,lambda t: (pl.ds(pl.multiple_of(t*8,8),8),slice(None)),rbuf,lambda seq,head: (pl.ds(pl.multiple_of((seq*heads+head)*8,8),8),slice(None)))],r_.o2send,r_.o2recv)
    outward.start()

    part=r_.acc
    def spread(first,buf,terms):
        def one(j):
            rr=pl.ds(pl.multiple_of(j*256,256),256)
            t=0.0
            for x,a,b in terms: t=t+dg(x[...],buf[rr,a:b],1,1)
            part[:,rr]=t if first else part[:,rr]+t
        loop(D//256,one)
    staged={}
    def stage(k,ref,shape):
        if k in staged: staged[k].wait()
        return r_.sta.at[pl.ds(0,shape[0]),pl.ds(0,shape[1])] if k==0 else r_.stb.at[pl.ds(0,shape[0]),pl.ds(0,shape[1])]
    def send(k,view,ref):
        staged[k]=pltpu.make_async_copy(view,ref,r_.stsem.at[k]); staged[k].start()
    ready("og"); spread(True,bufb,[(dgp,0,wv)])
    gh[0].late(); n2.finish()
    each(gh,"finish")
    load_job("dgate",0,[(r_.dgfull,every(FF))])
    c2=pltpu.make_async_copy(r_.n2c,r_.cola,ld.at[0,4]); c2.start()
    load_job("wqk",1,[(r_.wfull.at[:,pl.ds(0,2*wk)],whole(2*wk))])
    so.finish()
    r_.output[...]=res[...]+boxed(r_.boxo)
    ready("dgate"); c2.wait()
    n2s=r_.cola[...].reshape(N,D//n)
    v_=stage(0,r_.ogate,(D//n,FF))
    for a,b in tiles(FF,512): v_[:,a:b]=dg(n2s,bufa[0:N,a:b],0,0)
    send(0,v_,r_.ogate)
    load_job("wv",0,[(r_.wfull.at[:,pl.ds(2*wk,wv+128)],whole(wv+128))])
    outward.finish()
    for sq in range(seqs):
        fl=[]
        for e in range(2):
            for h in range(heads): fl.append(rbuf[(sq*heads+h)*8+e:(sq*heads+h)*8+e+1])
        fl=jnp.concatenate(fl+[jnp.zeros((-2*heads%8,ll),f32)]*(1 if 2*heads%8 else 0),axis=0)
        dsm[sq*ll:(sq+1)*ll,0:fl.shape[0]]=col_form(fl).astype(bf16)
    gd=[gather(dsm,r_.dsmfull,0),gather(dyq,r_.dyqfull,0)]
    each(gd,"start")
    ready("wqk"); spread(False,bufb,[(dyq.at[:,pl.ds(0,2*wk)],0,2*wk)])
    load_job("dup",1,[(r_.dufull,every(FF))])
    ready("wv")
    def final(j):
        rr=pl.ds(pl.multiple_of(j*256,256),256)
        pbf[:,rr]=(part[:,rr]+dg(dyq[:,2*wk:],bufa[rr,0:wv],1,1)+dg(dsm[...],bufa[rr,wv:wv+128],1,1)).astype(bf16)
    loop(D//256,final)
    split=ShardSplit(zc,pbf,r_.box,*zsems()); split.start()
    load_job("hid",0,[(r_.hidfull,every(FF))])
    gk[0].late()
    ready("dup")
    v_=stage(0,r_.oup,(D//n,FF))
    for a,b in tiles(FF,512): v_[:,a:b]=dg(n2s,bufb[0:N,a:b],0,0)
    send(0,v_,r_.oup)
    n1.finish(); cc.finish(); ca.finish(); gk[0].finish()
    each(gd,"middle")
    cb=pltpu.make_async_copy(r_.cotc,r_.colb,ld.at[1,5]); cb.start()
    ready("hid"); cb.wait()
    cots=r_.colb[...].reshape(N,D//n)
    v_=stage(1,r_.odown,(FF,D//n))
    for a,b in tiles(FF,256): v_[a:b,:]=dg(bufa[0:N,a:b],cots,0,0)
    send(1,v_,r_.odown)
    load_job("dgp",0,[(r_.dgpfull,every(wv))])
    split.finish()
    g=boxed(r_.box)
    sc=scale[...][:,0:1]
    gained=r_.gain[:,F_at]*g
    smalls,totals=r_.smalls,r_.totals
    smalls[s]=jnp.zeros(smalls.shape[1:],f32)
    smalls[s,0:1,0:F]=jnp.sum(g*tok[...].astype(f32)*sc,axis=0,keepdims=True)
    smalls[s,1:2,0:F]=gffn[0]
    smalls[s,2:3,0:DV]=grad_head
    lane=lax.broadcasted_iota(jnp.int32,(1,128),1)
    first=jnp.where(lax.rem(s,copies)==0,1.0,0.0)
    smalls[s,3:4,0:128]=first*(jnp.where(lane==at_head,sl,0.0)+jnp.where(lane==H+at_head,sb,0.0))
    for j in range(4): smalls[s,4+j:5+j,0:CH]=dt[j]
    sa=ShardAll("seq",n,smalls,*qsems()); sa.start()
    inner=shard_sum(2,row_form(gained*tok[...].astype(f32)))
    r_.gtok[...]=gres[...]+sc*(gained-tok[...].astype(f32)*(sc*sc*inner))
    sa.finish()
    t=smalls[0]
    for d in range(1,n): t=t+smalls[d]
    totals[z]=t
    za=ShardAll("shard",zc,totals,*zsems()); za.start()
    cb=pltpu.make_async_copy(r_.attc,r_.colb,ld.at[1,5]); cb.start()
    gk[1].finish()
    load_job("bra",1,[(r_.brafull,every(VW))])
    ready("bra"); cb.wait()
    atts=r_.colb[...].reshape(N,D//n)
    v_=stage(1,r_.oout,(VW,D//n))
    for a,b in tiles(VW,256): v_[a:b,:]=dg(bufb[0:N,a:b],atts,0,0)
    send(1,v_,r_.oout)
    cb=pltpu.make_async_copy(r_.n1c,r_.colb,ld.at[1,5]); cb.start()
    ready("dgp"); cb.wait()
    n1s=r_.colb[...].reshape(N,D//n)
    v_=stage(0,r_.oog,(D//n,wv))
    for a,b in tiles(wv,512): v_[:,a:b]=dg(n1s,bufa[0:N,a:b],0,0)
    send(0,v_,r_.oog)
    each(gd,"late"); za.finish(); each(gd,"finish")
    staged[0].wait(); staged[1].wait()

def layer(n,zc,copies,heads,DK,DV,H,ins):
    names=("tok","cot","gain","hgain","fgain","starts","dlog","dbias","wb","wd","qc","kc","vc","wq","wk","wv","wg","wo","wgate","wup","wdown")
    RN,F=ins[0].shape; D=F*zc; seqs=ins[5].shape[0]; ll=RN//seqs; L=n*ll; NC=L//SPAN; pairs=n//copies
    wk=heads*DK; wv=heads*DV; CH=2*DK+DV; FF=ins[19].shape[1]; N=n*RN; Dc=D//n; W=max(F,CH)
    bw=max(FF,wv+128,2*wk); big=max(D,N)
    specs=[VM]*5+[SM]*3+[VM]*10+[ANY]*3
    outs=[("output",S((RN,F)),VM),("gtok",S((RN,F)),VM),("smalls",S((n,8,W)),VM),("totals",S((zc,8,W)),VM)]
    for name,shape in (("ogate",(Dc,FF)),("oup",(Dc,FF)),("odown",(FF,Dc)),("oout",(wv,Dc)),("oog",(Dc,wv))): outs.append((name,S(shape),ANY))
    for name,shape in (("dyqfull",(N,heads*CH)),("dsmfull",(N,128)),("n1c",(n,RN,Dc)),("cotc",(n,RN,Dc)),("attc",(n,RN,Dc)),("n2c",(n,RN,Dc)),("wfull",(D,heads*CH+128)),("wgfull",(D,wv)),("wofull",(wv,D)),
        ("hidfull",(N,FF)),("dgfull",(N,FF)),("dufull",(N,FF)),("dgpfull",(N,wv)),("brafull",(N,wv))): outs.append((name,S(shape,bf16),ANY))
    V=pltpu.VMEM; sem=pltpu.SemaphoreType.DMA
    scratch=[("scale",V((RN,128),f32)),("ws",V((Dc,128),bf16)),("sbuf",V((D,128),bf16)),("tbuf",V((CH,128),bf16)),("tokfull",V((RN,D),bf16)),("normed",V((RN,D),bf16)),("cotfull",V((RN,D),bf16)),
        ("nfull",V((RN,D),bf16)),("pbf",V((RN,D),bf16)),("outpart",V((RN,D),bf16)),("acc",V((RN,D),f32)),("uv",V((RN,FF),f32)),("gv",V((RN,FF),f32)),("rbuf",V((pairs*8,ll),f32)),("taps",V((4,CH),f32)),
        ("bufa",V((big,bw),bf16)),("bufb",V((big,bw),bf16)),("dw",V((FF,D),bf16)),("u",V((L+16,CH),bf16)),("xr",V((n*8,ll),f32)),("xc",V((L,8),f32)),("q",V((L,DK),bf16)),("k",V((L,DK),bf16)),("v",V((L,DV),bf16)),
        ("s",V((NC,DK,DV),f32)),("w",V((NC,SPAN,DV),f32)),("t",V((NC,SPAN,SPAN),f32)),("qt",V((NC,2*SPAN,DK),bf16)),("mh",V((NC,2,DK,DK),bf16)),("gc",V((NC,8,128),f32)),("ds",V((NC,DK,DV),f32)),
        ("dpre",V((L+8,CH),f32)),("du",V((L,CH),bf16)),("dx",V((L,SPAN),f32)),("do",V((L,DV),bf16)),("dxr",V((n*8,ll),f32)),("gate",V((RN,wv),f32)),("oall",V((RN,wv),bf16)),("branch",V((RN,wv),bf16)),
        ("dob",V((RN,wv),bf16)),("dgp",V((RN,wv),bf16)),("dsm",V((RN,128),bf16)),("res",V((RN,F),f32)),("gres",V((RN,F),f32)),("nloc",V((RN,F),bf16)),("box",V((zc,RN,F),bf16)),("boxo",V((zc,RN,F),bf16)),
        ("hidden",V((RN,FF),bf16)),("dgate",V((RN,FF),bf16)),("dup",V((RN,FF),bf16)),("sums",V((3*zc,8,RN),f32)),("cola",V((n,RN,Dc),bf16)),("colb",V((n,RN,Dc),bf16)),("sta",V((Dc,max(FF,wv)),f32)),("stb",V((max(FF,wv),Dc),f32)),
        ("zsend",sem((16,zc))),("zrecv",sem((16,zc))),("qsend",sem((6,n))),("qrecv",sem((6,n))),("gsend",sem((16,links(n)))),("grecv",sem((16,links(n)))),("gloc",sem((16,))),("isend",sem((4,n))),("irecv",sem((4,n))),("i2send",sem((1,n))),("i2recv",sem((1,n))),
        ("osend",sem((1,pairs))),("orecv",sem((1,pairs))),("o2send",sem((4,pairs))),("o2recv",sem((4,pairs))),("ld",sem((2,6))),("stsem",sem((2,))),("free",pltpu.SemaphoreType.REGULAR)]
    all_names=names+tuple(o[0] for o in outs)+tuple(x[0] for x in scratch)
    r=pl.pallas_call(functools.partial(layer_kernel,(n,zc,copies,heads,DK,DV,H),all_names),name="layer",out_shape=tuple(o[1] for o in outs),in_specs=specs,out_specs=tuple(o[2] for o in outs),
        scratch_shapes=[x[1] for x in scratch],compiler_params=pltpu.CompilerParams(collective_id=1,has_side_effects=True,vmem_limit_bytes=63*2**20))(*ins)
    return SimpleNamespace(**{o[0]:x for o,x in zip(outs,r)})


def last_kernel(n,copies,heads,DK,DV,F,H,n1c,dyq,dsm,smalls,totals,*refs):
    moved=refs[:7]; oq,ok,ov,ob,od,qc,kc,vc,onorm,offn,ohead,olog,obias=refs[7:20]; moved_out=refs[20:27]; buf,sem,msem=refs[27:30]; held=refs[30:]
    step=buf.shape[1]//4
    fetch=[pltpu.make_async_copy(a,b,msem.at[j]) for j,(a,b) in enumerate(zip(moved,held))]
    for c in fetch: c.start()
    jobs=[pltpu.make_async_copy(dyq.at[:,pl.ds(j*step,step)],buf.at[:,pl.ds(j*step,step)],sem.at[j]) for j in range(4)]
    for c in jobs: c.start()
    moves=[pltpu.make_async_copy(a,b,msem.at[j]) for j,(a,b) in enumerate(zip(held,moved_out))]
    for f,c in zip(fetch,moves): f.wait(); c.start()
    n1=n1c[...].reshape(n1c.shape[0]*n1c.shape[1],n1c.shape[2])
    sm=dg(dsm[...],n1,0,0)
    ob[...]=sm[0:heads]; od[...]=sm[heads:2*heads]
    wk=heads*DK
    got=0
    for ref,start in ((oq,0),(ok,wk),(ov,2*wk)):
        for a in range(0,ref.shape[1],256):
            b=min(a+256,ref.shape[1])
            while got*step<start+b: jobs[got].wait(); got+=1
            ref[:,a:b]=dg(n1,buf[:,start+a:start+b],0,0)
    zc=totals.shape[0]
    for z in range(zc):
        onorm[0:1,z*F:(z+1)*F]=totals[z,0:1,0:F]
        offn[0:1,z*F:(z+1)*F]=totals[z,1:2,0:F]
    t=totals[0]
    for z in range(1,zc): t=t+totals[z]
    ohead[...]=t[2:3,0:DV]
    olog[...]=t[3:4,0:H]; obias[...]=t[3:4,H:2*H]
    s=lax.axis_index("seq")
    head=lax.div(s*heads,n)
    taps=0.0
    for sq in range(n//copies//heads): taps=taps+smalls[(sq*heads+head)*copies]
    cq,cv=qc.shape[1],vc.shape[1]
    for part in range(n//heads):
        @pl.when(lax.rem(s,n//heads)==part)
        def _():
            qc[...]=taps[4:8,part*cq:(part+1)*cq]
            kc[...]=taps[4:8,DK+part*cq:DK+(part+1)*cq]
            vc[...]=taps[4:8,2*DK+part*cv:2*DK+(part+1)*cv]
    for c in moves: c.wait()
def last(n,copies,heads,DK,DV,F,H,n1c,dyq,dsm,smalls,totals,cq,cv,moved):
    D=F*totals.shape[0]; Dc=n1c.shape[2]
    r=pl.pallas_call(functools.partial(last_kernel,n,copies,heads,DK,DV,F,H),name="last",
      out_shape=(S((Dc,heads*DK)),S((Dc,heads*DK)),S((Dc,heads*DV)),S((heads,Dc)),S((heads,Dc)),S((4,cq)),S((4,cq)),S((4,cv)),S((1,D)),S((1,D)),S((1,DV)),S((1,H)),S((1,H)))+tuple(S(x.shape) for x in moved),
      in_specs=[VM,ANY,VM,VM,VM]+[ANY]*7,out_specs=(VM,)*13+(ANY,)*7,scratch_shapes=[pltpu.VMEM(dyq.shape,bf16),pltpu.SemaphoreType.DMA((4,)),pltpu.SemaphoreType.DMA((7,))]+[pltpu.VMEM(x.shape,f32) for x in moved],
      compiler_params=pltpu.CompilerParams(vmem_limit_bytes=56*2**20))(n1c,dyq,dsm,smalls,totals,*moved)
    return r


def per_device(
    tokens, doc_starts, norm_gain, query_weight, key_weight, value_weight, outgate_weight,
    beta_weight, decay_weight, query_conv, key_conv, value_conv, decay_log, decay_bias, head_gain,
    output_weight, ffn_gain, gate_weight, up_weight, down_weight, cotangent,
):
    seq_count, local_len, feature_part = tokens.shape
    row_count = seq_count * local_len
    shard_count = lax.axis_size("shard")
    seq_devices = lax.axis_size("seq")
    head_count = beta_weight.shape[1]
    key_dim = query_weight.shape[1] // head_count
    value_dim = value_weight.shape[1] // head_count
    pairs = seq_count * head_count
    copies = seq_devices // pairs
    flat = lambda x: x.reshape(row_count, x.shape[2])
    tokens_flat, cot_flat = flat(tokens), flat(cotangent)
    head_row, norm_row, ffn_row = head_gain[None], norm_gain[None], ffn_gain[None]
    ran = layer(
        seq_devices, shard_count, copies, head_count, key_dim, value_dim, decay_log.shape[0],
        (
            tokens_flat, cot_flat, norm_row, head_row, ffn_row, doc_starts, decay_log, decay_bias, beta_weight.T,
            decay_weight.T, query_conv.T, key_conv.T, value_conv.T, query_weight, key_weight, value_weight, outgate_weight,
            output_weight, gate_weight, up_weight, down_weight,
        ),
    )
    (
        out_query, out_key, out_value, out_beta, out_decay, out_qconv, out_kconv, out_vconv, out_norm, out_ffn, out_head,
        out_log, out_bias, output, grad_tokens, out_gate, out_up, out_down, out_output, out_outgate,
    ) = last(
        seq_devices, copies, head_count, key_dim, value_dim, feature_part, decay_log.shape[0], ran.n1c, ran.dyqfull,
        ran.dsmfull, ran.smalls, ran.totals, query_conv.shape[0], value_conv.shape[0],
        (ran.output, ran.gtok, ran.ogate, ran.oup, ran.odown, ran.oout, ran.oog),
    )
    shape3 = (seq_count, local_len, feature_part)
    return (
        output.reshape(shape3), grad_tokens.reshape(shape3), out_norm[0], out_query, out_key, out_value, out_outgate,
        out_beta.T, out_decay.T, out_qconv.T, out_kconv.T, out_vconv.T, out_log[0], out_bias[0], out_head[0], out_output,
        out_ffn[0], out_gate, out_up, out_down,
    )


def solution(mesh):
    P = PartitionSpec
    rows, cols = P("seq", "shard"), P("shard", "seq")
    both, acts = P(("shard", "seq"), None), P(None, "seq", "shard")
    return jax.shard_map(
        per_device,
        mesh=mesh,
        in_specs=(acts, P(), P()) + (rows,) * 6 + (both,) * 3 + (P(), P(), P(), cols, P(), rows, rows, cols, acts),
        out_specs=(acts, acts, P()) + (rows,) * 6 + (both,) * 3 + (P(), P(), P(), cols, P(), rows, rows, cols),
        check_vma=False,
    )
```

```python
import functools
from types import SimpleNamespace
import jax, jax.numpy as jnp
from jax import lax
from jax.experimental import pallas as pl
from jax.experimental.pallas import tpu as pltpu
from jax.sharding import PartitionSpec
f32=jnp.float32; bf16=jnp.bfloat16
SPAN=128
EPSILON=1e-6
HI=lax.Precision.HIGHEST

def dg(a,b,ca=1,cb=0):
    return lax.dot_general(a,b,(((ca,),(cb,)),((),())),preferred_element_type=f32)
def halves(x):
    h=x.astype(bf16)
    return h,(x-h.astype(f32)).astype(bf16)
def mm3(a,b,ca=1,cb=0):
    ah,al=halves(a); bh,bl=halves(b)
    return dg(ah,bh,ca,cb)+(dg(al,bh,ca,cb)+dg(ah,bl,ca,cb))
def mm1(a,b,ca=1,cb=0):
    return dg(a.astype(bf16),b.astype(bf16),ca,cb)
def mmx(a,b,ca=1,cb=0):
    return lax.dot_general(a,b,(((ca,),(cb,)),((),())),preferred_element_type=f32,precision=HI)

def square_masks():
    i=lax.broadcasted_iota(jnp.int32,(SPAN,SPAN),0); j=lax.broadcasted_iota(jnp.int32,(SPAN,SPAN),1)
    return i,j
def positions(base,rows,cols,axis):
    return base+lax.broadcasted_iota(jnp.int32,(rows,cols),axis)
class Row:
    def __init__(self,ref,row):
        self.ref=ref; self.row=row; self.shape=ref.shape[1:]
    def __getitem__(self,e):
        return self.ref[self.row,e]

def doc_count(starts,pos):
    n=jnp.zeros(pos.shape,jnp.int32)
    for e in range(starts.shape[0]):
        n=n+jnp.where(starts[e]<=pos,1,0)
    return n
def doc_age(starts,pos):
    s=jnp.zeros(pos.shape,jnp.int32)
    for e in range(starts.shape[0]):
        s=jnp.where(starts[e]<=pos,starts[e],s)
    return pos-s
def count_at(starts,p):
    n=jnp.int32(0)
    for e in range(starts.shape[0]):
        n=n+jnp.where(starts[e]<=p,1,0)
    return n
def sigmoid(x):
    return 1.0/(1.0+jnp.exp(-x))
def softplus(x):
    return jnp.maximum(x,0.0)+jnp.log(1.0+jnp.exp(-jnp.abs(x)))

def inverses(blocks_a,t_ref):
    i,j=square_masks()
    eye=jnp.where(i==j,1.0,0.0)
    blocks=range(t_ref.shape[0])
    for n in blocks: t_ref[n]=eye-jnp.where((i//2)==(j//2),blocks_a(n),0.0)
    size=2
    while size<SPAN:
        part=((i//(2*size))==(j//(2*size)))&((i//size)!=(j//size))
        x=[dg(jnp.where(part,blocks_a(n),0.0).astype(bf16),t_ref[n].astype(bf16)).astype(bf16) for n in blocks]
        for n in blocks: t_ref[n]=t_ref[n]-dg(t_ref[n].astype(bf16),x[n])
        size*=2
    for n in blocks:
        Tb=t_ref[n].astype(bf16); Ah,Al=halves(blocks_a(n))
        rest=eye-Tb.astype(f32)-(dg(Ah,Tb)+dg(Al,Tb))
        t_ref[n]=Tb.astype(f32)+dg(Tb,rest.astype(bf16))

def position_rows(raw,starts,base,rate,bias):
    r=raw.shape[1]
    row=lax.broadcasted_iota(jnp.int32,(8,r),0)
    g=-rate*softplus(raw[1:2]+bias)
    i=lax.broadcasted_iota(jnp.int32,(r,r),0); j=lax.broadcasted_iota(jnp.int32,(r,r),1)
    G=mmx(jnp.broadcast_to(g,(8,r)),jnp.where((i<=j)&((i//SPAN)==(j//SPAN)),1.0,0.0))
    docs=doc_count(starts,positions(base,8,r,1)).astype(f32)
    out=jnp.where(row==0,sigmoid(raw[0:1]),0.0)
    for k,x in ((1,g),(2,G),(3,raw[1:2]),(4,docs)): out=jnp.where(row==k,x,out)
    return out

def span_terms(n,q,k,starts,xc,xr):
    i,j=square_masks()
    before=count_at(starts,n*SPAN-1).astype(f32)
    wide=lambda c: jnp.broadcast_to(c,(SPAN,128))
    beta=wide(xc[:,0:1]); G=wide(xc[:,2:3]); docs=wide(xc[:,4:5])
    incl=(i>=j)&(docs[:,:SPAN]==xr[4:5])
    D=jnp.where(incl,jnp.exp(jnp.where(incl,G[:,:SPAN]-xr[2:3],0.0)),0.0)
    gam=jnp.where(docs==before,jnp.exp(G),0.0)
    end=jnp.where(docs==docs[SPAN-1:SPAN],jnp.exp(G[SPAN-1:SPAN]-G),0.0)
    KK=dg(k,k,1,1); QK=dg(q,k,1,1)
    return beta,D,gam,end,KK,QK,i,j


SM=pl.BlockSpec(memory_space=pltpu.SMEM); VM=pl.BlockSpec(memory_space=pltpu.VMEM)
def S(shape,dt=f32): return jax.ShapeDtypeStruct(shape,dt)


MESH=pl.DeviceIdType.MESH
ANY=pl.BlockSpec(memory_space=pl.ANY)

def flip(s,bit):
    return s+bit-2*bit*lax.rem(lax.div(s,bit),2)

def flips(s,mask):
    bit=1
    while bit<=mask:
        if mask&bit: s=flip(s,bit)
        bit*=2
    return s

def greet(n,zc):
    s=lax.axis_index("seq"); z=lax.axis_index("shard")
    bar=pltpu.get_barrier_semaphore()
    for d in range(1,n):
        pl.semaphore_signal(bar,inc=1,device_id={"seq":lax.rem(s+d,n)},device_id_type=MESH)
    for d in range(1,zc):
        pl.semaphore_signal(bar,inc=1,device_id={"shard":lax.rem(z+d,zc)},device_id_type=MESH)
    pl.semaphore_wait(bar,n-1+zc-1)

def links(n):
    return 8 if n==8 else n

class SeqGather:
    def __init__(self,n,src,dst,axis,sems,c0=0):
        self.n=n; self.src=src; self.dst=dst; self.axis=axis; self.send,self.recv,self.loc=sems
        self.R,self.C=src.shape
        self.r0=0; self.nr=self.R; self.c0=c0
        self.s=lax.axis_index("seq")
        self.open=[]
    def slot(self,t,a,b):
        if self.axis==0:
            return self.dst.at[pl.ds(pl.multiple_of(t*self.R+self.r0+a,16),b-a),pl.ds(self.c0,self.C)]
        return self.dst.at[pl.ds(self.r0+a,b-a),pl.ds(pl.multiple_of(t*self.C,128),self.C)]
    def copy(self,src,t,a,b,k,to):
        c=pltpu.make_async_remote_copy(src_ref=src,dst_ref=self.slot(t,a,b),send_sem=self.send.at[k],recv_sem=self.recv.at[k],device_id={"seq":to},device_id_type=MESH)
        c.start()
        return c
    def pass_on(self,t,a,b,k,to):
        return self.copy(self.slot(t,a,b),t,a,b,k,to)
    def start(self):
        s=self.s; nr=self.nr
        mine=self.src.at[pl.ds(self.r0,nr),:]
        self.own=pltpu.make_async_copy(mine,self.slot(s,0,nr),self.loc)
        self.own.start()
        masks=(2,4) if self.n==8 else range(2,self.n,2)
        self.direct=[self.copy(mine,s,0,nr,i+1,flips(s,m)) for i,m in enumerate(masks)]
        self.open.append(self.copy(mine,s,0,nr,0,flip(s,1)))
    def middle(self):
        s=self.s; nr=self.nr; h=nr//2
        if self.n!=8: return
        x,y=flip(s,2),flip(s,4)
        self.direct[0].wait_recv()
        fa=self.pass_on(x,0,h,3,y)
        self.open.append(self.pass_on(x,0,nr,5,flip(s,1)))
        self.direct[1].wait_recv()
        fb=self.pass_on(y,h,nr,4,x)
        self.open.append(self.pass_on(y,0,nr,6,flip(s,1)))
        self.diag=(fa,fb)
    def late(self):
        s=self.s; nr=self.nr
        if self.n==8:
            for f in self.diag: f.wait_recv()
            self.open.append(self.pass_on(flips(s,6),0,nr,7,flip(s,1)))
            for f in self.diag: f.wait_send()
        else:
            for i,m in enumerate(range(2,self.n,2)):
                self.direct[i].wait_recv()
                self.open.append(self.pass_on(flips(s,m),0,nr,self.n//2+i,flip(s,1)))
        for f in self.direct: f.wait_send()
    def finish(self):
        for f in self.open: f.wait()
        self.own.wait()

class ShardGather:
    def __init__(self,zc,src,dst,send,recv):
        self.zc=zc; self.src=src; self.dst=dst; self.send=send; self.recv=recv
        self.z=lax.axis_index("shard"); self.C=src.shape[1]
    def slot(self):
        return self.dst.at[:,pl.ds(pl.multiple_of(self.z*self.C,128),self.C)]
    def start(self):
        self.own=pltpu.make_async_copy(self.src,self.slot(),self.recv.at[0]); self.own.start()
        self.cs=[]
        for d in range(1,self.zc):
            c=pltpu.make_async_remote_copy(src_ref=self.src,dst_ref=self.slot(),send_sem=self.send.at[d],recv_sem=self.recv.at[d],device_id={"shard":lax.rem(self.z+d,self.zc)},device_id_type=MESH)
            c.start(); self.cs.append(c)
    def finish(self):
        for c in self.cs: c.wait()
        self.own.wait()

class ShardSplit:
    def __init__(self,zc,src,box,send,recv):
        self.zc=zc; self.src=src; self.box=box; self.send=send; self.recv=recv
        self.z=lax.axis_index("shard"); self.C=box.shape[2]
    def start(self):
        C=self.C
        self.own=pltpu.make_async_copy(self.src.at[:,pl.ds(pl.multiple_of(self.z*C,128),C)],self.box.at[0],self.recv.at[0]); self.own.start()
        self.cs=[]
        for d in range(1,self.zc):
            to=lax.rem(self.z+d,self.zc)
            c=pltpu.make_async_remote_copy(src_ref=self.src.at[:,pl.ds(pl.multiple_of(to*C,128),C)],dst_ref=self.box.at[d],send_sem=self.send.at[d],recv_sem=self.recv.at[d],device_id={"shard":to},device_id_type=MESH)
            c.start(); self.cs.append(c)
    def finish(self):
        for c in self.cs: c.wait()
        self.own.wait()

class ShardAll:
    def __init__(self,axis,n,box,send,recv):
        self.axis=axis; self.n=n; self.box=box; self.send=send; self.recv=recv; self.me=lax.axis_index(axis)
    def start(self):
        self.cs=[]
        for d in range(1,self.n):
            c=pltpu.make_async_remote_copy(src_ref=self.box.at[self.me],dst_ref=self.box.at[self.me],send_sem=self.send.at[d],recv_sem=self.recv.at[d],device_id={self.axis:lax.rem(self.me+d,self.n)},device_id_type=MESH)
            c.start(); self.cs.append(c)
    def finish(self):
        for c in self.cs: c.wait()

class ColumnSplit:
    def __init__(self,n,src,dst,send,recv):
        self.n=n; self.src=src; self.dst=dst; self.send=send; self.recv=recv
        self.s=lax.axis_index("seq"); self.C=dst.shape[1]; self.R=src.shape[0]
    def start(self):
        n,s,C,R=self.n,self.s,self.C,self.R
        to_rows=self.dst.at[pl.ds(pl.multiple_of(s*R,16),R),:]
        block=lambda t: self.src.at[:,pl.ds(pl.multiple_of(t*C,128),C)]
        self.own=pltpu.make_async_copy(block(s),to_rows,self.recv.at[0]); self.own.start()
        self.cs=[]
        for d in range(1,n):
            t=lax.rem(s+d,n)
            c=pltpu.make_async_remote_copy(src_ref=block(t),dst_ref=to_rows,send_sem=self.send.at[d],recv_sem=self.recv.at[d],device_id={"seq":t},device_id_type=MESH)
            c.start(); self.cs.append(c)
    def finish(self):
        for c in self.cs: c.wait()
        self.own.wait()

class ToPairs:
    def __init__(self,n,copies,heads,local_len,src,rows_src,dst,rows_dst,DK,DV,send,recv,off=0):
        self.cs=[]
        self.__dict__.update(n=n,copies=copies,heads=heads,ll=local_len,src=src,rows_src=rows_src,dst=dst,rows_dst=rows_dst,DK=DK,DV=DV,send=send,recv=recv,off=off)
    def parts(self,t):
        s=lax.axis_index("seq"); ll,DK,DV,heads=self.ll,self.DK,self.DV,self.heads
        pair=lax.div(t,self.copies); seq=lax.div(pair,heads); head=lax.rem(pair,heads)
        rows=pl.ds(pl.multiple_of(seq*ll,ll),ll); to=pl.ds(pl.multiple_of(s*ll+self.off,16),ll)
        if self.rows_src is None:
            return [(a.at[rows,pl.ds(pl.multiple_of(head*DV,128),DV)],b.at[to,:]) for a,b in zip(self.src,self.dst)]
        wk=heads*DK
        out=[]
        for start,width,at in ((0,DK,0),(wk,DK,DK),(2*wk,DV,2*DK)):
            out.append((self.src.at[rows,pl.ds(pl.multiple_of(start+head*width,128),width)],self.dst.at[to,pl.ds(at,width)]))
        out.append((self.rows_src.at[pl.ds(pl.multiple_of(pair*8,8),8),:],self.rows_dst.at[pl.ds(pl.multiple_of(s*8,8),8),:]))
        return out
    def start(self,i):
        s=lax.axis_index("seq")
        for d in range(self.n):
            t=lax.rem(s+d,self.n)
            a,b=self.parts(t)[i]
            if d==0: c=pltpu.make_async_copy(a,b,self.recv.at[i,0])
            else: c=pltpu.make_async_remote_copy(src_ref=a,dst_ref=b,send_sem=self.send.at[i,d],recv_sem=self.recv.at[i,d],device_id={"seq":t},device_id_type=MESH)
            c.start(); self.cs.append(c)
    def finish(self):
        for c in self.cs: c.wait()

class FromPairs:
    def __init__(self,n,copies,heads,local_len,items,send,recv):
        self.__dict__.update(n=n,copies=copies,heads=heads,items=items,send=send,recv=recv)
    def start(self):
        s=lax.axis_index("seq"); pairs=self.n//self.copies; p=lax.div(s,self.copies); r=lax.rem(s,self.copies)
        seq=lax.div(p,self.heads); head=lax.rem(p,self.heads); self.cs=[]
        for d in range(pairs):
            t=lax.rem(p+d,pairs)*self.copies+r
            for i,(src,at,dst,to) in enumerate(self.items):
                a=src.at[at(t)]; b=dst.at[to(seq,head)]
                if d==0: c=pltpu.make_async_copy(a,b,self.recv.at[i,0])
                else: c=pltpu.make_async_remote_copy(src_ref=a,dst_ref=b,send_sem=self.send.at[i,d],recv_sem=self.recv.at[i,d],device_id={"seq":t},device_id_type=MESH)
                c.start(); self.cs.append(c)
    def finish(self):
        for c in self.cs: c.wait()

def flat_form(cols):
    r=cols.shape[0]
    i=lax.broadcasted_iota(jnp.int32,(r,r),0); j=lax.broadcasted_iota(jnp.int32,(r,r),1)
    return mmx(cols,jnp.where(i==j,1.0,0.0),0,0)

class SharedColumns:
    def __init__(self,n,zc,src,dst,sems):
        self.n=n; self.zc=zc; self.src=src; self.dst=dst; self.send,self.recv,self.zsend,self.zrecv=sems
        self.s=lax.axis_index("seq"); self.z=lax.axis_index("shard"); self.C=dst.shape[2]; self.q=src.shape[0]//zc
    def start(self):
        rows=pl.ds(pl.multiple_of(self.z*self.q,16),self.q)
        block=lambda t: self.src.at[rows,pl.ds(pl.multiple_of(t*self.C,128),self.C)]
        self.cs=[]
        for d in range(self.n):
            t=lax.rem(self.s+d,self.n)
            if d==0: c=pltpu.make_async_copy(block(t),self.dst.at[self.s,rows,:],self.recv.at[0])
            else: c=pltpu.make_async_remote_copy(src_ref=block(t),dst_ref=self.dst.at[self.s,rows,:],send_sem=self.send.at[d],recv_sem=self.recv.at[d],device_id={"seq":t},device_id_type=MESH)
            c.start(); self.cs.append(c)
    def middle(self):
        for c in self.cs: c.wait()
        strip=self.dst.at[:,pl.ds(pl.multiple_of(self.z*self.q,16),self.q),:]
        self.cs=[]
        for d in range(1,self.zc):
            c=pltpu.make_async_remote_copy(src_ref=strip,dst_ref=strip,send_sem=self.zsend.at[d],recv_sem=self.zrecv.at[d],device_id={"shard":lax.rem(self.z+d,self.zc)},device_id_type=MESH)
            c.start(); self.cs.append(c)
    def finish(self):
        for c in self.cs: c.wait()

def row_form(cols):
    return mmx(jnp.ones((8,cols.shape[1]),f32),cols,1,1)

def col_form(rows):
    r=rows.shape[1]
    i=lax.broadcasted_iota(jnp.int32,(r,r),0); j=lax.broadcasted_iota(jnp.int32,(r,r),1)
    return mmx(jnp.where(i==j,1.0,0.0),rows,1,1)

def gathers(n,pairs,sems):
    send,recv,loc=sems
    return [SeqGather(n,src,dst,axis,(send.at[i],recv.at[i],loc.at[i]),*c0) for i,(src,dst,axis,*c0) in enumerate(pairs)]
def gather_sems(n,k):
    return [pltpu.SemaphoreType.DMA((k,links(n))),pltpu.SemaphoreType.DMA((k,links(n))),pltpu.SemaphoreType.DMA((k,))]
def pair_sems(k):
    return [pltpu.SemaphoreType.DMA((k,)),pltpu.SemaphoreType.DMA((k,))]
def each(ops,name):
    for o in ops: getattr(o,name)()


def conv_pre(u,taps,age,base,rows):
    window=u[pl.ds(base,rows+16),:].astype(f32)
    pre=window[16:]*taps[3:4]
    for back in range(1,4):
        ok=jnp.where(age>=back,1.0,0.0)
        pre=pre+window[16-back:16-back+rows]*ok*taps[3-back:4-back]
    return pre,window

def tiles(width,step): return [(a,min(a+step,width)) for a in range(0,width,step)]

def layer_kernel(cfg,names,*refs):
    n,zc,copies,heads,DK,DV,H=cfg
    r_=SimpleNamespace(**dict(zip(names,refs)))
    tok,cot=r_.tok,r_.cot
    RN,F=tok.shape; D=F*zc; seqs=r_.starts.shape[0]; ll=RN//seqs; L=n*ll; NC=L//SPAN; per=ll//SPAN
    wk=heads*DK; wv=heads*DV; CH=2*DK+DV; FF=r_.wup.shape[1]; N=n*RN; VW=wv
    s=lax.axis_index("seq"); z=lax.axis_index("shard")
    pair=lax.div(s,copies); my_head=lax.rem(pair,heads); at_head=z*heads+my_head
    starts=Row(r_.starts,lax.div(pair,heads))
    count=[0,0,0]
    def zsems():
        count[0]+=1; return r_.zsend.at[count[0]-1],r_.zrecv.at[count[0]-1]
    def qsems():
        count[1]+=1; return r_.qsend.at[count[1]-1],r_.qrecv.at[count[1]-1]
    def gather(src,dst,axis,c0=0):
        count[2]+=1; i=count[2]-1
        return SeqGather(n,src,dst,axis,(r_.gsend.at[i],r_.grecv.at[i],r_.gloc.at[i]),c0)
    def span(m): return pl.ds(pl.multiple_of(m*SPAN,SPAN),SPAN)
    def loop(count_,body,unroll=1): lax.fori_loop(0,count_,lambda i,c: (body(i),c)[1],0,unroll=unroll)
    normed,scale=r_.normed,r_.scale
    pbuf=r_.tokfull.at[:,pl.ds(0,heads*CH)]
    gw_=r_.bufa.at[pl.ds(0,D),pl.ds(0,FF)]; uw_=r_.bufb.at[pl.ds(0,D),pl.ds(0,FF)]; dw_=r_.dw
    wbuf=r_.bufb
    gv=r_.gv; uv=r_.uv
    cotfull,oall,branch,pbf,u_ref,taps_ref=r_.cotfull,r_.oall,r_.branch,r_.pbf,r_.u,r_.taps
    xr_ref,xc_ref,q_ref,k_ref,v_ref,s_ref,w_ref,t_ref,qt_ref,mh_ref,gc_ref=r_.xr,r_.xc,r_.q,r_.k,r_.v,r_.s,r_.w,r_.t,r_.qt,r_.mh,r_.gc
    gate_ref,rbuf,dpre,du_ref,dx_ref,do_ref,dxr,ds_ref=r_.gate,r_.rbuf,r_.dpre,r_.du,r_.dx,r_.do,r_.dxr,r_.ds
    heads_v=pl.ds(0,DV); rest_v=pl.ds(DV,DV)

    greet(n,zc)
    zt=ShardGather(zc,tok,r_.tokfull,*zsems()); zt.start()
    put=lambda x,first: dg(x[...],jnp.where(lax.broadcasted_iota(jnp.int32,(x.shape[0],128),0)+first==lax.broadcasted_iota(jnp.int32,(x.shape[0],128),1),1.0,0.0).astype(bf16),0,0)
    ws=r_.ws
    ws[...]=(put(r_.wb,0)+put(r_.wd,heads)).astype(bf16)
    at_row=0
    for x in (r_.qc,r_.kc,r_.vc):
        ws[at_row:at_row+x.shape[1]]=(ws[at_row:at_row+x.shape[1]].astype(f32)+put(x,2*heads)).astype(bf16)
        at_row+=x.shape[1]
    ws_all=(ws,r_.wq,r_.wk,r_.wv); at=(wk*2+wv,0,wk,wk*2)
    gw=[gather(w,r_.wfull,0,a) for w,a in zip(ws_all,at)]
    each(gw,"start")
    u_ref[0:16]=jnp.zeros((16,CH),bf16)
    rbuf[...]=jnp.zeros(rbuf.shape,f32)
    dx_ref[...]=jnp.zeros(dx_ref.shape,f32)
    rate=jnp.exp(jnp.full((1,1),r_.dlog[at_head],f32)); bias=r_.dbias[at_head]
    each(gw,"middle")
    gb=[gather(r_.wg,r_.wgfull,0),gather(r_.wo,r_.wofull,1),gather(r_.wgate,gw_,0)]
    gu=[gather(r_.wup,uw_,0),gather(r_.wdown,dw_,1)]
    gb[0].start()
    zt.finish()
    zk=ShardGather(zc,cot,cotfull,*zsems()); zk.start()
    def norm(c):
        r=pl.ds(pl.multiple_of(c*32,32),32)
        x=r_.tokfull[r,:].astype(f32)
        sc=lax.rsqrt(jnp.sum(x*x,axis=1,keepdims=True)/D+EPSILON)
        normed[r,:]=(x*sc*r_.gain[...]).astype(bf16)
        scale[r,:]=jnp.broadcast_to(sc,(32,128))
    loop(RN//32,norm)
    n1=SharedColumns(n,zc,normed,r_.n1c,(*qsems(),*zsems())); n1.start()
    inward=ToPairs(n,copies,heads,ll,pbuf,rbuf,u_ref,xr_ref,DK,DV,r_.isend,r_.irecv,16)
    for i,g in enumerate(gw):
        g.late(); g.finish()
        width=ws_all[i].shape[1]
        buf=r_.sbuf if i==0 else wbuf.at[pl.ds(0,D),pl.ds(0,width)]
        c=pltpu.make_async_copy(r_.wfull.at[:,pl.ds(at[i],width)],buf,r_.ld.at[0,0]); c.start(); c.wait()
        if i==0:
            small=jnp.dot(normed[...],r_.sbuf[...],preferred_element_type=f32)
            for sq in range(seqs):
                fl=flat_form(small[sq*ll:(sq+1)*ll,0:8*((2*heads+7)//8)])
                for h in range(heads):
                    base=(sq*heads+h)*8
                    rbuf[base:base+1]=fl[h:h+1]
                    rbuf[base+1:base+2]=fl[heads+h:heads+h+1]
            cq=wk//n; cv=wv//n; step=D//n
            for kind,(width_c,total,skip) in enumerate(((cq,DK,0),(cq,DK,cq),(cv,DV,2*cq))):
                for j in range(total//width_c):
                    dev=my_head*(total//width_c)+j
                    to=(0,DK,2*DK)[kind]+j*width_c
                    r_.tbuf[to:to+width_c]=r_.sbuf[pl.ds(pl.multiple_of(dev*step+skip,16),width_c),:]
            ident=jnp.where(lax.broadcasted_iota(jnp.int32,(CH,CH),0)==lax.broadcasted_iota(jnp.int32,(CH,CH),1),1.0,0.0).astype(bf16)
            tt=dg(r_.tbuf[...],ident,0,0)
            taps_ref[...]=tt[2*heads:2*heads+4]
        else:
            def column(j,i=i):
                pbuf[:,pl.ds(pl.multiple_of(at[i]+j*256,128),256)]=jnp.dot(normed[...],wbuf[0:D,pl.ds(pl.multiple_of(j*256,256),256)],preferred_element_type=f32).astype(bf16)
            loop(width//256,column)
        inward.start((3,0,1,2)[i])
    gb[1].start()
    zk.finish()
    cc=SharedColumns(n,zc,cotfull,r_.cotc,(*qsems(),*zsems())); cc.start()
    n1.middle()
    gb[0].middle()
    inward.finish()
    gb[2].start()
    cc.middle()

    def turn(m):
        r=pl.ds(pl.multiple_of(m*8,8),8)
        x=position_rows(xr_ref[r,:],starts,m*ll,rate,bias)
        xr_ref[r,:]=x
        xc_ref[pl.ds(pl.multiple_of(m*ll,ll),ll),:]=col_form(x)
    loop(n,turn,4)
    taps=taps_ref[...]
    R=128
    def conv(c):
        base=pl.multiple_of(c*R,R)
        age=doc_age(starts,positions(base,R,128,0))[:,0:1]
        pre,unused=conv_pre(u_ref,taps,age,base,R)
        act=pre*sigmoid(pre)
        rows=pl.ds(base,R)
        aq=act[:,:DK]; ak=act[:,DK:2*DK]
        q_ref[rows,:]=(aq*lax.rsqrt(jnp.sum(aq*aq,axis=1,keepdims=True)+EPSILON)*DK**-0.5).astype(bf16)
        k_ref[rows,:]=(ak*lax.rsqrt(jnp.sum(ak*ak,axis=1,keepdims=True)+EPSILON)).astype(bf16)
        v_ref[rows,:]=act[:,2*DK:].astype(bf16)
    loop(L//R,conv)
    gb[1].middle()
    gu[1].start()
    kcol,pcol,ecol=pl.ds(0,DK),pl.ds(DK,SPAN),pl.ds(DK+SPAN,DK)
    def local(m):
        xr=xr_ref[pl.ds(pl.multiple_of(m*8,8),8),:]
        for e in range(per):
            b=m*per+e; rows=span(b)
            q=q_ref[rows,:]; k=k_ref[rows,:]; v=v_ref[rows,:]
            beta,Dm,gam,end,KK,QK,i,j=span_terms(b,q,k,starts,xc_ref[rows,:],xr[:,e*SPAN:(e+1)*SPAN])
            dx_ref[rows,0:SPAN]=jnp.where(i>j,beta[:,:SPAN]*Dm*KK,0.0)
            kf=k.astype(f32)
            dpre[rows,rest_v]=jnp.concatenate([beta]*(DV//128),axis=1)*v.astype(f32)
            du_ref[rows,kcol]=((beta*gam)*kf).astype(bf16)
            du_ref[rows,pcol]=(QK*Dm).astype(bf16)
            qt_ref[b,0:SPAN]=(gam*q.astype(f32)).astype(bf16)
            du_ref[rows,ecol]=(end*kf).astype(bf16)
            gc_ref[b]=jnp.broadcast_to(gam[SPAN-1:SPAN],(8,128))
    loop(n,local,4)
    inverses(lambda b: dx_ref[b*SPAN:(b+1)*SPAN,0:SPAN],t_ref)
    def solve(b):
        rows=span(b)
        Th,Tl=halves(t_ref[b]); Vh,Vl=halves(dpre[rows,rest_v]); bk=du_ref[rows,kcol]
        U=dg(Th,Vh)+(dg(Tl,Vh)+dg(Th,Vl)); Wk=dg(Th,bk)+dg(Tl,bk)
        Ub,Ul=halves(U); Wb,Wl=halves(Wk); Pm=du_ref[rows,pcol]; ek=du_ref[rows,ecol]
        dpre[rows,heads_v]=dg(Pm,Ub)
        w_ref[b]=U
        qt_ref[b,0:SPAN]=(qt_ref[b,0:SPAN].astype(f32)-dg(Pm,Wb)).astype(bf16)
        qt_ref[b,SPAN:]=Wb
        ds_ref[b]=dg(ek,Ub,0,0)+dg(ek,Ul,0,0)
        mh_ref[b,0],mh_ref[b,1]=halves(dg(ek,Wb,0,0)+dg(ek,Wl,0,0))
    loop(NC,solve,4)
    def chain(b,St):
        s_ref[b]=St
        sh,sl=halves(St); mh=mh_ref[b,0]
        return jnp.concatenate([gc_ref[b][0:1]]*(DV//128),axis=1)*St+ds_ref[b]-(dg(mh,sh)+(dg(mh,sl)+dg(mh_ref[b,1],sh)))
    lax.fori_loop(0,NC,chain,jnp.zeros((DK,DV),f32),unroll=2)
    def emit(b):
        rows=span(b)
        x=dg(qt_ref[b],s_ref[b].astype(bf16))
        do_ref[rows,:]=(dpre[rows,heads_v]+x[:SPAN]).astype(bf16)
        w_ref[b]=w_ref[b]-x[SPAN:]
    loop(NC,emit,4)
    seq_rows=lambda t: pl.ds(pl.multiple_of(t*ll,ll),ll)
    outward=FromPairs(n,copies,heads,ll,[(do_ref,lambda t: (seq_rows(t),slice(None)),oall,lambda seq,head: (seq_rows(seq),pl.ds(pl.multiple_of(head*DV,128),DV)))],r_.osend,r_.orecv)
    outward.start()

    gb[0].late(); gb[0].finish()
    c=pltpu.make_async_copy(r_.wgfull,wbuf.at[pl.ds(0,D),pl.ds(0,wv)],r_.ld.at[0,0]); c.start(); c.wait()
    def column(j):
        k_=pl.ds(pl.multiple_of(j*256,256),256)
        gate_ref[:,k_]=jnp.dot(normed[...],wbuf[0:D,k_],preferred_element_type=f32)
    loop(wv//256,column)
    gb[1].late(); gb[1].finish(); gb[2].middle()
    blocks=D//VW
    def load_wo(buf,sems):
        cs=[pltpu.make_async_copy(r_.wofull.at[:,pl.ds(j*VW,VW)],buf.at[pl.ds(j*VW,VW),pl.ds(0,VW)],sems.at[j]) for j in range(blocks)]
        for c in cs: c.start()
        return cs
    for c in load_wo(wbuf,r_.ld.at[0]): c.wait()
    outward.finish()
    def mix(c):
        r=pl.ds(pl.multiple_of(c*32,32),32)
        for h in range(heads):
            hc=pl.ds(h*DV,DV)
            o=oall[r,hc].astype(f32); g=gate_ref[r,hc]
            rho=lax.rsqrt(jnp.sum(o*o,axis=1,keepdims=True)/DV+EPSILON)
            branch[r,hc]=(o*rho*r_.hgain[...]*(g*sigmoid(g))).astype(bf16)
    loop(RN//32,mix)
    inner_tiles=VW//256
    def column(j):
        blk=lax.div(j,inner_tiles); at_=lax.rem(j,inner_tiles)
        w=wbuf[pl.ds(pl.multiple_of(blk*VW,16),VW),pl.ds(pl.multiple_of(at_*256,256),256)]
        pbf[:,pl.ds(pl.multiple_of(j*256,256),256)]=jnp.dot(branch[...],w,preferred_element_type=f32).astype(bf16)
    loop(D//256,column)
    split=ShardSplit(zc,pbf,r_.box,*zsems()); split.start()
    for d in range(1,n): pl.semaphore_signal(r_.free,inc=1,device_id={"seq":lax.rem(s+d,n)},device_id_type=MESH)
    pl.semaphore_wait(r_.free,n-1)
    gu[0].start()
    gu[1].middle()

    F_at=pl.ds(pl.multiple_of(z*F,128),F)
    fgain=r_.fgain[:,F_at]
    sums=r_.sums
    def shard_sum(k,rows8,meanwhile=None):
        sums[k*zc+z]=rows8
        tot=ShardAll("shard",zc,sums.at[pl.ds(k*zc,zc)],*zsems()); tot.start()
        if meanwhile: meanwhile()
        tot.finish()
        t=sums[k*zc]
        for d in range(1,zc): t=t+sums[k*zc+d]
        return col_form(t)[:,0:1]/D
    def boxed(box):
        g=box[0].astype(f32)
        for d in range(1,zc): g=g+box[d].astype(f32)
        return g
    res,gres,nloc,nfull,afull=r_.res,r_.gres,r_.nloc,r_.nfull,r_.normed
    split.finish()
    x=tok[...].astype(f32)+boxed(r_.box)
    res[...]=x
    sc=lax.rsqrt(shard_sum(0,row_form(x*x))+EPSILON)
    nloc[...]=(res[...]*sc*fgain).astype(bf16)
    zg=ShardGather(zc,nloc,nfull,*zsems()); zg.start()
    gb[2].late(); gb[2].finish(); gu[0].middle(); gu[1].late()
    gk=[gather(r_.dgp,r_.dgpfull,0),gather(branch,r_.brafull,0)]
    gk[1].start()
    zg.finish()
    for a,b in tiles(FF,512): gv[:,a:b]=jnp.dot(nfull[...],gw_[:,a:b],preferred_element_type=f32)
    gu[0].late(); gu[0].finish()
    for a,b in tiles(FF,512): uv[:,a:b]=jnp.dot(nfull[...],uw_[:,a:b],preferred_element_type=f32)
    hidden,dgate,dup=r_.hidden,r_.dgate,r_.dup
    def act(c):
        rr=pl.ds(pl.multiple_of(c*32,32),32)
        g=gv[rr,:]
        hidden[rr,:]=(g*sigmoid(g)*uv[rr,:]).astype(bf16)
    loop(RN//32,act)
    gh=[gather(hidden,r_.hidfull,0),gather(dgate,r_.dgfull,0),gather(dup,r_.dufull,0)]
    gu[1].finish()
    for a,b in tiles(FF,512):
        dh=dg(cotfull[...],dw_[a:b,:],1,1)
        g=gv[:,a:b]; sg=sigmoid(g)
        dgate[:,a:b]=(dh*uv[:,a:b]*sg*(1.0+g*(1.0-sg))).astype(bf16)
        dup[:,a:b]=(dh*(g*sg)).astype(bf16)
    each(gh[1:],"start")
    def back_two(j):
        rr=pl.ds(pl.multiple_of(j*256,256),256)
        pbf[:,rr]=(dg(dgate[...],gw_[rr,:],1,1)+dg(dup[...],uw_[rr,:],1,1)).astype(bf16)
    loop(D//256,back_two)
    split=ShardSplit(zc,pbf,r_.box,*zsems()); split.start()
    ld=r_.ld
    bufs=(r_.bufa,r_.bufb)
    loads={}
    def load_job(key,i,pieces):
        loads[key]=[]
        for j,(src,to) in enumerate(pieces):
            c=pltpu.make_async_copy(src,bufs[i].at[to],ld.at[i,j]); c.start(); loads[key].append(c)
    def ready(key):
        for c in loads[key]: c.wait()
    whole=lambda w: (pl.ds(0,D),pl.ds(0,w))
    every=lambda w: (pl.ds(0,N),pl.ds(0,w))
    loads["wo"]=load_wo(r_.bufa,ld.at[0])
    load_job("og",1,[(r_.wgfull,whole(wv))])
    def outp(j):
        c_=pl.ds(pl.multiple_of(j*256,256),256)
        r_.outpart[:,c_]=jnp.dot(hidden[...],dw_[:,c_],preferred_element_type=f32).astype(bf16)
    loop(D//256,outp)
    split.finish()
    gk[1].middle(); gh[1].middle()
    gh[0].start()
    g=boxed(r_.box)
    gained=fgain*g
    gffn=[None]
    def meanwhile(): gffn[0]=jnp.sum(g*res[...]*sc,axis=0,keepdims=True)
    inner=shard_sum(1,row_form(gained*res[...]),meanwhile)
    gr=cot[...].astype(f32)+sc*(gained-res[...]*(sc*sc*inner))
    gres[...]=gr
    nloc[...]=gr.astype(bf16)
    zg=ShardGather(zc,nloc,afull,*zsems()); zg.start()
    gh[2].middle()
    zg.finish()
    n2=SharedColumns(n,zc,nfull,r_.n2c,(*qsems(),*zsems())); n2.start()
    so=ShardSplit(zc,r_.outpart,r_.boxo,*zsems()); so.start()

    ready("wo")
    r_.dsm[...]=jnp.zeros(r_.dsm.shape,bf16)
    dob,dgp,bufa,bufb=r_.dob,r_.dgp,r_.bufa,r_.bufb
    def heads_back(c,gh_):
        r=pl.ds(pl.multiple_of(c*64,64),64)
        for h in range(heads):
            hc=pl.ds(h*DV,DV)
            dm=dg(afull[r,0:VW],bufa[h*DV:(h+1)*DV,0:VW],1,1)
            for j in range(1,blocks):
                dm=dm+dg(afull[r,j*VW:(j+1)*VW],bufa[j*VW+h*DV:j*VW+(h+1)*DV,0:VW],1,1)
            dm=dm.astype(bf16).astype(f32)
            o=oall[r,hc].astype(f32); g=gate_ref[r,hc]
            rho=lax.rsqrt(jnp.sum(o*o,axis=1,keepdims=True)/DV+EPSILON)
            zz=o*rho; sg=sigmoid(g); sil=g*sg
            gh_=gh_+jnp.sum(dm*zz*sil,axis=0,keepdims=True)
            dmg=dm*r_.hgain[...]
            dz=dmg*sil
            dob[r,hc],r_.dobl[r,hc]=halves(rho*(dz-zz*(jnp.sum(dz*zz,axis=1,keepdims=True)/DV)))
            dgp[r,hc]=(dmg*zz*sg*(1.0+g*(1.0-sg))).astype(bf16)
        return gh_
    grad_head=lax.fori_loop(0,RN//64,heads_back,jnp.zeros((1,DV),f32))
    inward=ToPairs(n,copies,heads,ll,(dob,r_.dobl),None,(do_ref,r_.dol),None,DK,DV,r_.i2send,r_.i2recv); inward.start(0); inward.start(1)
    each(gh[1:],"late"); gh[0].middle()
    gk[1].late()
    inward.finish()
    ca=SharedColumns(n,zc,afull,r_.attc,(*qsems(),*zsems())); ca.start()
    gk[0].start()

    dpre[L:L+8]=jnp.zeros((8,CH),f32)
    def early(b):
        ds_ref[b]=dg(qt_ref[b][0:SPAN],do_ref[span(b),:],0,0)+dg(qt_ref[b][0:SPAN],r_.dol[span(b),:],0,0)
    loop(NC,early,4)
    def chain_back(m,dS):
        b=NC-1-m
        x=ds_ref[b]
        ds_ref[b]=dS
        sh,sl=halves(dS); mh=mh_ref[b,0]
        return jnp.concatenate([gc_ref[b][0:1]]*(DV//128),axis=1)*dS+x-(dg(mh,sh,0,0)+(dg(mh,sl,0,0)+dg(mh_ref[b,1],sh,0,0)))
    lax.fori_loop(0,NC,chain_back,jnp.zeros((DK,DV),f32),unroll=2)
    def one_span(b,xr):
        rows=span(b)
        q=q_ref[rows,:]; k=k_ref[rows,:]; v=v_ref[rows,:]; dO=do_ref[rows,:]; dOl=r_.dol[rows,:]
        beta,Dm,gam,end,KK,QK,i,j=span_terms(b,q,k,starts,xc_ref[rows,:],xr)
        beta2=jnp.concatenate([beta]*(DV//128),axis=1)
        S0=s_ref[b]; dS1=ds_ref[b]
        S0h,S0l=halves(S0); dSh,dSl=halves(dS1)
        kf=k.astype(f32); qf=q.astype(f32); vf=v.astype(f32)
        W,Wl=halves(w_ref[b])
        Ph,Pl=halves(QK*Dm)
        dW=dg(Ph,dO,0,0)+(dg(Pl,dO,0,0)+dg(Ph,dOl,0,0))+jnp.concatenate([end]*(DV//128),axis=1)*(dg(k,dSh)+dg(k,dSl))
        Y=mm3(t_ref[b],dW,0,0)
        Yh,Yl=halves(Y)
        dOY=jnp.concatenate([dO,Yh],axis=0); dOYl=jnp.concatenate([dOl,Yl],axis=0)
        dPA=dg(dOY,W,1,1)+(dg(dOY,Wl,1,1)+dg(dOYl,W,1,1))
        GS=dg(dOY,S0h,1,1)+(dg(dOY,S0l,1,1)+dg(dOYl,S0h,1,1))
        dOS=GS[:SPAN]; YS=GS[SPAN:]
        Z=dg(W,dSh,1,1)+(dg(Wl,dSh,1,1)+dg(W,dSl,1,1))
        dPD=dPA[:SPAN]*Dm
        EA=jnp.where(i>j,-dPA[SPAN:]*Dm,0.0)
        A1=jnp.concatenate([dPD,beta[:,:SPAN]*EA],axis=0).astype(bf16)
        r1=dg(A1,k)
        r2=dg(A1,jnp.concatenate([q,k],axis=0),0,0)
        dpre[rows,0:DK]=gam*dOS+r1[:SPAN]
        dpre[rows,DK:2*DK]=r1[SPAN:]+r2-(beta*gam)*YS+end*Z
        dpre[rows,2*DK:]=beta2*Y
        EK=EA*KK
        kYS=jnp.sum(kf*YS,axis=1,keepdims=True)
        dbeta=jnp.sum(Y*vf,axis=1,keepdims=True)-gam*kYS+jnp.sum(EK,axis=1,keepdims=True)
        Fm=dPD*QK+beta[:,:SPAN]*EK
        dgam=jnp.sum(qf*dOS,axis=1,keepdims=True)-beta*kYS
        dend=jnp.sum(kf*Z,axis=1,keepdims=True)*end
        dG=jnp.sum(Fm,axis=1,keepdims=True)+dgam*gam-dend
        tail=jnp.sum(jnp.sum(S0*dS1,axis=0,keepdims=True),axis=1,keepdims=True)
        last=jnp.sum(dend,axis=0,keepdims=True)+gam[SPAN-1:SPAN]*tail
        row=lax.broadcasted_iota(jnp.int32,(SPAN,128),0)
        dG=dG+jnp.where(row==SPAN-1,last,0.0)
        dx_ref[rows,0:1]=(dbeta*beta*(1.0-beta))[:,0:1]
        dx_ref[rows,1:2]=dG[:,0:1]
        return jnp.sum(Fm,axis=0,keepdims=True)
    def local_back(m):
        r=pl.ds(pl.multiple_of(m*8,8),8)
        xr=xr_ref[r,:]
        dxr[r,:]=jnp.broadcast_to(jnp.concatenate([one_span(m*per+e,xr[:,e*SPAN:(e+1)*SPAN]) for e in range(per)],axis=1),(8,ll))
    loop(n,local_back,2)
    n2.middle(); ca.middle()
    il=lax.broadcasted_iota(jnp.int32,(ll,ll),0); jl=lax.broadcasted_iota(jnp.int32,(ll,ll),1)
    later=jnp.where((il>=jl)&((il//SPAN)==(jl//SPAN)),1.0,0.0)
    def turn_back(m,carry):
        r=pl.ds(pl.multiple_of(m*8,8),8)
        f=flat_form(dx_ref[pl.ds(pl.multiple_of(m*ll,ll),ll),0:8])
        dlog=mmx(jnp.broadcast_to(f[1:2]-dxr[r,:][0:1],(8,ll)),later)
        x=xr_ref[r,:]
        ddp=dlog*(-rate)*sigmoid(x[3:4]+bias)
        row=lax.broadcasted_iota(jnp.int32,(8,ll),0)
        dxr[r,:]=jnp.where(row==0,f[0:1],jnp.where(row==1,ddp,0.0))
        return (carry[0]+jnp.sum(dlog[0:1]*x[1:2],axis=1,keepdims=True),carry[1]+jnp.sum(ddp[0:1],axis=1,keepdims=True))
    zero=jnp.zeros((1,1),f32)
    sl,sb=lax.fori_loop(0,n,turn_back,(zero,zero),unroll=4)
    def norms(c,dt):
        base=pl.multiple_of(c*R,R)
        age=doc_age(starts,positions(base,R,128,0))[:,0:1]
        pre,window=conv_pre(u_ref,taps,age,base,R)
        sg=sigmoid(pre); a_=pre*sg
        rows=pl.ds(base,R)
        d=dpre[rows,:]
        def unit_back(a,dd,f):
            sc_=lax.rsqrt(jnp.sum(a*a,axis=1,keepdims=True)+EPSILON)
            dot=jnp.sum(a*dd,axis=1,keepdims=True)
            return f*(sc_*dd-a*(sc_*sc_*sc_*dot))
        dact=jnp.concatenate([unit_back(a_[:,:DK],d[:,:DK],DK**-0.5),unit_back(a_[:,DK:2*DK],d[:,DK:2*DK],1.0),d[:,2*DK:]],axis=1)
        dp=dact*sg*(1.0+pre*(1.0-sg))
        dpre[rows,:]=dp
        new=[]
        for j in range(4):
            back=3-j
            x=window[16-back:16-back+R]
            if back: x=x*jnp.where(age>=back,1.0,0.0)
            new.append(dt[j]+jnp.sum(x*dp,axis=0,keepdims=True))
        return tuple(new)
    dt=lax.fori_loop(0,L//R,norms,(jnp.zeros((1,CH),f32),)*4)
    def back(c):
        base=pl.multiple_of(c*R,R)
        window=dpre[pl.ds(base,R+8),:]
        age=doc_age(starts,positions(base,R+8,128,0))[:,0:1]
        d=window[:R]*taps[3:4]
        for sh in range(1,4):
            d=d+window[sh:sh+R]*jnp.where(age[sh:sh+R]>=sh,1.0,0.0)*taps[3-sh:4-sh]
        du_ref[pl.ds(base,R),:]=d.astype(bf16)
    loop(L//R,back)
    gk[0].middle()
    dyq,dsm=pbuf,r_.dsm
    cut=lambda start,width: (lambda t: (seq_rows(t),pl.ds(start,width)))
    to=lambda start,width: (lambda seq,head: (seq_rows(seq),pl.ds(pl.multiple_of(start+head*width,128),width)))
    outward=FromPairs(n,copies,heads,ll,[(du_ref,cut(0,DK),dyq,to(0,DK)),(du_ref,cut(DK,DK),dyq,to(wk,DK)),(du_ref,cut(2*DK,DV),dyq,to(2*wk,DV)),
        (dxr,lambda t: (pl.ds(pl.multiple_of(t*8,8),8),slice(None)),rbuf,lambda seq,head: (pl.ds(pl.multiple_of((seq*heads+head)*8,8),8),slice(None)))],r_.o2send,r_.o2recv)
    outward.start()

    part=r_.acc
    def spread(first,buf,terms):
        def one(j):
            rr=pl.ds(pl.multiple_of(j*256,256),256)
            t=0.0
            for x,a,b in terms: t=t+dg(x[...],buf[rr,a:b],1,1)
            part[:,rr]=t if first else part[:,rr]+t
        loop(D//256,one)
    staged={}
    def stage(k,ref,shape):
        if k in staged: staged[k].wait()
        return r_.sta.at[pl.ds(0,shape[0]),pl.ds(0,shape[1])] if k==0 else r_.stb.at[pl.ds(0,shape[0]),pl.ds(0,shape[1])]
    def send(k,view,ref):
        staged[k]=pltpu.make_async_copy(view,ref,r_.stsem.at[k]); staged[k].start()
    ready("og"); spread(True,bufb,[(dgp,0,wv)])
    gh[0].late(); n2.finish()
    each(gh,"finish")
    load_job("dgate",0,[(r_.dgfull,every(FF))])
    c2=pltpu.make_async_copy(r_.n2c,r_.cola,ld.at[0,4]); c2.start()
    load_job("wqk",1,[(r_.wfull.at[:,pl.ds(0,2*wk)],whole(2*wk))])
    so.finish()
    r_.output[...]=res[...]+boxed(r_.boxo)
    ready("dgate"); c2.wait()
    n2s=r_.cola[...].reshape(N,D//n)
    v_=stage(0,r_.ogate,(D//n,FF))
    for a,b in tiles(FF,512): v_[:,a:b]=dg(n2s,bufa[0:N,a:b],0,0)
    send(0,v_,r_.ogate)
    load_job("wv",0,[(r_.wfull.at[:,pl.ds(2*wk,wv+128)],whole(wv+128))])
    outward.finish()
    for sq in range(seqs):
        fl=[]
        for e in range(2):
            for h in range(heads): fl.append(rbuf[(sq*heads+h)*8+e:(sq*heads+h)*8+e+1])
        fl=jnp.concatenate(fl+[jnp.zeros((-2*heads%8,ll),f32)]*(1 if 2*heads%8 else 0),axis=0)
        dsm[sq*ll:(sq+1)*ll,0:fl.shape[0]]=col_form(fl).astype(bf16)
    gd=[gather(dsm,r_.dsmfull,0),gather(dyq,r_.dyqfull,0)]
    each(gd,"start")
    ready("wqk"); spread(False,bufb,[(dyq.at[:,pl.ds(0,2*wk)],0,2*wk)])
    load_job("dup",1,[(r_.dufull,every(FF))])
    ready("wv")
    def final(j):
        rr=pl.ds(pl.multiple_of(j*256,256),256)
        pbf[:,rr]=(part[:,rr]+dg(dyq[:,2*wk:],bufa[rr,0:wv],1,1)+dg(dsm[...],bufa[rr,wv:wv+128],1,1)).astype(bf16)
    loop(D//256,final)
    split=ShardSplit(zc,pbf,r_.box,*zsems()); split.start()
    load_job("hid",0,[(r_.hidfull,every(FF))])
    gk[0].late()
    ready("dup")
    v_=stage(0,r_.oup,(D//n,FF))
    for a,b in tiles(FF,512): v_[:,a:b]=dg(n2s,bufb[0:N,a:b],0,0)
    send(0,v_,r_.oup)
    n1.finish(); cc.finish(); ca.finish(); gk[0].finish()
    each(gd,"middle")
    cb=pltpu.make_async_copy(r_.cotc,r_.colb,ld.at[1,5]); cb.start()
    ready("hid"); cb.wait()
    cots=r_.colb[...].reshape(N,D//n)
    v_=stage(1,r_.odown,(FF,D//n))
    for a,b in tiles(FF,256): v_[a:b,:]=dg(bufa[0:N,a:b],cots,0,0)
    send(1,v_,r_.odown)
    load_job("dgp",0,[(r_.dgpfull,every(wv))])
    split.finish()
    g=boxed(r_.box)
    sc=scale[...][:,0:1]
    gained=r_.gain[:,F_at]*g
    smalls,totals=r_.smalls,r_.totals
    smalls[s]=jnp.zeros(smalls.shape[1:],f32)
    smalls[s,0:1,0:F]=jnp.sum(g*tok[...].astype(f32)*sc,axis=0,keepdims=True)
    smalls[s,1:2,0:F]=gffn[0]
    smalls[s,2:3,0:DV]=grad_head
    lane=lax.broadcasted_iota(jnp.int32,(1,128),1)
    first=jnp.where(lax.rem(s,copies)==0,1.0,0.0)
    smalls[s,3:4,0:128]=first*(jnp.where(lane==at_head,sl,0.0)+jnp.where(lane==H+at_head,sb,0.0))
    for j in range(4): smalls[s,4+j:5+j,0:CH]=dt[j]
    sa=ShardAll("seq",n,smalls,*qsems()); sa.start()
    inner=shard_sum(2,row_form(gained*tok[...].astype(f32)))
    r_.gtok[...]=gres[...]+sc*(gained-tok[...].astype(f32)*(sc*sc*inner))
    sa.finish()
    t=smalls[0]
    for d in range(1,n): t=t+smalls[d]
    totals[z]=t
    za=ShardAll("shard",zc,totals,*zsems()); za.start()
    cb=pltpu.make_async_copy(r_.attc,r_.colb,ld.at[1,5]); cb.start()
    gk[1].finish()
    load_job("bra",1,[(r_.brafull,every(VW))])
    ready("bra"); cb.wait()
    atts=r_.colb[...].reshape(N,D//n)
    v_=stage(1,r_.oout,(VW,D//n))
    for a,b in tiles(VW,256): v_[a:b,:]=dg(bufb[0:N,a:b],atts,0,0)
    send(1,v_,r_.oout)
    cb=pltpu.make_async_copy(r_.n1c,r_.colb,ld.at[1,5]); cb.start()
    ready("dgp"); cb.wait()
    n1s=r_.colb[...].reshape(N,D//n)
    v_=stage(0,r_.oog,(D//n,wv))
    for a,b in tiles(wv,512): v_[:,a:b]=dg(n1s,bufa[0:N,a:b],0,0)
    send(0,v_,r_.oog)
    each(gd,"late"); za.finish(); each(gd,"finish")
    staged[0].wait(); staged[1].wait()

def layer(n,zc,copies,heads,DK,DV,H,ins):
    names=("tok","cot","gain","hgain","fgain","starts","dlog","dbias","wb","wd","qc","kc","vc","wq","wk","wv","wg","wo","wgate","wup","wdown")
    RN,F=ins[0].shape; D=F*zc; seqs=ins[5].shape[0]; ll=RN//seqs; L=n*ll; NC=L//SPAN; pairs=n//copies
    wk=heads*DK; wv=heads*DV; CH=2*DK+DV; FF=ins[19].shape[1]; N=n*RN; Dc=D//n; W=max(F,CH)
    bw=max(FF,wv+128,2*wk); big=max(D,N)
    specs=[VM]*5+[SM]*3+[VM]*10+[ANY]*3
    outs=[("output",S((RN,F)),VM),("gtok",S((RN,F)),VM),("smalls",S((n,8,W)),VM),("totals",S((zc,8,W)),VM)]
    for name,shape in (("ogate",(Dc,FF)),("oup",(Dc,FF)),("odown",(FF,Dc)),("oout",(wv,Dc)),("oog",(Dc,wv))): outs.append((name,S(shape),ANY))
    for name,shape in (("dyqfull",(N,heads*CH)),("dsmfull",(N,128)),("n1c",(n,RN,Dc)),("cotc",(n,RN,Dc)),("attc",(n,RN,Dc)),("n2c",(n,RN,Dc)),("wfull",(D,heads*CH+128)),("wgfull",(D,wv)),("wofull",(wv,D)),
        ("hidfull",(N,FF)),("dgfull",(N,FF)),("dufull",(N,FF)),("dgpfull",(N,wv)),("brafull",(N,wv))): outs.append((name,S(shape,bf16),ANY))
    V=pltpu.VMEM; sem=pltpu.SemaphoreType.DMA
    scratch=[("scale",V((RN,128),f32)),("ws",V((Dc,128),bf16)),("sbuf",V((D,128),bf16)),("tbuf",V((CH,128),bf16)),("tokfull",V((RN,D),bf16)),("normed",V((RN,D),bf16)),("cotfull",V((RN,D),bf16)),
        ("nfull",V((RN,D),bf16)),("pbf",V((RN,D),bf16)),("outpart",V((RN,D),bf16)),("acc",V((RN,D),f32)),("uv",V((RN,FF),f32)),("gv",V((RN,FF),f32)),("rbuf",V((pairs*8,ll),f32)),("taps",V((4,CH),f32)),
        ("bufa",V((big,bw),bf16)),("bufb",V((big,bw),bf16)),("dw",V((FF,D),bf16)),("u",V((L+16,CH),bf16)),("xr",V((n*8,ll),f32)),("xc",V((L,8),f32)),("q",V((L,DK),bf16)),("k",V((L,DK),bf16)),("v",V((L,DV),bf16)),
        ("s",V((NC,DK,DV),f32)),("w",V((NC,SPAN,DV),f32)),("t",V((NC,SPAN,SPAN),f32)),("qt",V((NC,2*SPAN,DK),bf16)),("mh",V((NC,2,DK,DK),bf16)),("gc",V((NC,8,128),f32)),("ds",V((NC,DK,DV),f32)),
        ("dpre",V((L+8,CH),f32)),("du",V((L,CH),bf16)),("dx",V((L,SPAN),f32)),("do",V((L,DV),bf16)),("dxr",V((n*8,ll),f32)),("gate",V((RN,wv),f32)),("oall",V((RN,wv),bf16)),("branch",V((RN,wv),bf16)),
        ("dob",V((RN,wv),bf16)),("dobl",V((RN,wv),bf16)),("dol",V((L,DV),bf16)),("dgp",V((RN,wv),bf16)),("dsm",V((RN,128),bf16)),("res",V((RN,F),f32)),("gres",V((RN,F),f32)),("nloc",V((RN,F),bf16)),("box",V((zc,RN,F),bf16)),("boxo",V((zc,RN,F),bf16)),
        ("hidden",V((RN,FF),bf16)),("dgate",V((RN,FF),bf16)),("dup",V((RN,FF),bf16)),("sums",V((3*zc,8,RN),f32)),("cola",V((n,RN,Dc),bf16)),("colb",V((n,RN,Dc),bf16)),("sta",V((Dc,max(FF,wv)),f32)),("stb",V((max(FF,wv),Dc),f32)),
        ("zsend",sem((16,zc))),("zrecv",sem((16,zc))),("qsend",sem((6,n))),("qrecv",sem((6,n))),("gsend",sem((16,links(n)))),("grecv",sem((16,links(n)))),("gloc",sem((16,))),("isend",sem((4,n))),("irecv",sem((4,n))),("i2send",sem((2,n))),("i2recv",sem((2,n))),
        ("osend",sem((1,pairs))),("orecv",sem((1,pairs))),("o2send",sem((4,pairs))),("o2recv",sem((4,pairs))),("ld",sem((2,6))),("stsem",sem((2,))),("free",pltpu.SemaphoreType.REGULAR)]
    all_names=names+tuple(o[0] for o in outs)+tuple(x[0] for x in scratch)
    r=pl.pallas_call(functools.partial(layer_kernel,(n,zc,copies,heads,DK,DV,H),all_names),name="layer",out_shape=tuple(o[1] for o in outs),in_specs=specs,out_specs=tuple(o[2] for o in outs),
        scratch_shapes=[x[1] for x in scratch],compiler_params=pltpu.CompilerParams(collective_id=1,has_side_effects=True,vmem_limit_bytes=63*2**20))(*ins)
    return SimpleNamespace(**{o[0]:x for o,x in zip(outs,r)})


def last_kernel(n,copies,heads,DK,DV,F,H,n1c,dyq,dsm,smalls,totals,*refs):
    moved=refs[:7]; oq,ok,ov,ob,od,qc,kc,vc,onorm,offn,ohead,olog,obias=refs[7:20]; moved_out=refs[20:27]; buf,sem,msem=refs[27:30]; held=refs[30:]
    step=buf.shape[1]//4
    fetch=[pltpu.make_async_copy(a,b,msem.at[j]) for j,(a,b) in enumerate(zip(moved,held))]
    for c in fetch: c.start()
    jobs=[pltpu.make_async_copy(dyq.at[:,pl.ds(j*step,step)],buf.at[:,pl.ds(j*step,step)],sem.at[j]) for j in range(4)]
    for c in jobs: c.start()
    moves=[pltpu.make_async_copy(a,b,msem.at[j]) for j,(a,b) in enumerate(zip(held,moved_out))]
    for f,c in zip(fetch,moves): f.wait(); c.start()
    n1=n1c[...].reshape(n1c.shape[0]*n1c.shape[1],n1c.shape[2])
    sm=dg(dsm[...],n1,0,0)
    ob[...]=sm[0:heads]; od[...]=sm[heads:2*heads]
    wk=heads*DK
    got=0
    for ref,start in ((oq,0),(ok,wk),(ov,2*wk)):
        for a in range(0,ref.shape[1],256):
            b=min(a+256,ref.shape[1])
            while got*step<start+b: jobs[got].wait(); got+=1
            ref[:,a:b]=dg(n1,buf[:,start+a:start+b],0,0)
    zc=totals.shape[0]
    for z in range(zc):
        onorm[0:1,z*F:(z+1)*F]=totals[z,0:1,0:F]
        offn[0:1,z*F:(z+1)*F]=totals[z,1:2,0:F]
    t=totals[0]
    for z in range(1,zc): t=t+totals[z]
    ohead[...]=t[2:3,0:DV]
    olog[...]=t[3:4,0:H]; obias[...]=t[3:4,H:2*H]
    s=lax.axis_index("seq")
    head=lax.div(s*heads,n)
    taps=0.0
    for sq in range(n//copies//heads): taps=taps+smalls[(sq*heads+head)*copies]
    cq,cv=qc.shape[1],vc.shape[1]
    for part in range(n//heads):
        @pl.when(lax.rem(s,n//heads)==part)
        def _():
            qc[...]=taps[4:8,part*cq:(part+1)*cq]
            kc[...]=taps[4:8,DK+part*cq:DK+(part+1)*cq]
            vc[...]=taps[4:8,2*DK+part*cv:2*DK+(part+1)*cv]
    for c in moves: c.wait()
def last(n,copies,heads,DK,DV,F,H,n1c,dyq,dsm,smalls,totals,cq,cv,moved):
    D=F*totals.shape[0]; Dc=n1c.shape[2]
    r=pl.pallas_call(functools.partial(last_kernel,n,copies,heads,DK,DV,F,H),name="last",
      out_shape=(S((Dc,heads*DK)),S((Dc,heads*DK)),S((Dc,heads*DV)),S((heads,Dc)),S((heads,Dc)),S((4,cq)),S((4,cq)),S((4,cv)),S((1,D)),S((1,D)),S((1,DV)),S((1,H)),S((1,H)))+tuple(S(x.shape) for x in moved),
      in_specs=[VM,ANY,VM,VM,VM]+[ANY]*7,out_specs=(VM,)*13+(ANY,)*7,scratch_shapes=[pltpu.VMEM(dyq.shape,bf16),pltpu.SemaphoreType.DMA((4,)),pltpu.SemaphoreType.DMA((7,))]+[pltpu.VMEM(x.shape,f32) for x in moved],
      compiler_params=pltpu.CompilerParams(vmem_limit_bytes=56*2**20))(n1c,dyq,dsm,smalls,totals,*moved)
    return r


def per_device(
    tokens, doc_starts, norm_gain, query_weight, key_weight, value_weight, outgate_weight,
    beta_weight, decay_weight, query_conv, key_conv, value_conv, decay_log, decay_bias, head_gain,
    output_weight, ffn_gain, gate_weight, up_weight, down_weight, cotangent,
):
    seq_count, local_len, feature_part = tokens.shape
    row_count = seq_count * local_len
    shard_count = lax.axis_size("shard")
    seq_devices = lax.axis_size("seq")
    head_count = beta_weight.shape[1]
    key_dim = query_weight.shape[1] // head_count
    value_dim = value_weight.shape[1] // head_count
    pairs = seq_count * head_count
    copies = seq_devices // pairs
    flat = lambda x: x.reshape(row_count, x.shape[2])
    tokens_flat, cot_flat = flat(tokens), flat(cotangent)
    head_row, norm_row, ffn_row = head_gain[None], norm_gain[None], ffn_gain[None]
    ran = layer(
        seq_devices, shard_count, copies, head_count, key_dim, value_dim, decay_log.shape[0],
        (
            tokens_flat, cot_flat, norm_row, head_row, ffn_row, doc_starts, decay_log, decay_bias, beta_weight.T,
            decay_weight.T, query_conv.T, key_conv.T, value_conv.T, query_weight, key_weight, value_weight, outgate_weight,
            output_weight, gate_weight, up_weight, down_weight,
        ),
    )
    (
        out_query, out_key, out_value, out_beta, out_decay, out_qconv, out_kconv, out_vconv, out_norm, out_ffn, out_head,
        out_log, out_bias, output, grad_tokens, out_gate, out_up, out_down, out_output, out_outgate,
    ) = last(
        seq_devices, copies, head_count, key_dim, value_dim, feature_part, decay_log.shape[0], ran.n1c, ran.dyqfull,
        ran.dsmfull, ran.smalls, ran.totals, query_conv.shape[0], value_conv.shape[0],
        (ran.output, ran.gtok, ran.ogate, ran.oup, ran.odown, ran.oout, ran.oog),
    )
    shape3 = (seq_count, local_len, feature_part)
    return (
        output.reshape(shape3), grad_tokens.reshape(shape3), out_norm[0], out_query, out_key, out_value, out_outgate,
        out_beta.T, out_decay.T, out_qconv.T, out_kconv.T, out_vconv.T, out_log[0], out_bias[0], out_head[0], out_output,
        out_ffn[0], out_gate, out_up, out_down,
    )


def solution(mesh):
    P = PartitionSpec
    rows, cols = P("seq", "shard"), P("shard", "seq")
    both, acts = P(("shard", "seq"), None), P(None, "seq", "shard")
    return jax.shard_map(
        per_device,
        mesh=mesh,
        in_specs=(acts, P(), P()) + (rows,) * 6 + (both,) * 3 + (P(), P(), P(), cols, P(), rows, rows, cols, acts),
        out_specs=(acts, acts, P()) + (rows,) * 6 + (both,) * 3 + (P(), P(), P(), cols, P(), rows, rows, cols),
        check_vma=False,
    )
```

```python
import functools
from types import SimpleNamespace
import jax, jax.numpy as jnp
from jax import lax
from jax.experimental import pallas as pl
from jax.experimental.pallas import tpu as pltpu
from jax.sharding import PartitionSpec
f32=jnp.float32; bf16=jnp.bfloat16
SPAN=128
EPSILON=1e-6
HI=lax.Precision.HIGHEST

def dg(a,b,ca=1,cb=0):
    return lax.dot_general(a,b,(((ca,),(cb,)),((),())),preferred_element_type=f32)
def halves(x):
    h=x.astype(bf16)
    return h,(x-h.astype(f32)).astype(bf16)
def mm3(a,b,ca=1,cb=0):
    ah,al=halves(a); bh,bl=halves(b)
    return dg(ah,bh,ca,cb)+(dg(al,bh,ca,cb)+dg(ah,bl,ca,cb))
def mm1(a,b,ca=1,cb=0):
    return dg(a.astype(bf16),b.astype(bf16),ca,cb)
def mmx(a,b,ca=1,cb=0):
    return lax.dot_general(a,b,(((ca,),(cb,)),((),())),preferred_element_type=f32,precision=HI)

def square_masks():
    i=lax.broadcasted_iota(jnp.int32,(SPAN,SPAN),0); j=lax.broadcasted_iota(jnp.int32,(SPAN,SPAN),1)
    return i,j
def positions(base,rows,cols,axis):
    return base+lax.broadcasted_iota(jnp.int32,(rows,cols),axis)
class Row:
    def __init__(self,ref,row):
        self.ref=ref; self.row=row; self.shape=ref.shape[1:]
    def __getitem__(self,e):
        return self.ref[self.row,e]

def doc_count(starts,pos):
    n=jnp.zeros(pos.shape,jnp.int32)
    for e in range(starts.shape[0]):
        n=n+jnp.where(starts[e]<=pos,1,0)
    return n
def doc_age(starts,pos):
    s=jnp.zeros(pos.shape,jnp.int32)
    for e in range(starts.shape[0]):
        s=jnp.where(starts[e]<=pos,starts[e],s)
    return pos-s
def count_at(starts,p):
    n=jnp.int32(0)
    for e in range(starts.shape[0]):
        n=n+jnp.where(starts[e]<=p,1,0)
    return n
def sigmoid(x):
    return 1.0/(1.0+jnp.exp(-x))
def softplus(x):
    return jnp.maximum(x,0.0)+jnp.log(1.0+jnp.exp(-jnp.abs(x)))

def inverses(blocks_a,t_ref):
    i,j=square_masks()
    eye=jnp.where(i==j,1.0,0.0)
    blocks=range(t_ref.shape[0])
    for n in blocks: t_ref[n]=eye-jnp.where((i//2)==(j//2),blocks_a(n),0.0)
    size=2
    while size<SPAN:
        part=((i//(2*size))==(j//(2*size)))&((i//size)!=(j//size))
        x=[dg(jnp.where(part,blocks_a(n),0.0).astype(bf16),t_ref[n].astype(bf16)).astype(bf16) for n in blocks]
        for n in blocks: t_ref[n]=t_ref[n]-dg(t_ref[n].astype(bf16),x[n])
        size*=2
    for n in blocks:
        Tb=t_ref[n].astype(bf16); Ah,Al=halves(blocks_a(n))
        rest=eye-Tb.astype(f32)-(dg(Ah,Tb)+dg(Al,Tb))
        t_ref[n]=Tb.astype(f32)+dg(Tb,rest.astype(bf16))

def position_rows(raw,starts,base,rate,bias):
    r=raw.shape[1]
    row=lax.broadcasted_iota(jnp.int32,(8,r),0)
    g=-rate*softplus(raw[1:2]+bias)
    i=lax.broadcasted_iota(jnp.int32,(r,r),0); j=lax.broadcasted_iota(jnp.int32,(r,r),1)
    G=mmx(jnp.broadcast_to(g,(8,r)),jnp.where((i<=j)&((i//SPAN)==(j//SPAN)),1.0,0.0))
    docs=doc_count(starts,positions(base,8,r,1)).astype(f32)
    out=jnp.where(row==0,sigmoid(raw[0:1]),0.0)
    for k,x in ((1,g),(2,G),(3,raw[1:2]),(4,docs)): out=jnp.where(row==k,x,out)
    return out

def span_terms(n,q,k,starts,xc,xr):
    i,j=square_masks()
    before=count_at(starts,n*SPAN-1).astype(f32)
    wide=lambda c: jnp.broadcast_to(c,(SPAN,128))
    beta=wide(xc[:,0:1]); G=wide(xc[:,2:3]); docs=wide(xc[:,4:5])
    incl=(i>=j)&(docs[:,:SPAN]==xr[4:5])
    D=jnp.where(incl,jnp.exp(jnp.where(incl,G[:,:SPAN]-xr[2:3],0.0)),0.0)
    gam=jnp.where(docs==before,jnp.exp(G),0.0)
    end=jnp.where(docs==docs[SPAN-1:SPAN],jnp.exp(G[SPAN-1:SPAN]-G),0.0)
    KK=dg(k,k,1,1); QK=dg(q,k,1,1)
    return beta,D,gam,end,KK,QK,i,j


SM=pl.BlockSpec(memory_space=pltpu.SMEM); VM=pl.BlockSpec(memory_space=pltpu.VMEM)
def S(shape,dt=f32): return jax.ShapeDtypeStruct(shape,dt)


MESH=pl.DeviceIdType.MESH
ANY=pl.BlockSpec(memory_space=pl.ANY)

def flip(s,bit):
    return s+bit-2*bit*lax.rem(lax.div(s,bit),2)

def flips(s,mask):
    bit=1
    while bit<=mask:
        if mask&bit: s=flip(s,bit)
        bit*=2
    return s

def greet(n,zc):
    s=lax.axis_index("seq"); z=lax.axis_index("shard")
    bar=pltpu.get_barrier_semaphore()
    for d in range(1,n):
        pl.semaphore_signal(bar,inc=1,device_id={"seq":lax.rem(s+d,n)},device_id_type=MESH)
    for d in range(1,zc):
        pl.semaphore_signal(bar,inc=1,device_id={"shard":lax.rem(z+d,zc)},device_id_type=MESH)
    pl.semaphore_wait(bar,n-1+zc-1)

def links(n):
    return 8 if n==8 else n

class SeqGather:
    def __init__(self,n,src,dst,axis,sems,c0=0):
        self.n=n; self.src=src; self.dst=dst; self.axis=axis; self.send,self.recv,self.loc=sems
        self.R,self.C=src.shape
        self.r0=0; self.nr=self.R; self.c0=c0
        self.s=lax.axis_index("seq")
        self.open=[]
    def slot(self,t,a,b):
        if self.axis==0:
            return self.dst.at[pl.ds(pl.multiple_of(t*self.R+self.r0+a,16),b-a),pl.ds(self.c0,self.C)]
        return self.dst.at[pl.ds(self.r0+a,b-a),pl.ds(pl.multiple_of(t*self.C,128),self.C)]
    def copy(self,src,t,a,b,k,to):
        c=pltpu.make_async_remote_copy(src_ref=src,dst_ref=self.slot(t,a,b),send_sem=self.send.at[k],recv_sem=self.recv.at[k],device_id={"seq":to},device_id_type=MESH)
        c.start()
        return c
    def pass_on(self,t,a,b,k,to):
        return self.copy(self.slot(t,a,b),t,a,b,k,to)
    def start(self):
        s=self.s; nr=self.nr
        mine=self.src.at[pl.ds(self.r0,nr),:]
        self.own=pltpu.make_async_copy(mine,self.slot(s,0,nr),self.loc)
        self.own.start()
        masks=(2,4) if self.n==8 else range(2,self.n,2)
        self.direct=[self.copy(mine,s,0,nr,i+1,flips(s,m)) for i,m in enumerate(masks)]
        self.open.append(self.copy(mine,s,0,nr,0,flip(s,1)))
    def middle(self):
        s=self.s; nr=self.nr; h=nr//2
        if self.n!=8: return
        x,y=flip(s,2),flip(s,4)
        self.direct[0].wait_recv()
        fa=self.pass_on(x,0,h,3,y)
        self.open.append(self.pass_on(x,0,nr,5,flip(s,1)))
        self.direct[1].wait_recv()
        fb=self.pass_on(y,h,nr,4,x)
        self.open.append(self.pass_on(y,0,nr,6,flip(s,1)))
        self.diag=(fa,fb)
    def late(self):
        s=self.s; nr=self.nr
        if self.n==8:
            for f in self.diag: f.wait_recv()
            self.open.append(self.pass_on(flips(s,6),0,nr,7,flip(s,1)))
            for f in self.diag: f.wait_send()
        else:
            for i,m in enumerate(range(2,self.n,2)):
                self.direct[i].wait_recv()
                self.open.append(self.pass_on(flips(s,m),0,nr,self.n//2+i,flip(s,1)))
        for f in self.direct: f.wait_send()
    def finish(self):
        for f in self.open: f.wait()
        self.own.wait()

class ShardGather:
    def __init__(self,zc,src,dst,send,recv):
        self.zc=zc; self.src=src; self.dst=dst; self.send=send; self.recv=recv
        self.z=lax.axis_index("shard"); self.C=src.shape[1]
    def slot(self):
        return self.dst.at[:,pl.ds(pl.multiple_of(self.z*self.C,128),self.C)]
    def start(self):
        self.own=pltpu.make_async_copy(self.src,self.slot(),self.recv.at[0]); self.own.start()
        self.cs=[]
        for d in range(1,self.zc):
            c=pltpu.make_async_remote_copy(src_ref=self.src,dst_ref=self.slot(),send_sem=self.send.at[d],recv_sem=self.recv.at[d],device_id={"shard":lax.rem(self.z+d,self.zc)},device_id_type=MESH)
            c.start(); self.cs.append(c)
    def finish(self):
        for c in self.cs: c.wait()
        self.own.wait()

class ShardSplit:
    def __init__(self,zc,src,box,send,recv):
        self.zc=zc; self.src=src; self.box=box; self.send=send; self.recv=recv
        self.z=lax.axis_index("shard"); self.C=box.shape[2]
    def start(self):
        C=self.C
        self.own=pltpu.make_async_copy(self.src.at[:,pl.ds(pl.multiple_of(self.z*C,128),C)],self.box.at[0],self.recv.at[0]); self.own.start()
        self.cs=[]
        for d in range(1,self.zc):
            to=lax.rem(self.z+d,self.zc)
            c=pltpu.make_async_remote_copy(src_ref=self.src.at[:,pl.ds(pl.multiple_of(to*C,128),C)],dst_ref=self.box.at[d],send_sem=self.send.at[d],recv_sem=self.recv.at[d],device_id={"shard":to},device_id_type=MESH)
            c.start(); self.cs.append(c)
    def finish(self):
        for c in self.cs: c.wait()
        self.own.wait()

class ShardAll:
    def __init__(self,axis,n,box,send,recv):
        self.axis=axis; self.n=n; self.box=box; self.send=send; self.recv=recv; self.me=lax.axis_index(axis)
    def start(self):
        self.cs=[]
        for d in range(1,self.n):
            c=pltpu.make_async_remote_copy(src_ref=self.box.at[self.me],dst_ref=self.box.at[self.me],send_sem=self.send.at[d],recv_sem=self.recv.at[d],device_id={self.axis:lax.rem(self.me+d,self.n)},device_id_type=MESH)
            c.start(); self.cs.append(c)
    def finish(self):
        for c in self.cs: c.wait()

class ColumnSplit:
    def __init__(self,n,src,dst,send,recv):
        self.n=n; self.src=src; self.dst=dst; self.send=send; self.recv=recv
        self.s=lax.axis_index("seq"); self.C=dst.shape[1]; self.R=src.shape[0]
    def start(self):
        n,s,C,R=self.n,self.s,self.C,self.R
        to_rows=self.dst.at[pl.ds(pl.multiple_of(s*R,16),R),:]
        block=lambda t: self.src.at[:,pl.ds(pl.multiple_of(t*C,128),C)]
        self.own=pltpu.make_async_copy(block(s),to_rows,self.recv.at[0]); self.own.start()
        self.cs=[]
        for d in range(1,n):
            t=lax.rem(s+d,n)
            c=pltpu.make_async_remote_copy(src_ref=block(t),dst_ref=to_rows,send_sem=self.send.at[d],recv_sem=self.recv.at[d],device_id={"seq":t},device_id_type=MESH)
            c.start(); self.cs.append(c)
    def finish(self):
        for c in self.cs: c.wait()
        self.own.wait()

class ToPairs:
    def __init__(self,n,copies,heads,local_len,src,rows_src,dst,rows_dst,DK,DV,send,recv,off=0):
        self.cs=[]
        self.__dict__.update(n=n,copies=copies,heads=heads,ll=local_len,src=src,rows_src=rows_src,dst=dst,rows_dst=rows_dst,DK=DK,DV=DV,send=send,recv=recv,off=off)
    def parts(self,t):
        s=lax.axis_index("seq"); ll,DK,DV,heads=self.ll,self.DK,self.DV,self.heads
        pair=lax.div(t,self.copies); seq=lax.div(pair,heads); head=lax.rem(pair,heads)
        rows=pl.ds(pl.multiple_of(seq*ll,ll),ll); to=pl.ds(pl.multiple_of(s*ll+self.off,16),ll)
        if self.rows_src is None:
            return [(a.at[rows,pl.ds(pl.multiple_of(head*DV,128),DV)],b.at[to,:]) for a,b in zip(self.src,self.dst)]
        wk=heads*DK
        out=[]
        for start,width,at in ((0,DK,0),(wk,DK,DK),(2*wk,DV,2*DK)):
            out.append((self.src.at[rows,pl.ds(pl.multiple_of(start+head*width,128),width)],self.dst.at[to,pl.ds(at,width)]))
        out.append((self.rows_src.at[pl.ds(pl.multiple_of(pair*8,8),8),:],self.rows_dst.at[pl.ds(pl.multiple_of(s*8,8),8),:]))
        return out
    def start(self,i):
        s=lax.axis_index("seq")
        for d in range(self.n):
            t=lax.rem(s+d,self.n)
            a,b=self.parts(t)[i]
            if d==0: c=pltpu.make_async_copy(a,b,self.recv.at[i,0])
            else: c=pltpu.make_async_remote_copy(src_ref=a,dst_ref=b,send_sem=self.send.at[i,d],recv_sem=self.recv.at[i,d],device_id={"seq":t},device_id_type=MESH)
            c.start(); self.cs.append(c)
    def finish(self):
        for c in self.cs: c.wait()

class FromPairs:
    def __init__(self,n,copies,heads,local_len,items,send,recv):
        self.__dict__.update(n=n,copies=copies,heads=heads,items=items,send=send,recv=recv)
    def start(self):
        s=lax.axis_index("seq"); pairs=self.n//self.copies; p=lax.div(s,self.copies); r=lax.rem(s,self.copies)
        seq=lax.div(p,self.heads); head=lax.rem(p,self.heads); self.cs=[]
        for d in range(pairs):
            t=lax.rem(p+d,pairs)*self.copies+r
            for i,(src,at,dst,to) in enumerate(self.items):
                a=src.at[at(t)]; b=dst.at[to(seq,head)]
                if d==0: c=pltpu.make_async_copy(a,b,self.recv.at[i,0])
                else: c=pltpu.make_async_remote_copy(src_ref=a,dst_ref=b,send_sem=self.send.at[i,d],recv_sem=self.recv.at[i,d],device_id={"seq":t},device_id_type=MESH)
                c.start(); self.cs.append(c)
    def finish(self):
        for c in self.cs: c.wait()

def flat_form(cols):
    r=cols.shape[0]
    i=lax.broadcasted_iota(jnp.int32,(r,r),0); j=lax.broadcasted_iota(jnp.int32,(r,r),1)
    return mmx(cols,jnp.where(i==j,1.0,0.0),0,0)

class SharedColumns:
    def __init__(self,n,zc,src,dst,sems):
        self.n=n; self.zc=zc; self.src=src; self.dst=dst; self.send,self.recv,self.zsend,self.zrecv=sems
        self.s=lax.axis_index("seq"); self.z=lax.axis_index("shard"); self.C=dst.shape[2]; self.q=src.shape[0]//zc
    def start(self):
        rows=pl.ds(pl.multiple_of(self.z*self.q,16),self.q)
        block=lambda t: self.src.at[rows,pl.ds(pl.multiple_of(t*self.C,128),self.C)]
        self.cs=[]
        for d in range(self.n):
            t=lax.rem(self.s+d,self.n)
            if d==0: c=pltpu.make_async_copy(block(t),self.dst.at[self.s,rows,:],self.recv.at[0])
            else: c=pltpu.make_async_remote_copy(src_ref=block(t),dst_ref=self.dst.at[self.s,rows,:],send_sem=self.send.at[d],recv_sem=self.recv.at[d],device_id={"seq":t},device_id_type=MESH)
            c.start(); self.cs.append(c)
    def middle(self):
        for c in self.cs: c.wait()
        strip=self.dst.at[:,pl.ds(pl.multiple_of(self.z*self.q,16),self.q),:]
        self.cs=[]
        for d in range(1,self.zc):
            c=pltpu.make_async_remote_copy(src_ref=strip,dst_ref=strip,send_sem=self.zsend.at[d],recv_sem=self.zrecv.at[d],device_id={"shard":lax.rem(self.z+d,self.zc)},device_id_type=MESH)
            c.start(); self.cs.append(c)
    def finish(self):
        for c in self.cs: c.wait()

def row_form(cols):
    return mmx(jnp.ones((8,cols.shape[1]),f32),cols,1,1)

def col_form(rows):
    r=rows.shape[1]
    i=lax.broadcasted_iota(jnp.int32,(r,r),0); j=lax.broadcasted_iota(jnp.int32,(r,r),1)
    return mmx(jnp.where(i==j,1.0,0.0),rows,1,1)

def gathers(n,pairs,sems):
    send,recv,loc=sems
    return [SeqGather(n,src,dst,axis,(send.at[i],recv.at[i],loc.at[i]),*c0) for i,(src,dst,axis,*c0) in enumerate(pairs)]
def gather_sems(n,k):
    return [pltpu.SemaphoreType.DMA((k,links(n))),pltpu.SemaphoreType.DMA((k,links(n))),pltpu.SemaphoreType.DMA((k,))]
def pair_sems(k):
    return [pltpu.SemaphoreType.DMA((k,)),pltpu.SemaphoreType.DMA((k,))]
def each(ops,name):
    for o in ops: getattr(o,name)()


def conv_pre(u,taps,age,base,rows):
    window=u[pl.ds(base,rows+16),:].astype(f32)
    pre=window[16:]*taps[3:4]
    for back in range(1,4):
        ok=jnp.where(age>=back,1.0,0.0)
        pre=pre+window[16-back:16-back+rows]*ok*taps[3-back:4-back]
    return pre,window

def tiles(width,step): return [(a,min(a+step,width)) for a in range(0,width,step)]

def layer_kernel(cfg,names,*refs):
    n,zc,copies,heads,DK,DV,H=cfg
    r_=SimpleNamespace(**dict(zip(names,refs)))
    tok,cot=r_.tok,r_.cot
    RN,F=tok.shape; D=F*zc; seqs=r_.starts.shape[0]; ll=RN//seqs; L=n*ll; NC=L//SPAN; per=ll//SPAN
    wk=heads*DK; wv=heads*DV; CH=2*DK+DV; FF=r_.wup.shape[1]; N=n*RN; VW=wv
    s=lax.axis_index("seq"); z=lax.axis_index("shard")
    pair=lax.div(s,copies); my_head=lax.rem(pair,heads); at_head=z*heads+my_head
    starts=Row(r_.starts,lax.div(pair,heads))
    count=[0,0,0]
    def zsems():
        count[0]+=1; return r_.zsend.at[count[0]-1],r_.zrecv.at[count[0]-1]
    def qsems():
        count[1]+=1; return r_.qsend.at[count[1]-1],r_.qrecv.at[count[1]-1]
    def gather(src,dst,axis,c0=0):
        count[2]+=1; i=count[2]-1
        return SeqGather(n,src,dst,axis,(r_.gsend.at[i],r_.grecv.at[i],r_.gloc.at[i]),c0)
    def span(m): return pl.ds(pl.multiple_of(m*SPAN,SPAN),SPAN)
    def loop(count_,body,unroll=1): lax.fori_loop(0,count_,lambda i,c: (body(i),c)[1],0,unroll=unroll)
    normed,scale=r_.normed,r_.scale
    pbuf=r_.tokfull.at[:,pl.ds(0,heads*CH)]
    gw_=r_.bufa.at[pl.ds(0,D),pl.ds(0,FF)]; uw_=r_.bufb.at[pl.ds(0,D),pl.ds(0,FF)]; dw_=r_.dw
    wbuf=r_.bufb
    gv=r_.gv; uv=r_.uv
    cotfull,oall,branch,pbf,u_ref,taps_ref=r_.cotfull,r_.oall,r_.branch,r_.pbf,r_.u,r_.taps
    xr_ref,xc_ref,q_ref,k_ref,v_ref,s_ref,w_ref,t_ref,qt_ref,mh_ref,gc_ref=r_.xr,r_.xc,r_.q,r_.k,r_.v,r_.s,r_.w,r_.t,r_.qt,r_.mh,r_.gc
    gate_ref,rbuf,dpre,du_ref,dx_ref,do_ref,dxr,ds_ref=r_.gate,r_.rbuf,r_.dpre,r_.du,r_.dx,r_.do,r_.dxr,r_.ds
    heads_v=pl.ds(0,DV); rest_v=pl.ds(DV,DV)

    greet(n,zc)
    zt=ShardGather(zc,tok,r_.tokfull,*zsems()); zt.start()
    put=lambda x,first: dg(x[...],jnp.where(lax.broadcasted_iota(jnp.int32,(x.shape[0],128),0)+first==lax.broadcasted_iota(jnp.int32,(x.shape[0],128),1),1.0,0.0).astype(bf16),0,0)
    ws=r_.ws
    ws[...]=(put(r_.wb,0)+put(r_.wd,heads)).astype(bf16)
    at_row=0
    for x in (r_.qc,r_.kc,r_.vc):
        ws[at_row:at_row+x.shape[1]]=(ws[at_row:at_row+x.shape[1]].astype(f32)+put(x,2*heads)).astype(bf16)
        at_row+=x.shape[1]
    ws_all=(ws,r_.wq,r_.wk,r_.wv); at=(wk*2+wv,0,wk,wk*2)
    gw=[gather(w,r_.wfull,0,a) for w,a in zip(ws_all,at)]
    each(gw,"start")
    u_ref[0:16]=jnp.zeros((16,CH),bf16)
    rbuf[...]=jnp.zeros(rbuf.shape,f32)
    dx_ref[...]=jnp.zeros(dx_ref.shape,f32)
    rate=jnp.exp(jnp.full((1,1),r_.dlog[at_head],f32)); bias=r_.dbias[at_head]
    each(gw,"middle")
    gb=[gather(r_.wg,r_.wgfull,0),gather(r_.wo,r_.wofull,1),gather(r_.wgate,gw_,0)]
    gu=[gather(r_.wup,uw_,0),gather(r_.wdown,dw_,1)]
    gb[0].start()
    zt.finish()
    zk=ShardGather(zc,cot,cotfull,*zsems()); zk.start()
    def norm(c):
        r=pl.ds(pl.multiple_of(c*32,32),32)
        x=r_.tokfull[r,:].astype(f32)
        sc=lax.rsqrt(jnp.sum(x*x,axis=1,keepdims=True)/D+EPSILON)
        normed[r,:]=(x*sc*r_.gain[...]).astype(bf16)
        scale[r,:]=jnp.broadcast_to(sc,(32,128))
    loop(RN//32,norm)
    n1=SharedColumns(n,zc,normed,r_.n1c,(*qsems(),*zsems())); n1.start()
    inward=ToPairs(n,copies,heads,ll,pbuf,rbuf,u_ref,xr_ref,DK,DV,r_.isend,r_.irecv,16)
    for i,g in enumerate(gw):
        g.late(); g.finish()
        width=ws_all[i].shape[1]
        buf=r_.sbuf if i==0 else wbuf.at[pl.ds(0,D),pl.ds(0,width)]
        c=pltpu.make_async_copy(r_.wfull.at[:,pl.ds(at[i],width)],buf,r_.ld.at[0,0]); c.start(); c.wait()
        if i==0:
            small=jnp.dot(normed[...],r_.sbuf[...],preferred_element_type=f32)
            for sq in range(seqs):
                fl=flat_form(small[sq*ll:(sq+1)*ll,0:8*((2*heads+7)//8)])
                for h in range(heads):
                    base=(sq*heads+h)*8
                    rbuf[base:base+1]=fl[h:h+1]
                    rbuf[base+1:base+2]=fl[heads+h:heads+h+1]
            cq=wk//n; cv=wv//n; step=D//n
            for kind,(width_c,total,skip) in enumerate(((cq,DK,0),(cq,DK,cq),(cv,DV,2*cq))):
                for j in range(total//width_c):
                    dev=my_head*(total//width_c)+j
                    to=(0,DK,2*DK)[kind]+j*width_c
                    r_.tbuf[to:to+width_c]=r_.sbuf[pl.ds(pl.multiple_of(dev*step+skip,16),width_c),:]
            ident=jnp.where(lax.broadcasted_iota(jnp.int32,(CH,CH),0)==lax.broadcasted_iota(jnp.int32,(CH,CH),1),1.0,0.0).astype(bf16)
            tt=dg(r_.tbuf[...],ident,0,0)
            taps_ref[...]=tt[2*heads:2*heads+4]
        else:
            def column(j,i=i):
                pbuf[:,pl.ds(pl.multiple_of(at[i]+j*256,128),256)]=jnp.dot(normed[...],wbuf[0:D,pl.ds(pl.multiple_of(j*256,256),256)],preferred_element_type=f32).astype(bf16)
            loop(width//256,column)
        inward.start((3,0,1,2)[i])
    gb[1].start()
    zk.finish()
    cc=SharedColumns(n,zc,cotfull,r_.cotc,(*qsems(),*zsems())); cc.start()
    n1.middle()
    gb[0].middle()
    inward.finish()
    gb[2].start()
    cc.middle()

    def turn(m):
        r=pl.ds(pl.multiple_of(m*8,8),8)
        x=position_rows(xr_ref[r,:],starts,m*ll,rate,bias)
        xr_ref[r,:]=x
        xc_ref[pl.ds(pl.multiple_of(m*ll,ll),ll),:]=col_form(x)
    loop(n,turn,4)
    taps=taps_ref[...]
    R=128
    def conv(c):
        base=pl.multiple_of(c*R,R)
        age=doc_age(starts,positions(base,R,128,0))[:,0:1]
        pre,unused=conv_pre(u_ref,taps,age,base,R)
        act=pre*sigmoid(pre)
        rows=pl.ds(base,R)
        aq=act[:,:DK]; ak=act[:,DK:2*DK]
        q_ref[rows,:]=(aq*lax.rsqrt(jnp.sum(aq*aq,axis=1,keepdims=True)+EPSILON)*DK**-0.5).astype(bf16)
        k_ref[rows,:]=(ak*lax.rsqrt(jnp.sum(ak*ak,axis=1,keepdims=True)+EPSILON)).astype(bf16)
        v_ref[rows,:]=act[:,2*DK:].astype(bf16)
    loop(L//R,conv)
    gb[1].middle()
    gu[1].start()
    kcol,pcol,ecol=pl.ds(0,DK),pl.ds(DK,SPAN),pl.ds(DK+SPAN,DK)
    def local(m):
        xr=xr_ref[pl.ds(pl.multiple_of(m*8,8),8),:]
        for e in range(per):
            b=m*per+e; rows=span(b)
            q=q_ref[rows,:]; k=k_ref[rows,:]; v=v_ref[rows,:]
            beta,Dm,gam,end,KK,QK,i,j=span_terms(b,q,k,starts,xc_ref[rows,:],xr[:,e*SPAN:(e+1)*SPAN])
            dx_ref[rows,0:SPAN]=jnp.where(i>j,beta[:,:SPAN]*Dm*KK,0.0)
            kf=k.astype(f32)
            dpre[rows,rest_v]=jnp.concatenate([beta]*(DV//128),axis=1)*v.astype(f32)
            du_ref[rows,kcol]=((beta*gam)*kf).astype(bf16)
            du_ref[rows,pcol]=(QK*Dm).astype(bf16)
            qt_ref[b,0:SPAN]=(gam*q.astype(f32)).astype(bf16)
            du_ref[rows,ecol]=(end*kf).astype(bf16)
            gc_ref[b]=jnp.broadcast_to(gam[SPAN-1:SPAN],(8,128))
    loop(n,local,4)
    inverses(lambda b: dx_ref[b*SPAN:(b+1)*SPAN,0:SPAN],t_ref)
    def solve(b):
        rows=span(b)
        Th,Tl=halves(t_ref[b]); Vh,Vl=halves(dpre[rows,rest_v]); bk=du_ref[rows,kcol]
        U=dg(Th,Vh)+(dg(Tl,Vh)+dg(Th,Vl)); Wk=dg(Th,bk)+dg(Tl,bk)
        Ub,Ul=halves(U); Wb,Wl=halves(Wk); Pm=du_ref[rows,pcol]; ek=du_ref[rows,ecol]
        dpre[rows,heads_v]=dg(Pm,Ub)
        w_ref[b]=U
        qt_ref[b,0:SPAN]=(qt_ref[b,0:SPAN].astype(f32)-dg(Pm,Wb)).astype(bf16)
        qt_ref[b,SPAN:]=Wb
        ds_ref[b]=dg(ek,Ub,0,0)+dg(ek,Ul,0,0)
        mh_ref[b,0],mh_ref[b,1]=halves(dg(ek,Wb,0,0)+dg(ek,Wl,0,0))
    loop(NC,solve,4)
    def chain(b,St):
        s_ref[b]=St
        sh,sl=halves(St); mh=mh_ref[b,0]
        return jnp.concatenate([gc_ref[b][0:1]]*(DV//128),axis=1)*St+ds_ref[b]-(dg(mh,sh)+(dg(mh,sl)+dg(mh_ref[b,1],sh)))
    lax.fori_loop(0,NC,chain,jnp.zeros((DK,DV),f32),unroll=2)
    def emit(b):
        rows=span(b)
        x=dg(qt_ref[b],s_ref[b].astype(bf16))
        do_ref[rows,:]=(dpre[rows,heads_v]+x[:SPAN]).astype(bf16)
        w_ref[b]=w_ref[b]-x[SPAN:]
    loop(NC,emit,4)
    seq_rows=lambda t: pl.ds(pl.multiple_of(t*ll,ll),ll)
    outward=FromPairs(n,copies,heads,ll,[(do_ref,lambda t: (seq_rows(t),slice(None)),oall,lambda seq,head: (seq_rows(seq),pl.ds(pl.multiple_of(head*DV,128),DV)))],r_.osend,r_.orecv)
    outward.start()

    gb[0].late(); gb[0].finish()
    c=pltpu.make_async_copy(r_.wgfull,wbuf.at[pl.ds(0,D),pl.ds(0,wv)],r_.ld.at[0,0]); c.start(); c.wait()
    def column(j):
        k_=pl.ds(pl.multiple_of(j*256,256),256)
        gate_ref[:,k_]=jnp.dot(normed[...],wbuf[0:D,k_],preferred_element_type=f32)
    loop(wv//256,column)
    gb[1].late(); gb[1].finish(); gb[2].middle()
    blocks=D//VW
    def load_wo(buf,sems):
        cs=[pltpu.make_async_copy(r_.wofull.at[:,pl.ds(j*VW,VW)],buf.at[pl.ds(j*VW,VW),pl.ds(0,VW)],sems.at[j]) for j in range(blocks)]
        for c in cs: c.start()
        return cs
    for c in load_wo(wbuf,r_.ld.at[0]): c.wait()
    outward.finish()
    def mix(c):
        r=pl.ds(pl.multiple_of(c*32,32),32)
        for h in range(heads):
            hc=pl.ds(h*DV,DV)
            o=oall[r,hc].astype(f32); g=gate_ref[r,hc]
            rho=lax.rsqrt(jnp.sum(o*o,axis=1,keepdims=True)/DV+EPSILON)
            branch[r,hc]=(o*rho*r_.hgain[...]*(g*sigmoid(g))).astype(bf16)
    loop(RN//32,mix)
    inner_tiles=VW//256
    def column(j):
        blk=lax.div(j,inner_tiles); at_=lax.rem(j,inner_tiles)
        w=wbuf[pl.ds(pl.multiple_of(blk*VW,16),VW),pl.ds(pl.multiple_of(at_*256,256),256)]
        pbf[:,pl.ds(pl.multiple_of(j*256,256),256)]=jnp.dot(branch[...],w,preferred_element_type=f32).astype(bf16)
    loop(D//256,column)
    split=ShardSplit(zc,pbf,r_.box,*zsems()); split.start()
    for d in range(1,n): pl.semaphore_signal(r_.free,inc=1,device_id={"seq":lax.rem(s+d,n)},device_id_type=MESH)
    pl.semaphore_wait(r_.free,n-1)
    gu[0].start()
    gu[1].middle()

    F_at=pl.ds(pl.multiple_of(z*F,128),F)
    fgain=r_.fgain[:,F_at]
    sums=r_.sums
    def shard_sum(k,rows8,meanwhile=None):
        sums[k*zc+z]=rows8
        tot=ShardAll("shard",zc,sums.at[pl.ds(k*zc,zc)],*zsems()); tot.start()
        if meanwhile: meanwhile()
        tot.finish()
        t=sums[k*zc]
        for d in range(1,zc): t=t+sums[k*zc+d]
        return col_form(t)[:,0:1]/D
    def boxed(box):
        g=box[0].astype(f32)
        for d in range(1,zc): g=g+box[d].astype(f32)
        return g
    res,gres,nloc,nfull,afull=r_.res,r_.gres,r_.nloc,r_.nfull,r_.normed
    split.finish()
    x=tok[...].astype(f32)+boxed(r_.box)
    res[...]=x
    sc=lax.rsqrt(shard_sum(0,row_form(x*x))+EPSILON)
    nloc[...]=(res[...]*sc*fgain).astype(bf16)
    zg=ShardGather(zc,nloc,nfull,*zsems()); zg.start()
    gb[2].late(); gb[2].finish(); gu[0].middle(); gu[1].late()
    gk=[gather(r_.dgp,r_.dgpfull,0),gather(branch,r_.brafull,0)]
    gk[1].start()
    zg.finish()
    for a,b in tiles(FF,512): gv[:,a:b]=jnp.dot(nfull[...],gw_[:,a:b],preferred_element_type=f32)
    gu[0].late(); gu[0].finish()
    for a,b in tiles(FF,512): uv[:,a:b]=jnp.dot(nfull[...],uw_[:,a:b],preferred_element_type=f32)
    hidden,dgate,dup=r_.hidden,r_.dgate,r_.dup
    def act(c):
        rr=pl.ds(pl.multiple_of(c*32,32),32)
        g=gv[rr,:]
        hidden[rr,:]=(g*sigmoid(g)*uv[rr,:]).astype(bf16)
    loop(RN//32,act)
    gh=[gather(hidden,r_.hidfull,0),gather(dgate,r_.dgfull,0),gather(dup,r_.dufull,0)]
    gu[1].finish()
    for a,b in tiles(FF,512):
        dh=dg(cotfull[...],dw_[a:b,:],1,1)
        g=gv[:,a:b]; sg=sigmoid(g)
        dgate[:,a:b]=(dh*uv[:,a:b]*sg*(1.0+g*(1.0-sg))).astype(bf16)
        dup[:,a:b]=(dh*(g*sg)).astype(bf16)
    each(gh[1:],"start")
    def back_two(j):
        rr=pl.ds(pl.multiple_of(j*256,256),256)
        pbf[:,rr]=(dg(dgate[...],gw_[rr,:],1,1)+dg(dup[...],uw_[rr,:],1,1)).astype(bf16)
    loop(D//256,back_two)
    split=ShardSplit(zc,pbf,r_.box,*zsems()); split.start()
    ld=r_.ld
    bufs=(r_.bufa,r_.bufb)
    loads={}
    def load_job(key,i,pieces):
        loads[key]=[]
        for j,(src,to) in enumerate(pieces):
            c=pltpu.make_async_copy(src,bufs[i].at[to],ld.at[i,j]); c.start(); loads[key].append(c)
    def ready(key):
        for c in loads[key]: c.wait()
    whole=lambda w: (pl.ds(0,D),pl.ds(0,w))
    every=lambda w: (pl.ds(0,N),pl.ds(0,w))
    loads["wo"]=load_wo(r_.bufa,ld.at[0])
    load_job("og",1,[(r_.wgfull,whole(wv))])
    def outp(j):
        c_=pl.ds(pl.multiple_of(j*256,256),256)
        r_.outpart[:,c_]=jnp.dot(hidden[...],dw_[:,c_],preferred_element_type=f32).astype(bf16)
    loop(D//256,outp)
    split.finish()
    gk[1].middle(); gh[1].middle()
    gh[0].start()
    g=boxed(r_.box)
    gained=fgain*g
    gffn=[None]
    def meanwhile(): gffn[0]=jnp.sum(g*res[...]*sc,axis=0,keepdims=True)
    inner=shard_sum(1,row_form(gained*res[...]),meanwhile)
    gr=cot[...].astype(f32)+sc*(gained-res[...]*(sc*sc*inner))
    gres[...]=gr
    nloc[...]=gr.astype(bf16)
    zg=ShardGather(zc,nloc,afull,*zsems()); zg.start()
    gh[2].middle()
    zg.finish()
    n2=SharedColumns(n,zc,nfull,r_.n2c,(*qsems(),*zsems())); n2.start()
    so=ShardSplit(zc,r_.outpart,r_.boxo,*zsems()); so.start()

    ready("wo")
    r_.dsm[...]=jnp.zeros(r_.dsm.shape,bf16)
    dob,dgp,bufa,bufb=r_.dob,r_.dgp,r_.bufa,r_.bufb
    def heads_back(c,gh_):
        r=pl.ds(pl.multiple_of(c*64,64),64)
        for h in range(heads):
            hc=pl.ds(h*DV,DV)
            dm=dg(afull[r,0:VW],bufa[h*DV:(h+1)*DV,0:VW],1,1)
            for j in range(1,blocks):
                dm=dm+dg(afull[r,j*VW:(j+1)*VW],bufa[j*VW+h*DV:j*VW+(h+1)*DV,0:VW],1,1)
            dm=dm.astype(bf16).astype(f32)
            o=oall[r,hc].astype(f32); g=gate_ref[r,hc]
            rho=lax.rsqrt(jnp.sum(o*o,axis=1,keepdims=True)/DV+EPSILON)
            zz=o*rho; sg=sigmoid(g); sil=g*sg
            gh_=gh_+jnp.sum(dm*zz*sil,axis=0,keepdims=True)
            dmg=dm*r_.hgain[...]
            dz=dmg*sil
            dob[r,hc],r_.dobl[r,hc]=halves(rho*(dz-zz*(jnp.sum(dz*zz,axis=1,keepdims=True)/DV)))
            dgp[r,hc]=(dmg*zz*sg*(1.0+g*(1.0-sg))).astype(bf16)
        return gh_
    grad_head=lax.fori_loop(0,RN//64,heads_back,jnp.zeros((1,DV),f32))
    inward=ToPairs(n,copies,heads,ll,(dob,r_.dobl),None,(do_ref,r_.dol),None,DK,DV,r_.i2send,r_.i2recv); inward.start(0); inward.start(1)
    each(gh[1:],"late"); gh[0].middle()
    gk[1].late()
    inward.finish()
    ca=SharedColumns(n,zc,afull,r_.attc,(*qsems(),*zsems())); ca.start()
    gk[0].start()

    dpre[L:L+8]=jnp.zeros((8,CH),f32)
    def early(b):
        ds_ref[b]=dg(qt_ref[b][0:SPAN],do_ref[span(b),:],0,0)+dg(qt_ref[b][0:SPAN],r_.dol[span(b),:],0,0)
    loop(NC,early,4)
    def chain_back(m,dS):
        b=NC-1-m
        x=ds_ref[b]
        ds_ref[b]=dS
        sh,sl=halves(dS); mh=mh_ref[b,0]
        return jnp.concatenate([gc_ref[b][0:1]]*(DV//128),axis=1)*dS+x-(dg(mh,sh,0,0)+(dg(mh,sl,0,0)+dg(mh_ref[b,1],sh,0,0)))
    lax.fori_loop(0,NC,chain_back,jnp.zeros((DK,DV),f32),unroll=2)
    def one_span(b,xr):
        rows=span(b)
        q=q_ref[rows,:]; k=k_ref[rows,:]; v=v_ref[rows,:]; dO=do_ref[rows,:]; dOl=r_.dol[rows,:]
        beta,Dm,gam,end,KK,QK,i,j=span_terms(b,q,k,starts,xc_ref[rows,:],xr)
        beta2=jnp.concatenate([beta]*(DV//128),axis=1)
        S0=s_ref[b]; dS1=ds_ref[b]
        S0h,S0l=halves(S0); dSh,dSl=halves(dS1)
        kf=k.astype(f32); qf=q.astype(f32); vf=v.astype(f32)
        W,Wl=halves(w_ref[b])
        Ph,Pl=halves(QK*Dm)
        dW=dg(Ph,dO,0,0)+(dg(Pl,dO,0,0)+dg(Ph,dOl,0,0))+jnp.concatenate([end]*(DV//128),axis=1)*(dg(k,dSh)+dg(k,dSl))
        Y=mm3(t_ref[b],dW,0,0)
        Yh,Yl=halves(Y)
        dOY=jnp.concatenate([dO,Yh],axis=0); dOYl=jnp.concatenate([dOl,Yl],axis=0)
        dPA=dg(dOY,W,1,1)+(dg(dOY,Wl,1,1)+dg(dOYl,W,1,1))
        GS=dg(dOY,S0h,1,1)+(dg(dOY,S0l,1,1)+dg(dOYl,S0h,1,1))
        dOS=GS[:SPAN]; YS=GS[SPAN:]
        Z=dg(W,dSh,1,1)+(dg(Wl,dSh,1,1)+dg(W,dSl,1,1))
        dPD=dPA[:SPAN]*Dm
        EA=jnp.where(i>j,-dPA[SPAN:]*Dm,0.0)
        A1=jnp.concatenate([dPD,beta[:,:SPAN]*EA],axis=0).astype(bf16)
        r1=dg(A1,k)
        r2=dg(A1,jnp.concatenate([q,k],axis=0),0,0)
        dpre[rows,0:DK]=gam*dOS+r1[:SPAN]
        dpre[rows,DK:2*DK]=r1[SPAN:]+r2-(beta*gam)*YS+end*Z
        dpre[rows,2*DK:]=beta2*Y
        EK=EA*KK
        kYS=jnp.sum(kf*YS,axis=1,keepdims=True)
        dbeta=jnp.sum(Y*vf,axis=1,keepdims=True)-gam*kYS+jnp.sum(EK,axis=1,keepdims=True)
        Fm=dPD*QK+beta[:,:SPAN]*EK
        dgam=jnp.sum(qf*dOS,axis=1,keepdims=True)-beta*kYS
        dend=jnp.sum(kf*Z,axis=1,keepdims=True)*end
        dG=jnp.sum(Fm,axis=1,keepdims=True)+dgam*gam-dend
        tail=jnp.sum(jnp.sum(S0*dS1,axis=0,keepdims=True),axis=1,keepdims=True)
        last=jnp.sum(dend,axis=0,keepdims=True)+gam[SPAN-1:SPAN]*tail
        row=lax.broadcasted_iota(jnp.int32,(SPAN,128),0)
        dG=dG+jnp.where(row==SPAN-1,last,0.0)
        dx_ref[rows,0:1]=(dbeta*beta*(1.0-beta))[:,0:1]
        dx_ref[rows,1:2]=dG[:,0:1]
        return jnp.sum(Fm,axis=0,keepdims=True)
    def local_back(m):
        r=pl.ds(pl.multiple_of(m*8,8),8)
        xr=xr_ref[r,:]
        dxr[r,:]=jnp.broadcast_to(jnp.concatenate([one_span(m*per+e,xr[:,e*SPAN:(e+1)*SPAN]) for e in range(per)],axis=1),(8,ll))
    loop(n,local_back,2)
    n2.middle(); ca.middle()
    il=lax.broadcasted_iota(jnp.int32,(ll,ll),0); jl=lax.broadcasted_iota(jnp.int32,(ll,ll),1)
    later=jnp.where((il>=jl)&((il//SPAN)==(jl//SPAN)),1.0,0.0)
    def turn_back(m,carry):
        r=pl.ds(pl.multiple_of(m*8,8),8)
        f=flat_form(dx_ref[pl.ds(pl.multiple_of(m*ll,ll),ll),0:8])
        dlog=mmx(jnp.broadcast_to(f[1:2]-dxr[r,:][0:1],(8,ll)),later)
        x=xr_ref[r,:]
        ddp=dlog*(-rate)*sigmoid(x[3:4]+bias)
        row=lax.broadcasted_iota(jnp.int32,(8,ll),0)
        dxr[r,:]=jnp.where(row==0,f[0:1],jnp.where(row==1,ddp,0.0))
        return (carry[0]+jnp.sum(dlog[0:1]*x[1:2],axis=1,keepdims=True),carry[1]+jnp.sum(ddp[0:1],axis=1,keepdims=True))
    zero=jnp.zeros((1,1),f32)
    sl,sb=lax.fori_loop(0,n,turn_back,(zero,zero),unroll=4)
    def norms(c,dt):
        base=pl.multiple_of(c*R,R)
        age=doc_age(starts,positions(base,R,128,0))[:,0:1]
        pre,window=conv_pre(u_ref,taps,age,base,R)
        sg=sigmoid(pre); a_=pre*sg
        rows=pl.ds(base,R)
        d=dpre[rows,:]
        def unit_back(a,dd,f):
            sc_=lax.rsqrt(jnp.sum(a*a,axis=1,keepdims=True)+EPSILON)
            dot=jnp.sum(a*dd,axis=1,keepdims=True)
            return f*(sc_*dd-a*(sc_*sc_*sc_*dot))
        dact=jnp.concatenate([unit_back(a_[:,:DK],d[:,:DK],DK**-0.5),unit_back(a_[:,DK:2*DK],d[:,DK:2*DK],1.0),d[:,2*DK:]],axis=1)
        dp=dact*sg*(1.0+pre*(1.0-sg))
        dpre[rows,:]=dp
        new=[]
        for j in range(4):
            back=3-j
            x=window[16-back:16-back+R]
            if back: x=x*jnp.where(age>=back,1.0,0.0)
            new.append(dt[j]+jnp.sum(x*dp,axis=0,keepdims=True))
        return tuple(new)
    dt=lax.fori_loop(0,L//R,norms,(jnp.zeros((1,CH),f32),)*4)
    def back(c):
        base=pl.multiple_of(c*R,R)
        window=dpre[pl.ds(base,R+8),:]
        age=doc_age(starts,positions(base,R+8,128,0))[:,0:1]
        d=window[:R]*taps[3:4]
        for sh in range(1,4):
            d=d+window[sh:sh+R]*jnp.where(age[sh:sh+R]>=sh,1.0,0.0)*taps[3-sh:4-sh]
        du_ref[pl.ds(base,R),:]=d.astype(bf16)
    loop(L//R,back)
    gk[0].middle()
    dyq,dsm=pbuf,r_.dsm
    cut=lambda start,width: (lambda t: (seq_rows(t),pl.ds(start,width)))
    to=lambda start,width: (lambda seq,head: (seq_rows(seq),pl.ds(pl.multiple_of(start+head*width,128),width)))
    outward=FromPairs(n,copies,heads,ll,[(du_ref,cut(0,DK),dyq,to(0,DK)),(du_ref,cut(DK,DK),dyq,to(wk,DK)),(du_ref,cut(2*DK,DV),dyq,to(2*wk,DV)),
        (dxr,lambda t: (pl.ds(pl.multiple_of(t*8,8),8),slice(None)),rbuf,lambda seq,head: (pl.ds(pl.multiple_of((seq*heads+head)*8,8),8),slice(None)))],r_.o2send,r_.o2recv)
    outward.start()

    part=r_.acc
    def spread(first,buf,terms):
        def one(j):
            rr=pl.ds(pl.multiple_of(j*256,256),256)
            t=0.0
            for x,a,b in terms: t=t+dg(x[...],buf[rr,a:b],1,1)
            part[:,rr]=t if first else part[:,rr]+t
        loop(D//256,one)
    staged={}
    def stage(k,ref,shape):
        if k in staged: staged[k].wait()
        return r_.sta.at[pl.ds(0,shape[0]),pl.ds(0,shape[1])] if k==0 else r_.stb.at[pl.ds(0,shape[0]),pl.ds(0,shape[1])]
    def send(k,view,ref):
        staged[k]=pltpu.make_async_copy(view,ref,r_.stsem.at[k]); staged[k].start()
    ready("og"); spread(True,bufb,[(dgp,0,wv)])
    gh[0].late(); n2.finish()
    each(gh,"finish")
    load_job("dgate",0,[(r_.dgfull,every(FF))])
    c2=pltpu.make_async_copy(r_.n2c,r_.cola,ld.at[0,4]); c2.start()
    load_job("wqk",1,[(r_.wfull.at[:,pl.ds(0,2*wk)],whole(2*wk))])
    so.finish()
    r_.output[...]=res[...]+boxed(r_.boxo)
    ready("dgate"); c2.wait()
    n2s=r_.cola[...].reshape(N,D//n)
    v_=stage(0,r_.ogate,(D//n,FF))
    for a,b in tiles(FF,512): v_[:,a:b]=dg(n2s,bufa[0:N,a:b],0,0)
    send(0,v_,r_.ogate)
    load_job("wv",0,[(r_.wfull.at[:,pl.ds(2*wk,wv+128)],whole(wv+128))])
    outward.finish()
    for sq in range(seqs):
        fl=[]
        for e in range(2):
            for h in range(heads): fl.append(rbuf[(sq*heads+h)*8+e:(sq*heads+h)*8+e+1])
        fl=jnp.concatenate(fl+[jnp.zeros((-2*heads%8,ll),f32)]*(1 if 2*heads%8 else 0),axis=0)
        dsm[sq*ll:(sq+1)*ll,0:fl.shape[0]]=col_form(fl).astype(bf16)
    gd=[gather(dsm,r_.dsmfull,0),gather(dyq,r_.dyqfull,0)]
    each(gd,"start")
    ready("wqk"); spread(False,bufb,[(dyq.at[:,pl.ds(0,2*wk)],0,2*wk)])
    load_job("dup",1,[(r_.dufull,every(FF))])
    ready("wv")
    def final(j):
        rr=pl.ds(pl.multiple_of(j*256,256),256)
        pbf[:,rr]=(part[:,rr]+dg(dyq[:,2*wk:],bufa[rr,0:wv],1,1)+dg(dsm[...],bufa[rr,wv:wv+128],1,1)).astype(bf16)
    loop(D//256,final)
    split=ShardSplit(zc,pbf,r_.box,*zsems()); split.start()
    load_job("hid",0,[(r_.hidfull,every(FF))])
    gk[0].late()
    ready("dup")
    v_=stage(0,r_.oup,(D//n,FF))
    for a,b in tiles(FF,512): v_[:,a:b]=dg(n2s,bufb[0:N,a:b],0,0)
    send(0,v_,r_.oup)
    n1.finish(); cc.finish(); gk[0].finish()
    cb=pltpu.make_async_copy(r_.cotc,r_.colb,ld.at[1,5]); cb.start()
    ready("hid"); cb.wait()
    cots=r_.colb[...].reshape(N,D//n)
    v_=stage(1,r_.odown,(FF,D//n))
    for a,b in tiles(FF,256): v_[a:b,:]=dg(bufa[0:N,a:b],cots,0,0)
    send(1,v_,r_.odown)
    load_job("dgp",0,[(r_.dgpfull,every(wv))])
    cb=pltpu.make_async_copy(r_.n1c,r_.colb,ld.at[1,5]); cb.start()
    ready("dgp"); cb.wait()
    n1s=r_.colb[...].reshape(N,D//n)
    v_=stage(0,r_.oog,(D//n,wv))
    for a,b in tiles(wv,512): v_[:,a:b]=dg(n1s,bufa[0:N,a:b],0,0)
    send(0,v_,r_.oog)
    each(gd,"middle")
    ca.finish()
    split.finish()
    g=boxed(r_.box)
    sc=scale[...][:,0:1]
    gained=r_.gain[:,F_at]*g
    smalls,totals=r_.smalls,r_.totals
    smalls[s]=jnp.zeros(smalls.shape[1:],f32)
    smalls[s,0:1,0:F]=jnp.sum(g*tok[...].astype(f32)*sc,axis=0,keepdims=True)
    smalls[s,1:2,0:F]=gffn[0]
    smalls[s,2:3,0:DV]=grad_head
    lane=lax.broadcasted_iota(jnp.int32,(1,128),1)
    first=jnp.where(lax.rem(s,copies)==0,1.0,0.0)
    smalls[s,3:4,0:128]=first*(jnp.where(lane==at_head,sl,0.0)+jnp.where(lane==H+at_head,sb,0.0))
    for j in range(4): smalls[s,4+j:5+j,0:CH]=dt[j]
    sa=ShardAll("seq",n,smalls,*qsems()); sa.start()
    inner=shard_sum(2,row_form(gained*tok[...].astype(f32)))
    r_.gtok[...]=gres[...]+sc*(gained-tok[...].astype(f32)*(sc*sc*inner))
    sa.finish()
    t=smalls[0]
    for d in range(1,n): t=t+smalls[d]
    totals[z]=t
    za=ShardAll("shard",zc,totals,*zsems()); za.start()
    cb=pltpu.make_async_copy(r_.attc,r_.colb,ld.at[1,5]); cb.start()
    gk[1].finish()
    load_job("bra",1,[(r_.brafull,every(VW))])
    ready("bra"); cb.wait()
    atts=r_.colb[...].reshape(N,D//n)
    v_=stage(1,r_.oout,(VW,D//n))
    for a,b in tiles(VW,256): v_[a:b,:]=dg(bufb[0:N,a:b],atts,0,0)
    send(1,v_,r_.oout)
    each(gd,"late"); za.finish(); each(gd,"finish")
    staged[0].wait(); staged[1].wait()

def layer(n,zc,copies,heads,DK,DV,H,ins):
    names=("tok","cot","gain","hgain","fgain","starts","dlog","dbias","wb","wd","qc","kc","vc","wq","wk","wv","wg","wo","wgate","wup","wdown")
    RN,F=ins[0].shape; D=F*zc; seqs=ins[5].shape[0]; ll=RN//seqs; L=n*ll; NC=L//SPAN; pairs=n//copies
    wk=heads*DK; wv=heads*DV; CH=2*DK+DV; FF=ins[19].shape[1]; N=n*RN; Dc=D//n; W=max(F,CH)
    bw=max(FF,wv+128,2*wk); big=max(D,N)
    specs=[VM]*5+[SM]*3+[VM]*10+[ANY]*3
    outs=[("output",S((RN,F)),VM),("gtok",S((RN,F)),VM),("smalls",S((n,8,W)),VM),("totals",S((zc,8,W)),VM)]
    for name,shape in (("ogate",(Dc,FF)),("oup",(Dc,FF)),("odown",(FF,Dc)),("oout",(wv,Dc)),("oog",(Dc,wv))): outs.append((name,S(shape),ANY))
    for name,shape in (("dyqfull",(N,heads*CH)),("dsmfull",(N,128)),("n1c",(n,RN,Dc)),("cotc",(n,RN,Dc)),("attc",(n,RN,Dc)),("n2c",(n,RN,Dc)),("wfull",(D,heads*CH+128)),("wgfull",(D,wv)),("wofull",(wv,D)),
        ("hidfull",(N,FF)),("dgfull",(N,FF)),("dufull",(N,FF)),("dgpfull",(N,wv)),("brafull",(N,wv))): outs.append((name,S(shape,bf16),ANY))
    V=pltpu.VMEM; sem=pltpu.SemaphoreType.DMA
    scratch=[("scale",V((RN,128),f32)),("ws",V((Dc,128),bf16)),("sbuf",V((D,128),bf16)),("tbuf",V((CH,128),bf16)),("tokfull",V((RN,D),bf16)),("normed",V((RN,D),bf16)),("cotfull",V((RN,D),bf16)),
        ("nfull",V((RN,D),bf16)),("pbf",V((RN,D),bf16)),("outpart",V((RN,D),bf16)),("acc",V((RN,D),f32)),("uv",V((RN,FF),f32)),("gv",V((RN,FF),f32)),("rbuf",V((pairs*8,ll),f32)),("taps",V((4,CH),f32)),
        ("bufa",V((big,bw),bf16)),("bufb",V((big,bw),bf16)),("dw",V((FF,D),bf16)),("u",V((L+16,CH),bf16)),("xr",V((n*8,ll),f32)),("xc",V((L,8),f32)),("q",V((L,DK),bf16)),("k",V((L,DK),bf16)),("v",V((L,DV),bf16)),
        ("s",V((NC,DK,DV),f32)),("w",V((NC,SPAN,DV),f32)),("t",V((NC,SPAN,SPAN),f32)),("qt",V((NC,2*SPAN,DK),bf16)),("mh",V((NC,2,DK,DK),bf16)),("gc",V((NC,8,128),f32)),("ds",V((NC,DK,DV),f32)),
        ("dpre",V((L+8,CH),f32)),("du",V((L,CH),bf16)),("dx",V((L,SPAN),f32)),("do",V((L,DV),bf16)),("dxr",V((n*8,ll),f32)),("gate",V((RN,wv),f32)),("oall",V((RN,wv),bf16)),("branch",V((RN,wv),bf16)),
        ("dob",V((RN,wv),bf16)),("dobl",V((RN,wv),bf16)),("dol",V((L,DV),bf16)),("dgp",V((RN,wv),bf16)),("dsm",V((RN,128),bf16)),("res",V((RN,F),f32)),("gres",V((RN,F),f32)),("nloc",V((RN,F),bf16)),("box",V((zc,RN,F),bf16)),("boxo",V((zc,RN,F),bf16)),
        ("hidden",V((RN,FF),bf16)),("dgate",V((RN,FF),bf16)),("dup",V((RN,FF),bf16)),("sums",V((3*zc,8,RN),f32)),("cola",V((n,RN,Dc),bf16)),("colb",V((n,RN,Dc),bf16)),("sta",V((Dc,max(FF,wv)),f32)),("stb",V((max(FF,wv),Dc),f32)),
        ("zsend",sem((16,zc))),("zrecv",sem((16,zc))),("qsend",sem((6,n))),("qrecv",sem((6,n))),("gsend",sem((16,links(n)))),("grecv",sem((16,links(n)))),("gloc",sem((16,))),("isend",sem((4,n))),("irecv",sem((4,n))),("i2send",sem((2,n))),("i2recv",sem((2,n))),
        ("osend",sem((1,pairs))),("orecv",sem((1,pairs))),("o2send",sem((4,pairs))),("o2recv",sem((4,pairs))),("ld",sem((2,6))),("stsem",sem((2,))),("free",pltpu.SemaphoreType.REGULAR)]
    all_names=names+tuple(o[0] for o in outs)+tuple(x[0] for x in scratch)
    r=pl.pallas_call(functools.partial(layer_kernel,(n,zc,copies,heads,DK,DV,H),all_names),name="layer",out_shape=tuple(o[1] for o in outs),in_specs=specs,out_specs=tuple(o[2] for o in outs),
        scratch_shapes=[x[1] for x in scratch],compiler_params=pltpu.CompilerParams(collective_id=1,has_side_effects=True,vmem_limit_bytes=63*2**20))(*ins)
    return SimpleNamespace(**{o[0]:x for o,x in zip(outs,r)})


def last_kernel(n,copies,heads,DK,DV,F,H,n1c,dyq,dsm,smalls,totals,*refs):
    moved=refs[:7]; oq,ok,ov,ob,od,qc,kc,vc,onorm,offn,ohead,olog,obias=refs[7:20]; moved_out=refs[20:27]; buf,sem,msem=refs[27:30]; held=refs[30:]
    step=buf.shape[1]//4
    jobs=[pltpu.make_async_copy(dyq.at[:,pl.ds(j*step,step)],buf.at[:,pl.ds(j*step,step)],sem.at[j]) for j in range(4)]
    for c in jobs: c.start()
    fetch=[pltpu.make_async_copy(a,b,msem.at[j]) for j,(a,b) in enumerate(zip(moved,held))]
    for c in fetch: c.start()
    n1=n1c[...].reshape(n1c.shape[0]*n1c.shape[1],n1c.shape[2])
    sm=dg(dsm[...],n1,0,0)
    ob[...]=sm[0:heads]; od[...]=sm[heads:2*heads]
    wk=heads*DK
    got=0
    for ref,start in ((oq,0),(ok,wk),(ov,2*wk)):
        for a in range(0,ref.shape[1],256):
            b=min(a+256,ref.shape[1])
            while got*step<start+b: jobs[got].wait(); got+=1
            ref[:,a:b]=dg(n1,buf[:,start+a:start+b],0,0)
    moves=[pltpu.make_async_copy(a,b,msem.at[j]) for j,(a,b) in enumerate(zip(held,moved_out))]
    for f,c in zip(fetch,moves): f.wait(); c.start()
    zc=totals.shape[0]
    for z in range(zc):
        onorm[0:1,z*F:(z+1)*F]=totals[z,0:1,0:F]
        offn[0:1,z*F:(z+1)*F]=totals[z,1:2,0:F]
    t=totals[0]
    for z in range(1,zc): t=t+totals[z]
    ohead[...]=t[2:3,0:DV]
    olog[...]=t[3:4,0:H]; obias[...]=t[3:4,H:2*H]
    s=lax.axis_index("seq")
    head=lax.div(s*heads,n)
    taps=0.0
    for sq in range(n//copies//heads): taps=taps+smalls[(sq*heads+head)*copies]
    cq,cv=qc.shape[1],vc.shape[1]
    for part in range(n//heads):
        @pl.when(lax.rem(s,n//heads)==part)
        def _():
            qc[...]=taps[4:8,part*cq:(part+1)*cq]
            kc[...]=taps[4:8,DK+part*cq:DK+(part+1)*cq]
            vc[...]=taps[4:8,2*DK+part*cv:2*DK+(part+1)*cv]
    for c in moves: c.wait()
def last(n,copies,heads,DK,DV,F,H,n1c,dyq,dsm,smalls,totals,cq,cv,moved):
    D=F*totals.shape[0]; Dc=n1c.shape[2]
    r=pl.pallas_call(functools.partial(last_kernel,n,copies,heads,DK,DV,F,H),name="last",
      out_shape=(S((Dc,heads*DK)),S((Dc,heads*DK)),S((Dc,heads*DV)),S((heads,Dc)),S((heads,Dc)),S((4,cq)),S((4,cq)),S((4,cv)),S((1,D)),S((1,D)),S((1,DV)),S((1,H)),S((1,H)))+tuple(S(x.shape) for x in moved),
      in_specs=[VM,ANY,VM,VM,VM]+[ANY]*7,out_specs=(VM,)*13+(ANY,)*7,scratch_shapes=[pltpu.VMEM(dyq.shape,bf16),pltpu.SemaphoreType.DMA((4,)),pltpu.SemaphoreType.DMA((7,))]+[pltpu.VMEM(x.shape,f32) for x in moved],
      compiler_params=pltpu.CompilerParams(vmem_limit_bytes=56*2**20))(n1c,dyq,dsm,smalls,totals,*moved)
    return r


def per_device(
    tokens, doc_starts, norm_gain, query_weight, key_weight, value_weight, outgate_weight,
    beta_weight, decay_weight, query_conv, key_conv, value_conv, decay_log, decay_bias, head_gain,
    output_weight, ffn_gain, gate_weight, up_weight, down_weight, cotangent,
):
    seq_count, local_len, feature_part = tokens.shape
    row_count = seq_count * local_len
    shard_count = lax.axis_size("shard")
    seq_devices = lax.axis_size("seq")
    head_count = beta_weight.shape[1]
    key_dim = query_weight.shape[1] // head_count
    value_dim = value_weight.shape[1] // head_count
    pairs = seq_count * head_count
    copies = seq_devices // pairs
    flat = lambda x: x.reshape(row_count, x.shape[2])
    tokens_flat, cot_flat = flat(tokens), flat(cotangent)
    head_row, norm_row, ffn_row = head_gain[None], norm_gain[None], ffn_gain[None]
    ran = layer(
        seq_devices, shard_count, copies, head_count, key_dim, value_dim, decay_log.shape[0],
        (
            tokens_flat, cot_flat, norm_row, head_row, ffn_row, doc_starts, decay_log, decay_bias, beta_weight.T,
            decay_weight.T, query_conv.T, key_conv.T, value_conv.T, query_weight, key_weight, value_weight, outgate_weight,
            output_weight, gate_weight, up_weight, down_weight,
        ),
    )
    (
        out_query, out_key, out_value, out_beta, out_decay, out_qconv, out_kconv, out_vconv, out_norm, out_ffn, out_head,
        out_log, out_bias, output, grad_tokens, out_gate, out_up, out_down, out_output, out_outgate,
    ) = last(
        seq_devices, copies, head_count, key_dim, value_dim, feature_part, decay_log.shape[0], ran.n1c, ran.dyqfull,
        ran.dsmfull, ran.smalls, ran.totals, query_conv.shape[0], value_conv.shape[0],
        (ran.output, ran.gtok, ran.ogate, ran.oup, ran.odown, ran.oout, ran.oog),
    )
    shape3 = (seq_count, local_len, feature_part)
    return (
        output.reshape(shape3), grad_tokens.reshape(shape3), out_norm[0], out_query, out_key, out_value, out_outgate,
        out_beta.T, out_decay.T, out_qconv.T, out_kconv.T, out_vconv.T, out_log[0], out_bias[0], out_head[0], out_output,
        out_ffn[0], out_gate, out_up, out_down,
    )


def solution(mesh):
    P = PartitionSpec
    rows, cols = P("seq", "shard"), P("shard", "seq")
    both, acts = P(("shard", "seq"), None), P(None, "seq", "shard")
    return jax.shard_map(
        per_device,
        mesh=mesh,
        in_specs=(acts, P(), P()) + (rows,) * 6 + (both,) * 3 + (P(), P(), P(), cols, P(), rows, rows, cols, acts),
        out_specs=(acts, acts, P()) + (rows,) * 6 + (both,) * 3 + (P(), P(), P(), cols, P(), rows, rows, cols),
        check_vma=False,
    )
```
